32 devices in a mesh: crop: 2 (over y), row: 16 (over z, x, core).
Axes of the slice: x: 2, y: 2, z: 4, core: 2. Of those that a mesh axis runs over, the one named last changes fastest.
Arguments:
- pair: float32 [2, 64, 64, 128], P('crop', 'row'), may hold values from -6 to 6
- bins: int32 [2, 64, 64], P('crop', 'row'), may hold values from 0 to 63
- lengths: int32 [2], P('crop'), may hold values from 32 to 64, as said below
- mats: float32 [11, 128, 128], replicated, may hold values from -0.5 to 0.5
- mats_m: float32 [11, 128, 128], replicated, may hold values from -0.0010095568 to 0.0010095568
- mats_v: float32 [11, 128, 128], replicated, may hold values from 2.7901785e-07 to 1.1055424e-06
- pbias: float32 [128, 4], replicated, may hold values from -0.5 to 0.5
- pbias_m: float32 [128, 4], replicated, may hold values from -0.0010095568 to 0.0010095568
- pbias_v: float32 [128, 4], replicated, may hold values from 1.0528976e-08 to 4.2115904e-08
- head: float32 [128, 64], replicated, may hold values from -0.5 to 0.5
- head_m: float32 [128, 64], replicated, may hold values from -0.0010095568 to 0.0010095568
- head_v: float32 [128, 64], replicated, may hold values from 2.7901785e-07 to 1.1055424e-06
- norms: float32 [8, 128], replicated, may hold values from 0.5 to 1.5
- norms_m: float32 [8, 128], replicated, may hold values from -0.0010095568 to 0.0010095568
- norms_v: float32 [8, 128], replicated, may hold values from 2.7901785e-07 to 1.1055424e-06
Outputs:
- grad_norm: float32 [], replicated
- loss_sum: float32 [], replicated
- loss_count: float32 [], replicated
- mats_m_new: float32 [11, 128, 128], replicated
- mats_v_new: float32 [11, 128, 128], replicated
- mats_new: float32 [11, 128, 128], replicated
- mats_low: bfloat16 [11, 128, 128], replicated
- pbias_m_new: float32 [128, 4], replicated
- pbias_v_new: float32 [128, 4], replicated
- pbias_new: float32 [128, 4], replicated
- head_m_new: float32 [128, 64], replicated
- head_v_new: float32 [128, 64], replicated
- head_new: float32 [128, 64], replicated
- norms_m_new: float32 [8, 128], replicated
- norms_v_new: float32 [8, 128], replicated
- norms_new: float32 [8, 128], replicated
The draws below stay inside these ranges and needn't reach their ends.
Inputs may be any that keep to these rules, and one draw needn't show every extreme that they name: `lengths`: each crop's length lies between 32 and 64; in every draw some crop, drawn from the seed, has length 64.
All inputs are finite; a program needn't handle non-finite values.
Results may differ from the reference program's by a relative error of at most 0.0024.
The reference program's roundings to bfloat16 on the way (of `pl`) count: a program that leaves them out, or rounds other values in their place, can miss the bound.
Values may be sent and summed in bfloat16 or wider, within the bound.
No kernel may reach another device: no remote copies, remote signals or barrier semaphores. Data moves between devices by JAX's collectives and lax.ppermute only.
A program may use at most 512 MiB of HBM per device.

```python
import math
import jax
import jax.numpy as jnp
from jax import lax

C = 128
HEADS = 4
BINS = 64
STEP = 5
CROPS = 2
N = 64
NPARAM = 189952


def draw_lengths(key, part):
    key = jax.random.fold_in(key, 11)
    first, second = jax.random.split(key)
    spread = jax.random.randint(first, (CROPS,), N // 2, N + 1)
    full = jax.random.randint(second, (), 0, CROPS)
    return jnp.where(jnp.arange(CROPS) == full, N, spread).astype(jnp.int32)


def plant(drawn, own_key, low, largest):
    index_at = [jax.random.randint(jax.random.fold_in(own_key, axis), (), 0, length) for axis, length in enumerate(drawn.shape)]
    longest = drawn.shape.index(max(drawn.shape))
    neighbour = index_at[:longest] + [(index_at[longest] + 1) % drawn.shape[longest]] + index_at[longest + 1:]
    return drawn.at[tuple(index_at)].set(low).at[tuple(neighbour)].set(largest)


def level_of(stream_key, shape, shards, low, largest):
    factor_of, own = 1.0, jax.random.fold_in(stream_key, 6)
    for dim, shards_of in shards:
        heights = jnp.exp(jax.random.uniform(jax.random.fold_in(own, dim), (shards_of,), jnp.float32, low / len(shards), largest / len(shards)))
        factor_of = factor_of * jnp.repeat(heights, shape[dim] // shards_of).reshape([-1 if axis == dim else 1 for axis in range(len(shape))])
    return factor_of


def centred(key, dims, deviation, limit, cuts=(), dtype=jnp.bfloat16):
    drawn = deviation * jax.random.normal(key, dims, jnp.float32)
    if cuts:
        drawn = drawn * level_of(key, dims, cuts, -0.22, 0.18)
    return jnp.clip(drawn, -limit, limit).astype(dtype)


def setup_inputs(seed: int = 0) -> dict:
    arg_keys = jax.random.split(jax.random.key(seed), 16)
    return {
        "pair": centred(arg_keys[0], (CROPS, N, N, C), 1.0, 6.0, ((0, 2), (1, 16)), jnp.float32),
        "bins": plant(jax.random.randint(arg_keys[1], (CROPS, N, N), 0, BINS), jax.random.fold_in(arg_keys[1], 1), 0, BINS - 1).astype(jnp.int32),
        "lengths": draw_lengths(jax.random.fold_in(arg_keys[15], 71), 0),
        "mats": centred(arg_keys[3], (11, C, C), C ** -0.5, 0.5, (), jnp.float32),
        "mats_m": centred(arg_keys[4], (11, C, C), (0.11 * NPARAM ** -0.5), 0.0010095568, (), jnp.float32),
        "mats_v": jnp.clip(jnp.exp(jax.random.uniform(arg_keys[5], (11, C, C), jnp.float32, math.log(2.790178541545174e-07), math.log(1.1055424238293199e-06))), 2.790178541545174e-07, 1.1055424238293199e-06),
        "pbias": centred(arg_keys[6], (C, HEADS), C ** -0.5, 0.5, (), jnp.float32),
        "pbias_m": centred(arg_keys[7], (C, HEADS), (0.11 * NPARAM ** -0.5), 0.0010095568, (), jnp.float32),
        "pbias_v": jnp.clip(jnp.exp(jax.random.uniform(arg_keys[8], (C, HEADS), jnp.float32, math.log(1.0528975913359773e-08), math.log(4.211590365343909e-08))), 1.0528975913359773e-08, 4.211590365343909e-08),
        "head": centred(arg_keys[9], (C, BINS), C ** -0.5, 0.5, (), jnp.float32),
        "head_m": centred(arg_keys[10], (C, BINS), (0.11 * NPARAM ** -0.5), 0.0010095568, (), jnp.float32),
        "head_v": jnp.clip(jnp.exp(jax.random.uniform(arg_keys[11], (C, BINS), jnp.float32, math.log(2.790178541545174e-07), math.log(1.1055424238293199e-06))), 2.790178541545174e-07, 1.1055424238293199e-06),
        "norms": jnp.clip(1.0 + 0.1 * jax.random.normal(arg_keys[12], (8, C), jnp.float32), 0.5, 1.5),
        "norms_m": centred(arg_keys[13], (8, C), (0.11 * NPARAM ** -0.5), 0.0010095568, (), jnp.float32),
        "norms_v": jnp.clip(jnp.exp(jax.random.uniform(arg_keys[14], (8, C), jnp.float32, math.log(2.790178541545174e-07), math.log(1.1055424238293199e-06))), 2.790178541545174e-07, 1.1055424238293199e-06),
    }


@jax.custom_vjp
def low(v):
    return lax.optimization_barrier(v.astype(jnp.bfloat16)).astype(jnp.float32)

@jax.custom_vjp
def low_back(v):
    return v

def low_keep(v):
    return (low(v), None)

def low_pass(kept, grad):
    return (grad,)

def back_keep(v):
    return (v, None)

def back_low(kept, grad):
    return (low(grad),)
low.defvjp(low_keep, low_pass)
low_back.defvjp(back_keep, back_low)
HIGH = lax.Precision.HIGHEST
EPS_NORM = 1e-05
CLIP = 1.0
RATE = 0.05
BETA1 = 0.9
BETA2 = 0.95
ADAM_EPS = 1e-08
WDECAY = 0.01

def layer_norm(v, gain, shift):
    mean = lax.optimization_barrier(jnp.mean(v, axis=-1, keepdims=True))
    cent = v - mean
    var = lax.optimization_barrier(jnp.mean(cent * cent, axis=-1, keepdims=True))
    return cent * lax.rsqrt(var + EPS_NORM) * gain + shift

def project(v, weight):
    return low_back(jnp.einsum('ijc,cd->ijd', v, weight, precision=HIGH))

def forward(params, pair, bins, length):
    mats, pbias, head, norms = params
    wl = low(mats)
    pl = low(pbias)
    hl = low(head)
    width = mats.shape[1]
    count_tok = pair.shape[0]
    col_ok = jnp.arange(count_tok) < length
    pmask = (col_ok[:, None] & col_ok[None, :]).astype(jnp.float32)
    m3 = pmask[..., None]
    h0 = low(layer_norm(pair, norms[0], norms[1]))
    proj = project(h0, jnp.concatenate([wl[0], wl[1], wl[2], wl[3], wl[4]], axis=1))
    side_a = jax.nn.sigmoid(proj[..., width:2 * width]) * proj[..., :width] * m3
    side_b = jax.nn.sigmoid(proj[..., 3 * width:4 * width]) * proj[..., 2 * width:3 * width] * m3
    a_low = low(low_back(side_a))
    b_low = low(low_back(side_b))
    gate = jax.nn.sigmoid(proj[..., 4 * width:])
    prod = low_back(jnp.einsum('ikc,jkc->ijc', a_low, b_low, precision=HIGH))
    y_low = low(layer_norm(prod, norms[2], norms[3]))
    z1 = pair + gate * project(y_low, wl[5])
    h1 = low(layer_norm(z1, norms[4], norms[5]))
    qkvg = project(h1, jnp.concatenate([wl[6], wl[7], wl[8], wl[9]], axis=1))
    query = low(qkvg[..., :width])
    keys = low(qkvg[..., width:2 * width])
    values = low(qkvg[..., 2 * width:3 * width])
    gate2 = jax.nn.sigmoid(qkvg[..., 3 * width:])
    tbias = low(project(h1, pl))
    tb_heads = jnp.transpose(tbias, (2, 0, 1))
    heads = pbias.shape[1]
    size_head = width // heads

    def row_attn(args):
        qi, ki, vi = args
        qh = qi.reshape(count_tok, heads, size_head)
        kh = ki.reshape(count_tok, heads, size_head)
        vh = vi.reshape(count_tok, heads, size_head)
        score = jnp.einsum('jhd,khd->hjk', qh, kh, precision=HIGH) * size_head ** (-0.5) + tb_heads
        score = jnp.where(col_ok[None, None, :], score, -1000000000.0)
        score = low_back(score)
        prob = jax.nn.softmax(score, axis=-1)
        out = jnp.einsum('hjk,khd->jhd', low(prob), vh, precision=HIGH).reshape(count_tok, width)
        return low_back(out)
    att = lax.map(jax.checkpoint(row_attn), (query, keys, values))
    u_low = low(gate2 * att)
    z2 = z1 + project(u_low, wl[10])
    h2 = low(layer_norm(z2, norms[6], norms[7]))
    logits = project(h2, hl)
    lse = jax.nn.logsumexp(logits, axis=-1)
    onehot = (bins[..., None] == jnp.arange(logits.shape[-1])).astype(jnp.float32)
    pick = lax.optimization_barrier(jnp.sum(logits * onehot, axis=-1))
    return jnp.sum(pmask * (lse - pick))

def adam(weight, grad, first, second):
    first_new = BETA1 * first + (1.0 - BETA1) * grad
    second_new = BETA2 * second + (1.0 - BETA2) * grad * grad
    m_hat = first_new / (1.0 - BETA1 ** STEP)
    v_hat = second_new / (1.0 - BETA2 ** STEP)
    weight_new = weight - RATE * (m_hat / (jnp.sqrt(v_hat) + ADAM_EPS) + WDECAY * weight)
    return (first_new, second_new, weight_new)

def reference(pair, bins, lengths, mats, mats_m, mats_v, pbias, pbias_m, pbias_v, head, head_m, head_v, norms, norms_m, norms_v):
    params = (mats, pbias, head, norms)

    def total(prm):
        acc = jnp.float32(0.0)
        for crop in range(pair.shape[0]):
            acc = acc + forward(prm, pair[crop], bins[crop], lengths[crop])
        return acc
    loss_sum, pull = jax.vjp(total, params)
    grads = pull(jnp.float32(1.0))[0]
    count = jnp.float32(0.0)
    for crop in range(pair.shape[0]):
        col_ok = (jnp.arange(pair.shape[1]) < lengths[crop]).astype(jnp.float32)
        count = count + jnp.sum(col_ok) * jnp.sum(col_ok)
    grad_norm = jnp.sqrt(sum((jnp.sum(g * g) for g in grads)))
    factor = jnp.minimum(1.0, CLIP / grad_norm)
    firsts = (mats_m, pbias_m, head_m, norms_m)
    seconds = (mats_v, pbias_v, head_v, norms_v)
    res = [adam(w, g * factor, m, v) for w, g, m, v in zip(params, grads, firsts, seconds)]
    return (grad_norm, loss_sum, count, res[0][0], res[0][1], res[0][2], res[0][2].astype(jnp.bfloat16), res[1][0], res[1][1], res[1][2], res[2][0], res[2][1], res[2][2], res[3][0], res[3][1], res[3][2])
```

```python
import jax
import jax.numpy as jnp
from jax import lax
from jax.sharding import PartitionSpec as P

STEP = 5
SMALL = 64


EPS_NORM = 1e-05
CLIP = 1.0
RATE = 0.05
BETA1 = 0.9
BETA2 = 0.95
ADAM_EPS = 1e-08
WDECAY = 0.01


def norm_fwd(v, gain, shift):
    mean = jnp.mean(v, axis=-1, keepdims=True)
    cent = v - mean
    rstd = lax.rsqrt(jnp.mean(cent * cent, axis=-1, keepdims=True) + EPS_NORM)
    unit = cent * rstd
    return (unit * gain + shift, unit, rstd)


def norm_back(grad, unit, rstd, gain):
    dgain = jnp.sum(grad * unit, axis=(0, 1))
    dshift = jnp.sum(grad, axis=(0, 1))
    dunit = grad * gain
    dval = rstd * (
        dunit
        - jnp.mean(dunit, axis=-1, keepdims=True)
        - unit * jnp.mean(dunit * unit, axis=-1, keepdims=True)
    )
    return (dval, dgain, dshift)


def matmul(value, weight):
    flat = value.reshape(-1, value.shape[-1])
    out = jnp.dot(flat, weight, preferred_element_type=jnp.float32)
    return out.reshape(value.shape[:-1] + (weight.shape[1],))


def wgrad(value, grad):
    return jnp.einsum("ijc,ijd->cd", value, grad, preferred_element_type=jnp.float32)


def adam(weight, grad, first, second):
    first_new = BETA1 * first + (1.0 - BETA1) * grad
    second_new = BETA2 * second + (1.0 - BETA2) * grad * grad
    m_hat = first_new / (1.0 - BETA1**STEP)
    v_hat = second_new / (1.0 - BETA2**STEP)
    weight_new = weight - RATE * (m_hat / (jnp.sqrt(v_hat) + ADAM_EPS) + WDECAY * weight)
    return (first_new, second_new, weight_new)


def general_step(
    pair,
    bins,
    lengths,
    mats,
    mats_m,
    mats_v,
    pbias,
    pbias_m,
    pbias_v,
    head,
    head_m,
    head_v,
    norms,
    norms_m,
    norms_v,
):
    bf = jnp.bfloat16
    fl = jnp.float32
    width = mats.shape[1]
    rows = pair.shape[1]
    cols = pair.shape[2]
    heads = pbias.shape[1]
    size_head = width // heads
    scale = size_head ** (-0.5)
    start_pair = pair[0]
    first_row = lax.axis_index("row") * rows
    limit = lengths[0]
    row_ok = first_row + jnp.arange(rows) < limit
    col_ok = jnp.arange(cols) < limit
    pmask = (row_ok[:, None] & col_ok[None, :]).astype(fl)
    m3 = pmask[..., None]
    wl = mats.astype(bf)
    pl = pbias.astype(bf)
    hl = head.astype(bf)
    w_tri = jnp.concatenate([wl[0], wl[1], wl[2], wl[3], wl[4]], axis=1)
    w_att = jnp.concatenate([wl[6], wl[7], wl[8], wl[9]], axis=1)
    h0, unit0, rstd0 = norm_fwd(start_pair, norms[0], norms[1])
    h0b = h0.astype(bf)
    proj = matmul(h0b, w_tri)
    sig_a = jax.nn.sigmoid(proj[..., width : 2 * width])
    sig_b = jax.nn.sigmoid(proj[..., 3 * width : 4 * width])
    gate = jax.nn.sigmoid(proj[..., 4 * width :])
    a_low = (sig_a * proj[..., :width] * m3).astype(bf)
    b_low = (sig_b * proj[..., 2 * width : 3 * width] * m3).astype(bf)
    b_all = lax.all_gather(b_low, "row", axis=0, tiled=True)
    prod = jnp.einsum("ikc,jkc->ijc", a_low, b_all, preferred_element_type=fl)
    y_val, unit2, rstd2 = norm_fwd(prod, norms[2], norms[3])
    y_low = y_val.astype(bf)
    out1 = matmul(y_low, wl[5])
    z1 = start_pair + gate * out1
    h1, unit4, rstd4 = norm_fwd(z1, norms[4], norms[5])
    h1b = h1.astype(bf)
    qkvg = matmul(h1b, w_att)
    query = qkvg[..., :width].astype(bf).reshape(rows, cols, heads, size_head)
    keys = qkvg[..., width : 2 * width].astype(bf).reshape(rows, cols, heads, size_head)
    values = qkvg[..., 2 * width : 3 * width].astype(bf).reshape(rows, cols, heads, size_head)
    gate2 = jax.nn.sigmoid(qkvg[..., 3 * width :])
    tb_low = matmul(h1b, pl).astype(bf)
    tb_all = lax.all_gather(tb_low, "row", axis=0, tiled=True)
    tb_heads = jnp.transpose(tb_all, (2, 0, 1)).astype(fl)
    scores = (
        jnp.einsum("ijhd,ikhd->ihjk", query, keys, preferred_element_type=fl) * scale
        + tb_heads[None]
    )
    scores = jnp.where(col_ok[None, None, None, :], scores, -1000000000.0)
    probs = jax.nn.softmax(scores, axis=-1)
    p_low = probs.astype(bf)
    att = jnp.einsum("ihjk,ikhd->ijhd", p_low, values, preferred_element_type=fl).reshape(
        rows, cols, width
    )
    u_low = (gate2 * att).astype(bf)
    z2 = z1 + matmul(u_low, wl[10])
    h2, unit6, rstd6 = norm_fwd(z2, norms[6], norms[7])
    h2b = h2.astype(bf)
    logits = matmul(h2b, hl)
    lse = jax.nn.logsumexp(logits, axis=-1)
    onehot = (bins[0][..., None] == jnp.arange(logits.shape[-1])).astype(fl)
    pick = jnp.sum(logits * onehot, axis=-1)
    loss = jnp.sum(pmask * (lse - pick))
    count = jnp.sum(pmask)
    dlog = (m3 * (jnp.exp(logits - lse[..., None]) - onehot)).astype(bf)
    dhead = wgrad(h2b, dlog)
    dz2, dg6, ds6 = norm_back(matmul(dlog, hl.T), unit6, rstd6, norms[6])
    dout2 = dz2.astype(bf)
    dw10 = wgrad(u_low, dout2)
    du = matmul(dout2, wl[10].T)
    dgate2 = du * att
    datt = (du * gate2).astype(bf).reshape(rows, cols, heads, size_head)
    dprob = jnp.einsum("ijhd,ikhd->ihjk", datt, values, preferred_element_type=fl)
    dvals = jnp.einsum("ihjk,ijhd->ikhd", p_low, datt, preferred_element_type=fl)
    dscore = (probs * (dprob - jnp.sum(dprob * probs, axis=-1, keepdims=True))).astype(bf)
    dquery = jnp.einsum("ihjk,ikhd->ijhd", dscore, keys, preferred_element_type=fl) * scale
    dkeys = jnp.einsum("ihjk,ijhd->ikhd", dscore, query, preferred_element_type=fl) * scale
    dtb = jnp.sum(dscore.astype(fl), axis=0)
    dtb_own = lax.psum_scatter(dtb, "row", scatter_dimension=1, tiled=True)
    dtb_low = jnp.transpose(dtb_own, (1, 2, 0)).astype(bf)
    dpbias = wgrad(h1b, dtb_low)
    dqkvg = jnp.concatenate(
        [
            dquery.reshape(rows, cols, width),
            dkeys.reshape(rows, cols, width),
            dvals.reshape(rows, cols, width),
            dgate2 * gate2 * (1.0 - gate2),
        ],
        axis=-1,
    ).astype(bf)
    dw_att = wgrad(h1b, dqkvg)
    dh1 = matmul(dqkvg, w_att.T) + matmul(dtb_low, pl.T)
    dn4, dg4, ds4 = norm_back(dh1, unit4, rstd4, norms[4])
    dz1 = dz2 + dn4
    dout1 = (dz1 * gate).astype(bf)
    dw5 = wgrad(y_low, dout1)
    dgate = dz1 * out1
    dxn, dg2, ds2 = norm_back(matmul(dout1, wl[5].T), unit2, rstd2, norms[2])
    dx_low = dxn.astype(bf)
    dside_a = jnp.einsum("ijc,jkc->ikc", dx_low, b_all, preferred_element_type=fl)
    dside_b = lax.psum_scatter(
        jnp.einsum("ijc,ikc->jkc", dx_low, a_low, preferred_element_type=fl),
        "row",
        scatter_dimension=0,
        tiled=True,
    )
    da_r = dside_a.astype(bf).astype(fl)
    db_r = dside_b.astype(bf).astype(fl)
    dproj = jnp.concatenate(
        [
            da_r * sig_a * m3,
            da_r * proj[..., :width] * m3 * sig_a * (1.0 - sig_a),
            db_r * sig_b * m3,
            db_r * proj[..., 2 * width : 3 * width] * m3 * sig_b * (1.0 - sig_b),
            dgate * gate * (1.0 - gate),
        ],
        axis=-1,
    ).astype(bf)
    dw_tri = wgrad(h0b, dproj)
    dh0 = matmul(dproj, w_tri.T)
    unused, dg0, ds0 = norm_back(dh0, unit0, rstd0, norms[0])
    pieces = [dw_tri[:, idx * width : (idx + 1) * width] for idx in range(5)]
    pieces = (
        pieces + [dw5] + [dw_att[:, idx * width : (idx + 1) * width] for idx in range(4)] + [dw10]
    )
    dmats = jnp.stack(pieces)
    dnorms = jnp.stack([dg0, ds0, dg2, ds2, dg4, ds4, dg6, ds6])
    dmats, dpbias, dhead, dnorms, loss, count = lax.psum(
        (dmats, dpbias, dhead, dnorms, loss, count), ("crop", "row")
    )
    grad_norm = jnp.sqrt(
        jnp.sum(dmats * dmats)
        + jnp.sum(dpbias * dpbias)
        + jnp.sum(dhead * dhead)
        + jnp.sum(dnorms * dnorms)
    )
    factor = jnp.minimum(1.0, CLIP / grad_norm)
    new_mats = adam(mats, dmats * factor, mats_m, mats_v)
    new_pbias = adam(pbias, dpbias * factor, pbias_m, pbias_v)
    new_head = adam(head, dhead * factor, head_m, head_v)
    new_norms = adam(norms, dnorms * factor, norms_m, norms_v)
    return (
        grad_norm,
        loss,
        count,
        new_mats[0],
        new_mats[1],
        new_mats[2],
        new_mats[2].astype(bf),
        new_pbias[0],
        new_pbias[1],
        new_pbias[2],
        new_head[0],
        new_head[1],
        new_head[2],
        new_norms[0],
        new_norms[1],
        new_norms[2],
    )


def same_core_groups(size):
    return [list(range(core, size, 2)) for core in range(2)]


def core_swap(value, size):
    return lax.ppermute(value, "row", [(idx, idx ^ 1) for idx in range(size)])


def gather_rows(value, size):
    chips = size // 2
    copies = jnp.broadcast_to(value[None], (chips,) + value.shape)
    mine = lax.all_to_all(
        copies, "row", 0, 0, axis_index_groups=same_core_groups(size), tiled=True
    )
    other = core_swap(mine, size)
    first = lax.axis_index("row") % 2 == 0
    even = jnp.where(first, mine, other)
    odd = jnp.where(first, other, mine)
    both = jnp.stack([even, odd], axis=1)
    return both.reshape((size * value.shape[0],) + value.shape[1:])


def sum_everywhere(flat, crops, size):
    rows = flat.shape[0]
    core = lax.axis_index("row") % 2
    halves = flat.reshape(2, rows // 2, flat.shape[1])
    keep = lax.dynamic_index_in_dim(halves, core, 0, keepdims=False)
    give = lax.dynamic_index_in_dim(halves, 1 - core, 0, keepdims=False)
    half = keep + core_swap(give, size)
    count = crops * size // 2
    groups = [
        [crop * size + idx for crop in range(crops) for idx in range(core_at, size, 2)]
        for core_at in range(2)
    ]
    parts = lax.all_to_all(
        half.reshape(count, -1, flat.shape[1]),
        ("crop", "row"),
        0,
        0,
        axis_index_groups=groups,
        tiled=True,
    )
    total = jnp.sum(parts, axis=0)
    copies = jnp.broadcast_to(total[None], (count,) + total.shape)
    mine = lax.all_to_all(
        copies, ("crop", "row"), 0, 0, axis_index_groups=groups, tiled=True
    ).reshape(rows // 2, -1)
    other = core_swap(mine, size)
    first = core == 0
    return jnp.concatenate([jnp.where(first, mine, other), jnp.where(first, other, mine)], axis=0)


def fast_step(
    crops,
    size,
    pair,
    bins,
    lengths,
    mats,
    mats_m,
    mats_v,
    pbias,
    pbias_m,
    pbias_v,
    head,
    head_m,
    head_v,
    norms,
    norms_m,
    norms_v,
):
    bf = jnp.bfloat16
    fl = jnp.float32
    width = mats.shape[1]
    rows = pair.shape[1]
    cols = pair.shape[2]
    heads = pbias.shape[1]
    size_head = width // heads
    scale = size_head ** (-0.5)
    start_pair = pair[0]
    first_row = lax.axis_index("row") * rows
    limit = lengths[0]
    row_ok = first_row + jnp.arange(rows) < limit
    col_ok = jnp.arange(cols) < limit
    pmask = (row_ok[:, None] & col_ok[None, :]).astype(fl)
    m3 = pmask[..., None]
    wl = mats.astype(bf)
    pl = pbias.astype(bf)
    hl = head.astype(bf)
    w_tri = jnp.concatenate([wl[0], wl[1], wl[2], wl[3], wl[4]], axis=1)
    w_att = jnp.concatenate([wl[6], wl[7], wl[8], wl[9]], axis=1)
    h0, unit0, rstd0 = norm_fwd(start_pair, norms[0], norms[1])
    h0b = h0.astype(bf)
    w_own = jnp.concatenate([wl[0], wl[1], wl[4]], axis=1)
    proj = matmul(h0b, w_own)
    sig_a = jax.nn.sigmoid(proj[..., width : 2 * width])
    gate = jax.nn.sigmoid(proj[..., 2 * width :])
    a_low = (sig_a * proj[..., :width] * m3).astype(bf)
    h0_all = gather_rows(h0b, size)
    proj_b = matmul(h0_all, w_tri[:, 2 * width : 4 * width])
    sig_b = jax.nn.sigmoid(proj_b[..., width:])
    lin_b = proj_b[..., :width]
    mask_all = (col_ok[:, None] & col_ok[None, :]).astype(fl)[..., None]
    b_all = (sig_b * lin_b * mask_all).astype(bf)
    prod = jnp.einsum("ikc,jkc->ijc", a_low, b_all, preferred_element_type=fl)
    y_val, unit2, rstd2 = norm_fwd(prod, norms[2], norms[3])
    y_low = y_val.astype(bf)
    out1 = matmul(y_low, wl[5])
    z1 = start_pair + gate * out1
    h1, unit4, rstd4 = norm_fwd(z1, norms[4], norms[5])
    h1b = h1.astype(bf)
    qkvg = matmul(h1b, w_att)
    query = qkvg[..., :width].astype(bf).reshape(rows, cols, heads, size_head)
    keys = qkvg[..., width : 2 * width].astype(bf).reshape(rows, cols, heads, size_head)
    values = qkvg[..., 2 * width : 3 * width].astype(bf).reshape(rows, cols, heads, size_head)
    gate2 = jax.nn.sigmoid(qkvg[..., 3 * width :])
    tb_low = matmul(h1b, pl).astype(bf)
    tb_all = lax.all_to_all(
        jnp.broadcast_to(tb_low[None], (size,) + tb_low.shape), "row", 0, 0, tiled=True
    ).reshape((size * rows,) + tb_low.shape[1:])
    tb_heads = jnp.transpose(tb_all, (2, 0, 1)).astype(fl)
    scores = (
        jnp.einsum("ijhd,ikhd->ihjk", query, keys, preferred_element_type=fl) * scale
        + tb_heads[None]
    )
    scores = jnp.where(col_ok[None, None, None, :], scores, -1000000000.0)
    probs = jax.nn.softmax(scores, axis=-1)
    p_low = probs.astype(bf)
    att = jnp.einsum("ihjk,ikhd->ijhd", p_low, values, preferred_element_type=fl).reshape(
        rows, cols, width
    )
    u_low = (gate2 * att).astype(bf)
    z2 = z1 + matmul(u_low, wl[10])
    h2, unit6, rstd6 = norm_fwd(z2, norms[6], norms[7])
    h2b = h2.astype(bf)
    logits = matmul(h2b, hl)
    lse = jax.nn.logsumexp(logits, axis=-1)
    onehot = (bins[0][..., None] == jnp.arange(logits.shape[-1])).astype(fl)
    pick = jnp.sum(logits * onehot, axis=-1)
    loss = jnp.sum(pmask * (lse - pick))
    count = jnp.sum(pmask)
    dlog = (m3 * (jnp.exp(logits - lse[..., None]) - onehot)).astype(bf)
    dhead = wgrad(h2b, dlog)
    dz2, dg6, ds6 = norm_back(matmul(dlog, hl.T), unit6, rstd6, norms[6])
    dout2 = dz2.astype(bf)
    dw10 = wgrad(u_low, dout2)
    du = matmul(dout2, wl[10].T)
    dgate2 = du * att
    datt = (du * gate2).astype(bf).reshape(rows, cols, heads, size_head)
    dprob = jnp.einsum("ijhd,ikhd->ihjk", datt, values, preferred_element_type=fl)
    dvals = jnp.einsum("ihjk,ijhd->ikhd", p_low, datt, preferred_element_type=fl)
    dscore = (probs * (dprob - jnp.sum(dprob * probs, axis=-1, keepdims=True))).astype(bf)
    dquery = jnp.einsum("ihjk,ikhd->ijhd", dscore, keys, preferred_element_type=fl) * scale
    dkeys = jnp.einsum("ihjk,ijhd->ikhd", dscore, query, preferred_element_type=fl) * scale
    dtb = jnp.sum(dscore.astype(fl), axis=0)
    dtb = jnp.transpose(dtb, (1, 0, 2)).reshape(size, rows, heads, cols)
    dtb_own = jnp.sum(lax.all_to_all(dtb, "row", 0, 0, tiled=True), axis=0)
    dtb_low = jnp.transpose(dtb_own, (0, 2, 1)).astype(bf)
    dpbias = wgrad(h1b, dtb_low)
    dqkvg = jnp.concatenate(
        [
            dquery.reshape(rows, cols, width),
            dkeys.reshape(rows, cols, width),
            dvals.reshape(rows, cols, width),
            dgate2 * gate2 * (1.0 - gate2),
        ],
        axis=-1,
    ).astype(bf)
    dw_att = wgrad(h1b, dqkvg)
    dh1 = matmul(dqkvg, w_att.T) + matmul(dtb_low, pl.T)
    dn4, dg4, ds4 = norm_back(dh1, unit4, rstd4, norms[4])
    dz1 = dz2 + dn4
    dout1 = (dz1 * gate).astype(bf)
    dw5 = wgrad(y_low, dout1)
    dgate = dz1 * out1
    dxn, dg2, ds2 = norm_back(matmul(dout1, wl[5].T), unit2, rstd2, norms[2])
    dx_low = dxn.astype(bf)
    dside_a = jnp.einsum("ijc,jkc->ikc", dx_low, b_all, preferred_element_type=fl)
    dside_b = jnp.einsum("ijc,ikc->jkc", dx_low, a_low, preferred_element_type=fl)
    da_r = dside_a.astype(bf).astype(fl)
    own = jnp.concatenate(
        [
            da_r * sig_a * m3,
            da_r * proj[..., :width] * m3 * sig_a * (1.0 - sig_a),
            dgate * gate * (1.0 - gate),
        ],
        axis=-1,
    ).astype(bf)
    shared = jnp.concatenate(
        [
            dside_b * sig_b * mask_all,
            dside_b * lin_b * mask_all * sig_b * (1.0 - sig_b),
        ],
        axis=-1,
    ).astype(bf)
    dw_own = wgrad(h0b, own)
    dw_shared = wgrad(h0_all, shared)
    sum_own = jnp.sum(own.astype(fl), axis=(0, 1))
    sum_shared = jnp.sum(shared.astype(fl), axis=(0, 1))
    dw_tri = jnp.concatenate(
        [dw_own[:, : 2 * width], dw_shared, dw_own[:, 2 * width :]], axis=1
    )
    sum_tri = jnp.concatenate([sum_own[: 2 * width], sum_shared, sum_own[2 * width :]])
    w_tri_f = w_tri.astype(fl)
    ds0 = jnp.sum(w_tri_f * sum_tri[None, :], axis=1)
    dg0 = (jnp.sum(w_tri_f * dw_tri, axis=1) - norms[1] * ds0) / norms[0]
    pieces = [dw_tri[:, idx * width : (idx + 1) * width] for idx in range(5)]
    pieces = (
        pieces + [dw5] + [dw_att[:, idx * width : (idx + 1) * width] for idx in range(4)] + [dw10]
    )
    bins_n = head.shape[1]
    flat = jnp.concatenate(
        pieces
        + [
            dhead.reshape(-1, width),
            dpbias.reshape(-1, width),
            jnp.stack([dg0, ds0, dg2, ds2, dg4, ds4, dg6, ds6]),
            jnp.stack([jnp.full((width,), loss), jnp.full((width,), count)]),
        ],
        axis=0,
    )
    used = flat.shape[0]
    step = crops * size * 8
    flat = jnp.pad(flat, ((0, -used % step), (0, 0)))
    flat = sum_everywhere(flat, crops, size)
    sizes = [mats.shape[0] * width, bins_n * width // width, heads, norms.shape[0], 2]
    starts = [sum(sizes[:idx]) for idx in range(6)]
    dmats = flat[: starts[1]].reshape(mats.shape)
    dhead = flat[starts[1] : starts[2]].reshape(head.shape)
    dpbias = flat[starts[2] : starts[3]].reshape(pbias.shape)
    dnorms = flat[starts[3] : starts[4]]
    loss = flat[starts[4], 0]
    count = flat[starts[4] + 1, 0]
    grad_norm = jnp.sqrt(
        jnp.sum(dmats * dmats)
        + jnp.sum(dpbias * dpbias)
        + jnp.sum(dhead * dhead)
        + jnp.sum(dnorms * dnorms)
    )
    factor = jnp.minimum(1.0, CLIP / grad_norm)
    new_mats = adam(mats, dmats * factor, mats_m, mats_v)
    new_pbias = adam(pbias, dpbias * factor, pbias_m, pbias_v)
    new_head = adam(head, dhead * factor, head_m, head_v)
    new_norms = adam(norms, dnorms * factor, norms_m, norms_v)
    return (
        grad_norm,
        loss,
        count,
        new_mats[0],
        new_mats[1],
        new_mats[2],
        new_mats[2].astype(bf),
        new_pbias[0],
        new_pbias[1],
        new_pbias[2],
        new_head[0],
        new_head[1],
        new_head[2],
        new_norms[0],
        new_norms[1],
        new_norms[2],
    )


def solution(mesh):
    crops, size = mesh.shape["crop"], mesh.shape["row"]

    def on_device(*args):
        if args[0].shape[2] <= SMALL:
            return fast_step(crops, size, *args)
        return general_step(*args)

    in_specs = (
        P("crop", "row", None, None),
        P("crop", "row", None),
        P("crop"),
        P(),
        P(),
        P(),
        P(),
        P(),
        P(),
        P(),
        P(),
        P(),
        P(),
        P(),
        P(),
    )
    out_specs = (P(), P(), P(), P(), P(), P(), P(), P(), P(), P(), P(), P(), P(), P(), P(), P())
    return jax.shard_map(
        on_device, mesh=mesh, in_specs=in_specs, out_specs=out_specs, check_vma=False
    )
```

```python
import functools

import jax
import jax.numpy as jnp
from jax import lax
from jax.experimental import pallas as pl
from jax.experimental.pallas import tpu as pltpu
from jax.sharding import PartitionSpec as P

STEP = 5


EPS_NORM = 1e-05
CLIP = 1.0
RATE = 0.05
BETA1 = 0.9
BETA2 = 0.95
ADAM_EPS = 1e-08
WDECAY = 0.01


def norm_fwd(v, gain, shift):
    mean = jnp.mean(v, axis=-1, keepdims=True)
    cent = v - mean
    rstd = lax.rsqrt(jnp.mean(cent * cent, axis=-1, keepdims=True) + EPS_NORM)
    unit = cent * rstd
    return (unit * gain + shift, unit, rstd)


def norm_back(grad, unit, rstd, gain):
    dgain = jnp.sum(grad * unit, axis=(0, 1))
    dshift = jnp.sum(grad, axis=(0, 1))
    dunit = grad * gain
    dval = rstd * (
        dunit
        - jnp.mean(dunit, axis=-1, keepdims=True)
        - unit * jnp.mean(dunit * unit, axis=-1, keepdims=True)
    )
    return (dval, dgain, dshift)


def matmul(value, weight):
    flat = value.reshape(-1, value.shape[-1])
    out = jnp.dot(flat, weight, preferred_element_type=jnp.float32)
    return out.reshape(value.shape[:-1] + (weight.shape[1],))


def wgrad(value, grad):
    return jnp.einsum("ijc,ijd->cd", value, grad, preferred_element_type=jnp.float32)


def adam(weight, grad, first, second):
    first_new = BETA1 * first + (1.0 - BETA1) * grad
    second_new = BETA2 * second + (1.0 - BETA2) * grad * grad
    m_hat = first_new / (1.0 - BETA1**STEP)
    v_hat = second_new / (1.0 - BETA2**STEP)
    weight_new = weight - RATE * (m_hat / (jnp.sqrt(v_hat) + ADAM_EPS) + WDECAY * weight)
    return (first_new, second_new, weight_new)


def general_step(
    pair,
    bins,
    lengths,
    mats,
    mats_m,
    mats_v,
    pbias,
    pbias_m,
    pbias_v,
    head,
    head_m,
    head_v,
    norms,
    norms_m,
    norms_v,
):
    bf = jnp.bfloat16
    fl = jnp.float32
    width = mats.shape[1]
    rows = pair.shape[1]
    cols = pair.shape[2]
    heads = pbias.shape[1]
    size_head = width // heads
    scale = size_head ** (-0.5)
    start_pair = pair[0]
    first_row = lax.axis_index("row") * rows
    limit = lengths[0]
    row_ok = first_row + jnp.arange(rows) < limit
    col_ok = jnp.arange(cols) < limit
    pmask = (row_ok[:, None] & col_ok[None, :]).astype(fl)
    m3 = pmask[..., None]
    wl = mats.astype(bf)
    pl = pbias.astype(bf)
    hl = head.astype(bf)
    w_tri = jnp.concatenate([wl[0], wl[1], wl[2], wl[3], wl[4]], axis=1)
    w_att = jnp.concatenate([wl[6], wl[7], wl[8], wl[9]], axis=1)
    h0, unit0, rstd0 = norm_fwd(start_pair, norms[0], norms[1])
    h0b = h0.astype(bf)
    proj = matmul(h0b, w_tri)
    sig_a = jax.nn.sigmoid(proj[..., width : 2 * width])
    sig_b = jax.nn.sigmoid(proj[..., 3 * width : 4 * width])
    gate = jax.nn.sigmoid(proj[..., 4 * width :])
    a_low = (sig_a * proj[..., :width] * m3).astype(bf)
    b_low = (sig_b * proj[..., 2 * width : 3 * width] * m3).astype(bf)
    b_all = lax.all_gather(b_low, "row", axis=0, tiled=True)
    prod = jnp.einsum("ikc,jkc->ijc", a_low, b_all, preferred_element_type=fl)
    y_val, unit2, rstd2 = norm_fwd(prod, norms[2], norms[3])
    y_low = y_val.astype(bf)
    out1 = matmul(y_low, wl[5])
    z1 = start_pair + gate * out1
    h1, unit4, rstd4 = norm_fwd(z1, norms[4], norms[5])
    h1b = h1.astype(bf)
    qkvg = matmul(h1b, w_att)
    query = qkvg[..., :width].astype(bf).reshape(rows, cols, heads, size_head)
    keys = qkvg[..., width : 2 * width].astype(bf).reshape(rows, cols, heads, size_head)
    values = qkvg[..., 2 * width : 3 * width].astype(bf).reshape(rows, cols, heads, size_head)
    gate2 = jax.nn.sigmoid(qkvg[..., 3 * width :])
    tb_low = matmul(h1b, pl).astype(bf)
    tb_all = lax.all_gather(tb_low, "row", axis=0, tiled=True)
    tb_heads = jnp.transpose(tb_all, (2, 0, 1)).astype(fl)
    scores = (
        jnp.einsum("ijhd,ikhd->ihjk", query, keys, preferred_element_type=fl) * scale
        + tb_heads[None]
    )
    scores = jnp.where(col_ok[None, None, None, :], scores, -1000000000.0)
    probs = jax.nn.softmax(scores, axis=-1)
    p_low = probs.astype(bf)
    att = jnp.einsum("ihjk,ikhd->ijhd", p_low, values, preferred_element_type=fl).reshape(
        rows, cols, width
    )
    u_low = (gate2 * att).astype(bf)
    z2 = z1 + matmul(u_low, wl[10])
    h2, unit6, rstd6 = norm_fwd(z2, norms[6], norms[7])
    h2b = h2.astype(bf)
    logits = matmul(h2b, hl)
    lse = jax.nn.logsumexp(logits, axis=-1)
    onehot = (bins[0][..., None] == jnp.arange(logits.shape[-1])).astype(fl)
    pick = jnp.sum(logits * onehot, axis=-1)
    loss = jnp.sum(pmask * (lse - pick))
    count = jnp.sum(pmask)
    dlog = (m3 * (jnp.exp(logits - lse[..., None]) - onehot)).astype(bf)
    dhead = wgrad(h2b, dlog)
    dz2, dg6, ds6 = norm_back(matmul(dlog, hl.T), unit6, rstd6, norms[6])
    dout2 = dz2.astype(bf)
    dw10 = wgrad(u_low, dout2)
    du = matmul(dout2, wl[10].T)
    dgate2 = du * att
    datt = (du * gate2).astype(bf).reshape(rows, cols, heads, size_head)
    dprob = jnp.einsum("ijhd,ikhd->ihjk", datt, values, preferred_element_type=fl)
    dvals = jnp.einsum("ihjk,ijhd->ikhd", p_low, datt, preferred_element_type=fl)
    dscore = (probs * (dprob - jnp.sum(dprob * probs, axis=-1, keepdims=True))).astype(bf)
    dquery = jnp.einsum("ihjk,ikhd->ijhd", dscore, keys, preferred_element_type=fl) * scale
    dkeys = jnp.einsum("ihjk,ijhd->ikhd", dscore, query, preferred_element_type=fl) * scale
    dtb = jnp.sum(dscore.astype(fl), axis=0)
    dtb_own = lax.psum_scatter(dtb, "row", scatter_dimension=1, tiled=True)
    dtb_low = jnp.transpose(dtb_own, (1, 2, 0)).astype(bf)
    dpbias = wgrad(h1b, dtb_low)
    dqkvg = jnp.concatenate(
        [
            dquery.reshape(rows, cols, width),
            dkeys.reshape(rows, cols, width),
            dvals.reshape(rows, cols, width),
            dgate2 * gate2 * (1.0 - gate2),
        ],
        axis=-1,
    ).astype(bf)
    dw_att = wgrad(h1b, dqkvg)
    dh1 = matmul(dqkvg, w_att.T) + matmul(dtb_low, pl.T)
    dn4, dg4, ds4 = norm_back(dh1, unit4, rstd4, norms[4])
    dz1 = dz2 + dn4
    dout1 = (dz1 * gate).astype(bf)
    dw5 = wgrad(y_low, dout1)
    dgate = dz1 * out1
    dxn, dg2, ds2 = norm_back(matmul(dout1, wl[5].T), unit2, rstd2, norms[2])
    dx_low = dxn.astype(bf)
    dside_a = jnp.einsum("ijc,jkc->ikc", dx_low, b_all, preferred_element_type=fl)
    dside_b = lax.psum_scatter(
        jnp.einsum("ijc,ikc->jkc", dx_low, a_low, preferred_element_type=fl),
        "row",
        scatter_dimension=0,
        tiled=True,
    )
    da_r = dside_a.astype(bf).astype(fl)
    db_r = dside_b.astype(bf).astype(fl)
    dproj = jnp.concatenate(
        [
            da_r * sig_a * m3,
            da_r * proj[..., :width] * m3 * sig_a * (1.0 - sig_a),
            db_r * sig_b * m3,
            db_r * proj[..., 2 * width : 3 * width] * m3 * sig_b * (1.0 - sig_b),
            dgate * gate * (1.0 - gate),
        ],
        axis=-1,
    ).astype(bf)
    dw_tri = wgrad(h0b, dproj)
    dh0 = matmul(dproj, w_tri.T)
    unused, dg0, ds0 = norm_back(dh0, unit0, rstd0, norms[0])
    pieces = [dw_tri[:, idx * width : (idx + 1) * width] for idx in range(5)]
    pieces = (
        pieces + [dw5] + [dw_att[:, idx * width : (idx + 1) * width] for idx in range(4)] + [dw10]
    )
    dmats = jnp.stack(pieces)
    dnorms = jnp.stack([dg0, ds0, dg2, ds2, dg4, ds4, dg6, ds6])
    dmats, dpbias, dhead, dnorms, loss, count = lax.psum(
        (dmats, dpbias, dhead, dnorms, loss, count), ("crop", "row")
    )
    grad_norm = jnp.sqrt(
        jnp.sum(dmats * dmats)
        + jnp.sum(dpbias * dpbias)
        + jnp.sum(dhead * dhead)
        + jnp.sum(dnorms * dnorms)
    )
    factor = jnp.minimum(1.0, CLIP / grad_norm)
    new_mats = adam(mats, dmats * factor, mats_m, mats_v)
    new_pbias = adam(pbias, dpbias * factor, pbias_m, pbias_v)
    new_head = adam(head, dhead * factor, head_m, head_v)
    new_norms = adam(norms, dnorms * factor, norms_m, norms_v)
    return (
        grad_norm,
        loss,
        count,
        new_mats[0],
        new_mats[1],
        new_mats[2],
        new_mats[2].astype(bf),
        new_pbias[0],
        new_pbias[1],
        new_pbias[2],
        new_head[0],
        new_head[1],
        new_head[2],
        new_norms[0],
        new_norms[1],
        new_norms[2],
    )


BF = jnp.bfloat16
FL = jnp.float32
VMEM_LIMIT = 24 * 2**20


def dot(lhs, rhs, left=1, right=0):
    return lax.dot_general(
        lhs, rhs, (((left,), (right,)), ((), ())), preferred_element_type=FL
    )


def sharp(lhs, rhs):
    return lax.dot_general(
        lhs,
        rhs,
        (((1,), (1,)), ((), ())),
        preferred_element_type=FL,
        precision=lax.Precision.HIGHEST,
    )


def row_norm(val, gain, shift):
    mean = jnp.mean(val, axis=-1, keepdims=True)
    cent = val - mean
    rstd = lax.rsqrt(jnp.mean(cent * cent, axis=-1, keepdims=True) + EPS_NORM)
    unit = cent * rstd
    return (unit * gain + shift).astype(BF), unit, rstd


def row_norm_back(grad, unit, rstd, gain):
    dgain = jnp.sum(grad * unit, axis=0, keepdims=True)
    dshift = jnp.sum(grad, axis=0, keepdims=True)
    dunit = grad * gain
    dval = rstd * (
        dunit
        - jnp.mean(dunit, axis=-1, keepdims=True)
        - unit * jnp.mean(dunit * unit, axis=-1, keepdims=True)
    )
    return dval, dgain, dshift


def iota(shape, dim):
    return lax.broadcasted_iota(jnp.int32, shape, dim)


def start_kernel(copies, pair_ref, norms_ref, out_ref, buf_ref, sems):
    h0, _, _ = row_norm(pair_ref[...], norms_ref[0:1], norms_ref[1:2])
    buf_ref[...] = h0
    moves = [
        pltpu.make_async_copy(buf_ref, out_ref.at[idx], sems.at[idx]) for idx in range(copies)
    ]
    for move in moves:
        move.start()
    for move in moves:
        move.wait()


def triangle_kernel(
    dims,
    scal_ref,
    own_ref,
    other_ref,
    pair_ref,
    norms_ref,
    wl_ref,
    pbt_ref,
    tb_ref,
    b_ref,
    fb1_ref,
    fb2_ref,
    loc_ref,
    y_ref,
    h1_ref,
    part_ref,
):
    rows, cols, width, heads, size = dims
    pairs = rows * cols
    limit, first_row, chip, core = (scal_ref[idx] for idx in range(4))
    spot = iota((pairs, width), 0)
    col_ok = spot % cols < limit
    row_in = spot // cols

    def mask_of(block_row):
        return jnp.where(jnp.logical_and(col_ok, row_in + block_row < limit), 1.0, 0.0).astype(FL)

    w_b = jnp.concatenate([wl_ref[2], wl_ref[3]], axis=1)

    def side_b(idx, _):
        for src, half in ((own_ref, core), (other_ref, 1 - core)):
            proj = dot(src[idx], w_b)
            sig = jax.nn.sigmoid(proj[:, width:])
            block = 2 * idx + half
            fac = sig * mask_of(block * rows)
            side = fac * proj[:, :width]
            base = pl.multiple_of(block * pairs, pairs)
            b_ref[pl.ds(base, pairs), :] = side.astype(BF).astype(FL)
            fb1_ref[pl.ds(base, pairs), :] = fac
            fb2_ref[pl.ds(base, pairs), :] = side * (1.0 - sig)
        return 0

    lax.fori_loop(0, size // 2, side_b, 0)

    w_own = jnp.concatenate([wl_ref[0], wl_ref[1], wl_ref[4]], axis=1)
    proj = dot(own_ref[chip], w_own)
    sig = jax.nn.sigmoid(proj[:, width : 2 * width])
    fac = sig * mask_of(first_row)
    side = fac * proj[:, :width]
    a_val = side.astype(BF).astype(FL)
    gate = jax.nn.sigmoid(proj[:, 2 * width :])
    loc_ref[0] = a_val
    loc_ref[1] = fac
    loc_ref[2] = side * (1.0 - sig)
    loc_ref[3] = gate

    a_rows = [a_val[idx * cols : (idx + 1) * cols] for idx in range(rows)]

    def products(j, _):
        b_j = b_ref[pl.ds(pl.multiple_of(j * cols, cols), cols), :]
        for idx in range(rows):
            prod = a_rows[idx] * b_j
            fold = jnp.sum(prod.reshape(cols // 8, 8, width), axis=0)
            part_ref[pl.ds(pl.multiple_of((idx * cols + j) * 8, 8), 8), :] = fold
        return 0

    lax.fori_loop(0, cols, products, 0, unroll=2)
    x_val = part_ref[pl.ds(0, pairs, stride=8), :]
    for idx in range(1, 8):
        x_val = x_val + part_ref[pl.ds(idx, pairs, stride=8), :]

    y_low, unit2, rstd2 = row_norm(x_val, norms_ref[2:3], norms_ref[3:4])
    out1 = dot(y_low, wl_ref[5])
    z1 = pair_ref[...] + gate * out1
    h1, unit4, rstd4 = row_norm(z1, norms_ref[4:5], norms_ref[5:6])
    tbt = dot(pbt_ref[...].astype(BF), h1, 1, 1).astype(BF).astype(FL)
    half = pairs // 2
    block = jnp.concatenate([tbt[:, :half], tbt[:, half:]], axis=0)
    for idx in range(size):
        tb_ref[idx] = block
    y_ref[...] = y_low
    h1_ref[...] = h1
    loc_ref[4] = out1
    loc_ref[5] = unit2
    loc_ref[6] = jnp.broadcast_to(rstd2, unit2.shape)
    loc_ref[7] = z1
    loc_ref[8] = unit4
    loc_ref[9] = jnp.broadcast_to(rstd4, unit4.shape)


def project_kernel(
    dims,
    h1_ref,
    own_ref,
    other_ref,
    wl_ref,
    kcat_ref,
    vcat_ref,
    qblk_ref,
    gate2_ref,
    own_t_ref,
    other_t_ref,
):
    rows, cols, width, heads, size = dims
    w_att = jnp.concatenate([wl_ref[6], wl_ref[7], wl_ref[8], wl_ref[9]], axis=1)
    proj = dot(h1_ref[...], w_att)
    gate2_ref[...] = jax.nn.sigmoid(proj[:, 3 * width :])
    lane_head = iota((cols, width), 1) // (width // heads)
    zero = jnp.zeros((cols, width), BF)
    for idx in range(rows):
        at, side = idx // 2, idx % 2
        lanes = slice(side * width, (side + 1) * width)
        span = slice(idx * cols, (idx + 1) * cols)
        query = proj[span, :width].astype(BF)
        qblk_ref[at, side * cols : (side + 1) * cols, lanes] = query
        qblk_ref[at, (1 - side) * cols : (2 - side) * cols, lanes] = zero
        for head in range(heads):
            put = slice(head * cols, (head + 1) * cols)
            keep = lane_head == head
            kcat_ref[at, put, lanes] = jnp.where(keep, proj[span, width : 2 * width], 0.0).astype(BF)
            vcat_ref[at, put, lanes] = jnp.where(
                keep, proj[span, 2 * width : 3 * width], 0.0
            ).astype(BF)
    extra = own_t_ref.shape[1] - width
    for src, dst in ((own_ref, own_t_ref), (other_ref, other_t_ref)):
        for idx in range(size // 2):
            dst[idx, :width, :] = src[idx].astype(FL).T.astype(BF)
            dst[idx, width:, :] = jnp.ones((extra, rows * cols), BF)


def attention_kernel(
    dims,
    scal_ref,
    tb_ref,
    kcat_ref,
    vcat_ref,
    qblk_ref,
    gate2_ref,
    loc_ref,
    norms_ref,
    wl_ref,
    headt_ref,
    bins_ref,
    dtb_ref,
    pl_ref,
    dsl_ref,
    dblk_ref,
    u_ref,
    dout2_ref,
    dz2_ref,
    dgate2_ref,
    h2_ref,
    dlog_ref,
    stat_ref,
    bias_ref,
    prob_ref,
    swap_ref,
):
    rows, cols, width, heads, size = dims
    pairs, lines = rows * cols, heads * cols
    scale = (width // heads) ** (-0.5)
    limit, first_row = scal_ref[0], scal_ref[1]

    for half in range(2):
        for jl in range(2):
            lanes = slice(jl * cols, (jl + 1) * cols)
            got = [
                tb_ref[pl.ds(half * heads + head, size, stride=2 * heads), :][:, lanes]
                for head in range(heads)
            ]
            for duo in range(heads // 2):
                line = jnp.concatenate([got[2 * duo], got[2 * duo + 1]], axis=1)
                bias_ref[duo, pl.ds(2 * half + jl, size, stride=rows), :] = line
                bias_ref[duo, pl.ds(cols + 2 * half + jl, size, stride=rows), :] = line
    bias = jnp.concatenate([bias_ref[duo].T for duo in range(heads // 2)], axis=0)
    key_ok = iota((lines, 2 * cols), 0) % cols < limit
    att = []
    for at in range(rows // 2):
        score = dot(kcat_ref[at], qblk_ref[at], 1, 1) * scale + bias
        score = jnp.where(key_ok, score, -1000000000.0).reshape(heads, cols, 2 * cols)
        top = jnp.max(score, axis=1, keepdims=True)
        grown = jnp.exp(score - top)
        prob = (grown / jnp.sum(grown, axis=1, keepdims=True)).reshape(lines, 2 * cols)
        prob_ref[at] = prob
        low = prob.astype(BF)
        pl_ref[at] = low
        both = dot(low, vcat_ref[at], 0, 0)
        att += [both[:cols, :width], both[cols:, width:]]
    att = jnp.concatenate(att, axis=0)
    gate2 = gate2_ref[...]
    u_low = (gate2 * att).astype(BF)
    u_ref[...] = u_low
    z2 = loc_ref[7] + dot(u_low, wl_ref[10])
    h2, unit6, rstd6 = row_norm(z2, norms_ref[6:7], norms_ref[7:8])
    h2_ref[...] = h2
    headt = headt_ref[...].astype(BF)
    logits = dot(headt, h2, 1, 1)
    spot = iota((1, pairs), 1)
    ok = jnp.logical_and(spot % cols < limit, spot // cols + first_row < limit)
    mask = jnp.where(ok, 1.0, 0.0).astype(FL)
    bins = jnp.concatenate([bins_ref[idx : idx + 1, :] for idx in range(rows)], axis=1)
    onehot = jnp.where(iota(logits.shape, 0) == bins, 1.0, 0.0).astype(FL)
    top = jnp.max(logits, axis=0, keepdims=True)
    lse = top + jnp.log(jnp.sum(jnp.exp(logits - top), axis=0, keepdims=True))
    pick = jnp.sum(logits * onehot, axis=0, keepdims=True)
    loss = jnp.sum(mask * (lse - pick), axis=1, keepdims=True)
    count = jnp.sum(mask, axis=1, keepdims=True)
    dlog = (mask * (jnp.exp(logits - lse) - onehot)).astype(BF)
    dlog_ref[...] = dlog
    dz2, dg6, ds6 = row_norm_back(dot(dlog, headt, 0, 0), unit6, rstd6, norms_ref[6:7])
    dz2_ref[...] = dz2
    stat_ref[0:1, :] = dg6
    stat_ref[1:2, :] = ds6
    stat_ref[2:3, :] = jnp.broadcast_to(loss, (1, width))
    stat_ref[3:4, :] = jnp.broadcast_to(count, (1, width))
    stat_ref[4:8, :] = jnp.zeros((4, width), FL)
    dout2 = dz2.astype(BF)
    dout2_ref[...] = dout2
    du = dot(dout2, wl_ref[10], 1, 1)
    dgate2_ref[...] = (du * att * gate2 * (1.0 - gate2)).astype(BF)
    datt = (du * gate2).astype(BF)
    zero = jnp.zeros((cols, width), BF)
    total = None
    for at in range(rows // 2):
        first = datt[(2 * at) * cols : (2 * at + 1) * cols]
        second = datt[(2 * at + 1) * cols : (2 * at + 2) * cols]
        block = jnp.concatenate(
            [
                jnp.concatenate([first, zero], axis=1),
                jnp.concatenate([zero, second], axis=1),
            ],
            axis=0,
        )
        dblk_ref[at] = block
        dprob = dot(vcat_ref[at], block, 1, 1)
        prob = prob_ref[at]
        inner = jnp.sum((dprob * prob).reshape(heads, cols, 2 * cols), axis=1, keepdims=True)
        dscore = prob.reshape(heads, cols, 2 * cols) * (
            dprob.reshape(heads, cols, 2 * cols) - inner
        )
        low = dscore.reshape(lines, 2 * cols).astype(BF)
        dsl_ref[at] = low
        total = low.astype(FL) if total is None else total + low.astype(FL)
    for duo in range(heads // 2):
        turned = total[duo * 2 * cols : (duo + 1) * 2 * cols].T
        swap_ref[duo] = turned[:cols] + turned[cols:]
    for half in range(2):
        for head in range(heads):
            inside = slice((head % 2) * cols, (head % 2 + 1) * cols)
            line = jnp.concatenate(
                [
                    swap_ref[head // 2, pl.ds(2 * half + jl, size, stride=rows), :][:, inside]
                    for jl in range(2)
                ],
                axis=1,
            )
            dtb_ref[pl.ds(half * heads + head, size, stride=2 * heads), :] = line


def attention_grad_kernel(
    dims,
    kcat_ref,
    qblk_ref,
    pl_ref,
    dsl_ref,
    dblk_ref,
    u_ref,
    dout2_ref,
    dgate2_ref,
    h1_ref,
    h2_ref,
    dlog_ref,
    wl_ref,
    early_ref,
    dh1_ref,
    dqkvg_ref,
):
    rows, cols, width, heads, size = dims
    scale = (width // heads) ** (-0.5)
    lane_head = iota((cols, width), 1) // (width // heads)

    def diagonal(val):
        out = jnp.zeros((cols, width), FL)
        for head in range(heads):
            out = jnp.where(lane_head == head, val[head * cols : (head + 1) * cols], out)
        return out

    for at in range(rows // 2):
        dquery = dot(dsl_ref[at], kcat_ref[at], 0, 0)
        dkeys = dot(dsl_ref[at], qblk_ref[at])
        dvals = dot(pl_ref[at], dblk_ref[at])
        for side in range(2):
            idx = 2 * at + side
            lanes = slice(side * width, (side + 1) * width)
            span = slice(idx * cols, (idx + 1) * cols)
            dqkvg_ref[span, :width] = (
                dquery[side * cols : (side + 1) * cols, lanes] * scale
            ).astype(BF)
            dqkvg_ref[span, width : 2 * width] = (diagonal(dkeys[:, lanes]) * scale).astype(BF)
            dqkvg_ref[span, 2 * width : 3 * width] = diagonal(dvals[:, lanes]).astype(BF)
    dqkvg_ref[:, 3 * width :] = dgate2_ref[...]
    dqkvg = dqkvg_ref[...]
    w_att = jnp.concatenate([wl_ref[6], wl_ref[7], wl_ref[8], wl_ref[9]], axis=1)
    dh1_ref[...] = dot(dqkvg, w_att, 1, 1)
    dw_att = dot(h1_ref[...], dqkvg, 0, 0)
    for idx in range(4):
        early_ref[idx * width : (idx + 1) * width, :] = dw_att[:, idx * width : (idx + 1) * width]
    early_ref[4 * width : 5 * width, :] = dot(u_ref[...], dout2_ref[...], 0, 0)
    early_ref[5 * width :, :] = dot(dlog_ref[...], h2_ref[...])


def triangle_grad_kernel(
    dims,
    scal_ref,
    dtb_ref,
    early_ref,
    dh1_ref,
    dz2_ref,
    stat_ref,
    h1_ref,
    y_ref,
    loc_ref,
    b_ref,
    fb1_ref,
    fb2_ref,
    own_t_ref,
    other_t_ref,
    norms_ref,
    wl_ref,
    pbt_ref,
    keep_ref,
    give_ref,
    flat_ref,
    dx_ref,
):
    rows, cols, width, heads, size = dims
    pairs = rows * cols
    chip, core = scal_ref[2], scal_ref[3]
    got = dtb_ref[0]
    for idx in range(1, size):
        got = got + dtb_ref[idx]
    dtbt = jnp.concatenate([got[:heads], got[heads:]], axis=1).astype(BF)
    h1 = h1_ref[...]
    dpbt = dot(dtbt, h1)
    dh1 = dh1_ref[...] + dot(dtbt, pbt_ref[...].astype(BF), 0, 0)
    dn4, dg4, ds4 = row_norm_back(dh1, loc_ref[8], loc_ref[9], norms_ref[4:5])
    dz1 = dz2_ref[...] + dn4
    gate = loc_ref[3]
    dout1 = (dz1 * gate).astype(BF)
    dgate = dz1 * loc_ref[4] * gate * (1.0 - gate)
    dx, dg2, ds2 = row_norm_back(
        dot(dout1, wl_ref[5], 1, 1), loc_ref[5], loc_ref[6], norms_ref[2:3]
    )
    dx_ref[...] = dx.astype(BF).astype(FL)

    def da_step(j, acc):
        b_j = b_ref[pl.ds(pl.multiple_of(j * cols, cols), cols), :]
        return tuple(
            acc[idx] + dx_ref[pl.ds(idx * cols + j, 1), :] * b_j for idx in range(rows)
        )

    acc = lax.fori_loop(
        0, cols, da_step, tuple(jnp.zeros((cols, width), FL) for _ in range(rows)), unroll=2
    )
    da = jnp.concatenate(acc, axis=0).astype(BF).astype(FL)
    own = jnp.concatenate(
        [
            (da * loc_ref[1]).astype(BF),
            (da * loc_ref[2]).astype(BF),
            dgate.astype(BF),
        ],
        axis=1,
    )
    dw_own = dot(own_t_ref[chip], own)

    a_rows = [loc_ref[0, idx * cols : (idx + 1) * cols, :] for idx in range(rows)]

    def db_step(idx, acc):
        for src, half in ((own_t_ref, core), (other_t_ref, 1 - core)):
            block = 2 * idx + half
            pieces = []
            for row in range(rows):
                j = block * rows + row
                base = pl.multiple_of(j * cols, cols)
                db = dx_ref[pl.ds(j, 1), :] * a_rows[0]
                for own_row in range(1, rows):
                    db = db + dx_ref[pl.ds(own_row * cols + j, 1), :] * a_rows[own_row]
                pieces.append(
                    jnp.concatenate(
                        [
                            (db * fb1_ref[pl.ds(base, cols), :]).astype(BF),
                            (db * fb2_ref[pl.ds(base, cols), :]).astype(BF),
                        ],
                        axis=1,
                    )
                )
            acc = acc + dot(src[idx], jnp.concatenate(pieces, axis=0))
        return acc

    tall = own_t_ref.shape[1]
    dw_b = jnp.zeros((tall, 2 * width), FL)
    for idx in range(size // 2):
        dw_b = db_step(idx, dw_b)

    parts = [
        dw_own[:, :width],
        dw_own[:, width : 2 * width],
        dw_b[:, :width],
        dw_b[:, width:],
        dw_own[:, 2 * width :],
    ]
    ones = jnp.ones((8, width), FL)
    ds0 = jnp.zeros((8, width), FL)
    mixed = jnp.zeros((width, width), FL)
    for idx, part in enumerate(parts):
        weight = wl_ref[idx].astype(FL)
        flat_ref[idx * width : (idx + 1) * width, :] = part[:width]
        mixed = mixed + weight * part[:width]
        ds0 = ds0 + sharp(part[width : width + 8], weight)
    dg0 = (sharp(ones, mixed) - norms_ref[1:2] * ds0) / norms_ref[0:1]
    flat_ref[5 * width : 6 * width, :] = dot(y_ref[...], dout1, 0, 0)
    mats = 11 * width
    flat_ref[6 * width : mats, :] = early_ref[: 5 * width, :]
    bins_n = early_ref.shape[0] - 5 * width
    flat_ref[mats : mats + bins_n, :] = early_ref[5 * width :, :]
    base = mats + bins_n
    flat_ref[base : base + heads, :] = dpbt
    flat_ref[base + heads : base + 8, :] = jnp.zeros((8 - heads, width), FL)
    base += 8
    for idx, line in enumerate((dg0[:1], ds0[:1], dg2, ds2, dg4, ds4)):
        flat_ref[base + idx : base + idx + 1, :] = line
    flat_ref[base + 6 : base + 10, :] = stat_ref[0:4, :]
    total = flat_ref.shape[0]
    flat_ref[base + 10 :, :] = jnp.zeros((total - base - 10, width), FL)
    half = total // 2
    keep_ref[...] = flat_ref[pl.ds(pl.multiple_of(core * half, half), half), :]
    give_ref[...] = flat_ref[pl.ds(pl.multiple_of((1 - core) * half, half), half), :]


def update_kernel(
    dims,
    scal_ref,
    mine_ref,
    other_ref,
    mats_ref,
    mats_m_ref,
    mats_v_ref,
    pb_ref,
    pb_m_ref,
    pb_v_ref,
    head_ref,
    head_m_ref,
    head_v_ref,
    norms_ref,
    norms_m_ref,
    norms_v_ref,
    scalars_ref,
    mats_m_out,
    mats_v_out,
    mats_out,
    mats_low_out,
    pb_m_out,
    pb_v_out,
    pb_out,
    head_m_out,
    head_v_out,
    head_out,
    norms_m_out,
    norms_v_out,
    norms_out,
    flat_ref,
    m_buf,
    v_buf,
    w_buf,
    low_buf,
    sems,
):
    rows, cols, width, heads, size = dims
    core = scal_ref[3]
    half = mine_ref.shape[0]
    flat_ref[pl.ds(pl.multiple_of(core * half, half), half), :] = mine_ref[...]
    flat_ref[pl.ds(pl.multiple_of((1 - core) * half, half), half), :] = other_ref[...]
    count = mats_ref.shape[0]
    mats = count * width
    bins_n = head_ref.shape[0]
    base = mats + bins_n
    grads = flat_ref[: base + 16, :]
    square = jnp.sum(grads * grads, axis=0, keepdims=True)
    norm = jnp.sqrt(jnp.sum(square, axis=1, keepdims=True))
    factor = jnp.minimum(1.0, CLIP / norm)
    scalars_ref[0:1, :] = jnp.broadcast_to(norm, (1, width))
    scalars_ref[1:3, :] = flat_ref[base + 16 : base + 18, :]
    scalars_ref[3:8, :] = jnp.zeros((5, width), FL)

    def step(weight, grad, first, second):
        return adam(weight, grad * factor, first, second)

    moves = []
    for idx in range(count):
        first, second, weight = step(
            mats_ref[idx],
            flat_ref[idx * width : (idx + 1) * width, :],
            mats_m_ref[idx],
            mats_v_ref[idx],
        )
        m_buf[idx] = first
        v_buf[idx] = second
        w_buf[idx] = weight
        low_buf[idx] = weight.astype(BF)
        for at, (buf, out) in enumerate(
            ((m_buf, mats_m_out), (v_buf, mats_v_out), (w_buf, mats_out), (low_buf, mats_low_out))
        ):
            move = pltpu.make_async_copy(buf.at[idx], out.at[idx], sems.at[at, idx])
            move.start()
            moves.append(move)
    small = (
        (mats, bins_n, head_ref, head_m_ref, head_v_ref, head_m_out, head_v_out, head_out),
        (base, heads, pb_ref, pb_m_ref, pb_v_ref, pb_m_out, pb_v_out, pb_out),
        (base + 8, 8, norms_ref, norms_m_ref, norms_v_ref, norms_m_out, norms_v_out, norms_out),
    )
    for at, tall, w_in, m_in, v_in, m_out, v_out, w_out in small:
        m_out[...], v_out[...], w_out[...] = step(
            w_in[...], flat_ref[at : at + tall, :], m_in[...], v_in[...]
        )
    for move in moves:
        move.wait()


def in_vmem(value):
    return pltpu.with_memory_space_constraint(value, pltpu.VMEM)


def call(kernel, args, outs, scratch=(), limit=VMEM_LIMIT, flops=10**7):
    spots = {"s": pltpu.SMEM, "v": pltpu.VMEM, "k": pltpu.VMEM, "a": pl.ANY}
    arrays = [in_vmem(value) if kind == "k" else value for value, kind in args]
    shapes = [
        pltpu.VMEM(shape, kind) if spot == "k" else jax.ShapeDtypeStruct(shape, kind)
        for shape, kind, spot in outs
    ]
    return pl.pallas_call(
        kernel,
        out_shape=shapes,
        in_specs=[pl.BlockSpec(memory_space=spots[kind]) for _, kind in args],
        out_specs=[pl.BlockSpec(memory_space=spots[spot]) for _, _, spot in outs],
        scratch_shapes=list(scratch),
        compiler_params=pltpu.CompilerParams(vmem_limit_bytes=limit),
        cost_estimate=pl.CostEstimate(flops=flops, bytes_accessed=10**6, transcendentals=0),
    )(*arrays)


def same_core_groups(crops, size):
    return [
        [crop * size + idx for crop in range(crops) for idx in range(core, size, 2)]
        for core in range(2)
    ]


def core_swap(value, size):
    return lax.ppermute(value, "row", [(idx, idx ^ 1) for idx in range(size)])


def fast_step(
    crops,
    size,
    pair,
    bins,
    lengths,
    mats,
    mats_m,
    mats_v,
    pbias,
    pbias_m,
    pbias_v,
    head,
    head_m,
    head_v,
    norms,
    norms_m,
    norms_v,
):
    rows, cols, width = pair.shape[1:]
    heads, bins_n = pbias.shape[1], head.shape[1]
    pairs, lines = rows * cols, heads * cols
    dims = (rows, cols, width, heads, size)
    chips = size // 2
    place = lax.axis_index("row")
    scal = jnp.stack([lengths[0], place * rows, place // 2, place % 2]).astype(jnp.int32)
    start = pair.reshape(pairs, width)
    wl = mats.astype(BF)
    pbt, headt = pbias.T, head.T

    (copies,) = call(
        functools.partial(start_kernel, chips),
        [(start, "v"), (norms, "v")],
        [((chips, pairs, width), BF, "a")],
        [pltpu.VMEM((pairs, width), BF), pltpu.SemaphoreType.DMA((chips,))],
    )
    near = [list(range(core, size, 2)) for core in range(2)]
    own = lax.all_to_all(copies, "row", 0, 0, axis_index_groups=near, tiled=True)
    other = core_swap(own, size)

    full = (size * pairs, width)
    tb, b_all, fb1, fb2, loc, y_low, h1 = call(
        functools.partial(triangle_kernel, dims),
        [
            (scal, "s"),
            (own, "k"),
            (other, "k"),
            (start, "k"),
            (norms, "k"),
            (wl, "k"),
            (pbt, "k"),
        ],
        [
            ((size, 2 * heads, 2 * cols), FL, "v"),
            (full, FL, "k"),
            (full, FL, "k"),
            (full, FL, "k"),
            ((10, pairs, width), FL, "k"),
            ((pairs, width), BF, "k"),
            ((pairs, width), BF, "k"),
        ],
        [pltpu.VMEM((pairs * 8, width), FL)],
    )

    tb_all = lax.all_to_all(tb, "row", 0, 0, tiled=True)
    tall = width + 16
    kcat, vcat, qblk, gate2, own_t, other_t = call(
        functools.partial(project_kernel, dims),
        [(h1, "k"), (own, "k"), (other, "k"), (wl, "k")],
        [
            ((rows // 2, lines, 2 * width), BF, "k"),
            ((rows // 2, lines, 2 * width), BF, "k"),
            ((rows // 2, 2 * cols, 2 * width), BF, "k"),
            ((pairs, width), FL, "k"),
            ((chips, tall, pairs), BF, "k"),
            ((chips, tall, pairs), BF, "k"),
        ],
    )
    dtb, pl_low, dsl, dblk, u_low, dout2, dz2, dgate2, h2, dlog, stat = call(
        functools.partial(attention_kernel, dims),
        [
            (scal, "s"),
            (tb_all.reshape(size * 2 * heads, 2 * cols), "k"),
            (kcat, "k"),
            (vcat, "k"),
            (qblk, "k"),
            (gate2, "k"),
            (loc, "k"),
            (norms, "k"),
            (wl, "k"),
            (headt, "k"),
            (bins[0], "k"),
        ],
        [
            ((size * 2 * heads, 2 * cols), FL, "v"),
            ((rows // 2, lines, 2 * cols), BF, "k"),
            ((rows // 2, lines, 2 * cols), BF, "k"),
            ((rows // 2, 2 * cols, 2 * width), BF, "k"),
            ((pairs, width), BF, "k"),
            ((pairs, width), BF, "k"),
            ((pairs, width), FL, "k"),
            ((pairs, width), BF, "k"),
            ((pairs, width), BF, "k"),
            ((bins_n, pairs), BF, "k"),
            ((8, width), FL, "k"),
        ],
        [
            pltpu.VMEM((heads // 2, 2 * cols, 2 * cols), FL),
            pltpu.VMEM((rows // 2, lines, 2 * cols), FL),
            pltpu.VMEM((heads // 2, cols, 2 * cols), FL),
        ],
    )

    dtb_all = lax.all_to_all(dtb.reshape(size, 2 * heads, 2 * cols), "row", 0, 0, tiled=True)
    early, dh1 = call(
        functools.partial(attention_grad_kernel, dims),
        [
            (value, "k")
            for value in (
                kcat,
                qblk,
                pl_low,
                dsl,
                dblk,
                u_low,
                dout2,
                dgate2,
                h1,
                h2,
                dlog,
                wl,
            )
        ],
        [((5 * width + bins_n, width), FL, "k"), ((pairs, width), FL, "k")],
        [pltpu.VMEM((pairs, 4 * width), BF)],
    )
    used = mats.shape[0] * width + bins_n + 18
    unit = 8 * crops * size
    total = -(-used // unit) * unit
    keep, give = call(
        functools.partial(triangle_grad_kernel, dims),
        [(scal, "s")]
        + [
            (value, "k")
            for value in (
                dtb_all,
                early,
                dh1,
                dz2,
                stat,
                h1,
                y_low,
                loc,
                b_all,
                fb1,
                fb2,
                own_t,
                other_t,
                norms,
                wl,
                pbt,
            )
        ],
        [((total // 2, width), FL, "v"), ((total // 2, width), FL, "v")],
        [pltpu.VMEM((total, width), FL), pltpu.VMEM((pairs, width), FL)],
    )

    half = keep + core_swap(give, size)
    count = crops * chips
    groups = same_core_groups(crops, size)
    axes = ("crop", "row")
    parts = lax.all_to_all(
        half.reshape(count, -1, width), axes, 0, 0, axis_index_groups=groups, tiled=True
    )
    share = jnp.sum(parts, axis=0)
    spread = jnp.broadcast_to(share[None], (count,) + share.shape)
    mine = lax.all_to_all(spread, axes, 0, 0, axis_index_groups=groups, tiled=True)
    mine = mine.reshape(total // 2, width)
    other_half = core_swap(mine, size)

    number = mats.shape[0]
    big, low = ((number, width, width), FL, "a"), ((number, width, width), BF, "a")
    pb_out, head_out = ((heads, width), FL, "v"), ((bins_n, width), FL, "v")
    norm_out = ((norms.shape[0], width), FL, "v")
    res = call(
        functools.partial(update_kernel, dims),
        [(scal, "s")]
        + [
            (value, "k")
            for value in (
                mine,
                other_half,
                mats,
                mats_m,
                mats_v,
                pbt,
                pbias_m.T,
                pbias_v.T,
                headt,
                head_m.T,
                head_v.T,
                norms,
                norms_m,
                norms_v,
            )
        ],
        [((8, width), FL, "v"), big, big, big, low]
        + [pb_out] * 3
        + [head_out] * 3
        + [norm_out] * 3,
        [pltpu.VMEM((total, width), FL)]
        + [pltpu.VMEM((number, width, width), FL)] * 3
        + [pltpu.VMEM((number, width, width), BF), pltpu.SemaphoreType.DMA((4, number))],
    )
    scalars = res[0]
    return (
        scalars[0, 0],
        scalars[1, 0],
        scalars[2, 0],
        *res[1:5],
        *(value.T for value in res[5:11]),
        *res[11:14],
    )


def small_enough(pair, heads, size):
    _, rows, cols, width = pair.shape
    held = 4 * size * rows * cols * width * 4 + 4 * rows * heads * cols * cols * 4
    return (
        held <= 2**24
        and width == 2 * cols
        and rows == 4
        and heads == 4
        and size % 2 == 0
        and rows * size == cols
    )


def solution(mesh):
    crops, size = mesh.shape["crop"], mesh.shape["row"]

    def on_device(*args):
        if small_enough(args[0], args[6].shape[1], size):
            return fast_step(crops, size, *args)
        return general_step(*args)

    in_specs = (
        P("crop", "row", None, None),
        P("crop", "row", None),
        P("crop"),
        P(),
        P(),
        P(),
        P(),
        P(),
        P(),
        P(),
        P(),
        P(),
        P(),
        P(),
        P(),
    )
    out_specs = (P(), P(), P(), P(), P(), P(), P(), P(), P(), P(), P(), P(), P(), P(), P(), P())
    return jax.shard_map(
        on_device, mesh=mesh, in_specs=in_specs, out_specs=out_specs, check_vma=False
    )
```

```python
import functools

import jax
import jax.numpy as jnp
from jax import lax
from jax.experimental import pallas as pl
from jax.experimental.pallas import tpu as pltpu
from jax.sharding import PartitionSpec as P

STEP = 5


EPS_NORM = 1e-05
CLIP = 1.0
RATE = 0.05
BETA1 = 0.9
BETA2 = 0.95
ADAM_EPS = 1e-08
WDECAY = 0.01


def norm_fwd(v, gain, shift):
    mean = jnp.mean(v, axis=-1, keepdims=True)
    cent = v - mean
    rstd = lax.rsqrt(jnp.mean(cent * cent, axis=-1, keepdims=True) + EPS_NORM)
    unit = cent * rstd
    return (unit * gain + shift, unit, rstd)


def norm_back(grad, unit, rstd, gain):
    dgain = jnp.sum(grad * unit, axis=(0, 1))
    dshift = jnp.sum(grad, axis=(0, 1))
    dunit = grad * gain
    dval = rstd * (
        dunit
        - jnp.mean(dunit, axis=-1, keepdims=True)
        - unit * jnp.mean(dunit * unit, axis=-1, keepdims=True)
    )
    return (dval, dgain, dshift)


def matmul(value, weight):
    flat = value.reshape(-1, value.shape[-1])
    out = jnp.dot(flat, weight, preferred_element_type=jnp.float32)
    return out.reshape(value.shape[:-1] + (weight.shape[1],))


def wgrad(value, grad):
    return jnp.einsum("ijc,ijd->cd", value, grad, preferred_element_type=jnp.float32)


def adam(weight, grad, first, second):
    first_new = BETA1 * first + (1.0 - BETA1) * grad
    second_new = BETA2 * second + (1.0 - BETA2) * grad * grad
    m_hat = first_new / (1.0 - BETA1**STEP)
    v_hat = second_new / (1.0 - BETA2**STEP)
    weight_new = weight - RATE * (m_hat / (jnp.sqrt(v_hat) + ADAM_EPS) + WDECAY * weight)
    return (first_new, second_new, weight_new)


def general_step(
    pair,
    bins,
    lengths,
    mats,
    mats_m,
    mats_v,
    pbias,
    pbias_m,
    pbias_v,
    head,
    head_m,
    head_v,
    norms,
    norms_m,
    norms_v,
):
    bf = jnp.bfloat16
    fl = jnp.float32
    width = mats.shape[1]
    rows = pair.shape[1]
    cols = pair.shape[2]
    heads = pbias.shape[1]
    size_head = width // heads
    scale = size_head ** (-0.5)
    start_pair = pair[0]
    first_row = lax.axis_index("row") * rows
    limit = lengths[0]
    row_ok = first_row + jnp.arange(rows) < limit
    col_ok = jnp.arange(cols) < limit
    pmask = (row_ok[:, None] & col_ok[None, :]).astype(fl)
    m3 = pmask[..., None]
    wl = mats.astype(bf)
    pl = pbias.astype(bf)
    hl = head.astype(bf)
    w_tri = jnp.concatenate([wl[0], wl[1], wl[2], wl[3], wl[4]], axis=1)
    w_att = jnp.concatenate([wl[6], wl[7], wl[8], wl[9]], axis=1)
    h0, unit0, rstd0 = norm_fwd(start_pair, norms[0], norms[1])
    h0b = h0.astype(bf)
    proj = matmul(h0b, w_tri)
    sig_a = jax.nn.sigmoid(proj[..., width : 2 * width])
    sig_b = jax.nn.sigmoid(proj[..., 3 * width : 4 * width])
    gate = jax.nn.sigmoid(proj[..., 4 * width :])
    a_low = (sig_a * proj[..., :width] * m3).astype(bf)
    b_low = (sig_b * proj[..., 2 * width : 3 * width] * m3).astype(bf)
    b_all = lax.all_gather(b_low, "row", axis=0, tiled=True)
    prod = jnp.einsum("ikc,jkc->ijc", a_low, b_all, preferred_element_type=fl)
    y_val, unit2, rstd2 = norm_fwd(prod, norms[2], norms[3])
    y_low = y_val.astype(bf)
    out1 = matmul(y_low, wl[5])
    z1 = start_pair + gate * out1
    h1, unit4, rstd4 = norm_fwd(z1, norms[4], norms[5])
    h1b = h1.astype(bf)
    qkvg = matmul(h1b, w_att)
    query = qkvg[..., :width].astype(bf).reshape(rows, cols, heads, size_head)
    keys = qkvg[..., width : 2 * width].astype(bf).reshape(rows, cols, heads, size_head)
    values = qkvg[..., 2 * width : 3 * width].astype(bf).reshape(rows, cols, heads, size_head)
    gate2 = jax.nn.sigmoid(qkvg[..., 3 * width :])
    tb_low = matmul(h1b, pl).astype(bf)
    tb_all = lax.all_gather(tb_low, "row", axis=0, tiled=True)
    tb_heads = jnp.transpose(tb_all, (2, 0, 1)).astype(fl)
    scores = (
        jnp.einsum("ijhd,ikhd->ihjk", query, keys, preferred_element_type=fl) * scale
        + tb_heads[None]
    )
    scores = jnp.where(col_ok[None, None, None, :], scores, -1000000000.0)
    probs = jax.nn.softmax(scores, axis=-1)
    p_low = probs.astype(bf)
    att = jnp.einsum("ihjk,ikhd->ijhd", p_low, values, preferred_element_type=fl).reshape(
        rows, cols, width
    )
    u_low = (gate2 * att).astype(bf)
    z2 = z1 + matmul(u_low, wl[10])
    h2, unit6, rstd6 = norm_fwd(z2, norms[6], norms[7])
    h2b = h2.astype(bf)
    logits = matmul(h2b, hl)
    lse = jax.nn.logsumexp(logits, axis=-1)
    onehot = (bins[0][..., None] == jnp.arange(logits.shape[-1])).astype(fl)
    pick = jnp.sum(logits * onehot, axis=-1)
    loss = jnp.sum(pmask * (lse - pick))
    count = jnp.sum(pmask)
    dlog = (m3 * (jnp.exp(logits - lse[..., None]) - onehot)).astype(bf)
    dhead = wgrad(h2b, dlog)
    dz2, dg6, ds6 = norm_back(matmul(dlog, hl.T), unit6, rstd6, norms[6])
    dout2 = dz2.astype(bf)
    dw10 = wgrad(u_low, dout2)
    du = matmul(dout2, wl[10].T)
    dgate2 = du * att
    datt = (du * gate2).astype(bf).reshape(rows, cols, heads, size_head)
    dprob = jnp.einsum("ijhd,ikhd->ihjk", datt, values, preferred_element_type=fl)
    dvals = jnp.einsum("ihjk,ijhd->ikhd", p_low, datt, preferred_element_type=fl)
    dscore = (probs * (dprob - jnp.sum(dprob * probs, axis=-1, keepdims=True))).astype(bf)
    dquery = jnp.einsum("ihjk,ikhd->ijhd", dscore, keys, preferred_element_type=fl) * scale
    dkeys = jnp.einsum("ihjk,ijhd->ikhd", dscore, query, preferred_element_type=fl) * scale
    dtb = jnp.sum(dscore.astype(fl), axis=0)
    dtb_own = lax.psum_scatter(dtb, "row", scatter_dimension=1, tiled=True)
    dtb_low = jnp.transpose(dtb_own, (1, 2, 0)).astype(bf)
    dpbias = wgrad(h1b, dtb_low)
    dqkvg = jnp.concatenate(
        [
            dquery.reshape(rows, cols, width),
            dkeys.reshape(rows, cols, width),
            dvals.reshape(rows, cols, width),
            dgate2 * gate2 * (1.0 - gate2),
        ],
        axis=-1,
    ).astype(bf)
    dw_att = wgrad(h1b, dqkvg)
    dh1 = matmul(dqkvg, w_att.T) + matmul(dtb_low, pl.T)
    dn4, dg4, ds4 = norm_back(dh1, unit4, rstd4, norms[4])
    dz1 = dz2 + dn4
    dout1 = (dz1 * gate).astype(bf)
    dw5 = wgrad(y_low, dout1)
    dgate = dz1 * out1
    dxn, dg2, ds2 = norm_back(matmul(dout1, wl[5].T), unit2, rstd2, norms[2])
    dx_low = dxn.astype(bf)
    dside_a = jnp.einsum("ijc,jkc->ikc", dx_low, b_all, preferred_element_type=fl)
    dside_b = lax.psum_scatter(
        jnp.einsum("ijc,ikc->jkc", dx_low, a_low, preferred_element_type=fl),
        "row",
        scatter_dimension=0,
        tiled=True,
    )
    da_r = dside_a.astype(bf).astype(fl)
    db_r = dside_b.astype(bf).astype(fl)
    dproj = jnp.concatenate(
        [
            da_r * sig_a * m3,
            da_r * proj[..., :width] * m3 * sig_a * (1.0 - sig_a),
            db_r * sig_b * m3,
            db_r * proj[..., 2 * width : 3 * width] * m3 * sig_b * (1.0 - sig_b),
            dgate * gate * (1.0 - gate),
        ],
        axis=-1,
    ).astype(bf)
    dw_tri = wgrad(h0b, dproj)
    dh0 = matmul(dproj, w_tri.T)
    unused, dg0, ds0 = norm_back(dh0, unit0, rstd0, norms[0])
    pieces = [dw_tri[:, idx * width : (idx + 1) * width] for idx in range(5)]
    pieces = (
        pieces + [dw5] + [dw_att[:, idx * width : (idx + 1) * width] for idx in range(4)] + [dw10]
    )
    dmats = jnp.stack(pieces)
    dnorms = jnp.stack([dg0, ds0, dg2, ds2, dg4, ds4, dg6, ds6])
    dmats, dpbias, dhead, dnorms, loss, count = lax.psum(
        (dmats, dpbias, dhead, dnorms, loss, count), ("crop", "row")
    )
    grad_norm = jnp.sqrt(
        jnp.sum(dmats * dmats)
        + jnp.sum(dpbias * dpbias)
        + jnp.sum(dhead * dhead)
        + jnp.sum(dnorms * dnorms)
    )
    factor = jnp.minimum(1.0, CLIP / grad_norm)
    new_mats = adam(mats, dmats * factor, mats_m, mats_v)
    new_pbias = adam(pbias, dpbias * factor, pbias_m, pbias_v)
    new_head = adam(head, dhead * factor, head_m, head_v)
    new_norms = adam(norms, dnorms * factor, norms_m, norms_v)
    return (
        grad_norm,
        loss,
        count,
        new_mats[0],
        new_mats[1],
        new_mats[2],
        new_mats[2].astype(bf),
        new_pbias[0],
        new_pbias[1],
        new_pbias[2],
        new_head[0],
        new_head[1],
        new_head[2],
        new_norms[0],
        new_norms[1],
        new_norms[2],
    )


BF = jnp.bfloat16
FL = jnp.float32
VMEM_LIMIT = 24 * 2**20


def dot(lhs, rhs, left=1, right=0):
    return lax.dot_general(
        lhs, rhs, (((left,), (right,)), ((), ())), preferred_element_type=FL
    )


def sharp(lhs, rhs):
    return lax.dot_general(
        lhs,
        rhs,
        (((1,), (1,)), ((), ())),
        preferred_element_type=FL,
        precision=lax.Precision.HIGHEST,
    )


def row_norm(val, gain, shift):
    mean = jnp.mean(val, axis=-1, keepdims=True)
    cent = val - mean
    rstd = lax.rsqrt(jnp.mean(cent * cent, axis=-1, keepdims=True) + EPS_NORM)
    unit = cent * rstd
    return (unit * gain + shift).astype(BF), unit, rstd


def row_norm_back(grad, unit, rstd, gain):
    dgain = jnp.sum(grad * unit, axis=0, keepdims=True)
    dshift = jnp.sum(grad, axis=0, keepdims=True)
    dunit = grad * gain
    dval = rstd * (
        dunit
        - jnp.mean(dunit, axis=-1, keepdims=True)
        - unit * jnp.mean(dunit * unit, axis=-1, keepdims=True)
    )
    return dval, dgain, dshift


def iota(shape, dim):
    return lax.broadcasted_iota(jnp.int32, shape, dim)


def fetch(pairs, sems):
    moves = [
        pltpu.make_async_copy(src, dst, sems.at[idx]) for idx, (src, dst) in enumerate(pairs)
    ]
    for move in moves:
        move.start()
    return moves


def start_kernel(copies, pair_hbm, norms_hbm, out_ref, pair_ref, norms_ref, sems):
    moves = fetch([(pair_hbm, pair_ref), (norms_hbm, norms_ref)], sems)
    for move in moves:
        move.wait()
    h0, _, _ = row_norm(pair_ref[...], norms_ref[0:1], norms_ref[1:2])
    for idx in range(copies):
        out_ref[idx] = h0


def pair_mask(dims, limit):
    rows, cols, width, _, _ = dims
    spot = iota((rows * cols, width), 0)
    col_ok = spot % cols < limit
    row_in = spot // cols

    def mask_of(block_row):
        return jnp.where(jnp.logical_and(col_ok, row_in + block_row < limit), 1.0, 0.0).astype(FL)

    return mask_of


def own_sides(h0, wl_ref, mask):
    width = h0.shape[1]
    w_own = jnp.concatenate([wl_ref[0], wl_ref[1], wl_ref[4]], axis=1)
    proj = dot(h0, w_own)
    fac = jax.nn.sigmoid(proj[:, width : 2 * width]) * mask
    return fac * proj[:, :width], fac, jax.nn.sigmoid(proj[:, 2 * width :])


def triangle_kernel(
    dims,
    scal_ref,
    own_ref,
    other_ref,
    pair_hbm,
    norms_ref,
    wl_ref,
    pbt_ref,
    tb_ref,
    side_hbm,
    fac_hbm,
    x_ref,
    z1_ref,
    h1_ref,
    pair_ref,
    b_ref,
    side_ref,
    fac_ref,
    part_ref,
    sems,
):
    rows, cols, width, heads, size = dims
    pairs = rows * cols
    limit, first_row, chip, core = (scal_ref[idx] for idx in range(4))
    (pair_move,) = fetch([(pair_hbm, pair_ref)], sems)
    mask_of = pair_mask(dims, limit)

    w_b = jnp.concatenate([wl_ref[2], wl_ref[3]], axis=1)

    def side_b(idx, _):
        for src, half in ((own_ref, core), (other_ref, 1 - core)):
            proj = dot(src[idx], w_b)
            sig = jax.nn.sigmoid(proj[:, width:])
            block = 2 * idx + half
            fac = sig * mask_of(block * rows)
            side = fac * proj[:, :width]
            base = pl.multiple_of(block * pairs, pairs)
            b_ref[pl.ds(base, pairs), :] = side.astype(BF).astype(FL)
            side_ref[pl.ds(base, pairs), :] = side
            fac_ref[pl.ds(base, pairs), :] = fac
        return 0

    lax.fori_loop(0, size // 2, side_b, 0)
    moves = fetch([(side_ref, side_hbm), (fac_ref, fac_hbm)], sems.at[pl.ds(1, 2)])

    side, _, gate = own_sides(own_ref[chip], wl_ref, mask_of(first_row))
    a_val = side.astype(BF).astype(FL)

    a_rows = [a_val[idx * cols : (idx + 1) * cols] for idx in range(rows)]

    def products(j, _):
        b_j = b_ref[pl.ds(pl.multiple_of(j * cols, cols), cols), :]
        for idx in range(rows):
            prod = a_rows[idx] * b_j
            fold = jnp.sum(prod.reshape(cols // 8, 8, width), axis=0)
            part_ref[pl.ds(pl.multiple_of((idx * cols + j) * 8, 8), 8), :] = fold
        return 0

    lax.fori_loop(0, cols, products, 0, unroll=2)
    x_val = part_ref[pl.ds(0, pairs, stride=8), :]
    for idx in range(1, 8):
        x_val = x_val + part_ref[pl.ds(idx, pairs, stride=8), :]

    x_ref[...] = x_val
    y_low, _, _ = row_norm(x_val, norms_ref[2:3], norms_ref[3:4])
    pair_move.wait()
    z1 = pair_ref[...] + gate * dot(y_low, wl_ref[5])
    z1_ref[...] = z1
    h1, _, _ = row_norm(z1, norms_ref[4:5], norms_ref[5:6])
    h1_ref[...] = h1
    tbt = dot(pbt_ref[...].astype(BF), h1, 1, 1).astype(BF).astype(FL)
    half = pairs // 2
    block = jnp.concatenate([tbt[:, :half], tbt[:, half:]], axis=0)
    for idx in range(size):
        tb_ref[idx] = block
    for move in moves:
        move.wait()


def project_kernel(
    dims,
    scal_ref,
    h1_ref,
    own_ref,
    other_ref,
    wl_ref,
    kcat_ref,
    vcat_ref,
    qblk_ref,
    gate2_ref,
    h0_ref,
    own_t_hbm,
    other_t_hbm,
    own_t_ref,
    other_t_ref,
    sems,
):
    rows, cols, width, heads, size = dims
    extra = own_t_ref.shape[1] - width
    for src, dst in ((own_ref, own_t_ref), (other_ref, other_t_ref)):
        for idx in range(size // 2):
            dst[idx, :width, :] = src[idx].astype(FL).T.astype(BF)
            dst[idx, width:, :] = jnp.ones((extra, rows * cols), BF)
    moves = fetch([(own_t_ref, own_t_hbm), (other_t_ref, other_t_hbm)], sems)
    h0_ref[...] = own_ref[scal_ref[2]]
    w_att = jnp.concatenate([wl_ref[6], wl_ref[7], wl_ref[8], wl_ref[9]], axis=1)
    proj = dot(h1_ref[...], w_att)
    gate2_ref[...] = jax.nn.sigmoid(proj[:, 3 * width :])
    lane_head = iota((cols, width), 1) // (width // heads)
    zero = jnp.zeros((cols, width), BF)
    for idx in range(rows):
        at, side = idx // 2, idx % 2
        lanes = slice(side * width, (side + 1) * width)
        span = slice(idx * cols, (idx + 1) * cols)
        query = proj[span, :width].astype(BF)
        qblk_ref[at, side * cols : (side + 1) * cols, lanes] = query
        qblk_ref[at, (1 - side) * cols : (2 - side) * cols, lanes] = zero
        for head in range(heads):
            put = slice(head * cols, (head + 1) * cols)
            keep = lane_head == head
            kcat_ref[at, put, lanes] = jnp.where(keep, proj[span, width : 2 * width], 0.0).astype(BF)
            vcat_ref[at, put, lanes] = jnp.where(
                keep, proj[span, 2 * width : 3 * width], 0.0
            ).astype(BF)
    for move in moves:
        move.wait()


def attention_kernel(
    dims,
    scal_ref,
    tb_ref,
    kcat_ref,
    vcat_ref,
    qblk_ref,
    gate2_ref,
    z1_ref,
    norms_ref,
    wl_ref,
    headt_hbm,
    bins_hbm,
    dtb_ref,
    pl_ref,
    dsl_ref,
    dblk_ref,
    u_ref,
    dout2_ref,
    dz2_ref,
    dgate2_ref,
    h2_ref,
    dlog_ref,
    stat_ref,
    bias_ref,
    prob_ref,
    swap_ref,
    headt_ref,
    bins_ref,
    sems,
):
    rows, cols, width, heads, size = dims
    pairs, lines = rows * cols, heads * cols
    scale = (width // heads) ** (-0.5)
    limit, first_row = scal_ref[0], scal_ref[1]
    moves = fetch([(headt_hbm, headt_ref), (bins_hbm, bins_ref)], sems)

    for half in range(2):
        for jl in range(2):
            lanes = slice(jl * cols, (jl + 1) * cols)
            got = [
                tb_ref[pl.ds(half * heads + head, size, stride=2 * heads), :][:, lanes]
                for head in range(heads)
            ]
            for duo in range(heads // 2):
                line = jnp.concatenate([got[2 * duo], got[2 * duo + 1]], axis=1)
                bias_ref[duo, pl.ds(2 * half + jl, size, stride=rows), :] = line
                bias_ref[duo, pl.ds(cols + 2 * half + jl, size, stride=rows), :] = line
    bias = jnp.concatenate([bias_ref[duo].T for duo in range(heads // 2)], axis=0)
    key_ok = iota((lines, 2 * cols), 0) % cols < limit
    att = []
    for at in range(rows // 2):
        score = dot(kcat_ref[at], qblk_ref[at], 1, 1) * scale + bias
        score = jnp.where(key_ok, score, -1000000000.0).reshape(heads, cols, 2 * cols)
        top = jnp.max(score, axis=1, keepdims=True)
        grown = jnp.exp(score - top)
        prob = (grown / jnp.sum(grown, axis=1, keepdims=True)).reshape(lines, 2 * cols)
        prob_ref[at] = prob
        low = prob.astype(BF)
        pl_ref[at] = low
        both = dot(low, vcat_ref[at], 0, 0)
        att += [both[:cols, :width], both[cols:, width:]]
    att = jnp.concatenate(att, axis=0)
    gate2 = gate2_ref[...]
    u_low = (gate2 * att).astype(BF)
    u_ref[...] = u_low
    z2 = z1_ref[...] + dot(u_low, wl_ref[10])
    h2, unit6, rstd6 = row_norm(z2, norms_ref[6:7], norms_ref[7:8])
    h2_ref[...] = h2
    for move in moves:
        move.wait()
    headt = headt_ref[...].astype(BF)
    logits = dot(headt, h2, 1, 1)
    spot = iota((1, pairs), 1)
    ok = jnp.logical_and(spot % cols < limit, spot // cols + first_row < limit)
    mask = jnp.where(ok, 1.0, 0.0).astype(FL)
    bins = jnp.concatenate([bins_ref[idx : idx + 1, :] for idx in range(rows)], axis=1)
    onehot = jnp.where(iota(logits.shape, 0) == bins, 1.0, 0.0).astype(FL)
    top = jnp.max(logits, axis=0, keepdims=True)
    lse = top + jnp.log(jnp.sum(jnp.exp(logits - top), axis=0, keepdims=True))
    pick = jnp.sum(logits * onehot, axis=0, keepdims=True)
    loss = jnp.sum(mask * (lse - pick), axis=1, keepdims=True)
    count = jnp.sum(mask, axis=1, keepdims=True)
    dlog = (mask * (jnp.exp(logits - lse) - onehot)).astype(BF)
    dlog_ref[...] = dlog
    dz2, dg6, ds6 = row_norm_back(dot(dlog, headt, 0, 0), unit6, rstd6, norms_ref[6:7])
    dz2_ref[...] = dz2
    stat_ref[0:1, :] = dg6
    stat_ref[1:2, :] = ds6
    stat_ref[2:3, :] = jnp.broadcast_to(loss, (1, width))
    stat_ref[3:4, :] = jnp.broadcast_to(count, (1, width))
    stat_ref[4:8, :] = jnp.zeros((4, width), FL)
    dout2 = dz2.astype(BF)
    dout2_ref[...] = dout2
    du = dot(dout2, wl_ref[10], 1, 1)
    dgate2_ref[...] = (du * att * gate2 * (1.0 - gate2)).astype(BF)
    datt = (du * gate2).astype(BF)
    zero = jnp.zeros((cols, width), BF)
    total = None
    for at in range(rows // 2):
        first = datt[(2 * at) * cols : (2 * at + 1) * cols]
        second = datt[(2 * at + 1) * cols : (2 * at + 2) * cols]
        block = jnp.concatenate(
            [
                jnp.concatenate([first, zero], axis=1),
                jnp.concatenate([zero, second], axis=1),
            ],
            axis=0,
        )
        dblk_ref[at] = block
        dprob = dot(vcat_ref[at], block, 1, 1)
        prob = prob_ref[at]
        inner = jnp.sum((dprob * prob).reshape(heads, cols, 2 * cols), axis=1, keepdims=True)
        dscore = prob.reshape(heads, cols, 2 * cols) * (
            dprob.reshape(heads, cols, 2 * cols) - inner
        )
        low = dscore.reshape(lines, 2 * cols).astype(BF)
        dsl_ref[at] = low
        total = low.astype(FL) if total is None else total + low.astype(FL)
    for duo in range(heads // 2):
        turned = total[duo * 2 * cols : (duo + 1) * 2 * cols].T
        swap_ref[duo] = turned[:cols] + turned[cols:]
    for half in range(2):
        for head in range(heads):
            inside = slice((head % 2) * cols, (head % 2 + 1) * cols)
            line = jnp.concatenate(
                [
                    swap_ref[head // 2, pl.ds(2 * half + jl, size, stride=rows), :][:, inside]
                    for jl in range(2)
                ],
                axis=1,
            )
            dtb_ref[pl.ds(half * heads + head, size, stride=2 * heads), :] = line


def attention_grad_kernel(
    dims,
    scal_ref,
    kcat_ref,
    qblk_ref,
    pl_ref,
    dsl_ref,
    dblk_ref,
    u_ref,
    dout2_ref,
    dgate2_ref,
    h1_ref,
    h2_ref,
    dlog_ref,
    h0_ref,
    x_ref,
    z1_ref,
    norms_ref,
    wl_ref,
    early_ref,
    dh1_ref,
    loc_ref,
    y_ref,
    dqkvg_ref,
):
    rows, cols, width, heads, size = dims
    mask = pair_mask(dims, scal_ref[0])(scal_ref[1])
    side, fac, gate = own_sides(h0_ref[...], wl_ref, mask)
    y_low, unit2, rstd2 = row_norm(x_ref[...], norms_ref[2:3], norms_ref[3:4])
    _, unit4, rstd4 = row_norm(z1_ref[...], norms_ref[4:5], norms_ref[5:6])
    y_ref[...] = y_low
    loc_ref[0] = side.astype(BF).astype(FL)
    loc_ref[1] = fac
    loc_ref[2] = side * (1.0 - fac)
    loc_ref[3] = gate
    loc_ref[4] = dot(y_low, wl_ref[5])
    loc_ref[5] = unit2
    loc_ref[6] = jnp.broadcast_to(rstd2, unit2.shape)
    loc_ref[7] = unit4
    loc_ref[8] = jnp.broadcast_to(rstd4, unit4.shape)
    scale = (width // heads) ** (-0.5)
    lane_head = iota((cols, width), 1) // (width // heads)

    def diagonal(val):
        out = jnp.zeros((cols, width), FL)
        for head in range(heads):
            out = jnp.where(lane_head == head, val[head * cols : (head + 1) * cols], out)
        return out

    for at in range(rows // 2):
        dquery = dot(dsl_ref[at], kcat_ref[at], 0, 0)
        dkeys = dot(dsl_ref[at], qblk_ref[at])
        dvals = dot(pl_ref[at], dblk_ref[at])
        for side in range(2):
            idx = 2 * at + side
            lanes = slice(side * width, (side + 1) * width)
            span = slice(idx * cols, (idx + 1) * cols)
            dqkvg_ref[span, :width] = (
                dquery[side * cols : (side + 1) * cols, lanes] * scale
            ).astype(BF)
            dqkvg_ref[span, width : 2 * width] = (diagonal(dkeys[:, lanes]) * scale).astype(BF)
            dqkvg_ref[span, 2 * width : 3 * width] = diagonal(dvals[:, lanes]).astype(BF)
    dqkvg_ref[:, 3 * width :] = dgate2_ref[...]
    dqkvg = dqkvg_ref[...]
    w_att = jnp.concatenate([wl_ref[6], wl_ref[7], wl_ref[8], wl_ref[9]], axis=1)
    dh1_ref[...] = dot(dqkvg, w_att, 1, 1)
    dw_att = dot(h1_ref[...], dqkvg, 0, 0)
    for idx in range(4):
        early_ref[idx * width : (idx + 1) * width, :] = dw_att[:, idx * width : (idx + 1) * width]
    early_ref[4 * width : 5 * width, :] = dot(u_ref[...], dout2_ref[...], 0, 0)
    early_ref[5 * width :, :] = dot(dlog_ref[...], h2_ref[...])


def triangle_grad_kernel(
    dims,
    scal_ref,
    dtb_ref,
    early_ref,
    dh1_ref,
    dz2_ref,
    stat_ref,
    h1_ref,
    y_ref,
    loc_ref,
    side_hbm,
    fac_hbm,
    own_t_hbm,
    other_t_hbm,
    norms_ref,
    wl_ref,
    pbt_ref,
    keep_ref,
    give_ref,
    flat_ref,
    dx_ref,
    side_ref,
    fac_ref,
    own_t_ref,
    other_t_ref,
    sems,
):
    rows, cols, width, heads, size = dims
    pairs = rows * cols
    chip, core = scal_ref[2], scal_ref[3]
    moves = fetch(
        [
            (side_hbm, side_ref),
            (own_t_hbm, own_t_ref),
            (other_t_hbm, other_t_ref),
            (fac_hbm, fac_ref),
        ],
        sems,
    )
    got = dtb_ref[0]
    for idx in range(1, size):
        got = got + dtb_ref[idx]
    dtbt = jnp.concatenate([got[:heads], got[heads:]], axis=1).astype(BF)
    h1 = h1_ref[...]
    dpbt = dot(dtbt, h1)
    dh1 = dh1_ref[...] + dot(dtbt, pbt_ref[...].astype(BF), 0, 0)
    dn4, dg4, ds4 = row_norm_back(dh1, loc_ref[7], loc_ref[8], norms_ref[4:5])
    dz1 = dz2_ref[...] + dn4
    gate = loc_ref[3]
    dout1 = (dz1 * gate).astype(BF)
    dgate = dz1 * loc_ref[4] * gate * (1.0 - gate)
    dx, dg2, ds2 = row_norm_back(
        dot(dout1, wl_ref[5], 1, 1), loc_ref[5], loc_ref[6], norms_ref[2:3]
    )
    dx_ref[...] = dx.astype(BF).astype(FL)

    moves[0].wait()

    def da_step(j, acc):
        b_j = side_ref[pl.ds(pl.multiple_of(j * cols, cols), cols), :].astype(BF).astype(FL)
        return tuple(
            acc[idx] + dx_ref[pl.ds(idx * cols + j, 1), :] * b_j for idx in range(rows)
        )

    acc = lax.fori_loop(
        0, cols, da_step, tuple(jnp.zeros((cols, width), FL) for _ in range(rows)), unroll=2
    )
    da = jnp.concatenate(acc, axis=0).astype(BF).astype(FL)
    own = jnp.concatenate(
        [
            (da * loc_ref[1]).astype(BF),
            (da * loc_ref[2]).astype(BF),
            dgate.astype(BF),
        ],
        axis=1,
    )
    for move in moves[1:]:
        move.wait()
    dw_own = dot(own_t_ref[chip], own)

    a_rows = [loc_ref[0, idx * cols : (idx + 1) * cols, :] for idx in range(rows)]

    def db_step(idx, acc):
        for src, half in ((own_t_ref, core), (other_t_ref, 1 - core)):
            block = 2 * idx + half
            pieces = []
            for row in range(rows):
                j = block * rows + row
                base = pl.multiple_of(j * cols, cols)
                db = dx_ref[pl.ds(j, 1), :] * a_rows[0]
                for own_row in range(1, rows):
                    db = db + dx_ref[pl.ds(own_row * cols + j, 1), :] * a_rows[own_row]
                fac = fac_ref[pl.ds(base, cols), :]
                rest = side_ref[pl.ds(base, cols), :] * (1.0 - fac)
                pieces.append(
                    jnp.concatenate([(db * fac).astype(BF), (db * rest).astype(BF)], axis=1)
                )
            acc = acc + dot(src[idx], jnp.concatenate(pieces, axis=0))
        return acc

    tall = own_t_ref.shape[1]
    dw_b = jnp.zeros((tall, 2 * width), FL)
    for idx in range(size // 2):
        dw_b = db_step(idx, dw_b)

    parts = [
        dw_own[:, :width],
        dw_own[:, width : 2 * width],
        dw_b[:, :width],
        dw_b[:, width:],
        dw_own[:, 2 * width :],
    ]
    ones = jnp.ones((8, width), FL)
    ds0 = jnp.zeros((8, width), FL)
    mixed = jnp.zeros((width, width), FL)
    for idx, part in enumerate(parts):
        weight = wl_ref[idx].astype(FL)
        flat_ref[idx * width : (idx + 1) * width, :] = part[:width]
        mixed = mixed + weight * part[:width]
        ds0 = ds0 + sharp(part[width : width + 8], weight)
    dg0 = (sharp(ones, mixed) - norms_ref[1:2] * ds0) / norms_ref[0:1]
    flat_ref[5 * width : 6 * width, :] = dot(y_ref[...], dout1, 0, 0)
    mats = 11 * width
    flat_ref[6 * width : mats, :] = early_ref[: 5 * width, :]
    bins_n = early_ref.shape[0] - 5 * width
    flat_ref[mats : mats + bins_n, :] = early_ref[5 * width :, :]
    base = mats + bins_n
    flat_ref[base : base + heads, :] = dpbt
    flat_ref[base + heads : base + 8, :] = jnp.zeros((8 - heads, width), FL)
    base += 8
    for idx, line in enumerate((dg0[:1], ds0[:1], dg2, ds2, dg4, ds4)):
        flat_ref[base + idx : base + idx + 1, :] = line
    flat_ref[base + 6 : base + 10, :] = stat_ref[0:4, :]
    total = flat_ref.shape[0]
    flat_ref[base + 10 :, :] = jnp.zeros((total - base - 10, width), FL)
    half = total // 2
    keep_ref[...] = flat_ref[pl.ds(pl.multiple_of(core * half, half), half), :]
    give_ref[...] = flat_ref[pl.ds(pl.multiple_of((1 - core) * half, half), half), :]


def update_kernel(
    dims,
    scal_ref,
    mine_ref,
    other_ref,
    mats_hbm,
    mats_m_ref,
    mats_v_ref,
    pb_ref,
    pb_m_ref,
    pb_v_ref,
    head_ref,
    head_m_ref,
    head_v_ref,
    norms_ref,
    norms_m_ref,
    norms_v_ref,
    norm_out,
    loss_out,
    count_out,
    mats_m_out,
    mats_v_out,
    mats_out,
    mats_low_out,
    pb_m_out,
    pb_v_out,
    pb_out,
    head_m_out,
    head_v_out,
    head_out,
    norms_m_out,
    norms_v_out,
    norms_out,
    flat_ref,
    m_buf,
    v_buf,
    w_buf,
    low_buf,
    mats_ref,
    sems,
    mats_sem,
):
    rows, cols, width, heads, size = dims
    (mats_move,) = fetch([(mats_hbm, mats_ref)], mats_sem)
    core = scal_ref[3]
    half = mine_ref.shape[0]
    flat_ref[pl.ds(pl.multiple_of(core * half, half), half), :] = mine_ref[...]
    flat_ref[pl.ds(pl.multiple_of((1 - core) * half, half), half), :] = other_ref[...]
    count = mats_ref.shape[0]
    mats = count * width
    bins_n = head_ref.shape[0]
    base = mats + bins_n
    grads = flat_ref[: base + 16, :]
    square = jnp.sum(grads * grads, axis=0, keepdims=True)
    norm = jnp.sqrt(jnp.sum(square, axis=1, keepdims=True))
    factor = jnp.minimum(1.0, CLIP / norm)
    norm_out[...] = norm
    loss_out[...] = flat_ref[base + 16 : base + 17, 0:1]
    count_out[...] = flat_ref[base + 17 : base + 18, 0:1]

    def step(weight, grad, first, second):
        return adam(weight, grad * factor, first, second)

    moves = []
    mats_move.wait()
    for idx in range(count):
        first, second, weight = step(
            mats_ref[idx],
            flat_ref[idx * width : (idx + 1) * width, :],
            mats_m_ref[idx],
            mats_v_ref[idx],
        )
        m_buf[idx] = first
        v_buf[idx] = second
        w_buf[idx] = weight
        low_buf[idx] = weight.astype(BF)
        for at, (buf, out) in enumerate(
            ((m_buf, mats_m_out), (v_buf, mats_v_out), (w_buf, mats_out), (low_buf, mats_low_out))
        ):
            move = pltpu.make_async_copy(buf.at[idx], out.at[idx], sems.at[at, idx])
            move.start()
            moves.append(move)
    small = (
        (mats, bins_n, head_ref, head_m_ref, head_v_ref, head_m_out, head_v_out, head_out),
        (base, heads, pb_ref, pb_m_ref, pb_v_ref, pb_m_out, pb_v_out, pb_out),
        (base + 8, 8, norms_ref, norms_m_ref, norms_v_ref, norms_m_out, norms_v_out, norms_out),
    )
    for at, tall, w_in, m_in, v_in, m_out, v_out, w_out in small:
        m_out[...], v_out[...], w_out[...] = step(
            w_in[...], flat_ref[at : at + tall, :], m_in[...], v_in[...]
        )
    for move in moves:
        move.wait()


def call(kernel, args, outs, scratch=(), limit=VMEM_LIMIT, flops=10**7):
    spots = {"s": pltpu.SMEM, "v": pltpu.VMEM, "h": pltpu.HBM}
    return pl.pallas_call(
        kernel,
        out_shape=[
            pltpu.HBM(shape, kind) if spot == "h" else jax.ShapeDtypeStruct(shape, kind)
            for shape, kind, spot in outs
        ],
        in_specs=[pl.BlockSpec(memory_space=spots[spot]) for _, spot in args],
        out_specs=[pl.BlockSpec(memory_space=spots[spot]) for _, _, spot in outs],
        scratch_shapes=list(scratch),
        compiler_params=pltpu.CompilerParams(vmem_limit_bytes=limit),
        cost_estimate=pl.CostEstimate(flops=flops, bytes_accessed=10**6, transcendentals=0),
    )(
        *(
            pltpu.with_memory_space_constraint(value, pltpu.HBM) if spot == "h" else value
            for value, spot in args
        )
    )


def same_core_groups(crops, size):
    return [
        [crop * size + idx for crop in range(crops) for idx in range(core, size, 2)]
        for core in range(2)
    ]


def core_swap(value, size):
    return lax.ppermute(value, "row", [(idx, idx ^ 1) for idx in range(size)])


def fast_step(
    crops,
    size,
    pair,
    bins,
    lengths,
    mats,
    mats_m,
    mats_v,
    pbias,
    pbias_m,
    pbias_v,
    head,
    head_m,
    head_v,
    norms,
    norms_m,
    norms_v,
):
    rows, cols, width = pair.shape[1:]
    heads, bins_n = pbias.shape[1], head.shape[1]
    pairs, lines = rows * cols, heads * cols
    dims = (rows, cols, width, heads, size)
    chips = size // 2
    place = lax.axis_index("row")
    scal = jnp.stack([lengths[0], place * rows, place // 2, place % 2]).astype(jnp.int32)
    start = pair.reshape(pairs, width)
    wl = mats.astype(BF)
    pbt, headt = pbias.T, head.T

    (copies,) = call(
        functools.partial(start_kernel, chips),
        [(start, "h"), (norms, "h")],
        [((chips, pairs, width), BF, "v")],
        [
            pltpu.VMEM((pairs, width), FL),
            pltpu.VMEM(norms.shape, FL),
            pltpu.SemaphoreType.DMA((2,)),
        ],
    )
    near = [list(range(core, size, 2)) for core in range(2)]
    own = lax.all_to_all(copies, "row", 0, 0, axis_index_groups=near, tiled=True)
    other = core_swap(own, size)

    full = (size * pairs, width)
    tb, side_b, fac_b, x_val, z1, h1 = call(
        functools.partial(triangle_kernel, dims),
        [
            (scal, "s"),
            (own, "v"),
            (other, "v"),
            (start, "h"),
            (norms, "v"),
            (wl, "v"),
            (pbt, "v"),
        ],
        [
            ((size, 2 * heads, 2 * cols), FL, "v"),
            (full, FL, "h"),
            (full, FL, "h"),
            ((pairs, width), FL, "v"),
            ((pairs, width), FL, "v"),
            ((pairs, width), BF, "v"),
        ],
        [
            pltpu.VMEM((pairs, width), FL),
            pltpu.VMEM(full, FL),
            pltpu.VMEM(full, FL),
            pltpu.VMEM(full, FL),
            pltpu.VMEM((pairs * 8, width), FL),
            pltpu.SemaphoreType.DMA((3,)),
        ],
    )

    tb_all = lax.all_to_all(tb, "row", 0, 0, tiled=True)
    turned = (chips, width + 16, pairs)
    kcat, vcat, qblk, gate2, h0, own_t, other_t = call(
        functools.partial(project_kernel, dims),
        [(scal, "s"), (h1, "v"), (own, "v"), (other, "v"), (wl, "v")],
        [
            ((rows // 2, lines, 2 * width), BF, "v"),
            ((rows // 2, lines, 2 * width), BF, "v"),
            ((rows // 2, 2 * cols, 2 * width), BF, "v"),
            ((pairs, width), FL, "v"),
            ((pairs, width), BF, "v"),
            (turned, BF, "h"),
            (turned, BF, "h"),
        ],
        [pltpu.VMEM(turned, BF), pltpu.VMEM(turned, BF), pltpu.SemaphoreType.DMA((2,))],
    )
    bias_shape = (size * 2 * heads, 2 * cols)
    dtb, pl_low, dsl, dblk, u_low, dout2, dz2, dgate2, h2, dlog, stat = call(
        functools.partial(attention_kernel, dims),
        [
            (scal, "s"),
            (tb_all.reshape(bias_shape), "v"),
            (kcat, "v"),
            (vcat, "v"),
            (qblk, "v"),
            (gate2, "v"),
            (z1, "v"),
            (norms, "v"),
            (wl, "v"),
            (headt, "h"),
            (bins[0], "h"),
        ],
        [
            (bias_shape, FL, "v"),
            ((rows // 2, lines, 2 * cols), BF, "v"),
            ((rows // 2, lines, 2 * cols), BF, "v"),
            ((rows // 2, 2 * cols, 2 * width), BF, "v"),
            ((pairs, width), BF, "v"),
            ((pairs, width), BF, "v"),
            ((pairs, width), FL, "v"),
            ((pairs, width), BF, "v"),
            ((pairs, width), BF, "v"),
            ((bins_n, pairs), BF, "v"),
            ((8, width), FL, "v"),
        ],
        [
            pltpu.VMEM((heads // 2, 2 * cols, 2 * cols), FL),
            pltpu.VMEM((rows // 2, lines, 2 * cols), FL),
            pltpu.VMEM((heads // 2, cols, 2 * cols), FL),
            pltpu.VMEM((bins_n, width), FL),
            pltpu.VMEM((rows, cols), jnp.int32),
            pltpu.SemaphoreType.DMA((2,)),
        ],
    )

    dtb_all = lax.all_to_all(dtb.reshape(size, 2 * heads, 2 * cols), "row", 0, 0, tiled=True)
    early, dh1, loc, y_low = call(
        functools.partial(attention_grad_kernel, dims),
        [(scal, "s")]
        + [
            (value, "v")
            for value in (
                kcat,
                qblk,
                pl_low,
                dsl,
                dblk,
                u_low,
                dout2,
                dgate2,
                h1,
                h2,
                dlog,
                h0,
                x_val,
                z1,
                norms,
                wl,
            )
        ],
        [
            ((5 * width + bins_n, width), FL, "v"),
            ((pairs, width), FL, "v"),
            ((9, pairs, width), FL, "v"),
            ((pairs, width), BF, "v"),
        ],
        [pltpu.VMEM((pairs, 4 * width), BF)],
    )
    used = mats.shape[0] * width + bins_n + 18
    unit = 8 * crops * size
    total = -(-used // unit) * unit
    keep, give = call(
        functools.partial(triangle_grad_kernel, dims),
        [(scal, "s")]
        + [(value, "v") for value in (dtb_all, early, dh1, dz2, stat, h1, y_low, loc)]
        + [(value, "h") for value in (side_b, fac_b, own_t, other_t)]
        + [(value, "v") for value in (norms, wl, pbt)],
        [((total // 2, width), FL, "v"), ((total // 2, width), FL, "v")],
        [
            pltpu.VMEM((total, width), FL),
            pltpu.VMEM((pairs, width), FL),
            pltpu.VMEM(full, FL),
            pltpu.VMEM(full, FL),
            pltpu.VMEM(turned, BF),
            pltpu.VMEM(turned, BF),
            pltpu.SemaphoreType.DMA((4,)),
        ],
    )

    half = keep + core_swap(give, size)
    count = crops * chips
    groups = same_core_groups(crops, size)
    axes = ("crop", "row")
    parts = lax.all_to_all(
        half.reshape(count, -1, width), axes, 0, 0, axis_index_groups=groups, tiled=True
    )
    share = jnp.sum(parts, axis=0)
    spread = jnp.broadcast_to(share[None], (count,) + share.shape)
    mine = lax.all_to_all(spread, axes, 0, 0, axis_index_groups=groups, tiled=True)
    mine = mine.reshape(total // 2, width)
    other_half = core_swap(mine, size)

    number = mats.shape[0]
    big, low = ((number, width, width), FL, "h"), ((number, width, width), BF, "h")
    pb_out, head_out = ((heads, width), FL, "v"), ((bins_n, width), FL, "v")
    norm_out = ((norms.shape[0], width), FL, "v")
    res = call(
        functools.partial(update_kernel, dims),
        [(scal, "s"), (mine, "v"), (other_half, "v"), (mats, "h")]
        + [
            (value, "v")
            for value in (
                mats_m,
                mats_v,
                pbt,
                pbias_m.T,
                pbias_v.T,
                headt,
                head_m.T,
                head_v.T,
                norms,
                norms_m,
                norms_v,
            )
        ],
        [((1, 1), FL, "v")] * 3
        + [big, big, big, low]
        + [pb_out] * 3
        + [head_out] * 3
        + [norm_out] * 3,
        [pltpu.VMEM((total, width), FL)]
        + [pltpu.VMEM((number, width, width), FL)] * 3
        + [
            pltpu.VMEM((number, width, width), BF),
            pltpu.VMEM((number, width, width), FL),
            pltpu.SemaphoreType.DMA((4, number)),
            pltpu.SemaphoreType.DMA((1,)),
        ],
    )
    return (
        *(value.reshape(()) for value in res[:3]),
        *res[3:7],
        *(value.T for value in res[7:13]),
        *res[13:16],
    )


def small_enough(pair, heads, size):
    _, rows, cols, width = pair.shape
    held = 4 * size * rows * cols * width * 4 + 4 * rows * heads * cols * cols * 4
    return (
        held <= 2**24
        and width == 2 * cols
        and rows == 4
        and heads == 4
        and size % 2 == 0
        and rows * size == cols
    )


def solution(mesh):
    crops, size = mesh.shape["crop"], mesh.shape["row"]

    def on_device(*args):
        if small_enough(args[0], args[6].shape[1], size):
            return fast_step(crops, size, *args)
        return general_step(*args)

    in_specs = (
        P("crop", "row", None, None),
        P("crop", "row", None),
        P("crop"),
        P(),
        P(),
        P(),
        P(),
        P(),
        P(),
        P(),
        P(),
        P(),
        P(),
        P(),
        P(),
    )
    out_specs = (P(), P(), P(), P(), P(), P(), P(), P(), P(), P(), P(), P(), P(), P(), P(), P())
    return jax.shard_map(
        on_device, mesh=mesh, in_specs=in_specs, out_specs=out_specs, check_vma=False
    )
```

```python
import functools

import jax
import jax.numpy as jnp
from jax import lax
from jax.experimental import pallas as pl
from jax.experimental.pallas import tpu as pltpu
from jax.sharding import PartitionSpec as P

STEP = 5


EPS_NORM = 1e-05
CLIP = 1.0
RATE = 0.05
BETA1 = 0.9
BETA2 = 0.95
ADAM_EPS = 1e-08
WDECAY = 0.01


def norm_fwd(v, gain, shift):
    mean = jnp.mean(v, axis=-1, keepdims=True)
    cent = v - mean
    rstd = lax.rsqrt(jnp.mean(cent * cent, axis=-1, keepdims=True) + EPS_NORM)
    unit = cent * rstd
    return (unit * gain + shift, unit, rstd)


def norm_back(grad, unit, rstd, gain):
    dgain = jnp.sum(grad * unit, axis=(0, 1))
    dshift = jnp.sum(grad, axis=(0, 1))
    dunit = grad * gain
    dval = rstd * (
        dunit
        - jnp.mean(dunit, axis=-1, keepdims=True)
        - unit * jnp.mean(dunit * unit, axis=-1, keepdims=True)
    )
    return (dval, dgain, dshift)


def matmul(value, weight):
    flat = value.reshape(-1, value.shape[-1])
    out = jnp.dot(flat, weight, preferred_element_type=jnp.float32)
    return out.reshape(value.shape[:-1] + (weight.shape[1],))


def wgrad(value, grad):
    return jnp.einsum("ijc,ijd->cd", value, grad, preferred_element_type=jnp.float32)


def adam(weight, grad, first, second):
    first_new = BETA1 * first + (1.0 - BETA1) * grad
    second_new = BETA2 * second + (1.0 - BETA2) * grad * grad
    m_hat = first_new / (1.0 - BETA1**STEP)
    v_hat = second_new / (1.0 - BETA2**STEP)
    weight_new = weight - RATE * (m_hat / (jnp.sqrt(v_hat) + ADAM_EPS) + WDECAY * weight)
    return (first_new, second_new, weight_new)


def general_step(
    pair,
    bins,
    lengths,
    mats,
    mats_m,
    mats_v,
    pbias,
    pbias_m,
    pbias_v,
    head,
    head_m,
    head_v,
    norms,
    norms_m,
    norms_v,
):
    bf = jnp.bfloat16
    fl = jnp.float32
    width = mats.shape[1]
    rows = pair.shape[1]
    cols = pair.shape[2]
    heads = pbias.shape[1]
    size_head = width // heads
    scale = size_head ** (-0.5)
    start_pair = pair[0]
    first_row = lax.axis_index("row") * rows
    limit = lengths[0]
    row_ok = first_row + jnp.arange(rows) < limit
    col_ok = jnp.arange(cols) < limit
    pmask = (row_ok[:, None] & col_ok[None, :]).astype(fl)
    m3 = pmask[..., None]
    wl = mats.astype(bf)
    pl = pbias.astype(bf)
    hl = head.astype(bf)
    w_tri = jnp.concatenate([wl[0], wl[1], wl[2], wl[3], wl[4]], axis=1)
    w_att = jnp.concatenate([wl[6], wl[7], wl[8], wl[9]], axis=1)
    h0, unit0, rstd0 = norm_fwd(start_pair, norms[0], norms[1])
    h0b = h0.astype(bf)
    proj = matmul(h0b, w_tri)
    sig_a = jax.nn.sigmoid(proj[..., width : 2 * width])
    sig_b = jax.nn.sigmoid(proj[..., 3 * width : 4 * width])
    gate = jax.nn.sigmoid(proj[..., 4 * width :])
    a_low = (sig_a * proj[..., :width] * m3).astype(bf)
    b_low = (sig_b * proj[..., 2 * width : 3 * width] * m3).astype(bf)
    b_all = lax.all_gather(b_low, "row", axis=0, tiled=True)
    prod = jnp.einsum("ikc,jkc->ijc", a_low, b_all, preferred_element_type=fl)
    y_val, unit2, rstd2 = norm_fwd(prod, norms[2], norms[3])
    y_low = y_val.astype(bf)
    out1 = matmul(y_low, wl[5])
    z1 = start_pair + gate * out1
    h1, unit4, rstd4 = norm_fwd(z1, norms[4], norms[5])
    h1b = h1.astype(bf)
    qkvg = matmul(h1b, w_att)
    query = qkvg[..., :width].astype(bf).reshape(rows, cols, heads, size_head)
    keys = qkvg[..., width : 2 * width].astype(bf).reshape(rows, cols, heads, size_head)
    values = qkvg[..., 2 * width : 3 * width].astype(bf).reshape(rows, cols, heads, size_head)
    gate2 = jax.nn.sigmoid(qkvg[..., 3 * width :])
    tb_low = matmul(h1b, pl).astype(bf)
    tb_all = lax.all_gather(tb_low, "row", axis=0, tiled=True)
    tb_heads = jnp.transpose(tb_all, (2, 0, 1)).astype(fl)
    scores = (
        jnp.einsum("ijhd,ikhd->ihjk", query, keys, preferred_element_type=fl) * scale
        + tb_heads[None]
    )
    scores = jnp.where(col_ok[None, None, None, :], scores, -1000000000.0)
    probs = jax.nn.softmax(scores, axis=-1)
    p_low = probs.astype(bf)
    att = jnp.einsum("ihjk,ikhd->ijhd", p_low, values, preferred_element_type=fl).reshape(
        rows, cols, width
    )
    u_low = (gate2 * att).astype(bf)
    z2 = z1 + matmul(u_low, wl[10])
    h2, unit6, rstd6 = norm_fwd(z2, norms[6], norms[7])
    h2b = h2.astype(bf)
    logits = matmul(h2b, hl)
    lse = jax.nn.logsumexp(logits, axis=-1)
    onehot = (bins[0][..., None] == jnp.arange(logits.shape[-1])).astype(fl)
    pick = jnp.sum(logits * onehot, axis=-1)
    loss = jnp.sum(pmask * (lse - pick))
    count = jnp.sum(pmask)
    dlog = (m3 * (jnp.exp(logits - lse[..., None]) - onehot)).astype(bf)
    dhead = wgrad(h2b, dlog)
    dz2, dg6, ds6 = norm_back(matmul(dlog, hl.T), unit6, rstd6, norms[6])
    dout2 = dz2.astype(bf)
    dw10 = wgrad(u_low, dout2)
    du = matmul(dout2, wl[10].T)
    dgate2 = du * att
    datt = (du * gate2).astype(bf).reshape(rows, cols, heads, size_head)
    dprob = jnp.einsum("ijhd,ikhd->ihjk", datt, values, preferred_element_type=fl)
    dvals = jnp.einsum("ihjk,ijhd->ikhd", p_low, datt, preferred_element_type=fl)
    dscore = (probs * (dprob - jnp.sum(dprob * probs, axis=-1, keepdims=True))).astype(bf)
    dquery = jnp.einsum("ihjk,ikhd->ijhd", dscore, keys, preferred_element_type=fl) * scale
    dkeys = jnp.einsum("ihjk,ijhd->ikhd", dscore, query, preferred_element_type=fl) * scale
    dtb = jnp.sum(dscore.astype(fl), axis=0)
    dtb_own = lax.psum_scatter(dtb, "row", scatter_dimension=1, tiled=True)
    dtb_low = jnp.transpose(dtb_own, (1, 2, 0)).astype(bf)
    dpbias = wgrad(h1b, dtb_low)
    dqkvg = jnp.concatenate(
        [
            dquery.reshape(rows, cols, width),
            dkeys.reshape(rows, cols, width),
            dvals.reshape(rows, cols, width),
            dgate2 * gate2 * (1.0 - gate2),
        ],
        axis=-1,
    ).astype(bf)
    dw_att = wgrad(h1b, dqkvg)
    dh1 = matmul(dqkvg, w_att.T) + matmul(dtb_low, pl.T)
    dn4, dg4, ds4 = norm_back(dh1, unit4, rstd4, norms[4])
    dz1 = dz2 + dn4
    dout1 = (dz1 * gate).astype(bf)
    dw5 = wgrad(y_low, dout1)
    dgate = dz1 * out1
    dxn, dg2, ds2 = norm_back(matmul(dout1, wl[5].T), unit2, rstd2, norms[2])
    dx_low = dxn.astype(bf)
    dside_a = jnp.einsum("ijc,jkc->ikc", dx_low, b_all, preferred_element_type=fl)
    dside_b = lax.psum_scatter(
        jnp.einsum("ijc,ikc->jkc", dx_low, a_low, preferred_element_type=fl),
        "row",
        scatter_dimension=0,
        tiled=True,
    )
    da_r = dside_a.astype(bf).astype(fl)
    db_r = dside_b.astype(bf).astype(fl)
    dproj = jnp.concatenate(
        [
            da_r * sig_a * m3,
            da_r * proj[..., :width] * m3 * sig_a * (1.0 - sig_a),
            db_r * sig_b * m3,
            db_r * proj[..., 2 * width : 3 * width] * m3 * sig_b * (1.0 - sig_b),
            dgate * gate * (1.0 - gate),
        ],
        axis=-1,
    ).astype(bf)
    dw_tri = wgrad(h0b, dproj)
    dh0 = matmul(dproj, w_tri.T)
    unused, dg0, ds0 = norm_back(dh0, unit0, rstd0, norms[0])
    pieces = [dw_tri[:, idx * width : (idx + 1) * width] for idx in range(5)]
    pieces = (
        pieces + [dw5] + [dw_att[:, idx * width : (idx + 1) * width] for idx in range(4)] + [dw10]
    )
    dmats = jnp.stack(pieces)
    dnorms = jnp.stack([dg0, ds0, dg2, ds2, dg4, ds4, dg6, ds6])
    dmats, dpbias, dhead, dnorms, loss, count = lax.psum(
        (dmats, dpbias, dhead, dnorms, loss, count), ("crop", "row")
    )
    grad_norm = jnp.sqrt(
        jnp.sum(dmats * dmats)
        + jnp.sum(dpbias * dpbias)
        + jnp.sum(dhead * dhead)
        + jnp.sum(dnorms * dnorms)
    )
    factor = jnp.minimum(1.0, CLIP / grad_norm)
    new_mats = adam(mats, dmats * factor, mats_m, mats_v)
    new_pbias = adam(pbias, dpbias * factor, pbias_m, pbias_v)
    new_head = adam(head, dhead * factor, head_m, head_v)
    new_norms = adam(norms, dnorms * factor, norms_m, norms_v)
    return (
        grad_norm,
        loss,
        count,
        new_mats[0],
        new_mats[1],
        new_mats[2],
        new_mats[2].astype(bf),
        new_pbias[0],
        new_pbias[1],
        new_pbias[2],
        new_head[0],
        new_head[1],
        new_head[2],
        new_norms[0],
        new_norms[1],
        new_norms[2],
    )


BF = jnp.bfloat16
FL = jnp.float32
VMEM_LIMIT = 24 * 2**20


def dot(lhs, rhs, left=1, right=0):
    return lax.dot_general(
        lhs, rhs, (((left,), (right,)), ((), ())), preferred_element_type=FL
    )


def lane_sums(val):
    return jnp.sum(val.T, axis=0, keepdims=True)


def row_norm(val, gain, shift):
    mean = jnp.mean(val, axis=-1, keepdims=True)
    cent = val - mean
    rstd = lax.rsqrt(jnp.mean(cent * cent, axis=-1, keepdims=True) + EPS_NORM)
    unit = cent * rstd
    return (unit * gain + shift).astype(BF), unit, rstd


def row_norm_back(grad, unit, rstd, gain):
    dgain = jnp.sum(grad * unit, axis=0, keepdims=True)
    dshift = jnp.sum(grad, axis=0, keepdims=True)
    dunit = grad * gain
    dval = rstd * (
        dunit
        - jnp.mean(dunit, axis=-1, keepdims=True)
        - unit * jnp.mean(dunit * unit, axis=-1, keepdims=True)
    )
    return dval, dgain, dshift


def iota(shape, dim):
    return lax.broadcasted_iota(jnp.int32, shape, dim)


def fetch(pairs, sems):
    moves = [
        pltpu.make_async_copy(src, dst, sems.at[idx]) for idx, (src, dst) in enumerate(pairs)
    ]
    for move in moves:
        move.start()
    return moves


def start_kernel(
    copies, pair_hbm, norms_hbm, mats_hbm, out_ref, wl_ref, pair_ref, norms_ref, mats_ref, sems
):
    moves = fetch(
        [(pair_hbm, pair_ref), (norms_hbm, norms_ref), (mats_hbm, mats_ref)], sems
    )
    moves[0].wait()
    moves[1].wait()
    h0, _, _ = row_norm(pair_ref[...], norms_ref[0:1], norms_ref[1:2])
    for idx in range(copies):
        out_ref[idx] = h0
    moves[2].wait()
    wl_ref[...] = mats_ref[...].astype(BF)


def pair_mask(dims, limit):
    rows, cols, width, _, _ = dims
    spot = iota((rows * cols, width), 0)
    col_ok = spot % cols < limit
    row_in = spot // cols

    def mask_of(block_row):
        return jnp.where(jnp.logical_and(col_ok, row_in + block_row < limit), 1.0, 0.0).astype(FL)

    return mask_of


def own_sides(h0, wl_ref, mask):
    width = h0.shape[1]
    w_own = jnp.concatenate([wl_ref[0], wl_ref[1], wl_ref[4]], axis=1)
    proj = dot(h0, w_own)
    fac = jax.nn.sigmoid(proj[:, width : 2 * width]) * mask
    return fac * proj[:, :width], fac, jax.nn.sigmoid(proj[:, 2 * width :])


def own_kernel(dims, scal_ref, copies_ref, wl_ref, a_ref, gate_ref):
    mask = pair_mask(dims, scal_ref[0])(scal_ref[1])
    side, _, gate = own_sides(copies_ref[0], wl_ref, mask)
    a_ref[...] = side.astype(BF).astype(FL)
    gate_ref[...] = gate


def triangle_kernel(
    dims,
    scal_ref,
    own_ref,
    other_ref,
    a_ref,
    gate_ref,
    pair_hbm,
    norms_hbm,
    wl_ref,
    pbt_hbm,
    tb_ref,
    side_hbm,
    fac_hbm,
    x_ref,
    z1_ref,
    h1_ref,
    pair_ref,
    norms_ref,
    pbt_ref,
    b_ref,
    side_ref,
    fac_ref,
    part_ref,
    sems,
):
    rows, cols, width, heads, size = dims
    pairs = rows * cols
    limit, core = scal_ref[0], scal_ref[3]
    mask_of = pair_mask(dims, limit)

    w_b = jnp.concatenate([wl_ref[2], wl_ref[3]], axis=1)
    moves = []
    for idx in range(size // 2):
        for src, half in ((own_ref, core), (other_ref, 1 - core)):
            proj = dot(src[idx], w_b)
            block = 2 * idx + half
            fac = jax.nn.sigmoid(proj[:, width:]) * mask_of(block * rows)
            side = (fac * proj[:, :width]).astype(BF)
            base = pl.multiple_of(block * pairs, pairs)
            b_ref[pl.ds(base, pairs), :] = side.astype(FL)
            side_ref[pl.ds(base, pairs), :] = side
            fac_ref[pl.ds(base, pairs), :] = fac.astype(BF)
        if idx % 2 == 1:
            span = pl.ds((idx - 1) * 2 * pairs, 4 * pairs)
            moves += fetch(
                [(side_ref.at[span], side_hbm.at[span]), (fac_ref.at[span], fac_hbm.at[span])],
                sems.at[pl.ds(idx - 1, 2)],
            )
    last = 2 * (size // 4)
    early_moves = fetch(
        [(norms_hbm, norms_ref), (pair_hbm, pair_ref), (pbt_hbm, pbt_ref)],
        sems.at[pl.ds(last, 3)],
    )

    a_val, gate = a_ref[...], gate_ref[...]
    a_rows = [a_val[idx * cols : (idx + 1) * cols] for idx in range(rows)]

    def products(j, _):
        b_j = b_ref[pl.ds(pl.multiple_of(j * cols, cols), cols), :]
        for idx in range(rows):
            prod = a_rows[idx] * b_j
            fold = jnp.sum(prod.reshape(cols // 8, 8, width), axis=0)
            part_ref[pl.ds(pl.multiple_of((idx * cols + j) * 8, 8), 8), :] = fold
        return 0

    lax.fori_loop(0, cols, products, 0, unroll=2)
    x_val = part_ref[pl.ds(0, pairs, stride=8), :]
    for idx in range(1, 8):
        x_val = x_val + part_ref[pl.ds(idx, pairs, stride=8), :]

    x_ref[...] = x_val
    for move in early_moves:
        move.wait()
    y_low, _, _ = row_norm(x_val, norms_ref[2:3], norms_ref[3:4])
    z1 = pair_ref[...] + gate * dot(y_low, wl_ref[5])
    z1_ref[...] = z1
    h1, _, _ = row_norm(z1, norms_ref[4:5], norms_ref[5:6])
    h1_ref[...] = h1
    tbt = dot(pbt_ref[...].astype(BF), h1, 1, 1).astype(BF).astype(FL)
    half = pairs // 2
    block = jnp.concatenate([tbt[:, :half], tbt[:, half:]], axis=0)
    for idx in range(size):
        tb_ref[idx] = block
    for move in moves:
        move.wait()


def project_kernel(
    dims,
    scal_ref,
    h1_ref,
    own_ref,
    other_ref,
    wl_ref,
    norms_in,
    pbt_in,
    kcat_ref,
    vcat_ref,
    qblk_ref,
    gate2_ref,
    h0_ref,
    norms_ref,
    pbt_ref,
    own_t_hbm,
    other_t_hbm,
    own_t_ref,
    other_t_ref,
    sems,
):
    rows, cols, width, heads, size = dims
    extra = own_t_ref.shape[1] - width
    for src, dst in ((own_ref, own_t_ref), (other_ref, other_t_ref)):
        for idx in range(size // 2):
            dst[idx, :width, :] = src[idx].astype(FL).T.astype(BF)
            dst[idx, width:, :] = jnp.ones((extra, rows * cols), BF)
    moves = fetch([(own_t_ref, own_t_hbm), (other_t_ref, other_t_hbm)], sems)
    h0_ref[...] = own_ref[scal_ref[2]]
    norms_ref[...] = norms_in[...]
    pbt_ref[...] = pbt_in[...]
    w_att = jnp.concatenate([wl_ref[6], wl_ref[7], wl_ref[8], wl_ref[9]], axis=1)
    proj = dot(h1_ref[...], w_att)
    gate2_ref[...] = jax.nn.sigmoid(proj[:, 3 * width :])
    lane_head = iota((cols, width), 1) // (width // heads)
    zero = jnp.zeros((cols, width), BF)
    for idx in range(rows):
        at, side = idx // 2, idx % 2
        lanes = slice(side * width, (side + 1) * width)
        span = slice(idx * cols, (idx + 1) * cols)
        query = proj[span, :width].astype(BF)
        qblk_ref[at, side * cols : (side + 1) * cols, lanes] = query
        qblk_ref[at, (1 - side) * cols : (2 - side) * cols, lanes] = zero
        for head in range(heads):
            put = slice(head * cols, (head + 1) * cols)
            keep = lane_head == head
            kcat_ref[at, put, lanes] = jnp.where(keep, proj[span, width : 2 * width], 0.0).astype(BF)
            vcat_ref[at, put, lanes] = jnp.where(
                keep, proj[span, 2 * width : 3 * width], 0.0
            ).astype(BF)
    for move in moves:
        move.wait()


def diagonal_block(first, second):
    zero = jnp.zeros(first.shape, first.dtype)
    return jnp.concatenate(
        [
            jnp.concatenate([first, zero], axis=1),
            jnp.concatenate([zero, second], axis=1),
        ],
        axis=0,
    )


def pack_places(dims):
    rows, cols, width, heads, _ = dims
    pairs, lines = rows * cols, heads * cols
    at, places = 0, {}
    for name, tall in (
        ("prob", rows // 2 * lines),
        ("dscore", rows // 2 * lines),
        ("datt", pairs),
        ("u", pairs),
        ("dout2", pairs),
        ("dgate2", pairs),
        ("h2", pairs),
        ("dlog", 2 * cols),
    ):
        places[name] = at
        at += tall
    return places, at


def attention_kernel(
    dims,
    scal_ref,
    tb_ref,
    kcat_ref,
    vcat_ref,
    qblk_ref,
    gate2_ref,
    z1_ref,
    norms_ref,
    wl_ref,
    headt_hbm,
    bins_hbm,
    dtb_ref,
    pack_ref,
    dz2_ref,
    stat_ref,
    bias_ref,
    prob_ref,
    swap_ref,
    headt_ref,
    bins_ref,
    sems,
):
    rows, cols, width, heads, size = dims
    pairs, lines = rows * cols, heads * cols
    places, _ = pack_places(dims)
    scale = (width // heads) ** (-0.5)
    limit, first_row = scal_ref[0], scal_ref[1]

    def put(name, val):
        pack_ref[places[name] : places[name] + val.shape[0], :] = val

    moves = fetch([(headt_hbm, headt_ref), (bins_hbm, bins_ref)], sems)

    for half in range(2):
        for jl in range(2):
            lanes = slice(jl * cols, (jl + 1) * cols)
            got = [
                tb_ref[pl.ds(half * heads + head, size, stride=2 * heads), :][:, lanes]
                for head in range(heads)
            ]
            for duo in range(heads // 2):
                line = jnp.concatenate([got[2 * duo], got[2 * duo + 1]], axis=1)
                bias_ref[duo, pl.ds(2 * half + jl, size, stride=rows), :] = line
                bias_ref[duo, pl.ds(cols + 2 * half + jl, size, stride=rows), :] = line
    bias = jnp.concatenate([bias_ref[duo].T for duo in range(heads // 2)], axis=0)
    key_ok = iota((lines, 2 * cols), 0) % cols < limit
    att = []
    for at in range(rows // 2):
        score = dot(kcat_ref[at], qblk_ref[at], 1, 1) * scale + bias
        score = jnp.where(key_ok, score, -1000000000.0).reshape(heads, cols, 2 * cols)
        top = jnp.max(score, axis=1, keepdims=True)
        grown = jnp.exp(score - top)
        prob = (grown / jnp.sum(grown, axis=1, keepdims=True)).reshape(lines, 2 * cols)
        prob_ref[at] = prob
        low = prob.astype(BF)
        pack_ref[places["prob"] + at * lines : places["prob"] + (at + 1) * lines, :] = low
        both = dot(low, vcat_ref[at], 0, 0)
        att += [both[:cols, :width], both[cols:, width:]]
    att = jnp.concatenate(att, axis=0)
    gate2 = gate2_ref[...]
    u_low = (gate2 * att).astype(BF)
    put("u", u_low)
    z2 = z1_ref[...] + dot(u_low, wl_ref[10])
    h2, unit6, rstd6 = row_norm(z2, norms_ref[6:7], norms_ref[7:8])
    put("h2", h2)
    for move in moves:
        move.wait()
    headt = headt_ref[...].astype(BF)
    logits = dot(headt, h2, 1, 1)
    spot = iota((1, pairs), 1)
    ok = jnp.logical_and(spot % cols < limit, spot // cols + first_row < limit)
    mask = jnp.where(ok, 1.0, 0.0).astype(FL)
    bins = jnp.concatenate([bins_ref[idx : idx + 1, :] for idx in range(rows)], axis=1)
    onehot = jnp.where(iota(logits.shape, 0) == bins, 1.0, 0.0).astype(FL)
    top = jnp.max(logits, axis=0, keepdims=True)
    lse = top + jnp.log(jnp.sum(jnp.exp(logits - top), axis=0, keepdims=True))
    pick = jnp.sum(logits * onehot, axis=0, keepdims=True)
    loss = jnp.sum(mask * (lse - pick), axis=1, keepdims=True)
    count = jnp.sum(mask, axis=1, keepdims=True)
    dlog = (mask * (jnp.exp(logits - lse) - onehot)).astype(BF)
    put("dlog", jnp.concatenate([dlog[:, :width], dlog[:, width:]], axis=0))
    dz2, dg6, ds6 = row_norm_back(dot(dlog, headt, 0, 0), unit6, rstd6, norms_ref[6:7])
    dz2_ref[...] = dz2
    stat_ref[0:1, :] = dg6
    stat_ref[1:2, :] = ds6
    stat_ref[2:3, :] = jnp.broadcast_to(loss, (1, width))
    stat_ref[3:4, :] = jnp.broadcast_to(count, (1, width))
    stat_ref[4:8, :] = jnp.zeros((4, width), FL)
    dout2 = dz2.astype(BF)
    put("dout2", dout2)
    du = dot(dout2, wl_ref[10], 1, 1)
    put("dgate2", (du * att * gate2 * (1.0 - gate2)).astype(BF))
    datt = (du * gate2).astype(BF)
    put("datt", datt)
    total = None
    for at in range(rows // 2):
        first = datt[(2 * at) * cols : (2 * at + 1) * cols]
        second = datt[(2 * at + 1) * cols : (2 * at + 2) * cols]
        block = diagonal_block(first, second)
        dprob = dot(vcat_ref[at], block, 1, 1)
        prob = prob_ref[at]
        inner = jnp.sum((dprob * prob).reshape(heads, cols, 2 * cols), axis=1, keepdims=True)
        dscore = prob.reshape(heads, cols, 2 * cols) * (
            dprob.reshape(heads, cols, 2 * cols) - inner
        )
        low = dscore.reshape(lines, 2 * cols).astype(BF)
        pack_ref[places["dscore"] + at * lines : places["dscore"] + (at + 1) * lines, :] = low
        total = low.astype(FL) if total is None else total + low.astype(FL)
    for duo in range(heads // 2):
        turned = total[duo * 2 * cols : (duo + 1) * 2 * cols].T
        swap_ref[duo] = turned[:cols] + turned[cols:]
    for half in range(2):
        for head in range(heads):
            inside = slice((head % 2) * cols, (head % 2 + 1) * cols)
            line = jnp.concatenate(
                [
                    swap_ref[head // 2, pl.ds(2 * half + jl, size, stride=rows), :][:, inside]
                    for jl in range(2)
                ],
                axis=1,
            )
            dtb_ref[pl.ds(half * heads + head, size, stride=2 * heads), :] = line


def attention_grad_kernel(
    dims,
    scal_ref,
    kcat_ref,
    qblk_ref,
    pack_ref,
    h1_ref,
    h0_ref,
    x_ref,
    norms_ref,
    wl_ref,
    early_ref,
    loc_ref,
    dqkvg_ref,
):
    rows, cols, width, heads, size = dims
    pairs, lines = rows * cols, heads * cols
    places, _ = pack_places(dims)

    def take(name, tall, skip=0):
        return pack_ref[places[name] + skip : places[name] + skip + tall, :]

    mask = pair_mask(dims, scal_ref[0])(scal_ref[1])
    side, fac, gate = own_sides(h0_ref[...], wl_ref, mask)
    y_low, _, _ = row_norm(x_ref[...], norms_ref[2:3], norms_ref[3:4])
    loc_ref[0] = side.astype(BF).astype(FL)
    loc_ref[1] = fac
    loc_ref[2] = gate
    loc_ref[3] = dot(y_low, wl_ref[5])
    scale = (width // heads) ** (-0.5)
    lane_head = iota((cols, width), 1) // (width // heads)

    def diagonal(val):
        out = jnp.zeros((cols, width), FL)
        for head in range(heads):
            out = jnp.where(lane_head == head, val[head * cols : (head + 1) * cols], out)
        return out

    for at in range(rows // 2):
        dscore = take("dscore", lines, at * lines)
        block = diagonal_block(
            take("datt", cols, 2 * at * cols), take("datt", cols, (2 * at + 1) * cols)
        )
        dquery = dot(dscore, kcat_ref[at], 0, 0)
        dkeys = dot(dscore, qblk_ref[at])
        dvals = dot(take("prob", lines, at * lines), block)
        for side in range(2):
            idx = 2 * at + side
            lanes = slice(side * width, (side + 1) * width)
            span = slice(idx * cols, (idx + 1) * cols)
            dqkvg_ref[span, :width] = (
                dquery[side * cols : (side + 1) * cols, lanes] * scale
            ).astype(BF)
            dqkvg_ref[span, width : 2 * width] = (diagonal(dkeys[:, lanes]) * scale).astype(BF)
            dqkvg_ref[span, 2 * width : 3 * width] = diagonal(dvals[:, lanes]).astype(BF)
    dqkvg_ref[:, 3 * width :] = take("dgate2", pairs)
    dqkvg = dqkvg_ref[...]
    w_att = jnp.concatenate([wl_ref[6], wl_ref[7], wl_ref[8], wl_ref[9]], axis=1)
    loc_ref[4] = dot(dqkvg, w_att, 1, 1)
    dw_att = dot(h1_ref[...], dqkvg, 0, 0)
    for idx in range(4):
        early_ref[idx * width : (idx + 1) * width, :] = dw_att[:, idx * width : (idx + 1) * width]
    early_ref[4 * width : 5 * width, :] = dot(take("u", pairs), take("dout2", pairs), 0, 0)
    dlog = take("dlog", 2 * cols)
    dlog = jnp.concatenate([dlog[:cols], dlog[cols:]], axis=1)
    early_ref[5 * width :, :] = dot(dlog, take("h2", pairs))


def triangle_grad_kernel(
    dims,
    scal_ref,
    dtb_ref,
    early_ref,
    dz2_ref,
    stat_ref,
    h1_ref,
    x_ref,
    z1_ref,
    loc_ref,
    side_hbm,
    fac_hbm,
    own_t_hbm,
    other_t_hbm,
    norms_ref,
    wl_ref,
    pbt_ref,
    keep_ref,
    give_ref,
    flat_ref,
    dx_ref,
    side_ref,
    fac_ref,
    own_t_ref,
    other_t_ref,
    sems,
):
    rows, cols, width, heads, size = dims
    pairs = rows * cols
    chip, core = scal_ref[2], scal_ref[3]
    moves = fetch(
        [
            (side_hbm, side_ref),
            (own_t_hbm, own_t_ref),
            (other_t_hbm, other_t_ref),
            (fac_hbm, fac_ref),
        ],
        sems,
    )
    y_low, unit2, rstd2 = row_norm(x_ref[...], norms_ref[2:3], norms_ref[3:4])
    _, unit4, rstd4 = row_norm(z1_ref[...], norms_ref[4:5], norms_ref[5:6])
    got = dtb_ref[0]
    for idx in range(1, size):
        got = got + dtb_ref[idx]
    dtbt = jnp.concatenate([got[:heads], got[heads:]], axis=1).astype(BF)
    h1 = h1_ref[...]
    dpbt = dot(dtbt, h1)
    dh1 = loc_ref[4] + dot(dtbt, pbt_ref[...].astype(BF), 0, 0)
    dn4, dg4, ds4 = row_norm_back(dh1, unit4, rstd4, norms_ref[4:5])
    dz1 = dz2_ref[...] + dn4
    gate = loc_ref[2]
    dout1 = (dz1 * gate).astype(BF)
    dgate = dz1 * loc_ref[3] * gate * (1.0 - gate)
    dx, dg2, ds2 = row_norm_back(dot(dout1, wl_ref[5], 1, 1), unit2, rstd2, norms_ref[2:3])
    dx_ref[...] = dx.astype(BF).astype(FL)

    moves[0].wait()

    def da_step(j, acc):
        b_j = side_ref[pl.ds(pl.multiple_of(j * cols, cols), cols), :].astype(FL)
        return tuple(
            acc[idx] + dx_ref[pl.ds(idx * cols + j, 1), :] * b_j for idx in range(rows)
        )

    acc = lax.fori_loop(
        0, cols, da_step, tuple(jnp.zeros((cols, width), FL) for _ in range(rows)), unroll=2
    )
    da = jnp.concatenate(acc, axis=0).astype(BF).astype(FL)
    own = jnp.concatenate(
        [
            (da * loc_ref[1]).astype(BF),
            (da * loc_ref[0] * (1.0 - loc_ref[1])).astype(BF),
            dgate.astype(BF),
        ],
        axis=1,
    )
    for move in moves[1:]:
        move.wait()
    dw_own = dot(own_t_ref[chip], own)

    a_rows = [loc_ref[0, idx * cols : (idx + 1) * cols, :] for idx in range(rows)]

    def db_step(idx, acc):
        for src, half in ((own_t_ref, core), (other_t_ref, 1 - core)):
            block = 2 * idx + half
            pieces = []
            for row in range(rows):
                j = block * rows + row
                base = pl.multiple_of(j * cols, cols)
                db = dx_ref[pl.ds(j, 1), :] * a_rows[0]
                for own_row in range(1, rows):
                    db = db + dx_ref[pl.ds(own_row * cols + j, 1), :] * a_rows[own_row]
                fac = fac_ref[pl.ds(base, cols), :].astype(FL)
                rest = side_ref[pl.ds(base, cols), :].astype(FL) * (1.0 - fac)
                pieces.append(
                    jnp.concatenate([(db * fac).astype(BF), (db * rest).astype(BF)], axis=1)
                )
            acc = acc + dot(src[idx], jnp.concatenate(pieces, axis=0))
        return acc

    tall = own_t_ref.shape[1]
    dw_b = jnp.zeros((tall, 2 * width), FL)
    for idx in range(size // 2):
        dw_b = db_step(idx, dw_b)

    parts = [
        dw_own[:, :width],
        dw_own[:, width : 2 * width],
        dw_b[:, :width],
        dw_b[:, width:],
        dw_own[:, 2 * width :],
    ]
    mixed = jnp.zeros((width, width), FL)
    summed = jnp.zeros((width, width), FL)
    for idx, part in enumerate(parts):
        weight = wl_ref[idx].astype(FL)
        flat_ref[idx * width : (idx + 1) * width, :] = part[:width]
        mixed = mixed + weight * part[:width]
        summed = summed + weight * part[width : width + 1]
    ds0 = lane_sums(summed)
    dg0 = (lane_sums(mixed) - norms_ref[1:2] * ds0) / norms_ref[0:1]
    flat_ref[5 * width : 6 * width, :] = dot(y_low, dout1, 0, 0)
    mats = 11 * width
    flat_ref[6 * width : mats, :] = early_ref[: 5 * width, :]
    bins_n = early_ref.shape[0] - 5 * width
    flat_ref[mats : mats + bins_n, :] = early_ref[5 * width :, :]
    base = mats + bins_n
    flat_ref[base : base + heads, :] = dpbt
    flat_ref[base + heads : base + 8, :] = jnp.zeros((8 - heads, width), FL)
    base += 8
    for idx, line in enumerate((dg0, ds0, dg2, ds2, dg4, ds4)):
        flat_ref[base + idx : base + idx + 1, :] = line
    flat_ref[base + 6 : base + 10, :] = stat_ref[0:4, :]
    total = flat_ref.shape[0]
    flat_ref[base + 10 :, :] = jnp.zeros((total - base - 10, width), FL)
    half = total // 2
    keep_ref[...] = flat_ref[pl.ds(pl.multiple_of(core * half, half), half), :]
    give_ref[...] = flat_ref[pl.ds(pl.multiple_of((1 - core) * half, half), half), :]


def update_kernel(
    dims,
    scal_ref,
    mine_ref,
    other_ref,
    mats_ref,
    mats_m_ref,
    mats_v_ref,
    pb_ref,
    pb_m_ref,
    pb_v_ref,
    head_ref,
    head_m_ref,
    head_v_ref,
    norms_ref,
    norms_m_ref,
    norms_v_ref,
    norm_out,
    loss_out,
    count_out,
    mats_m_out,
    mats_v_out,
    mats_out,
    mats_low_out,
    pb_m_out,
    pb_v_out,
    pb_out,
    head_m_out,
    head_v_out,
    head_out,
    norms_m_out,
    norms_v_out,
    norms_out,
    flat_ref,
    m_buf,
    v_buf,
    w_buf,
    low_buf,
    sems,
):
    rows, cols, width, heads, size = dims
    core = scal_ref[3]
    half = mine_ref.shape[0]
    flat_ref[pl.ds(pl.multiple_of(core * half, half), half), :] = mine_ref[...]
    flat_ref[pl.ds(pl.multiple_of((1 - core) * half, half), half), :] = other_ref[...]
    count = mats_ref.shape[0]
    mats = count * width
    bins_n = head_ref.shape[0]
    base = mats + bins_n
    grads = flat_ref[: base + 16, :]
    square = jnp.sum(grads * grads, axis=0, keepdims=True)
    norm = jnp.sqrt(jnp.sum(square, axis=1, keepdims=True))
    factor = jnp.minimum(1.0, CLIP / norm)
    norm_out[...] = norm
    loss_out[...] = flat_ref[base + 16 : base + 17, 0:1]
    count_out[...] = flat_ref[base + 17 : base + 18, 0:1]

    moves = []

    def send(at, idx, buf, out):
        move = pltpu.make_async_copy(buf.at[idx], out.at[idx], sems.at[at, idx])
        move.start()
        moves.append(move)

    def step(weight, grad, first, second):
        return adam(weight, grad * factor, first, second)

    for idx in range(count):
        m_buf[idx], v_buf[idx], weight = step(
            mats_ref[idx],
            flat_ref[idx * width : (idx + 1) * width, :],
            mats_m_ref[idx],
            mats_v_ref[idx],
        )
        w_buf[idx] = weight
        low_buf[idx] = weight.astype(BF)
        send(0, idx, m_buf, mats_m_out)
        send(1, idx, v_buf, mats_v_out)
        send(2, idx, w_buf, mats_out)
        send(3, idx, low_buf, mats_low_out)
    small = (
        (mats, bins_n, head_ref, head_m_ref, head_v_ref, head_m_out, head_v_out, head_out),
        (base, heads, pb_ref, pb_m_ref, pb_v_ref, pb_m_out, pb_v_out, pb_out),
        (base + 8, 8, norms_ref, norms_m_ref, norms_v_ref, norms_m_out, norms_v_out, norms_out),
    )
    for at, tall, w_in, m_in, v_in, m_out, v_out, w_out in small:
        m_out[...], v_out[...], w_out[...] = step(
            w_in[...], flat_ref[at : at + tall, :], m_in[...], v_in[...]
        )
    for move in moves:
        move.wait()


def call(kernel, args, outs, scratch=(), limit=VMEM_LIMIT, flops=10**7):
    spots = {"s": pltpu.SMEM, "v": pltpu.VMEM, "h": pltpu.HBM}
    return pl.pallas_call(
        kernel,
        out_shape=[
            pltpu.HBM(shape, kind) if spot == "h" else jax.ShapeDtypeStruct(shape, kind)
            for shape, kind, spot in outs
        ],
        in_specs=[pl.BlockSpec(memory_space=spots[spot]) for _, spot in args],
        out_specs=[pl.BlockSpec(memory_space=spots[spot]) for _, _, spot in outs],
        scratch_shapes=list(scratch),
        compiler_params=pltpu.CompilerParams(vmem_limit_bytes=limit),
        cost_estimate=pl.CostEstimate(flops=flops, bytes_accessed=10**6, transcendentals=0),
    )(
        *(
            pltpu.with_memory_space_constraint(value, pltpu.HBM) if spot == "h" else value
            for value, spot in args
        )
    )


def same_core_groups(crops, size):
    return [
        [crop * size + idx for crop in range(crops) for idx in range(core, size, 2)]
        for core in range(2)
    ]


def core_swap(value, size):
    return lax.ppermute(value, "row", [(idx, idx ^ 1) for idx in range(size)])


def fast_step(
    crops,
    size,
    pair,
    bins,
    lengths,
    mats,
    mats_m,
    mats_v,
    pbias,
    pbias_m,
    pbias_v,
    head,
    head_m,
    head_v,
    norms,
    norms_m,
    norms_v,
):
    rows, cols, width = pair.shape[1:]
    heads, bins_n = pbias.shape[1], head.shape[1]
    pairs, lines = rows * cols, heads * cols
    dims = (rows, cols, width, heads, size)
    chips = size // 2
    place = lax.axis_index("row")
    scal = jnp.stack([lengths[0], place * rows, place // 2, place % 2]).astype(jnp.int32)
    start = pair.reshape(pairs, width)
    pbt, headt = pbias.T, head.T

    copies, wl = call(
        functools.partial(start_kernel, chips),
        [(start, "h"), (norms, "h"), (mats, "h")],
        [((chips, pairs, width), BF, "v"), (mats.shape, BF, "v")],
        [
            pltpu.VMEM((pairs, width), FL),
            pltpu.VMEM(norms.shape, FL),
            pltpu.VMEM(mats.shape, FL),
            pltpu.SemaphoreType.DMA((3,)),
        ],
    )
    a_val, gate = call(
        functools.partial(own_kernel, dims),
        [(scal, "s"), (copies, "v"), (wl, "v")],
        [((pairs, width), FL, "v"), ((pairs, width), FL, "v")],
    )
    near = [list(range(core, size, 2)) for core in range(2)]
    own = lax.all_to_all(copies, "row", 0, 0, axis_index_groups=near, tiled=True)
    other = core_swap(own, size)

    full = (size * pairs, width)
    tb, side_b, fac_b, x_val, z1, h1 = call(
        functools.partial(triangle_kernel, dims),
        [
            (scal, "s"),
            (own, "v"),
            (other, "v"),
            (a_val, "v"),
            (gate, "v"),
            (start, "h"),
            (norms, "h"),
            (wl, "v"),
            (pbt, "h"),
        ],
        [
            ((size, 2 * heads, 2 * cols), FL, "v"),
            (full, BF, "h"),
            (full, BF, "h"),
            ((pairs, width), FL, "v"),
            ((pairs, width), FL, "v"),
            ((pairs, width), BF, "v"),
        ],
        [
            pltpu.VMEM((pairs, width), FL),
            pltpu.VMEM(norms.shape, FL),
            pltpu.VMEM(pbt.shape, FL),
            pltpu.VMEM(full, FL),
            pltpu.VMEM(full, BF),
            pltpu.VMEM(full, BF),
            pltpu.VMEM((pairs * 8, width), FL),
            pltpu.SemaphoreType.DMA((2 * (size // 4) + 3,)),
        ],
    )

    tb_all = lax.all_to_all(tb, "row", 0, 0, tiled=True)
    turned = (chips, width + 16, pairs)
    kcat, vcat, qblk, gate2, h0, norms_here, pbt_here, own_t, other_t = call(
        functools.partial(project_kernel, dims),
        [(scal, "s")] + [(value, "v") for value in (h1, own, other, wl, norms, pbt)],
        [
            ((rows // 2, lines, 2 * width), BF, "v"),
            ((rows // 2, lines, 2 * width), BF, "v"),
            ((rows // 2, 2 * cols, 2 * width), BF, "v"),
            ((pairs, width), FL, "v"),
            ((pairs, width), BF, "v"),
            (norms.shape, FL, "v"),
            (pbt.shape, FL, "v"),
            (turned, BF, "h"),
            (turned, BF, "h"),
        ],
        [pltpu.VMEM(turned, BF), pltpu.VMEM(turned, BF), pltpu.SemaphoreType.DMA((2,))],
    )
    bias_shape = (size * 2 * heads, 2 * cols)
    dtb, pack, dz2, stat = call(
        functools.partial(attention_kernel, dims),
        [
            (scal, "s"),
            (tb_all.reshape(bias_shape), "v"),
            (kcat, "v"),
            (vcat, "v"),
            (qblk, "v"),
            (gate2, "v"),
            (z1, "v"),
            (norms_here, "v"),
            (wl, "v"),
            (headt, "h"),
            (bins[0], "h"),
        ],
        [
            (bias_shape, FL, "v"),
            ((pack_places(dims)[1], width), BF, "v"),
            ((pairs, width), FL, "v"),
            ((8, width), FL, "v"),
        ],
        [
            pltpu.VMEM((heads // 2, 2 * cols, 2 * cols), FL),
            pltpu.VMEM((rows // 2, lines, 2 * cols), FL),
            pltpu.VMEM((heads // 2, cols, 2 * cols), FL),
            pltpu.VMEM((bins_n, width), FL),
            pltpu.VMEM((rows, cols), jnp.int32),
            pltpu.SemaphoreType.DMA((2,)),
        ],
    )

    dtb_all = lax.all_to_all(dtb.reshape(size, 2 * heads, 2 * cols), "row", 0, 0, tiled=True)
    early, loc = call(
        functools.partial(attention_grad_kernel, dims),
        [(scal, "s")]
        + [
            (value, "v")
            for value in (
                kcat,
                qblk,
                pack,
                h1,
                h0,
                x_val,
                norms_here,
                wl,
            )
        ],
        [((5 * width + bins_n, width), FL, "v"), ((5, pairs, width), FL, "v")],
        [pltpu.VMEM((pairs, 4 * width), BF)],
    )
    used = mats.shape[0] * width + bins_n + 18
    unit = 8 * crops * size
    total = -(-used // unit) * unit
    keep, give = call(
        functools.partial(triangle_grad_kernel, dims),
        [(scal, "s")]
        + [(value, "v") for value in (dtb_all, early, dz2, stat, h1, x_val, z1, loc)]
        + [(value, "h") for value in (side_b, fac_b, own_t, other_t)]
        + [(value, "v") for value in (norms_here, wl, pbt_here)],
        [((total // 2, width), FL, "v"), ((total // 2, width), FL, "v")],
        [
            pltpu.VMEM((total, width), FL),
            pltpu.VMEM((pairs, width), FL),
            pltpu.VMEM(full, BF),
            pltpu.VMEM(full, BF),
            pltpu.VMEM(turned, BF),
            pltpu.VMEM(turned, BF),
            pltpu.SemaphoreType.DMA((4,)),
        ],
    )

    half = keep + core_swap(give, size)
    count = crops * chips
    groups = same_core_groups(crops, size)
    axes = ("crop", "row")
    parts = lax.all_to_all(
        half.reshape(count, -1, width), axes, 0, 0, axis_index_groups=groups, tiled=True
    )
    share = jnp.sum(parts, axis=0)
    spread = jnp.broadcast_to(share[None], (count,) + share.shape)
    mine = lax.all_to_all(spread, axes, 0, 0, axis_index_groups=groups, tiled=True)
    mine = mine.reshape(total // 2, width)
    other_half = core_swap(mine, size)

    number = mats.shape[0]
    big, low = ((number, width, width), FL, "h"), ((number, width, width), BF, "h")
    pb_out, head_out = ((heads, width), FL, "v"), ((bins_n, width), FL, "v")
    norm_out = ((norms.shape[0], width), FL, "v")
    res = call(
        functools.partial(update_kernel, dims),
        [(scal, "s"), (mine, "v"), (other_half, "v"), (mats, "v")]
        + [
            (value, "v")
            for value in (
                mats_m,
                mats_v,
                pbt,
                pbias_m.T,
                pbias_v.T,
                headt,
                head_m.T,
                head_v.T,
                norms,
                norms_m,
                norms_v,
            )
        ],
        [((1, 1), FL, "v")] * 3
        + [big, big, big, low]
        + [pb_out] * 3
        + [head_out] * 3
        + [norm_out] * 3,
        [pltpu.VMEM((total, width), FL)]
        + [pltpu.VMEM((number, width, width), FL)] * 3
        + [
            pltpu.VMEM((number, width, width), BF),
            pltpu.SemaphoreType.DMA((4, number)),
        ],
    )
    return (
        *(value.reshape(()) for value in res[:3]),
        *res[3:7],
        *(value.T for value in res[7:13]),
        *res[13:16],
    )


def small_enough(pair, heads, size):
    _, rows, cols, width = pair.shape
    held = 4 * size * rows * cols * width * 4 + 4 * rows * heads * cols * cols * 4
    return (
        held <= 2**24
        and width == 2 * cols
        and rows == 4
        and heads == 4
        and size % 2 == 0
        and rows * size == cols
    )


def solution(mesh):
    crops, size = mesh.shape["crop"], mesh.shape["row"]

    def on_device(*args):
        if small_enough(args[0], args[6].shape[1], size):
            return fast_step(crops, size, *args)
        return general_step(*args)

    in_specs = (
        P("crop", "row", None, None),
        P("crop", "row", None),
        P("crop"),
        P(),
        P(),
        P(),
        P(),
        P(),
        P(),
        P(),
        P(),
        P(),
        P(),
        P(),
        P(),
    )
    out_specs = (P(), P(), P(), P(), P(), P(), P(), P(), P(), P(), P(), P(), P(), P(), P(), P())
    return jax.shard_map(
        on_device, mesh=mesh, in_specs=in_specs, out_specs=out_specs, check_vma=False
    )
```

```python
import functools

import jax
import jax.numpy as jnp
from jax import lax
from jax.experimental import pallas as pl
from jax.experimental.pallas import tpu as pltpu
from jax.sharding import PartitionSpec as P

STEP = 5


EPS_NORM = 1e-05
CLIP = 1.0
RATE = 0.05
BETA1 = 0.9
BETA2 = 0.95
ADAM_EPS = 1e-08
WDECAY = 0.01


def norm_fwd(v, gain, shift):
    mean = jnp.mean(v, axis=-1, keepdims=True)
    cent = v - mean
    rstd = lax.rsqrt(jnp.mean(cent * cent, axis=-1, keepdims=True) + EPS_NORM)
    unit = cent * rstd
    return (unit * gain + shift, unit, rstd)


def norm_back(grad, unit, rstd, gain):
    dgain = jnp.sum(grad * unit, axis=(0, 1))
    dshift = jnp.sum(grad, axis=(0, 1))
    dunit = grad * gain
    dval = rstd * (
        dunit
        - jnp.mean(dunit, axis=-1, keepdims=True)
        - unit * jnp.mean(dunit * unit, axis=-1, keepdims=True)
    )
    return (dval, dgain, dshift)


def matmul(value, weight):
    flat = value.reshape(-1, value.shape[-1])
    out = jnp.dot(flat, weight, preferred_element_type=jnp.float32)
    return out.reshape(value.shape[:-1] + (weight.shape[1],))


def wgrad(value, grad):
    return jnp.einsum("ijc,ijd->cd", value, grad, preferred_element_type=jnp.float32)


def adam(weight, grad, first, second):
    first_new = BETA1 * first + (1.0 - BETA1) * grad
    second_new = BETA2 * second + (1.0 - BETA2) * grad * grad
    m_hat = first_new / (1.0 - BETA1**STEP)
    v_hat = second_new / (1.0 - BETA2**STEP)
    weight_new = weight - RATE * (m_hat / (jnp.sqrt(v_hat) + ADAM_EPS) + WDECAY * weight)
    return (first_new, second_new, weight_new)


def general_step(
    pair,
    bins,
    lengths,
    mats,
    mats_m,
    mats_v,
    pbias,
    pbias_m,
    pbias_v,
    head,
    head_m,
    head_v,
    norms,
    norms_m,
    norms_v,
):
    bf = jnp.bfloat16
    fl = jnp.float32
    width = mats.shape[1]
    rows = pair.shape[1]
    cols = pair.shape[2]
    heads = pbias.shape[1]
    size_head = width // heads
    scale = size_head ** (-0.5)
    start_pair = pair[0]
    first_row = lax.axis_index("row") * rows
    limit = lengths[0]
    row_ok = first_row + jnp.arange(rows) < limit
    col_ok = jnp.arange(cols) < limit
    pmask = (row_ok[:, None] & col_ok[None, :]).astype(fl)
    m3 = pmask[..., None]
    wl = mats.astype(bf)
    pl = pbias.astype(bf)
    hl = head.astype(bf)
    w_tri = jnp.concatenate([wl[0], wl[1], wl[2], wl[3], wl[4]], axis=1)
    w_att = jnp.concatenate([wl[6], wl[7], wl[8], wl[9]], axis=1)
    h0, unit0, rstd0 = norm_fwd(start_pair, norms[0], norms[1])
    h0b = h0.astype(bf)
    proj = matmul(h0b, w_tri)
    sig_a = jax.nn.sigmoid(proj[..., width : 2 * width])
    sig_b = jax.nn.sigmoid(proj[..., 3 * width : 4 * width])
    gate = jax.nn.sigmoid(proj[..., 4 * width :])
    a_low = (sig_a * proj[..., :width] * m3).astype(bf)
    b_low = (sig_b * proj[..., 2 * width : 3 * width] * m3).astype(bf)
    b_all = lax.all_gather(b_low, "row", axis=0, tiled=True)
    prod = jnp.einsum("ikc,jkc->ijc", a_low, b_all, preferred_element_type=fl)
    y_val, unit2, rstd2 = norm_fwd(prod, norms[2], norms[3])
    y_low = y_val.astype(bf)
    out1 = matmul(y_low, wl[5])
    z1 = start_pair + gate * out1
    h1, unit4, rstd4 = norm_fwd(z1, norms[4], norms[5])
    h1b = h1.astype(bf)
    qkvg = matmul(h1b, w_att)
    query = qkvg[..., :width].astype(bf).reshape(rows, cols, heads, size_head)
    keys = qkvg[..., width : 2 * width].astype(bf).reshape(rows, cols, heads, size_head)
    values = qkvg[..., 2 * width : 3 * width].astype(bf).reshape(rows, cols, heads, size_head)
    gate2 = jax.nn.sigmoid(qkvg[..., 3 * width :])
    tb_low = matmul(h1b, pl).astype(bf)
    tb_all = lax.all_gather(tb_low, "row", axis=0, tiled=True)
    tb_heads = jnp.transpose(tb_all, (2, 0, 1)).astype(fl)
    scores = (
        jnp.einsum("ijhd,ikhd->ihjk", query, keys, preferred_element_type=fl) * scale
        + tb_heads[None]
    )
    scores = jnp.where(col_ok[None, None, None, :], scores, -1000000000.0)
    probs = jax.nn.softmax(scores, axis=-1)
    p_low = probs.astype(bf)
    att = jnp.einsum("ihjk,ikhd->ijhd", p_low, values, preferred_element_type=fl).reshape(
        rows, cols, width
    )
    u_low = (gate2 * att).astype(bf)
    z2 = z1 + matmul(u_low, wl[10])
    h2, unit6, rstd6 = norm_fwd(z2, norms[6], norms[7])
    h2b = h2.astype(bf)
    logits = matmul(h2b, hl)
    lse = jax.nn.logsumexp(logits, axis=-1)
    onehot = (bins[0][..., None] == jnp.arange(logits.shape[-1])).astype(fl)
    pick = jnp.sum(logits * onehot, axis=-1)
    loss = jnp.sum(pmask * (lse - pick))
    count = jnp.sum(pmask)
    dlog = (m3 * (jnp.exp(logits - lse[..., None]) - onehot)).astype(bf)
    dhead = wgrad(h2b, dlog)
    dz2, dg6, ds6 = norm_back(matmul(dlog, hl.T), unit6, rstd6, norms[6])
    dout2 = dz2.astype(bf)
    dw10 = wgrad(u_low, dout2)
    du = matmul(dout2, wl[10].T)
    dgate2 = du * att
    datt = (du * gate2).astype(bf).reshape(rows, cols, heads, size_head)
    dprob = jnp.einsum("ijhd,ikhd->ihjk", datt, values, preferred_element_type=fl)
    dvals = jnp.einsum("ihjk,ijhd->ikhd", p_low, datt, preferred_element_type=fl)
    dscore = (probs * (dprob - jnp.sum(dprob * probs, axis=-1, keepdims=True))).astype(bf)
    dquery = jnp.einsum("ihjk,ikhd->ijhd", dscore, keys, preferred_element_type=fl) * scale
    dkeys = jnp.einsum("ihjk,ijhd->ikhd", dscore, query, preferred_element_type=fl) * scale
    dtb = jnp.sum(dscore.astype(fl), axis=0)
    dtb_own = lax.psum_scatter(dtb, "row", scatter_dimension=1, tiled=True)
    dtb_low = jnp.transpose(dtb_own, (1, 2, 0)).astype(bf)
    dpbias = wgrad(h1b, dtb_low)
    dqkvg = jnp.concatenate(
        [
            dquery.reshape(rows, cols, width),
            dkeys.reshape(rows, cols, width),
            dvals.reshape(rows, cols, width),
            dgate2 * gate2 * (1.0 - gate2),
        ],
        axis=-1,
    ).astype(bf)
    dw_att = wgrad(h1b, dqkvg)
    dh1 = matmul(dqkvg, w_att.T) + matmul(dtb_low, pl.T)
    dn4, dg4, ds4 = norm_back(dh1, unit4, rstd4, norms[4])
    dz1 = dz2 + dn4
    dout1 = (dz1 * gate).astype(bf)
    dw5 = wgrad(y_low, dout1)
    dgate = dz1 * out1
    dxn, dg2, ds2 = norm_back(matmul(dout1, wl[5].T), unit2, rstd2, norms[2])
    dx_low = dxn.astype(bf)
    dside_a = jnp.einsum("ijc,jkc->ikc", dx_low, b_all, preferred_element_type=fl)
    dside_b = lax.psum_scatter(
        jnp.einsum("ijc,ikc->jkc", dx_low, a_low, preferred_element_type=fl),
        "row",
        scatter_dimension=0,
        tiled=True,
    )
    da_r = dside_a.astype(bf).astype(fl)
    db_r = dside_b.astype(bf).astype(fl)
    dproj = jnp.concatenate(
        [
            da_r * sig_a * m3,
            da_r * proj[..., :width] * m3 * sig_a * (1.0 - sig_a),
            db_r * sig_b * m3,
            db_r * proj[..., 2 * width : 3 * width] * m3 * sig_b * (1.0 - sig_b),
            dgate * gate * (1.0 - gate),
        ],
        axis=-1,
    ).astype(bf)
    dw_tri = wgrad(h0b, dproj)
    dh0 = matmul(dproj, w_tri.T)
    unused, dg0, ds0 = norm_back(dh0, unit0, rstd0, norms[0])
    pieces = [dw_tri[:, idx * width : (idx + 1) * width] for idx in range(5)]
    pieces = (
        pieces + [dw5] + [dw_att[:, idx * width : (idx + 1) * width] for idx in range(4)] + [dw10]
    )
    dmats = jnp.stack(pieces)
    dnorms = jnp.stack([dg0, ds0, dg2, ds2, dg4, ds4, dg6, ds6])
    dmats, dpbias, dhead, dnorms, loss, count = lax.psum(
        (dmats, dpbias, dhead, dnorms, loss, count), ("crop", "row")
    )
    grad_norm = jnp.sqrt(
        jnp.sum(dmats * dmats)
        + jnp.sum(dpbias * dpbias)
        + jnp.sum(dhead * dhead)
        + jnp.sum(dnorms * dnorms)
    )
    factor = jnp.minimum(1.0, CLIP / grad_norm)
    new_mats = adam(mats, dmats * factor, mats_m, mats_v)
    new_pbias = adam(pbias, dpbias * factor, pbias_m, pbias_v)
    new_head = adam(head, dhead * factor, head_m, head_v)
    new_norms = adam(norms, dnorms * factor, norms_m, norms_v)
    return (
        grad_norm,
        loss,
        count,
        new_mats[0],
        new_mats[1],
        new_mats[2],
        new_mats[2].astype(bf),
        new_pbias[0],
        new_pbias[1],
        new_pbias[2],
        new_head[0],
        new_head[1],
        new_head[2],
        new_norms[0],
        new_norms[1],
        new_norms[2],
    )


BF = jnp.bfloat16
FL = jnp.float32
VMEM_LIMIT = 24 * 2**20


def dot(lhs, rhs, left=1, right=0):
    return lax.dot_general(
        lhs, rhs, (((left,), (right,)), ((), ())), preferred_element_type=FL
    )


def lane_sums(val):
    return jnp.sum(val.T, axis=0, keepdims=True)


def row_norm(val, gain, shift):
    mean = jnp.mean(val, axis=-1, keepdims=True)
    cent = val - mean
    rstd = lax.rsqrt(jnp.mean(cent * cent, axis=-1, keepdims=True) + EPS_NORM)
    unit = cent * rstd
    return (unit * gain + shift).astype(BF), unit, rstd


def row_norm_back(grad, unit, rstd, gain):
    dgain = jnp.sum(grad * unit, axis=0, keepdims=True)
    dshift = jnp.sum(grad, axis=0, keepdims=True)
    dunit = grad * gain
    dval = rstd * (
        dunit
        - jnp.mean(dunit, axis=-1, keepdims=True)
        - unit * jnp.mean(dunit * unit, axis=-1, keepdims=True)
    )
    return dval, dgain, dshift


def iota(shape, dim):
    return lax.broadcasted_iota(jnp.int32, shape, dim)


def fetch(pairs, sems):
    moves = [
        pltpu.make_async_copy(src, dst, sems.at[idx]) for idx, (src, dst) in enumerate(pairs)
    ]
    for move in moves:
        move.start()
    return moves


def start_kernel(
    copies, pair_hbm, norms_hbm, mats_hbm, out_ref, wl_ref, pair_ref, norms_ref, mats_ref, sems
):
    moves = fetch(
        [(pair_hbm, pair_ref), (norms_hbm, norms_ref), (mats_hbm, mats_ref)], sems
    )
    moves[0].wait()
    moves[1].wait()
    h0, _, _ = row_norm(pair_ref[...], norms_ref[0:1], norms_ref[1:2])
    for idx in range(copies):
        out_ref[idx] = h0
    moves[2].wait()
    wl_ref[...] = mats_ref[...].astype(BF)


def pair_mask(dims, limit):
    rows, cols, width, _, _ = dims
    spot = iota((rows * cols, width), 0)
    col_ok = spot % cols < limit
    row_in = spot // cols

    def mask_of(block_row):
        return jnp.where(jnp.logical_and(col_ok, row_in + block_row < limit), 1.0, 0.0).astype(FL)

    return mask_of


def own_sides(h0, wl_ref, mask):
    width = h0.shape[1]
    w_own = jnp.concatenate([wl_ref[0], wl_ref[1], wl_ref[4]], axis=1)
    proj = dot(h0, w_own)
    fac = jax.nn.sigmoid(proj[:, width : 2 * width]) * mask
    return fac * proj[:, :width], fac, jax.nn.sigmoid(proj[:, 2 * width :])


def b_block(dims, h0, w_b, col_mask, start, limit):
    rows, cols, width, _, _ = dims
    proj = dot(h0, w_b)
    sig = jax.nn.sigmoid(proj[:, width:])
    lines = []
    for row in range(rows):
        row_ok = jnp.where(start + row < limit, 1.0, 0.0).astype(FL)
        lines.append(sig[row * cols : (row + 1) * cols] * (col_mask * row_ok))
    fac = jnp.concatenate(lines, axis=0)
    return (fac * proj[:, :width]).astype(BF), fac.astype(BF)


def col_mask_of(dims, limit):
    _, cols, width, _, _ = dims
    return jnp.where(iota((cols, width), 0) < limit, 1.0, 0.0).astype(FL)


def own_kernel(
    dims, scal_ref, copies_ref, own_ref, wl_ref, a_ref, gate_ref, h0_ref, side_ref, fac_ref
):
    rows, cols, width, heads, size = dims
    limit, core = scal_ref[0], scal_ref[3]
    mask = pair_mask(dims, limit)(scal_ref[1])
    h0 = copies_ref[0]
    h0_ref[...] = h0
    side, _, gate = own_sides(h0, wl_ref, mask)
    a_ref[...] = side.astype(BF).astype(FL)
    gate_ref[...] = gate
    col_mask = col_mask_of(dims, limit)
    w_b = jnp.concatenate([wl_ref[2], wl_ref[3]], axis=1)
    for idx in range(size // 2):
        side_ref[idx], fac_ref[idx] = b_block(
            dims, own_ref[idx], w_b, col_mask, (2 * idx + core) * rows, limit
        )


def triangle_kernel(
    dims,
    scal_ref,
    own_ref,
    other_ref,
    a_ref,
    gate_ref,
    own_side_ref,
    own_fac_ref,
    pair_hbm,
    norms_hbm,
    wl_ref,
    pbt_hbm,
    tb_ref,
    own_side_hbm,
    own_fac_hbm,
    other_side_hbm,
    other_fac_hbm,
    own_hbm,
    other_hbm,
    x_ref,
    z1_ref,
    h1_ref,
    pair_ref,
    norms_ref,
    pbt_ref,
    other_side_ref,
    other_fac_ref,
    part_ref,
    sems,
):
    rows, cols, width, heads, size = dims
    pairs, chips = rows * cols, size // 2
    limit, core = scal_ref[0], scal_ref[3]
    moves = fetch(
        [
            (norms_hbm, norms_ref),
            (pair_hbm, pair_ref),
            (pbt_hbm, pbt_ref),
            (own_side_ref, own_side_hbm),
            (own_fac_ref, own_fac_hbm),
            (own_ref, own_hbm),
            (other_ref, other_hbm),
        ],
        sems.at[pl.ds(0, 7)],
    )
    early_moves, moves = moves[:3], moves[3:]
    col_mask = col_mask_of(dims, limit)
    w_b = jnp.concatenate([wl_ref[2], wl_ref[3]], axis=1)
    a_rows = [a_ref[idx * cols : (idx + 1) * cols, :] for idx in range(rows)]

    def products(block, side):
        for row in range(rows):
            b_j = side[row * cols : (row + 1) * cols].astype(FL)
            for idx in range(rows):
                fold = jnp.sum((a_rows[idx] * b_j).reshape(cols // 8, 8, width), axis=0)
                at = pl.multiple_of((idx * cols + block * rows + row) * 8, 8)
                part_ref[pl.ds(at, 8), :] = fold

    for idx in range(chips):
        block = 2 * idx + 1 - core
        side, fac = b_block(dims, other_ref[idx], w_b, col_mask, block * rows, limit)
        other_side_ref[idx] = side
        other_fac_ref[idx] = fac
        products(block, side)
        products(2 * idx + core, own_side_ref[idx])
        if idx == chips // 2 - 1 or idx == chips - 1:
            late = idx == chips - 1
            span = pl.ds(chips // 2, chips - chips // 2) if late else pl.ds(0, chips // 2)
            moves += fetch(
                [
                    (other_side_ref.at[span], other_side_hbm.at[span]),
                    (other_fac_ref.at[span], other_fac_hbm.at[span]),
                ],
                sems.at[pl.ds(9 if late else 7, 2)],
            )
    x_val = part_ref[pl.ds(0, pairs, stride=8), :]
    for idx in range(1, 8):
        x_val = x_val + part_ref[pl.ds(idx, pairs, stride=8), :]

    x_ref[...] = x_val
    for move in early_moves:
        move.wait()
    y_low, _, _ = row_norm(x_val, norms_ref[2:3], norms_ref[3:4])
    z1 = pair_ref[...] + gate_ref[...] * dot(y_low, wl_ref[5])
    z1_ref[...] = z1
    h1, _, _ = row_norm(z1, norms_ref[4:5], norms_ref[5:6])
    h1_ref[...] = h1
    tbt = dot(pbt_ref[...].astype(BF), h1, 1, 1).astype(BF).astype(FL)
    half = pairs // 2
    block = jnp.concatenate([tbt[:, :half], tbt[:, half:]], axis=0)
    for idx in range(size):
        tb_ref[idx] = block
    for move in moves:
        move.wait()


def diagonal_block(first, second):
    zero = jnp.zeros(first.shape, first.dtype)
    return jnp.concatenate(
        [
            jnp.concatenate([first, zero], axis=1),
            jnp.concatenate([zero, second], axis=1),
        ],
        axis=0,
    )


def pack_places(dims):
    rows, cols, width, heads, _ = dims
    pairs, lines = rows * cols, heads * cols
    at, places = 0, {}
    for name, tall in (
        ("prob", rows // 2 * lines),
        ("dscore", rows // 2 * lines),
        ("datt", pairs),
        ("u", pairs),
        ("dout2", pairs),
        ("dgate2", pairs),
        ("h2", pairs),
        ("dlog", 2 * cols),
    ):
        places[name] = at
        at += tall
    return places, at


def attention_kernel(
    dims,
    scal_ref,
    tb_ref,
    h1_ref,
    z1_ref,
    wl_ref,
    norms_hbm,
    pbt_hbm,
    headt_hbm,
    bins_hbm,
    dtb_ref,
    pack_ref,
    dz2_ref,
    stat_ref,
    kcat_ref,
    qblk_ref,
    norms_ref,
    pbt_ref,
    vcat_ref,
    bias_ref,
    prob_ref,
    swap_ref,
    headt_ref,
    bins_ref,
    sems,
):
    rows, cols, width, heads, size = dims
    pairs, lines = rows * cols, heads * cols
    places, _ = pack_places(dims)
    scale = (width // heads) ** (-0.5)
    limit, first_row = scal_ref[0], scal_ref[1]

    def put(name, val):
        pack_ref[places[name] : places[name] + val.shape[0], :] = val

    moves = fetch(
        [
            (headt_hbm, headt_ref),
            (bins_hbm, bins_ref),
            (norms_hbm, norms_ref),
            (pbt_hbm, pbt_ref),
        ],
        sems,
    )
    w_att = jnp.concatenate([wl_ref[6], wl_ref[7], wl_ref[8], wl_ref[9]], axis=1)
    proj = dot(h1_ref[...], w_att)
    gate2 = jax.nn.sigmoid(proj[:, 3 * width :])
    lane_head = iota((cols, width), 1) // (width // heads)
    zero = jnp.zeros((cols, width), BF)
    for idx in range(rows):
        at, side = idx // 2, idx % 2
        lanes = slice(side * width, (side + 1) * width)
        span = slice(idx * cols, (idx + 1) * cols)
        query = proj[span, :width].astype(BF)
        qblk_ref[at, side * cols : (side + 1) * cols, lanes] = query
        qblk_ref[at, (1 - side) * cols : (2 - side) * cols, lanes] = zero
        for head in range(heads):
            spot = slice(head * cols, (head + 1) * cols)
            keep = lane_head == head
            kcat_ref[at, spot, lanes] = jnp.where(
                keep, proj[span, width : 2 * width], 0.0
            ).astype(BF)
            vcat_ref[at, spot, lanes] = jnp.where(
                keep, proj[span, 2 * width : 3 * width], 0.0
            ).astype(BF)

    for half in range(2):
        for jl in range(2):
            lanes = slice(jl * cols, (jl + 1) * cols)
            got = [
                tb_ref[pl.ds(half * heads + head, size, stride=2 * heads), :][:, lanes]
                for head in range(heads)
            ]
            for duo in range(heads // 2):
                line = jnp.concatenate([got[2 * duo], got[2 * duo + 1]], axis=1)
                bias_ref[duo, pl.ds(2 * half + jl, size, stride=rows), :] = line
                bias_ref[duo, pl.ds(cols + 2 * half + jl, size, stride=rows), :] = line
    bias = jnp.concatenate([bias_ref[duo].T for duo in range(heads // 2)], axis=0)
    key_ok = iota((lines, 2 * cols), 0) % cols < limit
    att = []
    for at in range(rows // 2):
        score = dot(kcat_ref[at], qblk_ref[at], 1, 1) * scale + bias
        score = jnp.where(key_ok, score, -1000000000.0).reshape(heads, cols, 2 * cols)
        top = jnp.max(score, axis=1, keepdims=True)
        grown = jnp.exp(score - top)
        prob = (grown / jnp.sum(grown, axis=1, keepdims=True)).reshape(lines, 2 * cols)
        prob_ref[at] = prob
        low = prob.astype(BF)
        pack_ref[places["prob"] + at * lines : places["prob"] + (at + 1) * lines, :] = low
        both = dot(low, vcat_ref[at], 0, 0)
        att += [both[:cols, :width], both[cols:, width:]]
    att = jnp.concatenate(att, axis=0)
    u_low = (gate2 * att).astype(BF)
    put("u", u_low)
    z2 = z1_ref[...] + dot(u_low, wl_ref[10])
    for move in moves:
        move.wait()
    h2, unit6, rstd6 = row_norm(z2, norms_ref[6:7], norms_ref[7:8])
    put("h2", h2)
    headt = headt_ref[...].astype(BF)
    logits = dot(headt, h2, 1, 1)
    spot = iota((1, pairs), 1)
    ok = jnp.logical_and(spot % cols < limit, spot // cols + first_row < limit)
    mask = jnp.where(ok, 1.0, 0.0).astype(FL)
    bins = jnp.concatenate([bins_ref[idx : idx + 1, :] for idx in range(rows)], axis=1)
    onehot = jnp.where(iota(logits.shape, 0) == bins, 1.0, 0.0).astype(FL)
    top = jnp.max(logits, axis=0, keepdims=True)
    lse = top + jnp.log(jnp.sum(jnp.exp(logits - top), axis=0, keepdims=True))
    pick = jnp.sum(logits * onehot, axis=0, keepdims=True)
    loss = jnp.sum(mask * (lse - pick), axis=1, keepdims=True)
    count = jnp.sum(mask, axis=1, keepdims=True)
    dlog = (mask * (jnp.exp(logits - lse) - onehot)).astype(BF)
    put("dlog", jnp.concatenate([dlog[:, :width], dlog[:, width:]], axis=0))
    dz2, dg6, ds6 = row_norm_back(dot(dlog, headt, 0, 0), unit6, rstd6, norms_ref[6:7])
    dz2_ref[...] = dz2
    stat_ref[0:1, :] = dg6
    stat_ref[1:2, :] = ds6
    stat_ref[2:3, :] = jnp.broadcast_to(loss, (1, width))
    stat_ref[3:4, :] = jnp.broadcast_to(count, (1, width))
    stat_ref[4:8, :] = jnp.zeros((4, width), FL)
    dout2 = dz2.astype(BF)
    put("dout2", dout2)
    du = dot(dout2, wl_ref[10], 1, 1)
    put("dgate2", (du * att * gate2 * (1.0 - gate2)).astype(BF))
    datt = (du * gate2).astype(BF)
    put("datt", datt)
    total = None
    for at in range(rows // 2):
        first = datt[(2 * at) * cols : (2 * at + 1) * cols]
        second = datt[(2 * at + 1) * cols : (2 * at + 2) * cols]
        block = diagonal_block(first, second)
        dprob = dot(vcat_ref[at], block, 1, 1)
        prob = prob_ref[at]
        inner = jnp.sum((dprob * prob).reshape(heads, cols, 2 * cols), axis=1, keepdims=True)
        dscore = prob.reshape(heads, cols, 2 * cols) * (
            dprob.reshape(heads, cols, 2 * cols) - inner
        )
        low = dscore.reshape(lines, 2 * cols).astype(BF)
        pack_ref[places["dscore"] + at * lines : places["dscore"] + (at + 1) * lines, :] = low
        total = low.astype(FL) if total is None else total + low.astype(FL)
    for duo in range(heads // 2):
        turned = total[duo * 2 * cols : (duo + 1) * 2 * cols].T
        swap_ref[duo] = turned[:cols] + turned[cols:]
    for half in range(2):
        for head in range(heads):
            inside = slice((head % 2) * cols, (head % 2 + 1) * cols)
            line = jnp.concatenate(
                [
                    swap_ref[head // 2, pl.ds(2 * half + jl, size, stride=rows), :][:, inside]
                    for jl in range(2)
                ],
                axis=1,
            )
            dtb_ref[pl.ds(half * heads + head, size, stride=2 * heads), :] = line


def attention_grad_kernel(
    dims,
    scal_ref,
    kcat_ref,
    qblk_ref,
    pack_ref,
    h1_ref,
    h0_ref,
    x_ref,
    norms_ref,
    wl_ref,
    early_ref,
    loc_ref,
    dqkvg_ref,
):
    rows, cols, width, heads, size = dims
    pairs, lines = rows * cols, heads * cols
    places, _ = pack_places(dims)

    def take(name, tall, skip=0):
        return pack_ref[places[name] + skip : places[name] + skip + tall, :]

    mask = pair_mask(dims, scal_ref[0])(scal_ref[1])
    side, fac, gate = own_sides(h0_ref[...], wl_ref, mask)
    y_low, _, _ = row_norm(x_ref[...], norms_ref[2:3], norms_ref[3:4])
    loc_ref[0] = side.astype(BF).astype(FL)
    loc_ref[1] = fac
    loc_ref[2] = gate
    loc_ref[3] = dot(y_low, wl_ref[5])
    scale = (width // heads) ** (-0.5)
    lane_head = iota((cols, width), 1) // (width // heads)

    def diagonal(val):
        out = jnp.zeros((cols, width), FL)
        for head in range(heads):
            out = jnp.where(lane_head == head, val[head * cols : (head + 1) * cols], out)
        return out

    for at in range(rows // 2):
        dscore = take("dscore", lines, at * lines)
        block = diagonal_block(
            take("datt", cols, 2 * at * cols), take("datt", cols, (2 * at + 1) * cols)
        )
        dquery = dot(dscore, kcat_ref[at], 0, 0)
        dkeys = dot(dscore, qblk_ref[at])
        dvals = dot(take("prob", lines, at * lines), block)
        for side in range(2):
            idx = 2 * at + side
            lanes = slice(side * width, (side + 1) * width)
            span = slice(idx * cols, (idx + 1) * cols)
            dqkvg_ref[span, :width] = (
                dquery[side * cols : (side + 1) * cols, lanes] * scale
            ).astype(BF)
            dqkvg_ref[span, width : 2 * width] = (diagonal(dkeys[:, lanes]) * scale).astype(BF)
            dqkvg_ref[span, 2 * width : 3 * width] = diagonal(dvals[:, lanes]).astype(BF)
    dqkvg_ref[:, 3 * width :] = take("dgate2", pairs)
    dqkvg = dqkvg_ref[...]
    w_att = jnp.concatenate([wl_ref[6], wl_ref[7], wl_ref[8], wl_ref[9]], axis=1)
    loc_ref[4] = dot(dqkvg, w_att, 1, 1)
    dw_att = dot(h1_ref[...], dqkvg, 0, 0)
    for idx in range(4):
        early_ref[idx * width : (idx + 1) * width, :] = dw_att[:, idx * width : (idx + 1) * width]
    early_ref[4 * width : 5 * width, :] = dot(take("u", pairs), take("dout2", pairs), 0, 0)
    dlog = take("dlog", 2 * cols)
    dlog = jnp.concatenate([dlog[:cols], dlog[cols:]], axis=1)
    early_ref[5 * width :, :] = dot(dlog, take("h2", pairs))


def triangle_grad_kernel(
    dims,
    scal_ref,
    dtb_ref,
    early_ref,
    dz2_ref,
    stat_ref,
    h1_ref,
    x_ref,
    z1_ref,
    loc_ref,
    own_side_hbm,
    own_fac_hbm,
    other_side_hbm,
    other_fac_hbm,
    own_hbm,
    other_hbm,
    norms_ref,
    wl_ref,
    pbt_ref,
    keep_ref,
    give_ref,
    flat_ref,
    dx_ref,
    own_side_ref,
    own_fac_ref,
    other_side_ref,
    other_fac_ref,
    own_ref,
    other_ref,
    sems,
):
    rows, cols, width, heads, size = dims
    pairs = rows * cols
    chip, core = scal_ref[2], scal_ref[3]
    moves = fetch(
        [
            (own_side_hbm, own_side_ref),
            (other_side_hbm, other_side_ref),
            (own_hbm, own_ref),
            (other_hbm, other_ref),
            (own_fac_hbm, own_fac_ref),
            (other_fac_hbm, other_fac_ref),
        ],
        sems,
    )
    y_low, unit2, rstd2 = row_norm(x_ref[...], norms_ref[2:3], norms_ref[3:4])
    _, unit4, rstd4 = row_norm(z1_ref[...], norms_ref[4:5], norms_ref[5:6])
    got = dtb_ref[0]
    for idx in range(1, size):
        got = got + dtb_ref[idx]
    dtbt = jnp.concatenate([got[:heads], got[heads:]], axis=1).astype(BF)
    h1 = h1_ref[...]
    dpbt = dot(dtbt, h1)
    dh1 = loc_ref[4] + dot(dtbt, pbt_ref[...].astype(BF), 0, 0)
    dn4, dg4, ds4 = row_norm_back(dh1, unit4, rstd4, norms_ref[4:5])
    dz1 = dz2_ref[...] + dn4
    gate = loc_ref[2]
    dout1 = (dz1 * gate).astype(BF)
    dgate = dz1 * loc_ref[3] * gate * (1.0 - gate)
    dx, dg2, ds2 = row_norm_back(dot(dout1, wl_ref[5], 1, 1), unit2, rstd2, norms_ref[2:3])
    dx_ref[...] = dx.astype(BF).astype(FL)

    moves[0].wait()
    moves[1].wait()

    def da_step(idx, acc):
        for side_ref, half in ((own_side_ref, core), (other_side_ref, 1 - core)):
            for row in range(rows):
                j = (2 * idx + half) * rows + row
                b_j = side_ref[idx, row * cols : (row + 1) * cols, :].astype(FL)
                acc = tuple(
                    acc[at] + dx_ref[pl.ds(at * cols + j, 1), :] * b_j for at in range(rows)
                )
        return acc

    acc = lax.fori_loop(
        0, size // 2, da_step, tuple(jnp.zeros((cols, width), FL) for _ in range(rows))
    )
    da = jnp.concatenate(acc, axis=0).astype(BF).astype(FL)
    own = jnp.concatenate(
        [
            (da * loc_ref[1]).astype(BF),
            (da * loc_ref[0] * (1.0 - loc_ref[1])).astype(BF),
            dgate.astype(BF),
        ],
        axis=1,
    )
    for move in moves[2:]:
        move.wait()
    ones = jnp.ones((16, pairs), BF)

    def products(h0, grads):
        return dot(h0, grads, 0, 0), dot(ones, grads)

    dw_own, sum_own = products(own_ref[chip], own)

    a_rows = [loc_ref[0, idx * cols : (idx + 1) * cols, :] for idx in range(rows)]

    def db_step(idx, acc):
        for src, side_ref, fac_ref, half in (
            (own_ref, own_side_ref, own_fac_ref, core),
            (other_ref, other_side_ref, other_fac_ref, 1 - core),
        ):
            lines = []
            for row in range(rows):
                j = (2 * idx + half) * rows + row
                db = dx_ref[pl.ds(j, 1), :] * a_rows[0]
                for own_row in range(1, rows):
                    db = db + dx_ref[pl.ds(own_row * cols + j, 1), :] * a_rows[own_row]
                lines.append(db.astype(BF))
            db = jnp.concatenate(lines, axis=0)
            fac = fac_ref[idx]
            grads = jnp.concatenate([db * fac, db * (side_ref[idx] * (1.0 - fac))], axis=1)
            main, sums = products(src[idx], grads)
            acc = (acc[0] + main, acc[1] + sums)
        return acc

    dw_b = (jnp.zeros((width, 2 * width), FL), jnp.zeros((16, 2 * width), FL))
    for idx in range(size // 2):
        dw_b = db_step(idx, dw_b)
    dw_b, sum_b = dw_b

    parts = [
        (val[:, at * width : (at + 1) * width], sums[:1, at * width : (at + 1) * width])
        for val, sums, at in (
            (dw_own, sum_own, 0),
            (dw_own, sum_own, 1),
            (dw_b, sum_b, 0),
            (dw_b, sum_b, 1),
            (dw_own, sum_own, 2),
        )
    ]
    mixed = jnp.zeros((width, width), FL)
    summed = jnp.zeros((width, width), FL)
    for idx, (part, sums) in enumerate(parts):
        weight = wl_ref[idx].astype(FL)
        flat_ref[idx * width : (idx + 1) * width, :] = part
        mixed = mixed + weight * part
        summed = summed + weight * sums
    ds0 = lane_sums(summed)
    dg0 = (lane_sums(mixed) - norms_ref[1:2] * ds0) / norms_ref[0:1]
    flat_ref[5 * width : 6 * width, :] = dot(y_low, dout1, 0, 0)
    mats = 11 * width
    flat_ref[6 * width : mats, :] = early_ref[: 5 * width, :]
    bins_n = early_ref.shape[0] - 5 * width
    flat_ref[mats : mats + bins_n, :] = early_ref[5 * width :, :]
    base = mats + bins_n
    flat_ref[base : base + heads, :] = dpbt
    flat_ref[base + heads : base + 8, :] = jnp.zeros((8 - heads, width), FL)
    base += 8
    for idx, line in enumerate((dg0, ds0, dg2, ds2, dg4, ds4)):
        flat_ref[base + idx : base + idx + 1, :] = line
    flat_ref[base + 6 : base + 10, :] = stat_ref[0:4, :]
    total = flat_ref.shape[0]
    flat_ref[base + 10 :, :] = jnp.zeros((total - base - 10, width), FL)
    half = total // 2
    keep_ref[...] = flat_ref[pl.ds(pl.multiple_of(core * half, half), half), :]
    give_ref[...] = flat_ref[pl.ds(pl.multiple_of((1 - core) * half, half), half), :]


def update_kernel(
    dims,
    scal_ref,
    mine_ref,
    other_ref,
    mats_ref,
    mats_m_ref,
    mats_v_ref,
    pb_ref,
    pb_m_ref,
    pb_v_ref,
    head_ref,
    head_m_ref,
    head_v_ref,
    norms_ref,
    norms_m_ref,
    norms_v_ref,
    norm_out,
    loss_out,
    count_out,
    mats_m_out,
    mats_v_out,
    mats_out,
    mats_low_out,
    pb_m_out,
    pb_v_out,
    pb_out,
    head_m_out,
    head_v_out,
    head_out,
    norms_m_out,
    norms_v_out,
    norms_out,
    flat_ref,
    scalar_buf,
    small_buf,
    pb_buf,
    m_buf,
    v_buf,
    w_buf,
    low_buf,
    sems,
    small_sems,
):
    rows, cols, width, heads, size = dims
    core = scal_ref[3]
    half = mine_ref.shape[0]
    flat_ref[pl.ds(pl.multiple_of(core * half, half), half), :] = mine_ref[...]
    flat_ref[pl.ds(pl.multiple_of((1 - core) * half, half), half), :] = other_ref[...]
    count = mats_ref.shape[0]
    mats = count * width
    bins_n = head_ref.shape[0]
    base = mats + bins_n
    grads = flat_ref[: base + 16, :]
    square = jnp.sum(grads * grads, axis=0, keepdims=True)
    norm = jnp.sqrt(jnp.sum(square, axis=1, keepdims=True))
    factor = jnp.minimum(1.0, CLIP / norm)
    scalar_buf[0] = norm
    scalar_buf[1] = flat_ref[base + 16 : base + 17, 0:1]
    scalar_buf[2] = flat_ref[base + 17 : base + 18, 0:1]

    moves = []

    def send(at, idx, buf, out):
        move = pltpu.make_async_copy(buf.at[idx], out.at[idx], sems.at[at, idx])
        move.start()
        moves.append(move)

    def step(weight, grad, first, second):
        return adam(weight, grad * factor, first, second)

    triples = []
    for at, tall, buf, skip, ins, outs in (
        (mats, bins_n, small_buf, 0, (head_ref, head_m_ref, head_v_ref), (head_m_out, head_v_out, head_out)),
        (base + 8, 8, small_buf, bins_n, (norms_ref, norms_m_ref, norms_v_ref), (norms_m_out, norms_v_out, norms_out)),
        (base, heads, pb_buf, 0, (pb_ref, pb_m_ref, pb_v_ref), (pb_m_out, pb_v_out, pb_out)),
    ):
        now = step(ins[0][...], flat_ref[at : at + tall, :], ins[1][...], ins[2][...])
        for idx, (val, out) in enumerate(zip(now, outs)):
            buf[idx, skip : skip + tall, :] = val
            triples.append((buf.at[idx, pl.ds(skip, tall)], out))
    triples += [
        (scalar_buf.at[idx], out) for idx, out in enumerate((norm_out, loss_out, count_out))
    ]
    moves += fetch(triples, small_sems)
    for idx in range(count):
        m_buf[idx], v_buf[idx], weight = step(
            mats_ref[idx],
            flat_ref[idx * width : (idx + 1) * width, :],
            mats_m_ref[idx],
            mats_v_ref[idx],
        )
        w_buf[idx] = weight
        low_buf[idx] = weight.astype(BF)
        send(0, idx, m_buf, mats_m_out)
        send(1, idx, v_buf, mats_v_out)
        send(2, idx, w_buf, mats_out)
        send(3, idx, low_buf, mats_low_out)
    for move in moves:
        move.wait()


def call(kernel, args, outs, scratch=(), limit=VMEM_LIMIT, flops=10**7):
    spots = {"s": pltpu.SMEM, "v": pltpu.VMEM, "h": pltpu.HBM}
    return pl.pallas_call(
        kernel,
        out_shape=[
            pltpu.HBM(shape, kind) if spot == "h" else jax.ShapeDtypeStruct(shape, kind)
            for shape, kind, spot in outs
        ],
        in_specs=[pl.BlockSpec(memory_space=spots[spot]) for _, spot in args],
        out_specs=[pl.BlockSpec(memory_space=spots[spot]) for _, _, spot in outs],
        scratch_shapes=list(scratch),
        compiler_params=pltpu.CompilerParams(vmem_limit_bytes=limit),
        cost_estimate=pl.CostEstimate(flops=flops, bytes_accessed=10**6, transcendentals=0),
    )(
        *(
            pltpu.with_memory_space_constraint(value, pltpu.HBM) if spot == "h" else value
            for value, spot in args
        )
    )


def same_core_groups(crops, size):
    return [
        [crop * size + idx for crop in range(crops) for idx in range(core, size, 2)]
        for core in range(2)
    ]


def core_swap(value, size):
    return lax.ppermute(value, "row", [(idx, idx ^ 1) for idx in range(size)])


def fast_step(
    crops,
    size,
    pair,
    bins,
    lengths,
    mats,
    mats_m,
    mats_v,
    pbias,
    pbias_m,
    pbias_v,
    head,
    head_m,
    head_v,
    norms,
    norms_m,
    norms_v,
):
    rows, cols, width = pair.shape[1:]
    heads, bins_n = pbias.shape[1], head.shape[1]
    pairs, lines = rows * cols, heads * cols
    dims = (rows, cols, width, heads, size)
    chips = size // 2
    place = lax.axis_index("row")
    scal = jnp.stack([lengths[0], place * rows, place // 2, place % 2]).astype(jnp.int32)
    start = pair.reshape(pairs, width)
    pbt, headt = pbias.T, head.T

    copies, wl = call(
        functools.partial(start_kernel, chips),
        [(start, "h"), (norms, "h"), (mats, "h")],
        [((chips, pairs, width), BF, "v"), (mats.shape, BF, "v")],
        [
            pltpu.VMEM((pairs, width), FL),
            pltpu.VMEM(norms.shape, FL),
            pltpu.VMEM(mats.shape, FL),
            pltpu.SemaphoreType.DMA((3,)),
        ],
    )
    near = [list(range(core, size, 2)) for core in range(2)]
    own = lax.all_to_all(copies, "row", 0, 0, axis_index_groups=near, tiled=True)
    other = core_swap(own, size)
    a_val, gate, h0, own_side, own_fac = call(
        functools.partial(own_kernel, dims),
        [(scal, "s"), (copies, "v"), (own, "v"), (wl, "v")],
        [
            ((pairs, width), FL, "v"),
            ((pairs, width), FL, "v"),
            ((pairs, width), BF, "v"),
            (own.shape, BF, "v"),
            (own.shape, BF, "v"),
        ],
    )
    tb, own_side, own_fac, other_side, other_fac, own_far, other_far, x_val, z1, h1 = call(
        functools.partial(triangle_kernel, dims),
        [
            (scal, "s"),
            (own, "v"),
            (other, "v"),
            (a_val, "v"),
            (gate, "v"),
            (own_side, "v"),
            (own_fac, "v"),
            (start, "h"),
            (norms, "h"),
            (wl, "v"),
            (pbt, "h"),
        ],
        [((size, 2 * heads, 2 * cols), FL, "v")]
        + [(own.shape, BF, "h")] * 6
        + [((pairs, width), FL, "v"), ((pairs, width), FL, "v"), ((pairs, width), BF, "v")],
        [
            pltpu.VMEM((pairs, width), FL),
            pltpu.VMEM(norms.shape, FL),
            pltpu.VMEM(pbt.shape, FL),
            pltpu.VMEM(own.shape, BF),
            pltpu.VMEM(own.shape, BF),
            pltpu.VMEM((pairs * 8, width), FL),
            pltpu.SemaphoreType.DMA((11,)),
        ],
    )

    tb_all = lax.all_to_all(tb, "row", 0, 0, tiled=True)
    bias_shape = (size * 2 * heads, 2 * cols)
    dtb, pack, dz2, stat, kcat, qblk, norms_here, pbt_here = call(
        functools.partial(attention_kernel, dims),
        [
            (scal, "s"),
            (tb_all.reshape(bias_shape), "v"),
            (h1, "v"),
            (z1, "v"),
            (wl, "v"),
            (norms, "h"),
            (pbt, "h"),
            (headt, "h"),
            (bins[0], "h"),
        ],
        [
            (bias_shape, FL, "v"),
            ((pack_places(dims)[1], width), BF, "v"),
            ((pairs, width), FL, "v"),
            ((8, width), FL, "v"),
            ((rows // 2, lines, 2 * width), BF, "v"),
            ((rows // 2, 2 * cols, 2 * width), BF, "v"),
            (norms.shape, FL, "v"),
            (pbt.shape, FL, "v"),
        ],
        [
            pltpu.VMEM((rows // 2, lines, 2 * width), BF),
            pltpu.VMEM((heads // 2, 2 * cols, 2 * cols), FL),
            pltpu.VMEM((rows // 2, lines, 2 * cols), FL),
            pltpu.VMEM((heads // 2, cols, 2 * cols), FL),
            pltpu.VMEM((bins_n, width), FL),
            pltpu.VMEM((rows, cols), jnp.int32),
            pltpu.SemaphoreType.DMA((4,)),
        ],
    )

    dtb_all = lax.all_to_all(dtb.reshape(size, 2 * heads, 2 * cols), "row", 0, 0, tiled=True)
    early, loc = call(
        functools.partial(attention_grad_kernel, dims),
        [(scal, "s")]
        + [
            (value, "v")
            for value in (
                kcat,
                qblk,
                pack,
                h1,
                h0,
                x_val,
                norms_here,
                wl,
            )
        ],
        [((5 * width + bins_n, width), FL, "v"), ((5, pairs, width), FL, "v")],
        [pltpu.VMEM((pairs, 4 * width), BF)],
    )
    used = mats.shape[0] * width + bins_n + 18
    unit = 8 * crops * size
    total = -(-used // unit) * unit
    keep, give = call(
        functools.partial(triangle_grad_kernel, dims),
        [(scal, "s")]
        + [(value, "v") for value in (dtb_all, early, dz2, stat, h1, x_val, z1, loc)]
        + [(value, "h") for value in (own_side, own_fac, other_side, other_fac, own_far, other_far)]
        + [(value, "v") for value in (norms_here, wl, pbt_here)],
        [((total // 2, width), FL, "v"), ((total // 2, width), FL, "v")],
        [
            pltpu.VMEM((total, width), FL),
            pltpu.VMEM((pairs, width), FL),
        ]
        + [pltpu.VMEM(own.shape, BF)] * 6
        + [
            pltpu.SemaphoreType.DMA((6,)),
        ],
    )

    half = keep + core_swap(give, size)
    count = crops * chips
    groups = same_core_groups(crops, size)
    axes = ("crop", "row")
    parts = lax.all_to_all(
        half.reshape(count, -1, width), axes, 0, 0, axis_index_groups=groups, tiled=True
    )
    share = jnp.sum(parts, axis=0)
    spread = jnp.broadcast_to(share[None], (count,) + share.shape)
    mine = lax.all_to_all(spread, axes, 0, 0, axis_index_groups=groups, tiled=True)
    mine = mine.reshape(total // 2, width)
    other_half = core_swap(mine, size)

    number = mats.shape[0]
    big, low = ((number, width, width), FL, "h"), ((number, width, width), BF, "h")
    pb_out, head_out = ((heads, width), FL, "h"), ((bins_n, width), FL, "h")
    norm_out = ((norms.shape[0], width), FL, "h")
    res = call(
        functools.partial(update_kernel, dims),
        [(scal, "s"), (mine, "v"), (other_half, "v"), (mats, "v")]
        + [
            (value, "v")
            for value in (
                mats_m,
                mats_v,
                pbt_here,
                pbias_m.T,
                pbias_v.T,
                headt,
                head_m.T,
                head_v.T,
                norms_here,
                norms_m,
                norms_v,
            )
        ],
        [((1, 1), FL, "h")] * 3
        + [big, big, big, low]
        + [pb_out] * 3
        + [head_out] * 3
        + [norm_out] * 3,
        [
            pltpu.VMEM((total, width), FL),
            pltpu.VMEM((3, 1, 1), FL),
            pltpu.VMEM((3, bins_n + norms.shape[0], width), FL),
            pltpu.VMEM((3, heads, width), FL),
        ]
        + [pltpu.VMEM((number, width, width), FL)] * 3
        + [
            pltpu.VMEM((number, width, width), BF),
            pltpu.SemaphoreType.DMA((4, number)),
            pltpu.SemaphoreType.DMA((12,)),
        ],
    )
    return (
        *(value.reshape(()) for value in res[:3]),
        *res[3:7],
        *(value.T for value in res[7:13]),
        *res[13:16],
    )


def small_enough(pair, heads, size):
    _, rows, cols, width = pair.shape
    held = 4 * size * rows * cols * width * 4 + 4 * rows * heads * cols * cols * 4
    return (
        held <= 2**24
        and width == 2 * cols
        and rows == 4
        and heads == 4
        and size % 2 == 0
        and rows * size == cols
    )


def solution(mesh):
    crops, size = mesh.shape["crop"], mesh.shape["row"]

    def on_device(*args):
        if small_enough(args[0], args[6].shape[1], size):
            return fast_step(crops, size, *args)
        return general_step(*args)

    in_specs = (
        P("crop", "row", None, None),
        P("crop", "row", None),
        P("crop"),
        P(),
        P(),
        P(),
        P(),
        P(),
        P(),
        P(),
        P(),
        P(),
        P(),
        P(),
        P(),
    )
    out_specs = (P(), P(), P(), P(), P(), P(), P(), P(), P(), P(), P(), P(), P(), P(), P(), P())
    return jax.shard_map(
        on_device, mesh=mesh, in_specs=in_specs, out_specs=out_specs, check_vma=False
    )
```

```python
import functools

import jax
import jax.numpy as jnp
from jax import lax
from jax.experimental import pallas as pl
from jax.experimental.pallas import tpu as pltpu
from jax.sharding import PartitionSpec as P

STEP = 5


EPS_NORM = 1e-05
CLIP = 1.0
RATE = 0.05
BETA1 = 0.9
BETA2 = 0.95
ADAM_EPS = 1e-08
WDECAY = 0.01


def norm_fwd(v, gain, shift):
    mean = jnp.mean(v, axis=-1, keepdims=True)
    cent = v - mean
    rstd = lax.rsqrt(jnp.mean(cent * cent, axis=-1, keepdims=True) + EPS_NORM)
    unit = cent * rstd
    return (unit * gain + shift, unit, rstd)


def norm_back(grad, unit, rstd, gain):
    dgain = jnp.sum(grad * unit, axis=(0, 1))
    dshift = jnp.sum(grad, axis=(0, 1))
    dunit = grad * gain
    dval = rstd * (
        dunit
        - jnp.mean(dunit, axis=-1, keepdims=True)
        - unit * jnp.mean(dunit * unit, axis=-1, keepdims=True)
    )
    return (dval, dgain, dshift)


def matmul(value, weight):
    flat = value.reshape(-1, value.shape[-1])
    out = jnp.dot(flat, weight, preferred_element_type=jnp.float32)
    return out.reshape(value.shape[:-1] + (weight.shape[1],))


def wgrad(value, grad):
    return jnp.einsum("ijc,ijd->cd", value, grad, preferred_element_type=jnp.float32)


def adam(weight, grad, first, second):
    first_new = BETA1 * first + (1.0 - BETA1) * grad
    second_new = BETA2 * second + (1.0 - BETA2) * grad * grad
    m_hat = first_new / (1.0 - BETA1**STEP)
    v_hat = second_new / (1.0 - BETA2**STEP)
    weight_new = weight - RATE * (m_hat / (jnp.sqrt(v_hat) + ADAM_EPS) + WDECAY * weight)
    return (first_new, second_new, weight_new)


def general_step(
    pair,
    bins,
    lengths,
    mats,
    mats_m,
    mats_v,
    pbias,
    pbias_m,
    pbias_v,
    head,
    head_m,
    head_v,
    norms,
    norms_m,
    norms_v,
):
    bf = jnp.bfloat16
    fl = jnp.float32
    width = mats.shape[1]
    rows = pair.shape[1]
    cols = pair.shape[2]
    heads = pbias.shape[1]
    size_head = width // heads
    scale = size_head ** (-0.5)
    start_pair = pair[0]
    first_row = lax.axis_index("row") * rows
    limit = lengths[0]
    row_ok = first_row + jnp.arange(rows) < limit
    col_ok = jnp.arange(cols) < limit
    pmask = (row_ok[:, None] & col_ok[None, :]).astype(fl)
    m3 = pmask[..., None]
    wl = mats.astype(bf)
    pl = pbias.astype(bf)
    hl = head.astype(bf)
    w_tri = jnp.concatenate([wl[0], wl[1], wl[2], wl[3], wl[4]], axis=1)
    w_att = jnp.concatenate([wl[6], wl[7], wl[8], wl[9]], axis=1)
    h0, unit0, rstd0 = norm_fwd(start_pair, norms[0], norms[1])
    h0b = h0.astype(bf)
    proj = matmul(h0b, w_tri)
    sig_a = jax.nn.sigmoid(proj[..., width : 2 * width])
    sig_b = jax.nn.sigmoid(proj[..., 3 * width : 4 * width])
    gate = jax.nn.sigmoid(proj[..., 4 * width :])
    a_low = (sig_a * proj[..., :width] * m3).astype(bf)
    b_low = (sig_b * proj[..., 2 * width : 3 * width] * m3).astype(bf)
    b_all = lax.all_gather(b_low, "row", axis=0, tiled=True)
    prod = jnp.einsum("ikc,jkc->ijc", a_low, b_all, preferred_element_type=fl)
    y_val, unit2, rstd2 = norm_fwd(prod, norms[2], norms[3])
    y_low = y_val.astype(bf)
    out1 = matmul(y_low, wl[5])
    z1 = start_pair + gate * out1
    h1, unit4, rstd4 = norm_fwd(z1, norms[4], norms[5])
    h1b = h1.astype(bf)
    qkvg = matmul(h1b, w_att)
    query = qkvg[..., :width].astype(bf).reshape(rows, cols, heads, size_head)
    keys = qkvg[..., width : 2 * width].astype(bf).reshape(rows, cols, heads, size_head)
    values = qkvg[..., 2 * width : 3 * width].astype(bf).reshape(rows, cols, heads, size_head)
    gate2 = jax.nn.sigmoid(qkvg[..., 3 * width :])
    tb_low = matmul(h1b, pl).astype(bf)
    tb_all = lax.all_gather(tb_low, "row", axis=0, tiled=True)
    tb_heads = jnp.transpose(tb_all, (2, 0, 1)).astype(fl)
    scores = (
        jnp.einsum("ijhd,ikhd->ihjk", query, keys, preferred_element_type=fl) * scale
        + tb_heads[None]
    )
    scores = jnp.where(col_ok[None, None, None, :], scores, -1000000000.0)
    probs = jax.nn.softmax(scores, axis=-1)
    p_low = probs.astype(bf)
    att = jnp.einsum("ihjk,ikhd->ijhd", p_low, values, preferred_element_type=fl).reshape(
        rows, cols, width
    )
    u_low = (gate2 * att).astype(bf)
    z2 = z1 + matmul(u_low, wl[10])
    h2, unit6, rstd6 = norm_fwd(z2, norms[6], norms[7])
    h2b = h2.astype(bf)
    logits = matmul(h2b, hl)
    lse = jax.nn.logsumexp(logits, axis=-1)
    onehot = (bins[0][..., None] == jnp.arange(logits.shape[-1])).astype(fl)
    pick = jnp.sum(logits * onehot, axis=-1)
    loss = jnp.sum(pmask * (lse - pick))
    count = jnp.sum(pmask)
    dlog = (m3 * (jnp.exp(logits - lse[..., None]) - onehot)).astype(bf)
    dhead = wgrad(h2b, dlog)
    dz2, dg6, ds6 = norm_back(matmul(dlog, hl.T), unit6, rstd6, norms[6])
    dout2 = dz2.astype(bf)
    dw10 = wgrad(u_low, dout2)
    du = matmul(dout2, wl[10].T)
    dgate2 = du * att
    datt = (du * gate2).astype(bf).reshape(rows, cols, heads, size_head)
    dprob = jnp.einsum("ijhd,ikhd->ihjk", datt, values, preferred_element_type=fl)
    dvals = jnp.einsum("ihjk,ijhd->ikhd", p_low, datt, preferred_element_type=fl)
    dscore = (probs * (dprob - jnp.sum(dprob * probs, axis=-1, keepdims=True))).astype(bf)
    dquery = jnp.einsum("ihjk,ikhd->ijhd", dscore, keys, preferred_element_type=fl) * scale
    dkeys = jnp.einsum("ihjk,ijhd->ikhd", dscore, query, preferred_element_type=fl) * scale
    dtb = jnp.sum(dscore.astype(fl), axis=0)
    dtb_own = lax.psum_scatter(dtb, "row", scatter_dimension=1, tiled=True)
    dtb_low = jnp.transpose(dtb_own, (1, 2, 0)).astype(bf)
    dpbias = wgrad(h1b, dtb_low)
    dqkvg = jnp.concatenate(
        [
            dquery.reshape(rows, cols, width),
            dkeys.reshape(rows, cols, width),
            dvals.reshape(rows, cols, width),
            dgate2 * gate2 * (1.0 - gate2),
        ],
        axis=-1,
    ).astype(bf)
    dw_att = wgrad(h1b, dqkvg)
    dh1 = matmul(dqkvg, w_att.T) + matmul(dtb_low, pl.T)
    dn4, dg4, ds4 = norm_back(dh1, unit4, rstd4, norms[4])
    dz1 = dz2 + dn4
    dout1 = (dz1 * gate).astype(bf)
    dw5 = wgrad(y_low, dout1)
    dgate = dz1 * out1
    dxn, dg2, ds2 = norm_back(matmul(dout1, wl[5].T), unit2, rstd2, norms[2])
    dx_low = dxn.astype(bf)
    dside_a = jnp.einsum("ijc,jkc->ikc", dx_low, b_all, preferred_element_type=fl)
    dside_b = lax.psum_scatter(
        jnp.einsum("ijc,ikc->jkc", dx_low, a_low, preferred_element_type=fl),
        "row",
        scatter_dimension=0,
        tiled=True,
    )
    da_r = dside_a.astype(bf).astype(fl)
    db_r = dside_b.astype(bf).astype(fl)
    dproj = jnp.concatenate(
        [
            da_r * sig_a * m3,
            da_r * proj[..., :width] * m3 * sig_a * (1.0 - sig_a),
            db_r * sig_b * m3,
            db_r * proj[..., 2 * width : 3 * width] * m3 * sig_b * (1.0 - sig_b),
            dgate * gate * (1.0 - gate),
        ],
        axis=-1,
    ).astype(bf)
    dw_tri = wgrad(h0b, dproj)
    dh0 = matmul(dproj, w_tri.T)
    unused, dg0, ds0 = norm_back(dh0, unit0, rstd0, norms[0])
    pieces = [dw_tri[:, idx * width : (idx + 1) * width] for idx in range(5)]
    pieces = (
        pieces + [dw5] + [dw_att[:, idx * width : (idx + 1) * width] for idx in range(4)] + [dw10]
    )
    dmats = jnp.stack(pieces)
    dnorms = jnp.stack([dg0, ds0, dg2, ds2, dg4, ds4, dg6, ds6])
    dmats, dpbias, dhead, dnorms, loss, count = lax.psum(
        (dmats, dpbias, dhead, dnorms, loss, count), ("crop", "row")
    )
    grad_norm = jnp.sqrt(
        jnp.sum(dmats * dmats)
        + jnp.sum(dpbias * dpbias)
        + jnp.sum(dhead * dhead)
        + jnp.sum(dnorms * dnorms)
    )
    factor = jnp.minimum(1.0, CLIP / grad_norm)
    new_mats = adam(mats, dmats * factor, mats_m, mats_v)
    new_pbias = adam(pbias, dpbias * factor, pbias_m, pbias_v)
    new_head = adam(head, dhead * factor, head_m, head_v)
    new_norms = adam(norms, dnorms * factor, norms_m, norms_v)
    return (
        grad_norm,
        loss,
        count,
        new_mats[0],
        new_mats[1],
        new_mats[2],
        new_mats[2].astype(bf),
        new_pbias[0],
        new_pbias[1],
        new_pbias[2],
        new_head[0],
        new_head[1],
        new_head[2],
        new_norms[0],
        new_norms[1],
        new_norms[2],
    )


BF = jnp.bfloat16
FL = jnp.float32
VMEM_LIMIT = 24 * 2**20
SPAN = 2.0**-12
DIGIT = 64


def dot(lhs, rhs, left=1, right=0):
    return lax.dot_general(
        lhs, rhs, (((left,), (right,)), ((), ())), preferred_element_type=FL
    )


def lane_sums(val):
    return jnp.sum(val.T, axis=0, keepdims=True)


def row_norm(val, gain, shift):
    mean = jnp.mean(val, axis=-1, keepdims=True)
    cent = val - mean
    rstd = lax.rsqrt(jnp.mean(cent * cent, axis=-1, keepdims=True) + EPS_NORM)
    unit = cent * rstd
    return (unit * gain + shift).astype(BF), unit, rstd


def row_norm_back(grad, unit, rstd, gain):
    dgain = jnp.sum(grad * unit, axis=0, keepdims=True)
    dshift = jnp.sum(grad, axis=0, keepdims=True)
    dunit = grad * gain
    dval = rstd * (
        dunit
        - jnp.mean(dunit, axis=-1, keepdims=True)
        - unit * jnp.mean(dunit * unit, axis=-1, keepdims=True)
    )
    return dval, dgain, dshift


def iota(shape, dim):
    return lax.broadcasted_iota(jnp.int32, shape, dim)


def fetch(pairs, sems):
    moves = [
        pltpu.make_async_copy(src, dst, sems.at[idx]) for idx, (src, dst) in enumerate(pairs)
    ]
    for move in moves:
        move.start()
    return moves


def start_kernel(
    copies, pair_hbm, norms_hbm, mats_hbm, out_ref, wl_ref, pair_ref, norms_ref, mats_ref, sems
):
    moves = fetch(
        [(pair_hbm, pair_ref), (norms_hbm, norms_ref), (mats_hbm, mats_ref)], sems
    )
    moves[0].wait()
    moves[1].wait()
    h0, _, _ = row_norm(pair_ref[...], norms_ref[0:1], norms_ref[1:2])
    for idx in range(copies):
        out_ref[idx] = h0
    moves[2].wait()
    wl_ref[...] = mats_ref[...].astype(BF)


def pair_mask(dims, limit):
    rows, cols, width, _, _ = dims
    spot = iota((rows * cols, width), 0)
    col_ok = spot % cols < limit
    row_in = spot // cols

    def mask_of(block_row):
        return jnp.where(jnp.logical_and(col_ok, row_in + block_row < limit), 1.0, 0.0).astype(FL)

    return mask_of


def own_sides(h0, wl_ref, mask):
    width = h0.shape[1]
    w_own = jnp.concatenate([wl_ref[0], wl_ref[1], wl_ref[4]], axis=1)
    proj = dot(h0, w_own)
    fac = jax.nn.sigmoid(proj[:, width : 2 * width]) * mask
    return fac * proj[:, :width], fac, jax.nn.sigmoid(proj[:, 2 * width :])


def b_block(dims, h0, w_b, col_mask, start, limit):
    rows, cols, width, _, _ = dims
    proj = dot(h0, w_b)
    sig = jax.nn.sigmoid(proj[:, width:])
    lines = []
    for row in range(rows):
        row_ok = jnp.where(start + row < limit, 1.0, 0.0).astype(FL)
        lines.append(sig[row * cols : (row + 1) * cols] * (col_mask * row_ok))
    fac = jnp.concatenate(lines, axis=0)
    return (fac * proj[:, :width]).astype(BF), fac.astype(BF)


def col_mask_of(dims, limit):
    _, cols, width, _, _ = dims
    return jnp.where(iota((cols, width), 0) < limit, 1.0, 0.0).astype(FL)


def own_kernel(
    dims, scal_ref, copies_ref, own_ref, wl_ref, a_ref, gate_ref, h0_ref, side_ref, fac_ref
):
    rows, cols, width, heads, size = dims
    limit, core = scal_ref[0], scal_ref[3]
    mask = pair_mask(dims, limit)(scal_ref[1])
    h0 = copies_ref[0]
    h0_ref[...] = h0
    side, _, gate = own_sides(h0, wl_ref, mask)
    a_ref[...] = side.astype(BF).astype(FL)
    gate_ref[...] = gate
    col_mask = col_mask_of(dims, limit)
    w_b = jnp.concatenate([wl_ref[2], wl_ref[3]], axis=1)
    for idx in range(size // 2):
        side_ref[idx], fac_ref[idx] = b_block(
            dims, own_ref[idx], w_b, col_mask, (2 * idx + core) * rows, limit
        )


def triangle_kernel(
    dims,
    scal_ref,
    own_ref,
    other_ref,
    a_ref,
    gate_ref,
    own_side_ref,
    own_fac_ref,
    pair_hbm,
    norms_hbm,
    wl_ref,
    pbt_hbm,
    tb_ref,
    own_side_hbm,
    own_fac_hbm,
    other_side_hbm,
    other_fac_hbm,
    own_hbm,
    other_hbm,
    x_ref,
    z1_ref,
    h1_ref,
    pair_ref,
    norms_ref,
    pbt_ref,
    other_side_ref,
    other_fac_ref,
    part_ref,
    sems,
):
    rows, cols, width, heads, size = dims
    pairs, chips = rows * cols, size // 2
    limit, core = scal_ref[0], scal_ref[3]
    moves = fetch(
        [
            (norms_hbm, norms_ref),
            (pair_hbm, pair_ref),
            (pbt_hbm, pbt_ref),
            (own_side_ref, own_side_hbm),
            (own_fac_ref, own_fac_hbm),
            (own_ref, own_hbm),
            (other_ref, other_hbm),
        ],
        sems.at[pl.ds(0, 7)],
    )
    early_moves, moves = moves[:3], moves[3:]
    col_mask = col_mask_of(dims, limit)
    w_b = jnp.concatenate([wl_ref[2], wl_ref[3]], axis=1)
    a_rows = [a_ref[idx * cols : (idx + 1) * cols, :] for idx in range(rows)]

    def products(block, side):
        for row in range(rows):
            b_j = side[row * cols : (row + 1) * cols].astype(FL)
            for idx in range(rows):
                fold = jnp.sum((a_rows[idx] * b_j).reshape(cols // 8, 8, width), axis=0)
                at = pl.multiple_of((idx * cols + block * rows + row) * 8, 8)
                part_ref[pl.ds(at, 8), :] = fold

    for idx in range(chips):
        block = 2 * idx + 1 - core
        side, fac = b_block(dims, other_ref[idx], w_b, col_mask, block * rows, limit)
        other_side_ref[idx] = side
        other_fac_ref[idx] = fac
        products(block, side)
        products(2 * idx + core, own_side_ref[idx])
        if idx == chips // 2 - 1 or idx == chips - 1:
            late = idx == chips - 1
            span = pl.ds(chips // 2, chips - chips // 2) if late else pl.ds(0, chips // 2)
            moves += fetch(
                [
                    (other_side_ref.at[span], other_side_hbm.at[span]),
                    (other_fac_ref.at[span], other_fac_hbm.at[span]),
                ],
                sems.at[pl.ds(9 if late else 7, 2)],
            )
    x_val = part_ref[pl.ds(0, pairs, stride=8), :]
    for idx in range(1, 8):
        x_val = x_val + part_ref[pl.ds(idx, pairs, stride=8), :]

    x_ref[...] = x_val
    for move in early_moves:
        move.wait()
    y_low, _, _ = row_norm(x_val, norms_ref[2:3], norms_ref[3:4])
    z1 = pair_ref[...] + gate_ref[...] * dot(y_low, wl_ref[5])
    z1_ref[...] = z1
    h1, _, _ = row_norm(z1, norms_ref[4:5], norms_ref[5:6])
    h1_ref[...] = h1
    tbt = dot(pbt_ref[...].astype(BF), h1, 1, 1).astype(BF).astype(FL)
    half = pairs // 2
    block = jnp.concatenate([tbt[:, :half], tbt[:, half:]], axis=0)
    for idx in range(size):
        tb_ref[idx] = block
    for move in moves:
        move.wait()


def diagonal_block(first, second):
    zero = jnp.zeros(first.shape, first.dtype)
    return jnp.concatenate(
        [
            jnp.concatenate([first, zero], axis=1),
            jnp.concatenate([zero, second], axis=1),
        ],
        axis=0,
    )


def pack_places(dims):
    rows, cols, width, heads, _ = dims
    pairs, lines = rows * cols, heads * cols
    at, places = 0, {}
    for name, tall in (
        ("prob", rows // 2 * lines),
        ("dscore", rows // 2 * lines),
        ("datt", pairs),
        ("u", pairs),
        ("dout2", pairs),
        ("dgate2", pairs),
        ("h2", pairs),
        ("dlog", 2 * cols),
    ):
        places[name] = at
        at += tall
    return places, at


def lane_ramp(width):
    return 1.0 + iota((1, width), 1).astype(FL) / width


def attention_kernel(
    dims,
    scal_ref,
    tb_ref,
    h1_ref,
    z1_ref,
    wl_ref,
    norms_hbm,
    pbt_hbm,
    headt_hbm,
    bins_hbm,
    dtb_ref,
    pack_ref,
    dz2_ref,
    stat_ref,
    kcat_ref,
    qblk_ref,
    norms_ref,
    pbt_ref,
    vcat_ref,
    bias_ref,
    prob_ref,
    swap_ref,
    headt_ref,
    bins_ref,
    sems,
):
    rows, cols, width, heads, size = dims
    pairs, lines = rows * cols, heads * cols
    places, _ = pack_places(dims)
    scale = (width // heads) ** (-0.5)
    limit, first_row = scal_ref[0], scal_ref[1]

    def put(name, val):
        pack_ref[places[name] : places[name] + val.shape[0], :] = val

    moves = fetch(
        [
            (headt_hbm, headt_ref),
            (bins_hbm, bins_ref),
            (norms_hbm, norms_ref),
            (pbt_hbm, pbt_ref),
        ],
        sems,
    )
    w_att = jnp.concatenate([wl_ref[6], wl_ref[7], wl_ref[8], wl_ref[9]], axis=1)
    proj = dot(h1_ref[...], w_att)
    gate2 = jax.nn.sigmoid(proj[:, 3 * width :])
    lane_head = iota((cols, width), 1) // (width // heads)
    zero = jnp.zeros((cols, width), BF)
    for idx in range(rows):
        at, side = idx // 2, idx % 2
        lanes = slice(side * width, (side + 1) * width)
        span = slice(idx * cols, (idx + 1) * cols)
        query = proj[span, :width].astype(BF)
        qblk_ref[at, side * cols : (side + 1) * cols, lanes] = query
        qblk_ref[at, (1 - side) * cols : (2 - side) * cols, lanes] = zero
        for head in range(heads):
            spot = slice(head * cols, (head + 1) * cols)
            keep = lane_head == head
            kcat_ref[at, spot, lanes] = jnp.where(
                keep, proj[span, width : 2 * width], 0.0
            ).astype(BF)
            vcat_ref[at, spot, lanes] = jnp.where(
                keep, proj[span, 2 * width : 3 * width], 0.0
            ).astype(BF)

    for half in range(2):
        for jl in range(2):
            lanes = slice(jl * cols, (jl + 1) * cols)
            got = [
                tb_ref[pl.ds(half * heads + head, size, stride=2 * heads), :][:, lanes]
                for head in range(heads)
            ]
            for duo in range(heads // 2):
                line = jnp.concatenate([got[2 * duo], got[2 * duo + 1]], axis=1)
                bias_ref[duo, pl.ds(2 * half + jl, size, stride=rows), :] = line
                bias_ref[duo, pl.ds(cols + 2 * half + jl, size, stride=rows), :] = line
    bias = jnp.concatenate([bias_ref[duo].T for duo in range(heads // 2)], axis=0)
    key_ok = iota((lines, 2 * cols), 0) % cols < limit
    att = []
    for at in range(rows // 2):
        score = dot(kcat_ref[at], qblk_ref[at], 1, 1) * scale + bias
        score = jnp.where(key_ok, score, -1000000000.0).reshape(heads, cols, 2 * cols)
        top = jnp.max(score, axis=1, keepdims=True)
        grown = jnp.exp(score - top)
        prob = (grown / jnp.sum(grown, axis=1, keepdims=True)).reshape(lines, 2 * cols)
        prob_ref[at] = prob
        low = prob.astype(BF)
        pack_ref[places["prob"] + at * lines : places["prob"] + (at + 1) * lines, :] = low
        both = dot(low, vcat_ref[at], 0, 0)
        att += [both[:cols, :width], both[cols:, width:]]
    att = jnp.concatenate(att, axis=0)
    u_low = (gate2 * att).astype(BF)
    put("u", u_low)
    z2 = z1_ref[...] + dot(u_low, wl_ref[10])
    for move in moves:
        move.wait()
    h2, unit6, rstd6 = row_norm(z2, norms_ref[6:7], norms_ref[7:8])
    put("h2", h2)
    headt = headt_ref[...].astype(BF)
    logits = dot(headt, h2, 1, 1)
    spot = iota((1, pairs), 1)
    ok = jnp.logical_and(spot % cols < limit, spot // cols + first_row < limit)
    mask = jnp.where(ok, 1.0, 0.0).astype(FL)
    bins = jnp.concatenate([bins_ref[idx : idx + 1, :] for idx in range(rows)], axis=1)
    onehot = jnp.where(iota(logits.shape, 0) == bins, 1.0, 0.0).astype(FL)
    top = jnp.max(logits, axis=0, keepdims=True)
    lse = top + jnp.log(jnp.sum(jnp.exp(logits - top), axis=0, keepdims=True))
    pick = jnp.sum(logits * onehot, axis=0, keepdims=True)
    loss = jnp.sum(mask * (lse - pick), axis=1, keepdims=True)
    dlog = (mask * (jnp.exp(logits - lse) - onehot)).astype(BF)
    put("dlog", jnp.concatenate([dlog[:, :width], dlog[:, width:]], axis=0))
    dz2, dg6, ds6 = row_norm_back(dot(dlog, headt, 0, 0), unit6, rstd6, norms_ref[6:7])
    dz2_ref[...] = dz2
    stat_ref[0:1, :] = dg6
    stat_ref[1:2, :] = ds6
    used = limit * limit
    ramp = lane_ramp(width)
    stat_ref[2:3, :] = loss * ramp
    stat_ref[3:4, :] = (used // DIGIT).astype(FL) * ramp
    stat_ref[4:5, :] = (used % DIGIT).astype(FL) * ramp
    stat_ref[5:8, :] = jnp.zeros((3, width), FL)
    dout2 = dz2.astype(BF)
    put("dout2", dout2)
    du = dot(dout2, wl_ref[10], 1, 1)
    put("dgate2", (du * att * gate2 * (1.0 - gate2)).astype(BF))
    datt = (du * gate2).astype(BF)
    put("datt", datt)
    total = None
    for at in range(rows // 2):
        first = datt[(2 * at) * cols : (2 * at + 1) * cols]
        second = datt[(2 * at + 1) * cols : (2 * at + 2) * cols]
        block = diagonal_block(first, second)
        dprob = dot(vcat_ref[at], block, 1, 1)
        prob = prob_ref[at]
        inner = jnp.sum((dprob * prob).reshape(heads, cols, 2 * cols), axis=1, keepdims=True)
        dscore = prob.reshape(heads, cols, 2 * cols) * (
            dprob.reshape(heads, cols, 2 * cols) - inner
        )
        low = dscore.reshape(lines, 2 * cols).astype(BF)
        pack_ref[places["dscore"] + at * lines : places["dscore"] + (at + 1) * lines, :] = low
        total = low.astype(FL) if total is None else total + low.astype(FL)
    for duo in range(heads // 2):
        turned = total[duo * 2 * cols : (duo + 1) * 2 * cols].T
        swap_ref[duo] = turned[:cols] + turned[cols:]
    for half in range(2):
        for head in range(heads):
            inside = slice((head % 2) * cols, (head % 2 + 1) * cols)
            line = jnp.concatenate(
                [
                    swap_ref[head // 2, pl.ds(2 * half + jl, size, stride=rows), :][:, inside]
                    for jl in range(2)
                ],
                axis=1,
            )
            dtb_ref[pl.ds(half * heads + head, size, stride=2 * heads), :] = line


def attention_grad_kernel(
    dims,
    scal_ref,
    kcat_ref,
    qblk_ref,
    pack_ref,
    h1_ref,
    h0_ref,
    x_ref,
    norms_ref,
    wl_ref,
    early_ref,
    loc_ref,
    dqkvg_ref,
):
    rows, cols, width, heads, size = dims
    pairs, lines = rows * cols, heads * cols
    places, _ = pack_places(dims)

    def take(name, tall, skip=0):
        return pack_ref[places[name] + skip : places[name] + skip + tall, :]

    mask = pair_mask(dims, scal_ref[0])(scal_ref[1])
    side, fac, gate = own_sides(h0_ref[...], wl_ref, mask)
    y_low, _, _ = row_norm(x_ref[...], norms_ref[2:3], norms_ref[3:4])
    loc_ref[0] = side.astype(BF).astype(FL)
    loc_ref[1] = fac
    loc_ref[2] = gate
    loc_ref[3] = dot(y_low, wl_ref[5])
    scale = (width // heads) ** (-0.5)
    lane_head = iota((cols, width), 1) // (width // heads)

    def diagonal(val):
        out = jnp.zeros((cols, width), FL)
        for head in range(heads):
            out = jnp.where(lane_head == head, val[head * cols : (head + 1) * cols], out)
        return out

    for at in range(rows // 2):
        dscore = take("dscore", lines, at * lines)
        block = diagonal_block(
            take("datt", cols, 2 * at * cols), take("datt", cols, (2 * at + 1) * cols)
        )
        dquery = dot(dscore, kcat_ref[at], 0, 0)
        dkeys = dot(dscore, qblk_ref[at])
        dvals = dot(take("prob", lines, at * lines), block)
        for side in range(2):
            idx = 2 * at + side
            lanes = slice(side * width, (side + 1) * width)
            span = slice(idx * cols, (idx + 1) * cols)
            dqkvg_ref[span, :width] = (
                dquery[side * cols : (side + 1) * cols, lanes] * scale
            ).astype(BF)
            dqkvg_ref[span, width : 2 * width] = (diagonal(dkeys[:, lanes]) * scale).astype(BF)
            dqkvg_ref[span, 2 * width : 3 * width] = diagonal(dvals[:, lanes]).astype(BF)
    dqkvg_ref[:, 3 * width :] = take("dgate2", pairs)
    dqkvg = dqkvg_ref[...]
    w_att = jnp.concatenate([wl_ref[6], wl_ref[7], wl_ref[8], wl_ref[9]], axis=1)
    loc_ref[4] = dot(dqkvg, w_att, 1, 1)
    dw_att = dot(h1_ref[...], dqkvg, 0, 0)
    for idx in range(4):
        early_ref[idx * width : (idx + 1) * width, :] = dw_att[:, idx * width : (idx + 1) * width]
    early_ref[4 * width : 5 * width, :] = dot(take("u", pairs), take("dout2", pairs), 0, 0)
    dlog = take("dlog", 2 * cols)
    dlog = jnp.concatenate([dlog[:cols], dlog[cols:]], axis=1)
    early_ref[5 * width :, :] = dot(dlog, take("h2", pairs))


def triangle_grad_kernel(
    dims,
    scal_ref,
    dtb_ref,
    early_ref,
    dz2_ref,
    stat_ref,
    h1_ref,
    x_ref,
    z1_ref,
    loc_ref,
    own_side_hbm,
    own_fac_hbm,
    other_side_hbm,
    other_fac_hbm,
    own_hbm,
    other_hbm,
    norms_ref,
    wl_ref,
    pbt_ref,
    keep_ref,
    give_ref,
    flat_ref,
    dx_ref,
    own_side_ref,
    own_fac_ref,
    other_side_ref,
    other_fac_ref,
    own_ref,
    other_ref,
    sems,
):
    rows, cols, width, heads, size = dims
    pairs = rows * cols
    chip, core = scal_ref[2], scal_ref[3]
    moves = fetch(
        [
            (own_side_hbm, own_side_ref),
            (other_side_hbm, other_side_ref),
            (own_hbm, own_ref),
            (other_hbm, other_ref),
            (own_fac_hbm, own_fac_ref),
            (other_fac_hbm, other_fac_ref),
        ],
        sems,
    )
    y_low, unit2, rstd2 = row_norm(x_ref[...], norms_ref[2:3], norms_ref[3:4])
    _, unit4, rstd4 = row_norm(z1_ref[...], norms_ref[4:5], norms_ref[5:6])
    got = dtb_ref[0]
    for idx in range(1, size):
        got = got + dtb_ref[idx]
    dtbt = jnp.concatenate([got[:heads], got[heads:]], axis=1).astype(BF)
    h1 = h1_ref[...]
    dpbt = dot(dtbt, h1)
    dh1 = loc_ref[4] + dot(dtbt, pbt_ref[...].astype(BF), 0, 0)
    dn4, dg4, ds4 = row_norm_back(dh1, unit4, rstd4, norms_ref[4:5])
    dz1 = dz2_ref[...] + dn4
    gate = loc_ref[2]
    dout1 = (dz1 * gate).astype(BF)
    dgate = dz1 * loc_ref[3] * gate * (1.0 - gate)
    dx, dg2, ds2 = row_norm_back(dot(dout1, wl_ref[5], 1, 1), unit2, rstd2, norms_ref[2:3])
    dx_ref[...] = dx.astype(BF).astype(FL)

    moves[0].wait()
    moves[1].wait()

    def da_step(idx, acc):
        for side_ref, half in ((own_side_ref, core), (other_side_ref, 1 - core)):
            for row in range(rows):
                j = (2 * idx + half) * rows + row
                b_j = side_ref[idx, row * cols : (row + 1) * cols, :].astype(FL)
                acc = tuple(
                    acc[at] + dx_ref[pl.ds(at * cols + j, 1), :] * b_j for at in range(rows)
                )
        return acc

    acc = lax.fori_loop(
        0, size // 2, da_step, tuple(jnp.zeros((cols, width), FL) for _ in range(rows))
    )
    da = jnp.concatenate(acc, axis=0).astype(BF).astype(FL)
    own = jnp.concatenate(
        [
            (da * loc_ref[1]).astype(BF),
            (da * loc_ref[0] * (1.0 - loc_ref[1])).astype(BF),
            dgate.astype(BF),
        ],
        axis=1,
    )
    for move in moves[2:]:
        move.wait()
    ones = jnp.ones((16, pairs), BF)

    def products(h0, grads):
        return dot(h0, grads, 0, 0), dot(ones, grads)

    dw_own, sum_own = products(own_ref[chip], own)

    a_rows = [loc_ref[0, idx * cols : (idx + 1) * cols, :] for idx in range(rows)]

    def db_step(idx, acc):
        for src, side_ref, fac_ref, half in (
            (own_ref, own_side_ref, own_fac_ref, core),
            (other_ref, other_side_ref, other_fac_ref, 1 - core),
        ):
            lines = []
            for row in range(rows):
                j = (2 * idx + half) * rows + row
                db = dx_ref[pl.ds(j, 1), :] * a_rows[0]
                for own_row in range(1, rows):
                    db = db + dx_ref[pl.ds(own_row * cols + j, 1), :] * a_rows[own_row]
                lines.append(db.astype(BF))
            db = jnp.concatenate(lines, axis=0)
            fac = fac_ref[idx]
            grads = jnp.concatenate([db * fac, db * (side_ref[idx] * (1.0 - fac))], axis=1)
            main, sums = products(src[idx], grads)
            acc = (acc[0] + main, acc[1] + sums)
        return acc

    dw_b = (jnp.zeros((width, 2 * width), FL), jnp.zeros((16, 2 * width), FL))
    for idx in range(size // 2):
        dw_b = db_step(idx, dw_b)
    dw_b, sum_b = dw_b

    parts = [
        (val[:, at * width : (at + 1) * width], sums[:1, at * width : (at + 1) * width])
        for val, sums, at in (
            (dw_own, sum_own, 0),
            (dw_own, sum_own, 1),
            (dw_b, sum_b, 0),
            (dw_b, sum_b, 1),
            (dw_own, sum_own, 2),
        )
    ]
    mixed = jnp.zeros((width, width), FL)
    summed = jnp.zeros((width, width), FL)
    for idx, (part, sums) in enumerate(parts):
        weight = wl_ref[idx].astype(FL)
        flat_ref[idx * width : (idx + 1) * width, :] = part
        mixed = mixed + weight * part
        summed = summed + weight * sums
    ds0 = lane_sums(summed)
    dg0 = (lane_sums(mixed) - norms_ref[1:2] * ds0) / norms_ref[0:1]
    flat_ref[5 * width : 6 * width, :] = dot(y_low, dout1, 0, 0)
    mats = 11 * width
    flat_ref[6 * width : mats, :] = early_ref[: 5 * width, :]
    bins_n = early_ref.shape[0] - 5 * width
    flat_ref[mats : mats + bins_n, :] = early_ref[5 * width :, :]
    base = mats + bins_n
    flat_ref[base : base + heads, :] = dpbt
    flat_ref[base + heads : base + 8, :] = jnp.zeros((8 - heads, width), FL)
    base += 8
    for idx, line in enumerate((dg0, ds0, dg2, ds2, dg4, ds4)):
        flat_ref[base + idx : base + idx + 1, :] = line
    flat_ref[base + 6 : base + 11, :] = stat_ref[0:5, :]
    total = flat_ref.shape[0]
    flat_ref[base + 11 :, :] = jnp.zeros((total - base - 11, width), FL)
    half = total // 2
    keep_ref[...] = flat_ref[pl.ds(pl.multiple_of(core * half, half), half), :]
    give_ref[...] = flat_ref[pl.ds(pl.multiple_of((1 - core) * half, half), half), :]


def update_kernel(
    dims,
    scal_ref,
    mine_ref,
    other_ref,
    mats_ref,
    mats_m_ref,
    mats_v_ref,
    pb_ref,
    pb_m_ref,
    pb_v_ref,
    head_ref,
    head_m_ref,
    head_v_ref,
    norms_ref,
    norms_m_ref,
    norms_v_ref,
    norm_out,
    loss_out,
    count_out,
    mats_m_out,
    mats_v_out,
    mats_out,
    mats_low_out,
    pb_m_out,
    pb_v_out,
    pb_out,
    head_m_out,
    head_v_out,
    head_out,
    norms_m_out,
    norms_v_out,
    norms_out,
    flat_ref,
    scalar_buf,
    small_buf,
    pb_buf,
    m_buf,
    v_buf,
    w_buf,
    low_buf,
    sems,
    small_sems,
):
    rows, cols, width, heads, size = dims
    core = scal_ref[3]
    half = mine_ref.shape[0]
    flat_ref[pl.ds(pl.multiple_of(core * half, half), half), :] = mine_ref[...]
    flat_ref[pl.ds(pl.multiple_of((1 - core) * half, half), half), :] = other_ref[...]
    count = mats_ref.shape[0]
    mats = count * width
    bins_n = head_ref.shape[0]
    base = mats + bins_n
    grads = flat_ref[: base + 16, :]
    square = jnp.sum(grads * grads, axis=0, keepdims=True)
    norm = jnp.sqrt(jnp.sum(square, axis=1, keepdims=True))
    factor = jnp.minimum(1.0, CLIP / norm)
    scalar_buf[0] = norm
    stats = jnp.mean(
        flat_ref[base + 16 : base + 24, :] / lane_ramp(width), axis=1, keepdims=True
    )
    scalar_buf[1] = stats[0:1]
    scalar_buf[2] = (DIGIT * jnp.round(stats[1:2]) + jnp.round(stats[2:3])) / size

    moves = []

    def send(at, idx, buf, out):
        move = pltpu.make_async_copy(buf.at[idx], out.at[idx], sems.at[at, idx])
        move.start()
        moves.append(move)

    def step(weight, grad, first, second):
        return adam(weight, grad * factor, first, second)

    triples = []
    for at, tall, buf, skip, ins, outs in (
        (mats, bins_n, small_buf, 0, (head_ref, head_m_ref, head_v_ref), (head_m_out, head_v_out, head_out)),
        (base + 8, 8, small_buf, bins_n, (norms_ref, norms_m_ref, norms_v_ref), (norms_m_out, norms_v_out, norms_out)),
        (base, heads, pb_buf, 0, (pb_ref, pb_m_ref, pb_v_ref), (pb_m_out, pb_v_out, pb_out)),
    ):
        now = step(ins[0][...], flat_ref[at : at + tall, :], ins[1][...], ins[2][...])
        for idx, (val, out) in enumerate(zip(now, outs)):
            buf[idx, skip : skip + tall, :] = val
            triples.append((buf.at[idx, pl.ds(skip, tall)], out))
    triples += [
        (scalar_buf.at[idx], out) for idx, out in enumerate((norm_out, loss_out, count_out))
    ]
    moves += fetch(triples, small_sems)
    for idx in range(count):
        m_buf[idx], v_buf[idx], weight = step(
            mats_ref[idx],
            flat_ref[idx * width : (idx + 1) * width, :],
            mats_m_ref[idx],
            mats_v_ref[idx],
        )
        w_buf[idx] = weight
        low_buf[idx] = weight.astype(BF)
        send(0, idx, m_buf, mats_m_out)
        send(1, idx, v_buf, mats_v_out)
        send(2, idx, w_buf, mats_out)
        send(3, idx, low_buf, mats_low_out)
    for move in moves:
        move.wait()


def call(kernel, args, outs, scratch=(), limit=VMEM_LIMIT, flops=10**7):
    spots = {"s": pltpu.SMEM, "v": pltpu.VMEM, "h": pltpu.HBM}
    return pl.pallas_call(
        kernel,
        out_shape=[
            pltpu.HBM(shape, kind) if spot == "h" else jax.ShapeDtypeStruct(shape, kind)
            for shape, kind, spot in outs
        ],
        in_specs=[pl.BlockSpec(memory_space=spots[spot]) for _, spot in args],
        out_specs=[pl.BlockSpec(memory_space=spots[spot]) for _, _, spot in outs],
        scratch_shapes=list(scratch),
        compiler_params=pltpu.CompilerParams(vmem_limit_bytes=limit),
        cost_estimate=pl.CostEstimate(flops=flops, bytes_accessed=10**6, transcendentals=0),
    )(
        *(
            pltpu.with_memory_space_constraint(value, pltpu.HBM) if spot == "h" else value
            for value, spot in args
        )
    )


def shrink(val):
    root = jnp.sqrt(jnp.abs(val) * SPAN)
    return jnp.where(val < 0.0, -root, root).astype(jnp.float16)


def grow(root):
    root = root.astype(FL)
    return root * jnp.abs(root) * (1.0 / SPAN)


def same_core_groups(crops, size):
    return [
        [crop * size + idx for crop in range(crops) for idx in range(core, size, 2)]
        for core in range(2)
    ]


def core_swap(value, size):
    return lax.ppermute(value, "row", [(idx, idx ^ 1) for idx in range(size)])


def fast_step(
    crops,
    size,
    pair,
    bins,
    lengths,
    mats,
    mats_m,
    mats_v,
    pbias,
    pbias_m,
    pbias_v,
    head,
    head_m,
    head_v,
    norms,
    norms_m,
    norms_v,
):
    rows, cols, width = pair.shape[1:]
    heads, bins_n = pbias.shape[1], head.shape[1]
    pairs, lines = rows * cols, heads * cols
    dims = (rows, cols, width, heads, size)
    chips = size // 2
    place = lax.axis_index("row")
    scal = jnp.stack([lengths[0], place * rows, place // 2, place % 2]).astype(jnp.int32)
    start = pair.reshape(pairs, width)
    pbt, headt = pbias.T, head.T

    copies, wl = call(
        functools.partial(start_kernel, chips),
        [(start, "h"), (norms, "h"), (mats, "h")],
        [((chips, pairs, width), BF, "v"), (mats.shape, BF, "v")],
        [
            pltpu.VMEM((pairs, width), FL),
            pltpu.VMEM(norms.shape, FL),
            pltpu.VMEM(mats.shape, FL),
            pltpu.SemaphoreType.DMA((3,)),
        ],
    )
    near = [list(range(core, size, 2)) for core in range(2)]
    own = lax.all_to_all(copies, "row", 0, 0, axis_index_groups=near, tiled=True)
    other = core_swap(own, size)
    a_val, gate, h0, own_side, own_fac = call(
        functools.partial(own_kernel, dims),
        [(scal, "s"), (copies, "v"), (own, "v"), (wl, "v")],
        [
            ((pairs, width), FL, "v"),
            ((pairs, width), FL, "v"),
            ((pairs, width), BF, "v"),
            (own.shape, BF, "v"),
            (own.shape, BF, "v"),
        ],
    )
    tb, own_side, own_fac, other_side, other_fac, own_far, other_far, x_val, z1, h1 = call(
        functools.partial(triangle_kernel, dims),
        [
            (scal, "s"),
            (own, "v"),
            (other, "v"),
            (a_val, "v"),
            (gate, "v"),
            (own_side, "v"),
            (own_fac, "v"),
            (start, "h"),
            (norms, "h"),
            (wl, "v"),
            (pbt, "h"),
        ],
        [((size, 2 * heads, 2 * cols), FL, "v")]
        + [(own.shape, BF, "h")] * 6
        + [((pairs, width), FL, "v"), ((pairs, width), FL, "v"), ((pairs, width), BF, "v")],
        [
            pltpu.VMEM((pairs, width), FL),
            pltpu.VMEM(norms.shape, FL),
            pltpu.VMEM(pbt.shape, FL),
            pltpu.VMEM(own.shape, BF),
            pltpu.VMEM(own.shape, BF),
            pltpu.VMEM((pairs * 8, width), FL),
            pltpu.SemaphoreType.DMA((11,)),
        ],
    )

    tb_all = lax.all_to_all(tb, "row", 0, 0, tiled=True)
    bias_shape = (size * 2 * heads, 2 * cols)
    dtb, pack, dz2, stat, kcat, qblk, norms_here, pbt_here = call(
        functools.partial(attention_kernel, dims),
        [
            (scal, "s"),
            (tb_all.reshape(bias_shape), "v"),
            (h1, "v"),
            (z1, "v"),
            (wl, "v"),
            (norms, "h"),
            (pbt, "h"),
            (headt, "h"),
            (bins[0], "h"),
        ],
        [
            (bias_shape, FL, "v"),
            ((pack_places(dims)[1], width), BF, "v"),
            ((pairs, width), FL, "v"),
            ((8, width), FL, "v"),
            ((rows // 2, lines, 2 * width), BF, "v"),
            ((rows // 2, 2 * cols, 2 * width), BF, "v"),
            (norms.shape, FL, "v"),
            (pbt.shape, FL, "v"),
        ],
        [
            pltpu.VMEM((rows // 2, lines, 2 * width), BF),
            pltpu.VMEM((heads // 2, 2 * cols, 2 * cols), FL),
            pltpu.VMEM((rows // 2, lines, 2 * cols), FL),
            pltpu.VMEM((heads // 2, cols, 2 * cols), FL),
            pltpu.VMEM((bins_n, width), FL),
            pltpu.VMEM((rows, cols), jnp.int32),
            pltpu.SemaphoreType.DMA((4,)),
        ],
    )

    dtb_all = lax.all_to_all(dtb.reshape(size, 2 * heads, 2 * cols), "row", 0, 0, tiled=True)
    early, loc = call(
        functools.partial(attention_grad_kernel, dims),
        [(scal, "s")]
        + [
            (value, "v")
            for value in (
                kcat,
                qblk,
                pack,
                h1,
                h0,
                x_val,
                norms_here,
                wl,
            )
        ],
        [((5 * width + bins_n, width), FL, "v"), ((5, pairs, width), FL, "v")],
        [pltpu.VMEM((pairs, 4 * width), BF)],
    )
    used = mats.shape[0] * width + bins_n + 24
    unit = 8 * crops * size
    total = -(-used // unit) * unit
    keep, give = call(
        functools.partial(triangle_grad_kernel, dims),
        [(scal, "s")]
        + [(value, "v") for value in (dtb_all, early, dz2, stat, h1, x_val, z1, loc)]
        + [(value, "h") for value in (own_side, own_fac, other_side, other_fac, own_far, other_far)]
        + [(value, "v") for value in (norms_here, wl, pbt_here)],
        [((total // 2, width), FL, "v"), ((total // 2, width), FL, "v")],
        [
            pltpu.VMEM((total, width), FL),
            pltpu.VMEM((pairs, width), FL),
        ]
        + [pltpu.VMEM(own.shape, BF)] * 6
        + [
            pltpu.SemaphoreType.DMA((6,)),
        ],
    )

    half = keep + core_swap(give, size)
    count = crops * chips
    groups = same_core_groups(crops, size)
    axes = ("crop", "row")
    parts = lax.all_to_all(
        shrink(half).reshape(count, -1, width), axes, 0, 0, axis_index_groups=groups, tiled=True
    )
    share = shrink(jnp.sum(grow(parts), axis=0))
    spread = jnp.broadcast_to(share[None], (count,) + share.shape)
    mine = lax.all_to_all(spread, axes, 0, 0, axis_index_groups=groups, tiled=True)
    mine = mine.reshape(total // 2, width)
    other_half = grow(core_swap(mine, size))
    mine = grow(mine)

    number = mats.shape[0]
    big, low = ((number, width, width), FL, "h"), ((number, width, width), BF, "h")
    pb_out, head_out = ((heads, width), FL, "h"), ((bins_n, width), FL, "h")
    norm_out = ((norms.shape[0], width), FL, "h")
    res = call(
        functools.partial(update_kernel, dims),
        [(scal, "s"), (mine, "v"), (other_half, "v"), (mats, "v")]
        + [
            (value, "v")
            for value in (
                mats_m,
                mats_v,
                pbt_here,
                pbias_m.T,
                pbias_v.T,
                headt,
                head_m.T,
                head_v.T,
                norms_here,
                norms_m,
                norms_v,
            )
        ],
        [((1, 1), FL, "h")] * 3
        + [big, big, big, low]
        + [pb_out] * 3
        + [head_out] * 3
        + [norm_out] * 3,
        [
            pltpu.VMEM((total, width), FL),
            pltpu.VMEM((3, 1, 1), FL),
            pltpu.VMEM((3, bins_n + norms.shape[0], width), FL),
            pltpu.VMEM((3, heads, width), FL),
        ]
        + [pltpu.VMEM((number, width, width), FL)] * 3
        + [
            pltpu.VMEM((number, width, width), BF),
            pltpu.SemaphoreType.DMA((4, number)),
            pltpu.SemaphoreType.DMA((12,)),
        ],
    )
    return (
        *(value.reshape(()) for value in res[:3]),
        *res[3:7],
        *(value.T for value in res[7:13]),
        *res[13:16],
    )


def small_enough(pair, heads, size):
    _, rows, cols, width = pair.shape
    held = 4 * size * rows * cols * width * 4 + 4 * rows * heads * cols * cols * 4
    return (
        held <= 2**24
        and width == 2 * cols
        and rows == 4
        and heads == 4
        and size % 2 == 0
        and rows * size == cols
    )


def solution(mesh):
    crops, size = mesh.shape["crop"], mesh.shape["row"]

    def on_device(*args):
        if small_enough(args[0], args[6].shape[1], size):
            return fast_step(crops, size, *args)
        return general_step(*args)

    in_specs = (
        P("crop", "row", None, None),
        P("crop", "row", None),
        P("crop"),
        P(),
        P(),
        P(),
        P(),
        P(),
        P(),
        P(),
        P(),
        P(),
        P(),
        P(),
        P(),
    )
    out_specs = (P(), P(), P(), P(), P(), P(), P(), P(), P(), P(), P(), P(), P(), P(), P(), P())
    return jax.shard_map(
        on_device, mesh=mesh, in_specs=in_specs, out_specs=out_specs, check_vma=False
    )
```

```python
import functools

import jax
import jax.numpy as jnp
from jax import lax
from jax.experimental import pallas as pl
from jax.experimental.pallas import tpu as pltpu
from jax.sharding import PartitionSpec as P

STEP = 5


EPS_NORM = 1e-05
CLIP = 1.0
RATE = 0.05
BETA1 = 0.9
BETA2 = 0.95
ADAM_EPS = 1e-08
WDECAY = 0.01


def norm_fwd(v, gain, shift):
    mean = jnp.mean(v, axis=-1, keepdims=True)
    cent = v - mean
    rstd = lax.rsqrt(jnp.mean(cent * cent, axis=-1, keepdims=True) + EPS_NORM)
    unit = cent * rstd
    return (unit * gain + shift, unit, rstd)


def norm_back(grad, unit, rstd, gain):
    dgain = jnp.sum(grad * unit, axis=(0, 1))
    dshift = jnp.sum(grad, axis=(0, 1))
    dunit = grad * gain
    dval = rstd * (
        dunit
        - jnp.mean(dunit, axis=-1, keepdims=True)
        - unit * jnp.mean(dunit * unit, axis=-1, keepdims=True)
    )
    return (dval, dgain, dshift)


def matmul(value, weight):
    flat = value.reshape(-1, value.shape[-1])
    out = jnp.dot(flat, weight, preferred_element_type=jnp.float32)
    return out.reshape(value.shape[:-1] + (weight.shape[1],))


def wgrad(value, grad):
    return jnp.einsum("ijc,ijd->cd", value, grad, preferred_element_type=jnp.float32)


def adam(weight, grad, first, second):
    first_new = BETA1 * first + (1.0 - BETA1) * grad
    second_new = BETA2 * second + (1.0 - BETA2) * grad * grad
    m_hat = first_new / (1.0 - BETA1**STEP)
    v_hat = second_new / (1.0 - BETA2**STEP)
    weight_new = weight - RATE * (m_hat / (jnp.sqrt(v_hat) + ADAM_EPS) + WDECAY * weight)
    return (first_new, second_new, weight_new)


def general_step(
    pair,
    bins,
    lengths,
    mats,
    mats_m,
    mats_v,
    pbias,
    pbias_m,
    pbias_v,
    head,
    head_m,
    head_v,
    norms,
    norms_m,
    norms_v,
):
    bf = jnp.bfloat16
    fl = jnp.float32
    width = mats.shape[1]
    rows = pair.shape[1]
    cols = pair.shape[2]
    heads = pbias.shape[1]
    size_head = width // heads
    scale = size_head ** (-0.5)
    start_pair = pair[0]
    first_row = lax.axis_index("row") * rows
    limit = lengths[0]
    row_ok = first_row + jnp.arange(rows) < limit
    col_ok = jnp.arange(cols) < limit
    pmask = (row_ok[:, None] & col_ok[None, :]).astype(fl)
    m3 = pmask[..., None]
    wl = mats.astype(bf)
    pl = pbias.astype(bf)
    hl = head.astype(bf)
    w_tri = jnp.concatenate([wl[0], wl[1], wl[2], wl[3], wl[4]], axis=1)
    w_att = jnp.concatenate([wl[6], wl[7], wl[8], wl[9]], axis=1)
    h0, unit0, rstd0 = norm_fwd(start_pair, norms[0], norms[1])
    h0b = h0.astype(bf)
    proj = matmul(h0b, w_tri)
    sig_a = jax.nn.sigmoid(proj[..., width : 2 * width])
    sig_b = jax.nn.sigmoid(proj[..., 3 * width : 4 * width])
    gate = jax.nn.sigmoid(proj[..., 4 * width :])
    a_low = (sig_a * proj[..., :width] * m3).astype(bf)
    b_low = (sig_b * proj[..., 2 * width : 3 * width] * m3).astype(bf)
    b_all = lax.all_gather(b_low, "row", axis=0, tiled=True)
    prod = jnp.einsum("ikc,jkc->ijc", a_low, b_all, preferred_element_type=fl)
    y_val, unit2, rstd2 = norm_fwd(prod, norms[2], norms[3])
    y_low = y_val.astype(bf)
    out1 = matmul(y_low, wl[5])
    z1 = start_pair + gate * out1
    h1, unit4, rstd4 = norm_fwd(z1, norms[4], norms[5])
    h1b = h1.astype(bf)
    qkvg = matmul(h1b, w_att)
    query = qkvg[..., :width].astype(bf).reshape(rows, cols, heads, size_head)
    keys = qkvg[..., width : 2 * width].astype(bf).reshape(rows, cols, heads, size_head)
    values = qkvg[..., 2 * width : 3 * width].astype(bf).reshape(rows, cols, heads, size_head)
    gate2 = jax.nn.sigmoid(qkvg[..., 3 * width :])
    tb_low = matmul(h1b, pl).astype(bf)
    tb_all = lax.all_gather(tb_low, "row", axis=0, tiled=True)
    tb_heads = jnp.transpose(tb_all, (2, 0, 1)).astype(fl)
    scores = (
        jnp.einsum("ijhd,ikhd->ihjk", query, keys, preferred_element_type=fl) * scale
        + tb_heads[None]
    )
    scores = jnp.where(col_ok[None, None, None, :], scores, -1000000000.0)
    probs = jax.nn.softmax(scores, axis=-1)
    p_low = probs.astype(bf)
    att = jnp.einsum("ihjk,ikhd->ijhd", p_low, values, preferred_element_type=fl).reshape(
        rows, cols, width
    )
    u_low = (gate2 * att).astype(bf)
    z2 = z1 + matmul(u_low, wl[10])
    h2, unit6, rstd6 = norm_fwd(z2, norms[6], norms[7])
    h2b = h2.astype(bf)
    logits = matmul(h2b, hl)
    lse = jax.nn.logsumexp(logits, axis=-1)
    onehot = (bins[0][..., None] == jnp.arange(logits.shape[-1])).astype(fl)
    pick = jnp.sum(logits * onehot, axis=-1)
    loss = jnp.sum(pmask * (lse - pick))
    count = jnp.sum(pmask)
    dlog = (m3 * (jnp.exp(logits - lse[..., None]) - onehot)).astype(bf)
    dhead = wgrad(h2b, dlog)
    dz2, dg6, ds6 = norm_back(matmul(dlog, hl.T), unit6, rstd6, norms[6])
    dout2 = dz2.astype(bf)
    dw10 = wgrad(u_low, dout2)
    du = matmul(dout2, wl[10].T)
    dgate2 = du * att
    datt = (du * gate2).astype(bf).reshape(rows, cols, heads, size_head)
    dprob = jnp.einsum("ijhd,ikhd->ihjk", datt, values, preferred_element_type=fl)
    dvals = jnp.einsum("ihjk,ijhd->ikhd", p_low, datt, preferred_element_type=fl)
    dscore = (probs * (dprob - jnp.sum(dprob * probs, axis=-1, keepdims=True))).astype(bf)
    dquery = jnp.einsum("ihjk,ikhd->ijhd", dscore, keys, preferred_element_type=fl) * scale
    dkeys = jnp.einsum("ihjk,ijhd->ikhd", dscore, query, preferred_element_type=fl) * scale
    dtb = jnp.sum(dscore.astype(fl), axis=0)
    dtb_own = lax.psum_scatter(dtb, "row", scatter_dimension=1, tiled=True)
    dtb_low = jnp.transpose(dtb_own, (1, 2, 0)).astype(bf)
    dpbias = wgrad(h1b, dtb_low)
    dqkvg = jnp.concatenate(
        [
            dquery.reshape(rows, cols, width),
            dkeys.reshape(rows, cols, width),
            dvals.reshape(rows, cols, width),
            dgate2 * gate2 * (1.0 - gate2),
        ],
        axis=-1,
    ).astype(bf)
    dw_att = wgrad(h1b, dqkvg)
    dh1 = matmul(dqkvg, w_att.T) + matmul(dtb_low, pl.T)
    dn4, dg4, ds4 = norm_back(dh1, unit4, rstd4, norms[4])
    dz1 = dz2 + dn4
    dout1 = (dz1 * gate).astype(bf)
    dw5 = wgrad(y_low, dout1)
    dgate = dz1 * out1
    dxn, dg2, ds2 = norm_back(matmul(dout1, wl[5].T), unit2, rstd2, norms[2])
    dx_low = dxn.astype(bf)
    dside_a = jnp.einsum("ijc,jkc->ikc", dx_low, b_all, preferred_element_type=fl)
    dside_b = lax.psum_scatter(
        jnp.einsum("ijc,ikc->jkc", dx_low, a_low, preferred_element_type=fl),
        "row",
        scatter_dimension=0,
        tiled=True,
    )
    da_r = dside_a.astype(bf).astype(fl)
    db_r = dside_b.astype(bf).astype(fl)
    dproj = jnp.concatenate(
        [
            da_r * sig_a * m3,
            da_r * proj[..., :width] * m3 * sig_a * (1.0 - sig_a),
            db_r * sig_b * m3,
            db_r * proj[..., 2 * width : 3 * width] * m3 * sig_b * (1.0 - sig_b),
            dgate * gate * (1.0 - gate),
        ],
        axis=-1,
    ).astype(bf)
    dw_tri = wgrad(h0b, dproj)
    dh0 = matmul(dproj, w_tri.T)
    unused, dg0, ds0 = norm_back(dh0, unit0, rstd0, norms[0])
    pieces = [dw_tri[:, idx * width : (idx + 1) * width] for idx in range(5)]
    pieces = (
        pieces + [dw5] + [dw_att[:, idx * width : (idx + 1) * width] for idx in range(4)] + [dw10]
    )
    dmats = jnp.stack(pieces)
    dnorms = jnp.stack([dg0, ds0, dg2, ds2, dg4, ds4, dg6, ds6])
    dmats, dpbias, dhead, dnorms, loss, count = lax.psum(
        (dmats, dpbias, dhead, dnorms, loss, count), ("crop", "row")
    )
    grad_norm = jnp.sqrt(
        jnp.sum(dmats * dmats)
        + jnp.sum(dpbias * dpbias)
        + jnp.sum(dhead * dhead)
        + jnp.sum(dnorms * dnorms)
    )
    factor = jnp.minimum(1.0, CLIP / grad_norm)
    new_mats = adam(mats, dmats * factor, mats_m, mats_v)
    new_pbias = adam(pbias, dpbias * factor, pbias_m, pbias_v)
    new_head = adam(head, dhead * factor, head_m, head_v)
    new_norms = adam(norms, dnorms * factor, norms_m, norms_v)
    return (
        grad_norm,
        loss,
        count,
        new_mats[0],
        new_mats[1],
        new_mats[2],
        new_mats[2].astype(bf),
        new_pbias[0],
        new_pbias[1],
        new_pbias[2],
        new_head[0],
        new_head[1],
        new_head[2],
        new_norms[0],
        new_norms[1],
        new_norms[2],
    )


BF = jnp.bfloat16
FL = jnp.float32
VMEM_LIMIT = 24 * 2**20
SPAN = 2.0**-12
DIGIT = 64


def dot(lhs, rhs, left=1, right=0):
    return lax.dot_general(
        lhs, rhs, (((left,), (right,)), ((), ())), preferred_element_type=FL
    )


def lane_sums(val):
    return jnp.sum(val.T, axis=0, keepdims=True)


def row_norm(val, gain, shift):
    mean = jnp.mean(val, axis=-1, keepdims=True)
    cent = val - mean
    rstd = lax.rsqrt(jnp.mean(cent * cent, axis=-1, keepdims=True) + EPS_NORM)
    unit = cent * rstd
    return (unit * gain + shift).astype(BF), unit, rstd


def row_norm_back(grad, unit, rstd, gain):
    dgain = jnp.sum(grad * unit, axis=0, keepdims=True)
    dshift = jnp.sum(grad, axis=0, keepdims=True)
    dunit = grad * gain
    dval = rstd * (
        dunit
        - jnp.mean(dunit, axis=-1, keepdims=True)
        - unit * jnp.mean(dunit * unit, axis=-1, keepdims=True)
    )
    return dval, dgain, dshift


def iota(shape, dim):
    return lax.broadcasted_iota(jnp.int32, shape, dim)


def fetch(pairs, sems):
    moves = [
        pltpu.make_async_copy(src, dst, sems.at[idx]) for idx, (src, dst) in enumerate(pairs)
    ]
    for move in moves:
        move.start()
    return moves


def start_kernel(
    copies, pair_hbm, norms_hbm, mats_hbm, out_ref, wl_ref, pair_ref, norms_ref, mats_ref, sems
):
    moves = fetch(
        [(pair_hbm, pair_ref), (norms_hbm, norms_ref), (mats_hbm, mats_ref)], sems
    )
    moves[0].wait()
    moves[1].wait()
    h0, _, _ = row_norm(pair_ref[...], norms_ref[0:1], norms_ref[1:2])
    for idx in range(copies):
        out_ref[idx] = h0
    moves[2].wait()
    wl_ref[...] = mats_ref[...].astype(BF)


def pair_mask(dims, limit):
    rows, cols, width, _, _ = dims
    spot = iota((rows * cols, width), 0)
    col_ok = spot % cols < limit
    row_in = spot // cols

    def mask_of(block_row):
        return jnp.where(jnp.logical_and(col_ok, row_in + block_row < limit), 1.0, 0.0).astype(FL)

    return mask_of


def own_sides(h0, wl_ref, mask):
    width = h0.shape[1]
    w_own = jnp.concatenate([wl_ref[0], wl_ref[1], wl_ref[4]], axis=1)
    proj = dot(h0, w_own)
    fac = jax.nn.sigmoid(proj[:, width : 2 * width]) * mask
    return fac * proj[:, :width], fac, jax.nn.sigmoid(proj[:, 2 * width :])


def b_block(dims, h0, w_b, col_mask, start, limit):
    rows, cols, width, _, _ = dims
    proj = dot(h0, w_b)
    sig = jax.nn.sigmoid(proj[:, width:])
    lines = []
    for row in range(rows):
        row_ok = jnp.where(start + row < limit, 1.0, 0.0).astype(FL)
        lines.append(sig[row * cols : (row + 1) * cols] * (col_mask * row_ok))
    fac = jnp.concatenate(lines, axis=0)
    return (fac * proj[:, :width]).astype(BF), fac.astype(BF)


def col_mask_of(dims, limit):
    _, cols, width, _, _ = dims
    return jnp.where(iota((cols, width), 0) < limit, 1.0, 0.0).astype(FL)


def own_kernel(
    dims, scal_ref, copies_ref, own_ref, wl_ref, a_ref, gate_ref, side_ref, fac_ref
):
    rows, cols, width, heads, size = dims
    limit, core = scal_ref[0], scal_ref[3]
    mask = pair_mask(dims, limit)(scal_ref[1])
    side, _, gate = own_sides(copies_ref[0], wl_ref, mask)
    a_ref[...] = side.astype(BF).astype(FL)
    gate_ref[...] = gate
    col_mask = col_mask_of(dims, limit)
    w_b = jnp.concatenate([wl_ref[2], wl_ref[3]], axis=1)
    for idx in range(size // 2):
        side_ref[idx], fac_ref[idx] = b_block(
            dims, own_ref[idx], w_b, col_mask, (2 * idx + core) * rows, limit
        )


def triangle_kernel(
    dims,
    scal_ref,
    own_ref,
    other_ref,
    a_ref,
    gate_ref,
    own_side_ref,
    own_fac_ref,
    pair_hbm,
    norms_hbm,
    wl_ref,
    pbt_hbm,
    tb_ref,
    own_side_hbm,
    own_fac_hbm,
    other_side_hbm,
    other_fac_hbm,
    x_ref,
    z1_ref,
    h1_ref,
    pair_ref,
    norms_ref,
    pbt_ref,
    other_side_ref,
    other_fac_ref,
    part_ref,
    sems,
):
    rows, cols, width, heads, size = dims
    pairs, chips = rows * cols, size // 2
    limit, core = scal_ref[0], scal_ref[3]
    moves = fetch(
        [
            (norms_hbm, norms_ref),
            (pair_hbm, pair_ref),
            (pbt_hbm, pbt_ref),
            (own_side_ref, own_side_hbm),
            (own_fac_ref, own_fac_hbm),
        ],
        sems.at[pl.ds(0, 5)],
    )
    early_moves, moves = moves[:3], moves[3:]
    col_mask = col_mask_of(dims, limit)
    w_b = jnp.concatenate([wl_ref[2], wl_ref[3]], axis=1)
    a_rows = [a_ref[idx * cols : (idx + 1) * cols, :] for idx in range(rows)]

    def products(block, side):
        for row in range(rows):
            b_j = side[row * cols : (row + 1) * cols].astype(FL)
            for idx in range(rows):
                fold = jnp.sum((a_rows[idx] * b_j).reshape(cols // 8, 8, width), axis=0)
                at = pl.multiple_of((idx * cols + block * rows + row) * 8, 8)
                part_ref[pl.ds(at, 8), :] = fold

    for idx in range(chips):
        block = 2 * idx + 1 - core
        side, fac = b_block(dims, other_ref[idx], w_b, col_mask, block * rows, limit)
        other_side_ref[idx] = side
        other_fac_ref[idx] = fac
        products(block, side)
        products(2 * idx + core, own_side_ref[idx])
        if idx == chips // 2 - 1 or idx == chips - 1:
            late = idx == chips - 1
            span = pl.ds(chips // 2, chips - chips // 2) if late else pl.ds(0, chips // 2)
            moves += fetch(
                [
                    (other_side_ref.at[span], other_side_hbm.at[span]),
                    (other_fac_ref.at[span], other_fac_hbm.at[span]),
                ],
                sems.at[pl.ds(7 if late else 5, 2)],
            )
    x_val = part_ref[pl.ds(0, pairs, stride=8), :]
    for idx in range(1, 8):
        x_val = x_val + part_ref[pl.ds(idx, pairs, stride=8), :]

    x_ref[...] = x_val
    for move in early_moves:
        move.wait()
    y_low, _, _ = row_norm(x_val, norms_ref[2:3], norms_ref[3:4])
    z1 = pair_ref[...] + gate_ref[...] * dot(y_low, wl_ref[5])
    z1_ref[...] = z1
    h1, _, _ = row_norm(z1, norms_ref[4:5], norms_ref[5:6])
    h1_ref[...] = h1
    tbt = dot(pbt_ref[...].astype(BF), h1, 1, 1).astype(BF).astype(FL)
    half = pairs // 2
    block = jnp.concatenate([tbt[:, :half], tbt[:, half:]], axis=0)
    for idx in range(size):
        tb_ref[idx] = block
    for move in moves:
        move.wait()


def diagonal_block(first, second):
    zero = jnp.zeros(first.shape, first.dtype)
    return jnp.concatenate(
        [
            jnp.concatenate([first, zero], axis=1),
            jnp.concatenate([zero, second], axis=1),
        ],
        axis=0,
    )


def pack_places(dims):
    rows, cols, width, heads, _ = dims
    pairs, lines = rows * cols, heads * cols
    at, places = 0, {}
    for name, tall in (
        ("prob", rows // 2 * lines),
        ("dscore", rows // 2 * lines),
        ("datt", pairs),
        ("u", pairs),
        ("dout2", pairs),
        ("dgate2", pairs),
        ("h2", pairs),
        ("dlog", 2 * cols),
    ):
        places[name] = at
        at += tall
    return places, at


def lane_ramp(width):
    return 1.0 + iota((1, width), 1).astype(FL) / width


def norm_line(small_ref, idx):
    at = small_ref.shape[1] - 8 + idx
    return small_ref[0, at : at + 1, :]


def attention_kernel(
    dims,
    scal_ref,
    tb_ref,
    h1_ref,
    z1_ref,
    wl_ref,
    bins_hbm,
    pb_hbm,
    pb_m_hbm,
    pb_v_hbm,
    head_hbm,
    head_m_hbm,
    head_v_hbm,
    norms_hbm,
    norms_m_hbm,
    norms_v_hbm,
    dtb_ref,
    pack_ref,
    dz2_ref,
    stat_ref,
    kcat_ref,
    qblk_ref,
    pb_ref,
    small_ref,
    vcat_ref,
    bias_ref,
    prob_ref,
    swap_ref,
    bins_ref,
    sems,
):
    rows, cols, width, heads, size = dims
    pairs, lines = rows * cols, heads * cols
    places, _ = pack_places(dims)
    scale = (width // heads) ** (-0.5)
    limit, first_row = scal_ref[0], scal_ref[1]

    def put(name, val):
        pack_ref[places[name] : places[name] + val.shape[0], :] = val

    bins_n = head_hbm.shape[0]
    moves = [(bins_hbm, bins_ref)]
    for idx, (pb, head, norms) in enumerate(
        (
            (pb_hbm, head_hbm, norms_hbm),
            (pb_m_hbm, head_m_hbm, norms_m_hbm),
            (pb_v_hbm, head_v_hbm, norms_v_hbm),
        )
    ):
        moves += [
            (head, small_ref.at[idx, pl.ds(0, bins_n)]),
            (norms, small_ref.at[idx, pl.ds(bins_n, 8)]),
            (pb, pb_ref.at[idx]),
        ]
    moves = fetch(moves, sems)
    w_att = jnp.concatenate([wl_ref[6], wl_ref[7], wl_ref[8], wl_ref[9]], axis=1)
    proj = dot(h1_ref[...], w_att)
    gate2 = jax.nn.sigmoid(proj[:, 3 * width :])
    lane_head = iota((cols, width), 1) // (width // heads)
    zero = jnp.zeros((cols, width), BF)
    for idx in range(rows):
        at, side = idx // 2, idx % 2
        lanes = slice(side * width, (side + 1) * width)
        span = slice(idx * cols, (idx + 1) * cols)
        query = proj[span, :width].astype(BF)
        qblk_ref[at, side * cols : (side + 1) * cols, lanes] = query
        qblk_ref[at, (1 - side) * cols : (2 - side) * cols, lanes] = zero
        for head in range(heads):
            spot = slice(head * cols, (head + 1) * cols)
            keep = lane_head == head
            kcat_ref[at, spot, lanes] = jnp.where(
                keep, proj[span, width : 2 * width], 0.0
            ).astype(BF)
            vcat_ref[at, spot, lanes] = jnp.where(
                keep, proj[span, 2 * width : 3 * width], 0.0
            ).astype(BF)

    for half in range(2):
        for jl in range(2):
            lanes = slice(jl * cols, (jl + 1) * cols)
            got = [
                tb_ref[pl.ds(half * heads + head, size, stride=2 * heads), :][:, lanes]
                for head in range(heads)
            ]
            for duo in range(heads // 2):
                line = jnp.concatenate([got[2 * duo], got[2 * duo + 1]], axis=1)
                bias_ref[duo, pl.ds(2 * half + jl, size, stride=rows), :] = line
                bias_ref[duo, pl.ds(cols + 2 * half + jl, size, stride=rows), :] = line
    bias = jnp.concatenate([bias_ref[duo].T for duo in range(heads // 2)], axis=0)
    key_ok = iota((lines, 2 * cols), 0) % cols < limit
    att = []
    for at in range(rows // 2):
        score = dot(kcat_ref[at], qblk_ref[at], 1, 1) * scale + bias
        score = jnp.where(key_ok, score, -1000000000.0).reshape(heads, cols, 2 * cols)
        top = jnp.max(score, axis=1, keepdims=True)
        grown = jnp.exp(score - top)
        prob = (grown / jnp.sum(grown, axis=1, keepdims=True)).reshape(lines, 2 * cols)
        prob_ref[at] = prob
        low = prob.astype(BF)
        pack_ref[places["prob"] + at * lines : places["prob"] + (at + 1) * lines, :] = low
        both = dot(low, vcat_ref[at], 0, 0)
        att += [both[:cols, :width], both[cols:, width:]]
    att = jnp.concatenate(att, axis=0)
    u_low = (gate2 * att).astype(BF)
    put("u", u_low)
    z2 = z1_ref[...] + dot(u_low, wl_ref[10])
    for move in moves[:3]:
        move.wait()
    h2, unit6, rstd6 = row_norm(z2, norm_line(small_ref, 6), norm_line(small_ref, 7))
    put("h2", h2)
    headt = small_ref[0, :bins_n, :].astype(BF)
    logits = dot(headt, h2, 1, 1)
    spot = iota((1, pairs), 1)
    ok = jnp.logical_and(spot % cols < limit, spot // cols + first_row < limit)
    mask = jnp.where(ok, 1.0, 0.0).astype(FL)
    bins = jnp.concatenate([bins_ref[idx : idx + 1, :] for idx in range(rows)], axis=1)
    onehot = jnp.where(iota(logits.shape, 0) == bins, 1.0, 0.0).astype(FL)
    top = jnp.max(logits, axis=0, keepdims=True)
    lse = top + jnp.log(jnp.sum(jnp.exp(logits - top), axis=0, keepdims=True))
    pick = jnp.sum(logits * onehot, axis=0, keepdims=True)
    loss = jnp.sum(mask * (lse - pick), axis=1, keepdims=True)
    dlog = (mask * (jnp.exp(logits - lse) - onehot)).astype(BF)
    put("dlog", jnp.concatenate([dlog[:, :width], dlog[:, width:]], axis=0))
    dz2, dg6, ds6 = row_norm_back(dot(dlog, headt, 0, 0), unit6, rstd6, norm_line(small_ref, 6))
    dz2_ref[...] = dz2
    stat_ref[0:1, :] = dg6
    stat_ref[1:2, :] = ds6
    used = limit * limit
    ramp = lane_ramp(width)
    stat_ref[2:3, :] = loss * ramp
    stat_ref[3:4, :] = (used // DIGIT).astype(FL) * ramp
    stat_ref[4:5, :] = (used % DIGIT).astype(FL) * ramp
    stat_ref[5:8, :] = jnp.zeros((3, width), FL)
    dout2 = dz2.astype(BF)
    put("dout2", dout2)
    du = dot(dout2, wl_ref[10], 1, 1)
    put("dgate2", (du * att * gate2 * (1.0 - gate2)).astype(BF))
    datt = (du * gate2).astype(BF)
    put("datt", datt)
    total = None
    for at in range(rows // 2):
        first = datt[(2 * at) * cols : (2 * at + 1) * cols]
        second = datt[(2 * at + 1) * cols : (2 * at + 2) * cols]
        block = diagonal_block(first, second)
        dprob = dot(vcat_ref[at], block, 1, 1)
        prob = prob_ref[at]
        inner = jnp.sum((dprob * prob).reshape(heads, cols, 2 * cols), axis=1, keepdims=True)
        dscore = prob.reshape(heads, cols, 2 * cols) * (
            dprob.reshape(heads, cols, 2 * cols) - inner
        )
        low = dscore.reshape(lines, 2 * cols).astype(BF)
        pack_ref[places["dscore"] + at * lines : places["dscore"] + (at + 1) * lines, :] = low
        total = low.astype(FL) if total is None else total + low.astype(FL)
    for duo in range(heads // 2):
        turned = total[duo * 2 * cols : (duo + 1) * 2 * cols].T
        swap_ref[duo] = turned[:cols] + turned[cols:]
    for half in range(2):
        for head in range(heads):
            inside = slice((head % 2) * cols, (head % 2 + 1) * cols)
            line = jnp.concatenate(
                [
                    swap_ref[head // 2, pl.ds(2 * half + jl, size, stride=rows), :][:, inside]
                    for jl in range(2)
                ],
                axis=1,
            )
            dtb_ref[pl.ds(half * heads + head, size, stride=2 * heads), :] = line
    for move in moves[3:]:
        move.wait()


def gradient_kernel(
    dims,
    scal_ref,
    dtb_ref,
    pack_ref,
    kcat_ref,
    qblk_ref,
    dz2_ref,
    stat_ref,
    h1_ref,
    x_ref,
    z1_ref,
    own_ref,
    other_ref,
    own_side_hbm,
    own_fac_hbm,
    other_side_hbm,
    other_fac_hbm,
    small_ref,
    wl_ref,
    pb_ref,
    keep_ref,
    give_ref,
    flat_ref,
    dx_ref,
    dqkvg_ref,
    own_side_ref,
    own_fac_ref,
    other_side_ref,
    other_fac_ref,
    sems,
):
    rows, cols, width, heads, size = dims
    pairs = rows * cols
    chip, core = scal_ref[2], scal_ref[3]
    moves = fetch(
        [
            (own_side_hbm, own_side_ref),
            (other_side_hbm, other_side_ref),
            (own_fac_hbm, own_fac_ref),
            (other_fac_hbm, other_fac_ref),
        ],
        sems,
    )
    lines = heads * cols
    places, _ = pack_places(dims)

    def take(name, tall, skip=0):
        return pack_ref[places[name] + skip : places[name] + skip + tall, :]

    mask = pair_mask(dims, scal_ref[0])(scal_ref[1])
    side, fac, gate = own_sides(own_ref[chip], wl_ref, mask)
    a_val = side.astype(BF).astype(FL)
    y_low, unit2, rstd2 = row_norm(x_ref[...], norm_line(small_ref, 2), norm_line(small_ref, 3))
    _, unit4, rstd4 = row_norm(z1_ref[...], norm_line(small_ref, 4), norm_line(small_ref, 5))
    out1 = dot(y_low, wl_ref[5])
    scale = (width // heads) ** (-0.5)
    lane_head = iota((cols, width), 1) // (width // heads)

    def diagonal(val):
        out = jnp.zeros((cols, width), FL)
        for head in range(heads):
            out = jnp.where(lane_head == head, val[head * cols : (head + 1) * cols], out)
        return out

    for at in range(rows // 2):
        dscore = take("dscore", lines, at * lines)
        block = diagonal_block(
            take("datt", cols, 2 * at * cols), take("datt", cols, (2 * at + 1) * cols)
        )
        dquery = dot(dscore, kcat_ref[at], 0, 0)
        dkeys = dot(dscore, qblk_ref[at])
        dvals = dot(take("prob", lines, at * lines), block)
        for side in range(2):
            idx = 2 * at + side
            lanes = slice(side * width, (side + 1) * width)
            span = slice(idx * cols, (idx + 1) * cols)
            dqkvg_ref[span, :width] = (
                dquery[side * cols : (side + 1) * cols, lanes] * scale
            ).astype(BF)
            dqkvg_ref[span, width : 2 * width] = (diagonal(dkeys[:, lanes]) * scale).astype(BF)
            dqkvg_ref[span, 2 * width : 3 * width] = diagonal(dvals[:, lanes]).astype(BF)
    dqkvg_ref[:, 3 * width :] = take("dgate2", pairs)
    dqkvg = dqkvg_ref[...]
    w_att = jnp.concatenate([wl_ref[6], wl_ref[7], wl_ref[8], wl_ref[9]], axis=1)
    dh1 = dot(dqkvg, w_att, 1, 1)
    h1 = h1_ref[...]
    dw_att = dot(h1, dqkvg, 0, 0)
    for idx in range(4):
        flat_ref[(6 + idx) * width : (7 + idx) * width, :] = dw_att[
            :, idx * width : (idx + 1) * width
        ]
    flat_ref[10 * width : 11 * width, :] = dot(take("u", pairs), take("dout2", pairs), 0, 0)
    mats = 11 * width
    dlog = take("dlog", 2 * cols)
    dlog = jnp.concatenate([dlog[:cols], dlog[cols:]], axis=1)
    flat_ref[mats : mats + dlog.shape[0], :] = dot(dlog, take("h2", pairs))
    got = dtb_ref[0]
    for idx in range(1, size):
        got = got + dtb_ref[idx]
    dtbt = jnp.concatenate([got[:heads], got[heads:]], axis=1).astype(BF)
    dpbt = dot(dtbt, h1)
    dh1 = dh1 + dot(dtbt, pb_ref[0].astype(BF), 0, 0)
    dn4, dg4, ds4 = row_norm_back(dh1, unit4, rstd4, norm_line(small_ref, 4))
    dz1 = dz2_ref[...] + dn4
    dout1 = (dz1 * gate).astype(BF)
    dgate = dz1 * out1 * gate * (1.0 - gate)
    dx, dg2, ds2 = row_norm_back(dot(dout1, wl_ref[5], 1, 1), unit2, rstd2, norm_line(small_ref, 2))
    dx_ref[...] = dx.astype(BF).astype(FL)

    moves[0].wait()
    moves[1].wait()

    def da_step(idx, acc):
        for side_ref, half in ((own_side_ref, core), (other_side_ref, 1 - core)):
            for row in range(rows):
                j = (2 * idx + half) * rows + row
                b_j = side_ref[idx, row * cols : (row + 1) * cols, :].astype(FL)
                acc = tuple(
                    acc[at] + dx_ref[pl.ds(at * cols + j, 1), :] * b_j for at in range(rows)
                )
        return acc

    acc = lax.fori_loop(
        0, size // 2, da_step, tuple(jnp.zeros((cols, width), FL) for _ in range(rows))
    )
    da = jnp.concatenate(acc, axis=0).astype(BF).astype(FL)
    own = jnp.concatenate(
        [
            (da * fac).astype(BF),
            (da * a_val * (1.0 - fac)).astype(BF),
            dgate.astype(BF),
        ],
        axis=1,
    )
    for move in moves[2:]:
        move.wait()
    ones = jnp.ones((16, pairs), BF)

    def products(h0, grads):
        return dot(h0, grads, 0, 0), dot(ones, grads)

    dw_own, sum_own = products(own_ref[chip], own)

    a_rows = [a_val[idx * cols : (idx + 1) * cols] for idx in range(rows)]

    def db_step(idx, acc):
        for src, side_ref, fac_ref, half in (
            (own_ref, own_side_ref, own_fac_ref, core),
            (other_ref, other_side_ref, other_fac_ref, 1 - core),
        ):
            lines = []
            for row in range(rows):
                j = (2 * idx + half) * rows + row
                db = dx_ref[pl.ds(j, 1), :] * a_rows[0]
                for own_row in range(1, rows):
                    db = db + dx_ref[pl.ds(own_row * cols + j, 1), :] * a_rows[own_row]
                lines.append(db.astype(BF))
            db = jnp.concatenate(lines, axis=0)
            fac_b = fac_ref[idx]
            grads = jnp.concatenate([db * fac_b, db * (side_ref[idx] * (1.0 - fac_b))], axis=1)
            main, sums = products(src[idx], grads)
            acc = (acc[0] + main, acc[1] + sums)
        return acc

    dw_b = (jnp.zeros((width, 2 * width), FL), jnp.zeros((16, 2 * width), FL))
    for idx in range(size // 2):
        dw_b = db_step(idx, dw_b)
    dw_b, sum_b = dw_b

    parts = [
        (val[:, at * width : (at + 1) * width], sums[:1, at * width : (at + 1) * width])
        for val, sums, at in (
            (dw_own, sum_own, 0),
            (dw_own, sum_own, 1),
            (dw_b, sum_b, 0),
            (dw_b, sum_b, 1),
            (dw_own, sum_own, 2),
        )
    ]
    mixed = jnp.zeros((width, width), FL)
    summed = jnp.zeros((width, width), FL)
    for idx, (part, sums) in enumerate(parts):
        weight = wl_ref[idx].astype(FL)
        flat_ref[idx * width : (idx + 1) * width, :] = part
        mixed = mixed + weight * part
        summed = summed + weight * sums
    ds0 = lane_sums(summed)
    dg0 = (lane_sums(mixed) - norm_line(small_ref, 1) * ds0) / norm_line(small_ref, 0)
    flat_ref[5 * width : 6 * width, :] = dot(y_low, dout1, 0, 0)
    base = mats + dlog.shape[0]
    flat_ref[base : base + heads, :] = dpbt
    flat_ref[base + heads : base + 8, :] = jnp.zeros((8 - heads, width), FL)
    base += 8
    for idx, line in enumerate((dg0, ds0, dg2, ds2, dg4, ds4)):
        flat_ref[base + idx : base + idx + 1, :] = line
    flat_ref[base + 6 : base + 11, :] = stat_ref[0:5, :]
    total = flat_ref.shape[0]
    flat_ref[base + 11 :, :] = jnp.zeros((total - base - 11, width), FL)
    half = total // 2
    keep_ref[...] = flat_ref[pl.ds(pl.multiple_of(core * half, half), half), :]
    give_ref[...] = flat_ref[pl.ds(pl.multiple_of((1 - core) * half, half), half), :]


def update_kernel(
    dims,
    scal_ref,
    mine_ref,
    other_ref,
    mats_ref,
    mats_m_ref,
    mats_v_ref,
    pb_ref,
    small_ref,
    norm_out,
    loss_out,
    count_out,
    mats_m_out,
    mats_v_out,
    mats_out,
    mats_low_out,
    pb_m_out,
    pb_v_out,
    pb_out,
    head_m_out,
    head_v_out,
    head_out,
    norms_m_out,
    norms_v_out,
    norms_out,
    flat_ref,
    scalar_buf,
    small_buf,
    pb_buf,
    m_buf,
    v_buf,
    w_buf,
    low_buf,
    sems,
    small_sems,
):
    rows, cols, width, heads, size = dims
    bins_n = small_ref.shape[1] - 8
    core = scal_ref[3]
    half = mine_ref.shape[0]
    flat_ref[pl.ds(pl.multiple_of(core * half, half), half), :] = mine_ref[...]
    flat_ref[pl.ds(pl.multiple_of((1 - core) * half, half), half), :] = other_ref[...]
    count = mats_ref.shape[0]
    mats = count * width
    base = mats + bins_n
    grads = flat_ref[: base + 16, :]
    square = jnp.sum(grads * grads, axis=0, keepdims=True)
    norm = jnp.sqrt(jnp.sum(square, axis=1, keepdims=True))
    factor = jnp.minimum(1.0, CLIP / norm)
    scalar_buf[0] = norm
    stats = jnp.mean(
        flat_ref[base + 16 : base + 24, :] / lane_ramp(width), axis=1, keepdims=True
    )
    scalar_buf[1] = stats[0:1]
    scalar_buf[2] = (DIGIT * jnp.round(stats[1:2]) + jnp.round(stats[2:3])) / size

    moves = []

    def send(at, idx, buf, out):
        move = pltpu.make_async_copy(buf.at[idx], out.at[idx], sems.at[at, idx])
        move.start()
        moves.append(move)

    def step(weight, grad, first, second):
        return adam(weight, grad * factor, first, second)

    def update_small():
        triples = []
        for at, tall, buf, ref, skip, outs in (
            (mats, bins_n, small_buf, small_ref, 0, (head_m_out, head_v_out, head_out)),
            (base + 8, 8, small_buf, small_ref, bins_n, (norms_m_out, norms_v_out, norms_out)),
            (base, heads, pb_buf, pb_ref, 0, (pb_m_out, pb_v_out, pb_out)),
        ):
            weight, first, second = (ref[idx, skip : skip + tall, :] for idx in range(3))
            now = step(weight, flat_ref[at : at + tall, :], first, second)
            for idx, (val, out) in enumerate(zip(now, outs)):
                buf[idx, skip : skip + tall, :] = val
                triples.append((buf.at[idx, pl.ds(skip, tall)], out))
        triples += [
            (scalar_buf.at[idx], out) for idx, out in enumerate((norm_out, loss_out, count_out))
        ]
        moves.extend(fetch(triples, small_sems))

    for idx in range(count):
        if idx == count // 2:
            update_small()
        m_buf[idx], v_buf[idx], weight = step(
            mats_ref[idx],
            flat_ref[idx * width : (idx + 1) * width, :],
            mats_m_ref[idx],
            mats_v_ref[idx],
        )
        w_buf[idx] = weight
        low_buf[idx] = weight.astype(BF)
        send(0, idx, m_buf, mats_m_out)
        send(1, idx, v_buf, mats_v_out)
        send(2, idx, w_buf, mats_out)
        send(3, idx, low_buf, mats_low_out)
    for move in moves:
        move.wait()


def call(kernel, args, outs, scratch=(), limit=VMEM_LIMIT, flops=10**7):
    spots = {"s": pltpu.SMEM, "v": pltpu.VMEM, "h": pltpu.HBM}
    return pl.pallas_call(
        kernel,
        out_shape=[
            pltpu.HBM(shape, kind) if spot == "h" else jax.ShapeDtypeStruct(shape, kind)
            for shape, kind, spot in outs
        ],
        in_specs=[pl.BlockSpec(memory_space=spots[spot]) for _, spot in args],
        out_specs=[pl.BlockSpec(memory_space=spots[spot]) for _, _, spot in outs],
        scratch_shapes=list(scratch),
        compiler_params=pltpu.CompilerParams(vmem_limit_bytes=limit),
        cost_estimate=pl.CostEstimate(flops=flops, bytes_accessed=10**6, transcendentals=0),
    )(
        *(
            pltpu.with_memory_space_constraint(value, pltpu.HBM) if spot == "h" else value
            for value, spot in args
        )
    )


def shrink(val):
    root = jnp.sqrt(jnp.abs(val) * SPAN)
    return jnp.where(val < 0.0, -root, root).astype(jnp.float16)


def grow(root):
    root = root.astype(FL)
    return root * jnp.abs(root) * (1.0 / SPAN)


def same_core_groups(crops, size):
    return [
        [crop * size + idx for crop in range(crops) for idx in range(core, size, 2)]
        for core in range(2)
    ]


def core_swap(value, size):
    return lax.ppermute(value, "row", [(idx, idx ^ 1) for idx in range(size)])


def fast_step(
    crops,
    size,
    pair,
    bins,
    lengths,
    mats,
    mats_m,
    mats_v,
    pbias,
    pbias_m,
    pbias_v,
    head,
    head_m,
    head_v,
    norms,
    norms_m,
    norms_v,
):
    rows, cols, width = pair.shape[1:]
    heads, bins_n = pbias.shape[1], head.shape[1]
    pairs, lines = rows * cols, heads * cols
    dims = (rows, cols, width, heads, size)
    chips = size // 2
    place = lax.axis_index("row")
    scal = jnp.stack([lengths[0], place * rows, place // 2, place % 2]).astype(jnp.int32)
    start = pair.reshape(pairs, width)
    pbt, headt = pbias.T, head.T

    copies, wl = call(
        functools.partial(start_kernel, chips),
        [(start, "h"), (norms, "h"), (mats, "h")],
        [((chips, pairs, width), BF, "v"), (mats.shape, BF, "v")],
        [
            pltpu.VMEM((pairs, width), FL),
            pltpu.VMEM(norms.shape, FL),
            pltpu.VMEM(mats.shape, FL),
            pltpu.SemaphoreType.DMA((3,)),
        ],
    )
    near = [list(range(core, size, 2)) for core in range(2)]
    own = lax.all_to_all(copies, "row", 0, 0, axis_index_groups=near, tiled=True)
    other = core_swap(own, size)
    a_val, gate, own_side, own_fac = call(
        functools.partial(own_kernel, dims),
        [(scal, "s"), (copies, "v"), (own, "v"), (wl, "v")],
        [
            ((pairs, width), FL, "v"),
            ((pairs, width), FL, "v"),
            (own.shape, BF, "v"),
            (own.shape, BF, "v"),
        ],
    )
    tb, own_side, own_fac, other_side, other_fac, x_val, z1, h1 = call(
        functools.partial(triangle_kernel, dims),
        [
            (scal, "s"),
            (own, "v"),
            (other, "v"),
            (a_val, "v"),
            (gate, "v"),
            (own_side, "v"),
            (own_fac, "v"),
            (start, "h"),
            (norms, "h"),
            (wl, "v"),
            (pbt, "h"),
        ],
        [((size, 2 * heads, 2 * cols), FL, "v")]
        + [(own.shape, BF, "h")] * 4
        + [((pairs, width), FL, "v"), ((pairs, width), FL, "v"), ((pairs, width), BF, "v")],
        [
            pltpu.VMEM((pairs, width), FL),
            pltpu.VMEM(norms.shape, FL),
            pltpu.VMEM(pbt.shape, FL),
            pltpu.VMEM(own.shape, BF),
            pltpu.VMEM(own.shape, BF),
            pltpu.VMEM((pairs * 8, width), FL),
            pltpu.SemaphoreType.DMA((9,)),
        ],
    )

    tb_all = lax.all_to_all(tb, "row", 0, 0, tiled=True)
    bias_shape = (size * 2 * heads, 2 * cols)
    small_args = (
        pbt,
        pbias_m.T,
        pbias_v.T,
        headt,
        head_m.T,
        head_v.T,
        norms,
        norms_m,
        norms_v,
    )
    dtb, pack, dz2, stat, kcat, qblk, pb_all, small_all = call(
        functools.partial(attention_kernel, dims),
        [
            (scal, "s"),
            (tb_all.reshape(bias_shape), "v"),
            (h1, "v"),
            (z1, "v"),
            (wl, "v"),
            (bins[0], "h"),
        ]
        + [(value, "h") for value in small_args],
        [
            (bias_shape, FL, "v"),
            ((pack_places(dims)[1], width), BF, "v"),
            ((pairs, width), FL, "v"),
            ((8, width), FL, "v"),
            ((rows // 2, lines, 2 * width), BF, "v"),
            ((rows // 2, 2 * cols, 2 * width), BF, "v"),
            ((3, heads, width), FL, "v"),
            ((3, bins_n + norms.shape[0], width), FL, "v"),
        ],
        [
            pltpu.VMEM((rows // 2, lines, 2 * width), BF),
            pltpu.VMEM((heads // 2, 2 * cols, 2 * cols), FL),
            pltpu.VMEM((rows // 2, lines, 2 * cols), FL),
            pltpu.VMEM((heads // 2, cols, 2 * cols), FL),
            pltpu.VMEM((rows, cols), jnp.int32),
            pltpu.SemaphoreType.DMA((10,)),
        ],
    )

    dtb_all = lax.all_to_all(dtb.reshape(size, 2 * heads, 2 * cols), "row", 0, 0, tiled=True)
    used = mats.shape[0] * width + bins_n + 24
    unit = 8 * crops * size
    total = -(-used // unit) * unit
    keep, give = call(
        functools.partial(gradient_kernel, dims),
        [(scal, "s")]
        + [
            (value, "v")
            for value in (dtb_all, pack, kcat, qblk, dz2, stat, h1, x_val, z1, own, other)
        ]
        + [(value, "h") for value in (own_side, own_fac, other_side, other_fac)]
        + [(value, "v") for value in (small_all, wl, pb_all)],
        [((total // 2, width), FL, "v"), ((total // 2, width), FL, "v")],
        [
            pltpu.VMEM((total, width), FL),
            pltpu.VMEM((pairs, width), FL),
            pltpu.VMEM((pairs, 4 * width), BF),
        ]
        + [pltpu.VMEM(own.shape, BF)] * 4
        + [
            pltpu.SemaphoreType.DMA((4,)),
        ],
    )

    half = keep + core_swap(give, size)
    count = crops * chips
    groups = same_core_groups(crops, size)
    axes = ("crop", "row")
    parts = lax.all_to_all(
        shrink(half).reshape(count, -1, width), axes, 0, 0, axis_index_groups=groups, tiled=True
    )
    share = shrink(jnp.sum(grow(parts), axis=0))
    spread = jnp.broadcast_to(share[None], (count,) + share.shape)
    mine = lax.all_to_all(spread, axes, 0, 0, axis_index_groups=groups, tiled=True)
    mine = mine.reshape(total // 2, width)
    other_half = grow(core_swap(mine, size))
    mine = grow(mine)

    number = mats.shape[0]
    big, low = ((number, width, width), FL, "h"), ((number, width, width), BF, "h")
    pb_out, head_out = ((heads, width), FL, "h"), ((bins_n, width), FL, "h")
    norm_out = ((norms.shape[0], width), FL, "h")
    res = call(
        functools.partial(update_kernel, dims),
        [(scal, "s")]
        + [
            (value, "v")
            for value in (mine, other_half, mats, mats_m, mats_v, pb_all, small_all)
        ],
        [((1, 1), FL, "h")] * 3
        + [big, big, big, low]
        + [pb_out] * 3
        + [head_out] * 3
        + [norm_out] * 3,
        [
            pltpu.VMEM((total, width), FL),
            pltpu.VMEM((3, 1, 1), FL),
            pltpu.VMEM((3, bins_n + norms.shape[0], width), FL),
            pltpu.VMEM((3, heads, width), FL),
        ]
        + [pltpu.VMEM((number, width, width), FL)] * 3
        + [
            pltpu.VMEM((number, width, width), BF),
            pltpu.SemaphoreType.DMA((4, number)),
            pltpu.SemaphoreType.DMA((12,)),
        ],
    )
    return (
        *(value.reshape(()) for value in res[:3]),
        *res[3:7],
        *(value.T for value in res[7:13]),
        *res[13:16],
    )


def small_enough(pair, heads, size):
    _, rows, cols, width = pair.shape
    held = 4 * size * rows * cols * width * 4 + 4 * rows * heads * cols * cols * 4
    return (
        held <= 2**24
        and width == 2 * cols
        and rows == 4
        and heads == 4
        and size % 2 == 0
        and rows * size == cols
    )


def solution(mesh):
    crops, size = mesh.shape["crop"], mesh.shape["row"]

    def on_device(*args):
        if small_enough(args[0], args[6].shape[1], size):
            return fast_step(crops, size, *args)
        return general_step(*args)

    in_specs = (
        P("crop", "row", None, None),
        P("crop", "row", None),
        P("crop"),
        P(),
        P(),
        P(),
        P(),
        P(),
        P(),
        P(),
        P(),
        P(),
        P(),
        P(),
        P(),
    )
    out_specs = (P(), P(), P(), P(), P(), P(), P(), P(), P(), P(), P(), P(), P(), P(), P(), P())
    return jax.shard_map(
        on_device, mesh=mesh, in_specs=in_specs, out_specs=out_specs, check_vma=False
    )
```

```python
import functools

import jax
import jax.numpy as jnp
from jax import lax
from jax.experimental import pallas as pl
from jax.experimental.pallas import tpu as pltpu
from jax.sharding import PartitionSpec as P

STEP = 5


EPS_NORM = 1e-05
CLIP = 1.0
RATE = 0.05
BETA1 = 0.9
BETA2 = 0.95
ADAM_EPS = 1e-08
WDECAY = 0.01


def norm_fwd(v, gain, shift):
    mean = jnp.mean(v, axis=-1, keepdims=True)
    cent = v - mean
    rstd = lax.rsqrt(jnp.mean(cent * cent, axis=-1, keepdims=True) + EPS_NORM)
    unit = cent * rstd
    return (unit * gain + shift, unit, rstd)


def norm_back(grad, unit, rstd, gain):
    dgain = jnp.sum(grad * unit, axis=(0, 1))
    dshift = jnp.sum(grad, axis=(0, 1))
    dunit = grad * gain
    dval = rstd * (
        dunit
        - jnp.mean(dunit, axis=-1, keepdims=True)
        - unit * jnp.mean(dunit * unit, axis=-1, keepdims=True)
    )
    return (dval, dgain, dshift)


def matmul(value, weight):
    flat = value.reshape(-1, value.shape[-1])
    out = jnp.dot(flat, weight, preferred_element_type=jnp.float32)
    return out.reshape(value.shape[:-1] + (weight.shape[1],))


def wgrad(value, grad):
    return jnp.einsum("ijc,ijd->cd", value, grad, preferred_element_type=jnp.float32)


def adam(weight, grad, first, second):
    first_new = BETA1 * first + (1.0 - BETA1) * grad
    second_new = BETA2 * second + (1.0 - BETA2) * grad * grad
    m_hat = first_new / (1.0 - BETA1**STEP)
    v_hat = second_new / (1.0 - BETA2**STEP)
    weight_new = weight - RATE * (m_hat / (jnp.sqrt(v_hat) + ADAM_EPS) + WDECAY * weight)
    return (first_new, second_new, weight_new)


def general_step(
    pair,
    bins,
    lengths,
    mats,
    mats_m,
    mats_v,
    pbias,
    pbias_m,
    pbias_v,
    head,
    head_m,
    head_v,
    norms,
    norms_m,
    norms_v,
):
    bf = jnp.bfloat16
    fl = jnp.float32
    width = mats.shape[1]
    rows = pair.shape[1]
    cols = pair.shape[2]
    heads = pbias.shape[1]
    size_head = width // heads
    scale = size_head ** (-0.5)
    start_pair = pair[0]
    first_row = lax.axis_index("row") * rows
    limit = lengths[0]
    row_ok = first_row + jnp.arange(rows) < limit
    col_ok = jnp.arange(cols) < limit
    pmask = (row_ok[:, None] & col_ok[None, :]).astype(fl)
    m3 = pmask[..., None]
    wl = mats.astype(bf)
    pl = pbias.astype(bf)
    hl = head.astype(bf)
    w_tri = jnp.concatenate([wl[0], wl[1], wl[2], wl[3], wl[4]], axis=1)
    w_att = jnp.concatenate([wl[6], wl[7], wl[8], wl[9]], axis=1)
    h0, unit0, rstd0 = norm_fwd(start_pair, norms[0], norms[1])
    h0b = h0.astype(bf)
    proj = matmul(h0b, w_tri)
    sig_a = jax.nn.sigmoid(proj[..., width : 2 * width])
    sig_b = jax.nn.sigmoid(proj[..., 3 * width : 4 * width])
    gate = jax.nn.sigmoid(proj[..., 4 * width :])
    a_low = (sig_a * proj[..., :width] * m3).astype(bf)
    b_low = (sig_b * proj[..., 2 * width : 3 * width] * m3).astype(bf)
    b_all = lax.all_gather(b_low, "row", axis=0, tiled=True)
    prod = jnp.einsum("ikc,jkc->ijc", a_low, b_all, preferred_element_type=fl)
    y_val, unit2, rstd2 = norm_fwd(prod, norms[2], norms[3])
    y_low = y_val.astype(bf)
    out1 = matmul(y_low, wl[5])
    z1 = start_pair + gate * out1
    h1, unit4, rstd4 = norm_fwd(z1, norms[4], norms[5])
    h1b = h1.astype(bf)
    qkvg = matmul(h1b, w_att)
    query = qkvg[..., :width].astype(bf).reshape(rows, cols, heads, size_head)
    keys = qkvg[..., width : 2 * width].astype(bf).reshape(rows, cols, heads, size_head)
    values = qkvg[..., 2 * width : 3 * width].astype(bf).reshape(rows, cols, heads, size_head)
    gate2 = jax.nn.sigmoid(qkvg[..., 3 * width :])
    tb_low = matmul(h1b, pl).astype(bf)
    tb_all = lax.all_gather(tb_low, "row", axis=0, tiled=True)
    tb_heads = jnp.transpose(tb_all, (2, 0, 1)).astype(fl)
    scores = (
        jnp.einsum("ijhd,ikhd->ihjk", query, keys, preferred_element_type=fl) * scale
        + tb_heads[None]
    )
    scores = jnp.where(col_ok[None, None, None, :], scores, -1000000000.0)
    probs = jax.nn.softmax(scores, axis=-1)
    p_low = probs.astype(bf)
    att = jnp.einsum("ihjk,ikhd->ijhd", p_low, values, preferred_element_type=fl).reshape(
        rows, cols, width
    )
    u_low = (gate2 * att).astype(bf)
    z2 = z1 + matmul(u_low, wl[10])
    h2, unit6, rstd6 = norm_fwd(z2, norms[6], norms[7])
    h2b = h2.astype(bf)
    logits = matmul(h2b, hl)
    lse = jax.nn.logsumexp(logits, axis=-1)
    onehot = (bins[0][..., None] == jnp.arange(logits.shape[-1])).astype(fl)
    pick = jnp.sum(logits * onehot, axis=-1)
    loss = jnp.sum(pmask * (lse - pick))
    count = jnp.sum(pmask)
    dlog = (m3 * (jnp.exp(logits - lse[..., None]) - onehot)).astype(bf)
    dhead = wgrad(h2b, dlog)
    dz2, dg6, ds6 = norm_back(matmul(dlog, hl.T), unit6, rstd6, norms[6])
    dout2 = dz2.astype(bf)
    dw10 = wgrad(u_low, dout2)
    du = matmul(dout2, wl[10].T)
    dgate2 = du * att
    datt = (du * gate2).astype(bf).reshape(rows, cols, heads, size_head)
    dprob = jnp.einsum("ijhd,ikhd->ihjk", datt, values, preferred_element_type=fl)
    dvals = jnp.einsum("ihjk,ijhd->ikhd", p_low, datt, preferred_element_type=fl)
    dscore = (probs * (dprob - jnp.sum(dprob * probs, axis=-1, keepdims=True))).astype(bf)
    dquery = jnp.einsum("ihjk,ikhd->ijhd", dscore, keys, preferred_element_type=fl) * scale
    dkeys = jnp.einsum("ihjk,ijhd->ikhd", dscore, query, preferred_element_type=fl) * scale
    dtb = jnp.sum(dscore.astype(fl), axis=0)
    dtb_own = lax.psum_scatter(dtb, "row", scatter_dimension=1, tiled=True)
    dtb_low = jnp.transpose(dtb_own, (1, 2, 0)).astype(bf)
    dpbias = wgrad(h1b, dtb_low)
    dqkvg = jnp.concatenate(
        [
            dquery.reshape(rows, cols, width),
            dkeys.reshape(rows, cols, width),
            dvals.reshape(rows, cols, width),
            dgate2 * gate2 * (1.0 - gate2),
        ],
        axis=-1,
    ).astype(bf)
    dw_att = wgrad(h1b, dqkvg)
    dh1 = matmul(dqkvg, w_att.T) + matmul(dtb_low, pl.T)
    dn4, dg4, ds4 = norm_back(dh1, unit4, rstd4, norms[4])
    dz1 = dz2 + dn4
    dout1 = (dz1 * gate).astype(bf)
    dw5 = wgrad(y_low, dout1)
    dgate = dz1 * out1
    dxn, dg2, ds2 = norm_back(matmul(dout1, wl[5].T), unit2, rstd2, norms[2])
    dx_low = dxn.astype(bf)
    dside_a = jnp.einsum("ijc,jkc->ikc", dx_low, b_all, preferred_element_type=fl)
    dside_b = lax.psum_scatter(
        jnp.einsum("ijc,ikc->jkc", dx_low, a_low, preferred_element_type=fl),
        "row",
        scatter_dimension=0,
        tiled=True,
    )
    da_r = dside_a.astype(bf).astype(fl)
    db_r = dside_b.astype(bf).astype(fl)
    dproj = jnp.concatenate(
        [
            da_r * sig_a * m3,
            da_r * proj[..., :width] * m3 * sig_a * (1.0 - sig_a),
            db_r * sig_b * m3,
            db_r * proj[..., 2 * width : 3 * width] * m3 * sig_b * (1.0 - sig_b),
            dgate * gate * (1.0 - gate),
        ],
        axis=-1,
    ).astype(bf)
    dw_tri = wgrad(h0b, dproj)
    dh0 = matmul(dproj, w_tri.T)
    unused, dg0, ds0 = norm_back(dh0, unit0, rstd0, norms[0])
    pieces = [dw_tri[:, idx * width : (idx + 1) * width] for idx in range(5)]
    pieces = (
        pieces + [dw5] + [dw_att[:, idx * width : (idx + 1) * width] for idx in range(4)] + [dw10]
    )
    dmats = jnp.stack(pieces)
    dnorms = jnp.stack([dg0, ds0, dg2, ds2, dg4, ds4, dg6, ds6])
    dmats, dpbias, dhead, dnorms, loss, count = lax.psum(
        (dmats, dpbias, dhead, dnorms, loss, count), ("crop", "row")
    )
    grad_norm = jnp.sqrt(
        jnp.sum(dmats * dmats)
        + jnp.sum(dpbias * dpbias)
        + jnp.sum(dhead * dhead)
        + jnp.sum(dnorms * dnorms)
    )
    factor = jnp.minimum(1.0, CLIP / grad_norm)
    new_mats = adam(mats, dmats * factor, mats_m, mats_v)
    new_pbias = adam(pbias, dpbias * factor, pbias_m, pbias_v)
    new_head = adam(head, dhead * factor, head_m, head_v)
    new_norms = adam(norms, dnorms * factor, norms_m, norms_v)
    return (
        grad_norm,
        loss,
        count,
        new_mats[0],
        new_mats[1],
        new_mats[2],
        new_mats[2].astype(bf),
        new_pbias[0],
        new_pbias[1],
        new_pbias[2],
        new_head[0],
        new_head[1],
        new_head[2],
        new_norms[0],
        new_norms[1],
        new_norms[2],
    )


BF = jnp.bfloat16
FL = jnp.float32
VMEM_LIMIT = 24 * 2**20
SPAN = 2.0**-12
DIGIT = 64


def dot(lhs, rhs, left=1, right=0):
    return lax.dot_general(
        lhs, rhs, (((left,), (right,)), ((), ())), preferred_element_type=FL
    )


def lane_sums(val):
    return jnp.sum(val.T, axis=0, keepdims=True)


def row_norm(val, gain, shift):
    mean = jnp.mean(val, axis=-1, keepdims=True)
    cent = val - mean
    rstd = lax.rsqrt(jnp.mean(cent * cent, axis=-1, keepdims=True) + EPS_NORM)
    unit = cent * rstd
    return (unit * gain + shift).astype(BF), unit, rstd


def row_norm_back(grad, unit, rstd, gain):
    dgain = jnp.sum(grad * unit, axis=0, keepdims=True)
    dshift = jnp.sum(grad, axis=0, keepdims=True)
    dunit = grad * gain
    dval = rstd * (
        dunit
        - jnp.mean(dunit, axis=-1, keepdims=True)
        - unit * jnp.mean(dunit * unit, axis=-1, keepdims=True)
    )
    return dval, dgain, dshift


def iota(shape, dim):
    return lax.broadcasted_iota(jnp.int32, shape, dim)


def fetch(pairs, sems):
    moves = [
        pltpu.make_async_copy(src, dst, sems.at[idx]) for idx, (src, dst) in enumerate(pairs)
    ]
    for move in moves:
        move.start()
    return moves


def start_kernel(
    copies, pair_hbm, norms_hbm, mats_hbm, out_ref, wl_ref, pair_ref, norms_ref, mats_ref, sems
):
    moves = fetch(
        [(pair_hbm, pair_ref), (norms_hbm, norms_ref), (mats_hbm, mats_ref)], sems
    )
    moves[0].wait()
    moves[1].wait()
    h0, _, _ = row_norm(pair_ref[...], norms_ref[0:1], norms_ref[1:2])
    for idx in range(copies):
        out_ref[idx] = h0
    moves[2].wait()
    wl_ref[...] = mats_ref[...].astype(BF)


def pair_mask(dims, limit):
    rows, cols, width, _, _ = dims
    spot = iota((rows * cols, width), 0)
    col_ok = spot % cols < limit
    row_in = spot // cols

    def mask_of(block_row):
        return jnp.where(jnp.logical_and(col_ok, row_in + block_row < limit), 1.0, 0.0).astype(FL)

    return mask_of


def own_sides(h0, wl_ref, mask):
    width = h0.shape[1]
    w_own = jnp.concatenate([wl_ref[0], wl_ref[1], wl_ref[4]], axis=1)
    proj = dot(h0, w_own)
    fac = jax.nn.sigmoid(proj[:, width : 2 * width]) * mask
    return fac * proj[:, :width], fac, jax.nn.sigmoid(proj[:, 2 * width :])


def b_block(dims, h0, w_b, col_mask, start, limit):
    rows, cols, width, _, _ = dims
    proj = dot(h0, w_b)
    sig = jax.nn.sigmoid(proj[:, width:])
    lines = []
    for row in range(rows):
        row_ok = jnp.where(start + row < limit, 1.0, 0.0).astype(FL)
        lines.append(sig[row * cols : (row + 1) * cols] * (col_mask * row_ok))
    fac = jnp.concatenate(lines, axis=0)
    return (fac * proj[:, :width]).astype(BF), fac.astype(BF)


def col_mask_of(dims, limit):
    _, cols, width, _, _ = dims
    return jnp.where(iota((cols, width), 0) < limit, 1.0, 0.0).astype(FL)


def x_products(dims, a_rows, side, put):
    rows, cols, width, _, _ = dims
    for row in range(rows):
        b_j = side[row * cols : (row + 1) * cols].astype(FL)
        for idx in range(rows):
            put(idx, row, jnp.sum((a_rows[idx] * b_j).reshape(cols // 8, 8, width), axis=0))


def own_kernel(
    dims, scal_ref, copies_ref, own_ref, wl_ref, a_ref, gate_ref, side_ref, fac_ref, part_ref
):
    rows, cols, width, heads, size = dims
    limit, core = scal_ref[0, 0], scal_ref[3, 0]
    mask = pair_mask(dims, limit)(scal_ref[1, 0])
    side, _, gate = own_sides(copies_ref[0], wl_ref, mask)
    a_val = side.astype(BF).astype(FL)
    a_ref[...] = a_val
    a_rows = [a_val[idx * cols : (idx + 1) * cols] for idx in range(rows)]
    gate_ref[...] = gate
    col_mask = col_mask_of(dims, limit)
    w_b = jnp.concatenate([wl_ref[2], wl_ref[3]], axis=1)
    for idx in range(size // 2):
        block = 2 * idx + core
        side, fac = b_block(dims, own_ref[idx], w_b, col_mask, block * rows, limit)
        side_ref[idx] = side
        fac_ref[idx] = fac


        def put(at, row, fold, idx=idx):
            part_ref[at, idx, row * 8 : (row + 1) * 8, :] = fold

        x_products(dims, a_rows, side, put)


def triangle_kernel(
    dims,
    scal_ref,
    own_ref,
    other_ref,
    a_ref,
    gate_ref,
    own_side_ref,
    own_fac_ref,
    own_part_ref,
    pair_hbm,
    norms_hbm,
    wl_ref,
    pbt_hbm,
    tb_ref,
    own_side_hbm,
    own_fac_hbm,
    other_side_hbm,
    other_fac_hbm,
    x_ref,
    z1_ref,
    h1_ref,
    pair_ref,
    norms_ref,
    pbt_ref,
    other_side_ref,
    other_fac_ref,
    part_ref,
    sems,
):
    rows, cols, width, heads, size = dims
    pairs, chips = rows * cols, size // 2
    limit, core = scal_ref[0, 0], scal_ref[3, 0]
    moves = fetch(
        [
            (norms_hbm, norms_ref),
            (pair_hbm, pair_ref),
            (pbt_hbm, pbt_ref),
            (own_side_ref, own_side_hbm),
            (own_fac_ref, own_fac_hbm),
        ],
        sems.at[pl.ds(0, 5)],
    )
    early_moves, moves = moves[:3], moves[3:]
    col_mask = col_mask_of(dims, limit)
    w_b = jnp.concatenate([wl_ref[2], wl_ref[3]], axis=1)
    a_rows = [a_ref[idx * cols : (idx + 1) * cols, :] for idx in range(rows)]

    for idx in range(chips):
        block = 2 * idx + 1 - core
        side, fac = b_block(dims, other_ref[idx], w_b, col_mask, block * rows, limit)
        other_side_ref[idx] = side
        other_fac_ref[idx] = fac

        def put(at, row, fold, block=block):
            start = pl.multiple_of((at * cols + block * rows + row) * 8, 8)
            part_ref[pl.ds(start, 8), :] = fold

        x_products(dims, a_rows, side, put)
        for at in range(rows):
            start = pl.multiple_of((at * cols + (2 * idx + core) * rows) * 8, 8 * rows)
            part_ref[pl.ds(start, 8 * rows), :] = own_part_ref[at, idx]
        if idx == chips // 2 - 1 or idx == chips - 1:
            late = idx == chips - 1
            span = pl.ds(chips // 2, chips - chips // 2) if late else pl.ds(0, chips // 2)
            moves += fetch(
                [
                    (other_side_ref.at[span], other_side_hbm.at[span]),
                    (other_fac_ref.at[span], other_fac_hbm.at[span]),
                ],
                sems.at[pl.ds(7 if late else 5, 2)],
            )
    x_val = part_ref[pl.ds(0, pairs, stride=8), :]
    for idx in range(1, 8):
        x_val = x_val + part_ref[pl.ds(idx, pairs, stride=8), :]

    x_ref[...] = x_val
    for move in early_moves:
        move.wait()
    y_low, _, _ = row_norm(x_val, norms_ref[2:3], norms_ref[3:4])
    z1 = pair_ref[...] + gate_ref[...] * dot(y_low, wl_ref[5])
    z1_ref[...] = z1
    h1, _, _ = row_norm(z1, norms_ref[4:5], norms_ref[5:6])
    h1_ref[...] = h1
    tbt = dot(pbt_ref[...].astype(BF), h1, 1, 1).astype(BF).astype(FL)
    half = pairs // 2
    block = jnp.concatenate([tbt[:, :half], tbt[:, half:]], axis=0)
    for idx in range(size):
        tb_ref[idx] = block
    for move in moves:
        move.wait()


def diagonal_block(first, second):
    zero = jnp.zeros(first.shape, first.dtype)
    return jnp.concatenate(
        [
            jnp.concatenate([first, zero], axis=1),
            jnp.concatenate([zero, second], axis=1),
        ],
        axis=0,
    )


def pack_places(dims):
    rows, cols, width, heads, _ = dims
    pairs, lines = rows * cols, heads * cols
    at, places = 0, {}
    for name, tall in (
        ("prob", rows // 2 * lines),
        ("dscore", rows // 2 * lines),
        ("datt", pairs),
        ("u", pairs),
        ("dout2", pairs),
        ("dgate2", pairs),
        ("h2", pairs),
        ("dlog", 2 * cols),
    ):
        places[name] = at
        at += tall
    return places, at


def lane_ramp(width):
    return 1.0 + iota((1, width), 1).astype(FL) / width


def norm_line(small_ref, idx):
    at = small_ref.shape[1] - 8 + idx
    return small_ref[0, at : at + 1, :]


def attention_kernel(
    dims,
    scal_ref,
    tb_ref,
    h1_ref,
    z1_ref,
    wl_ref,
    bins_hbm,
    pb_hbm,
    pb_m_hbm,
    pb_v_hbm,
    head_hbm,
    head_m_hbm,
    head_v_hbm,
    norms_hbm,
    norms_m_hbm,
    norms_v_hbm,
    dtb_ref,
    pack_ref,
    dz2_ref,
    stat_ref,
    kcat_ref,
    qblk_ref,
    pb_ref,
    small_ref,
    vcat_ref,
    bias_ref,
    prob_ref,
    swap_ref,
    bins_ref,
    sems,
):
    rows, cols, width, heads, size = dims
    pairs, lines = rows * cols, heads * cols
    places, _ = pack_places(dims)
    scale = (width // heads) ** (-0.5)
    limit, first_row = scal_ref[0, 0], scal_ref[1, 0]

    def put(name, val):
        pack_ref[places[name] : places[name] + val.shape[0], :] = val

    bins_n = head_hbm.shape[0]
    moves = [(bins_hbm, bins_ref)]
    for idx, (pb, head, norms) in enumerate(
        (
            (pb_hbm, head_hbm, norms_hbm),
            (pb_m_hbm, head_m_hbm, norms_m_hbm),
            (pb_v_hbm, head_v_hbm, norms_v_hbm),
        )
    ):
        moves += [
            (head, small_ref.at[idx, pl.ds(0, bins_n)]),
            (norms, small_ref.at[idx, pl.ds(bins_n, 8)]),
            (pb, pb_ref.at[idx]),
        ]
    moves = fetch(moves, sems)
    w_att = jnp.concatenate([wl_ref[6], wl_ref[7], wl_ref[8], wl_ref[9]], axis=1)
    proj = dot(h1_ref[...], w_att)
    gate2 = jax.nn.sigmoid(proj[:, 3 * width :])
    lane_head = iota((cols, width), 1) // (width // heads)
    zero = jnp.zeros((cols, width), BF)
    for idx in range(rows):
        at, side = idx // 2, idx % 2
        lanes = slice(side * width, (side + 1) * width)
        span = slice(idx * cols, (idx + 1) * cols)
        query = proj[span, :width].astype(BF)
        qblk_ref[at, side * cols : (side + 1) * cols, lanes] = query
        qblk_ref[at, (1 - side) * cols : (2 - side) * cols, lanes] = zero
        for head in range(heads):
            spot = slice(head * cols, (head + 1) * cols)
            keep = lane_head == head
            kcat_ref[at, spot, lanes] = jnp.where(
                keep, proj[span, width : 2 * width], 0.0
            ).astype(BF)
            vcat_ref[at, spot, lanes] = jnp.where(
                keep, proj[span, 2 * width : 3 * width], 0.0
            ).astype(BF)

    for half in range(2):
        for jl in range(2):
            lanes = slice(jl * cols, (jl + 1) * cols)
            got = [
                tb_ref[pl.ds(half * heads + head, size, stride=2 * heads), :][:, lanes]
                for head in range(heads)
            ]
            for duo in range(heads // 2):
                line = jnp.concatenate([got[2 * duo], got[2 * duo + 1]], axis=1)
                bias_ref[duo, pl.ds(2 * half + jl, size, stride=rows), :] = line
                bias_ref[duo, pl.ds(cols + 2 * half + jl, size, stride=rows), :] = line
    bias = jnp.concatenate([bias_ref[duo].T for duo in range(heads // 2)], axis=0)
    key_ok = iota((lines, 2 * cols), 0) % cols < limit
    att = []
    for at in range(rows // 2):
        score = dot(kcat_ref[at], qblk_ref[at], 1, 1) * scale + bias
        score = jnp.where(key_ok, score, -1000000000.0).reshape(heads, cols, 2 * cols)
        top = jnp.max(score, axis=1, keepdims=True)
        grown = jnp.exp(score - top)
        prob = (grown / jnp.sum(grown, axis=1, keepdims=True)).reshape(lines, 2 * cols)
        prob_ref[at] = prob
        low = prob.astype(BF)
        pack_ref[places["prob"] + at * lines : places["prob"] + (at + 1) * lines, :] = low
        both = dot(low, vcat_ref[at], 0, 0)
        att += [both[:cols, :width], both[cols:, width:]]
    att = jnp.concatenate(att, axis=0)
    u_low = (gate2 * att).astype(BF)
    put("u", u_low)
    z2 = z1_ref[...] + dot(u_low, wl_ref[10])
    for move in moves[:3]:
        move.wait()
    h2, unit6, rstd6 = row_norm(z2, norm_line(small_ref, 6), norm_line(small_ref, 7))
    put("h2", h2)
    headt = small_ref[0, :bins_n, :].astype(BF)
    logits = dot(headt, h2, 1, 1)
    spot = iota((1, pairs), 1)
    ok = jnp.logical_and(spot % cols < limit, spot // cols + first_row < limit)
    mask = jnp.where(ok, 1.0, 0.0).astype(FL)
    bins = jnp.concatenate([bins_ref[idx : idx + 1, :] for idx in range(rows)], axis=1)
    onehot = jnp.where(iota(logits.shape, 0) == bins, 1.0, 0.0).astype(FL)
    top = jnp.max(logits, axis=0, keepdims=True)
    lse = top + jnp.log(jnp.sum(jnp.exp(logits - top), axis=0, keepdims=True))
    pick = jnp.sum(logits * onehot, axis=0, keepdims=True)
    loss = jnp.sum(mask * (lse - pick), axis=1, keepdims=True)
    dlog = (mask * (jnp.exp(logits - lse) - onehot)).astype(BF)
    put("dlog", jnp.concatenate([dlog[:, :width], dlog[:, width:]], axis=0))
    dz2, dg6, ds6 = row_norm_back(dot(dlog, headt, 0, 0), unit6, rstd6, norm_line(small_ref, 6))
    dz2_ref[...] = dz2
    stat_ref[0:1, :] = dg6
    stat_ref[1:2, :] = ds6
    used = limit * limit
    ramp = lane_ramp(width)
    stat_ref[2:3, :] = loss * ramp
    stat_ref[3:4, :] = (used // DIGIT).astype(FL) * ramp
    stat_ref[4:5, :] = (used % DIGIT).astype(FL) * ramp
    stat_ref[5:8, :] = jnp.zeros((3, width), FL)
    dout2 = dz2.astype(BF)
    put("dout2", dout2)
    du = dot(dout2, wl_ref[10], 1, 1)
    put("dgate2", (du * att * gate2 * (1.0 - gate2)).astype(BF))
    datt = (du * gate2).astype(BF)
    put("datt", datt)
    total = None
    for at in range(rows // 2):
        first = datt[(2 * at) * cols : (2 * at + 1) * cols]
        second = datt[(2 * at + 1) * cols : (2 * at + 2) * cols]
        block = diagonal_block(first, second)
        dprob = dot(vcat_ref[at], block, 1, 1)
        prob = prob_ref[at]
        inner = jnp.sum((dprob * prob).reshape(heads, cols, 2 * cols), axis=1, keepdims=True)
        dscore = prob.reshape(heads, cols, 2 * cols) * (
            dprob.reshape(heads, cols, 2 * cols) - inner
        )
        low = dscore.reshape(lines, 2 * cols).astype(BF)
        pack_ref[places["dscore"] + at * lines : places["dscore"] + (at + 1) * lines, :] = low
        total = low.astype(FL) if total is None else total + low.astype(FL)
    for duo in range(heads // 2):
        turned = total[duo * 2 * cols : (duo + 1) * 2 * cols].T
        swap_ref[duo] = turned[:cols] + turned[cols:]
    for half in range(2):
        for head in range(heads):
            inside = slice((head % 2) * cols, (head % 2 + 1) * cols)
            line = jnp.concatenate(
                [
                    swap_ref[head // 2, pl.ds(2 * half + jl, size, stride=rows), :][:, inside]
                    for jl in range(2)
                ],
                axis=1,
            )
            dtb_ref[pl.ds(half * heads + head, size, stride=2 * heads), :] = line
    for move in moves[3:]:
        move.wait()


def gradient_kernel(
    dims,
    scal_ref,
    dtb_ref,
    pack_ref,
    kcat_ref,
    qblk_ref,
    dz2_ref,
    stat_ref,
    h1_ref,
    x_ref,
    z1_ref,
    own_ref,
    other_ref,
    own_side_hbm,
    own_fac_hbm,
    other_side_hbm,
    other_fac_hbm,
    small_ref,
    wl_ref,
    pb_ref,
    keep_ref,
    give_ref,
    flat_ref,
    dx_ref,
    dqkvg_ref,
    own_side_ref,
    own_fac_ref,
    other_side_ref,
    other_fac_ref,
    sems,
):
    rows, cols, width, heads, size = dims
    pairs = rows * cols
    chip, core = scal_ref[2, 0], scal_ref[3, 0]
    moves = fetch(
        [
            (own_side_hbm, own_side_ref),
            (other_side_hbm, other_side_ref),
            (own_fac_hbm, own_fac_ref),
            (other_fac_hbm, other_fac_ref),
        ],
        sems,
    )
    lines = heads * cols
    places, _ = pack_places(dims)

    def take(name, tall, skip=0):
        return pack_ref[places[name] + skip : places[name] + skip + tall, :]

    mask = pair_mask(dims, scal_ref[0, 0])(scal_ref[1, 0])
    side, fac, gate = own_sides(own_ref[chip], wl_ref, mask)
    a_val = side.astype(BF).astype(FL)
    y_low, unit2, rstd2 = row_norm(x_ref[...], norm_line(small_ref, 2), norm_line(small_ref, 3))
    _, unit4, rstd4 = row_norm(z1_ref[...], norm_line(small_ref, 4), norm_line(small_ref, 5))
    out1 = dot(y_low, wl_ref[5])
    scale = (width // heads) ** (-0.5)
    lane_head = iota((cols, width), 1) // (width // heads)

    def diagonal(val):
        out = jnp.zeros((cols, width), FL)
        for head in range(heads):
            out = jnp.where(lane_head == head, val[head * cols : (head + 1) * cols], out)
        return out

    for at in range(rows // 2):
        dscore = take("dscore", lines, at * lines)
        block = diagonal_block(
            take("datt", cols, 2 * at * cols), take("datt", cols, (2 * at + 1) * cols)
        )
        dquery = dot(dscore, kcat_ref[at], 0, 0)
        dkeys = dot(dscore, qblk_ref[at])
        dvals = dot(take("prob", lines, at * lines), block)
        for side in range(2):
            idx = 2 * at + side
            lanes = slice(side * width, (side + 1) * width)
            span = slice(idx * cols, (idx + 1) * cols)
            dqkvg_ref[span, :width] = (
                dquery[side * cols : (side + 1) * cols, lanes] * scale
            ).astype(BF)
            dqkvg_ref[span, width : 2 * width] = (diagonal(dkeys[:, lanes]) * scale).astype(BF)
            dqkvg_ref[span, 2 * width : 3 * width] = diagonal(dvals[:, lanes]).astype(BF)
    dqkvg_ref[:, 3 * width :] = take("dgate2", pairs)
    dqkvg = dqkvg_ref[...]
    w_att = jnp.concatenate([wl_ref[6], wl_ref[7], wl_ref[8], wl_ref[9]], axis=1)
    dh1 = dot(dqkvg, w_att, 1, 1)
    h1 = h1_ref[...]
    dw_att = dot(h1, dqkvg, 0, 0)
    for idx in range(4):
        flat_ref[(6 + idx) * width : (7 + idx) * width, :] = dw_att[
            :, idx * width : (idx + 1) * width
        ]
    flat_ref[10 * width : 11 * width, :] = dot(take("u", pairs), take("dout2", pairs), 0, 0)
    mats = 11 * width
    dlog = take("dlog", 2 * cols)
    dlog = jnp.concatenate([dlog[:cols], dlog[cols:]], axis=1)
    flat_ref[mats : mats + dlog.shape[0], :] = dot(dlog, take("h2", pairs))
    got = dtb_ref[0]
    for idx in range(1, size):
        got = got + dtb_ref[idx]
    dtbt = jnp.concatenate([got[:heads], got[heads:]], axis=1).astype(BF)
    dpbt = dot(dtbt, h1)
    dh1 = dh1 + dot(dtbt, pb_ref[0].astype(BF), 0, 0)
    dn4, dg4, ds4 = row_norm_back(dh1, unit4, rstd4, norm_line(small_ref, 4))
    dz1 = dz2_ref[...] + dn4
    dout1 = (dz1 * gate).astype(BF)
    dgate = dz1 * out1 * gate * (1.0 - gate)
    dx, dg2, ds2 = row_norm_back(dot(dout1, wl_ref[5], 1, 1), unit2, rstd2, norm_line(small_ref, 2))
    dx_ref[...] = dx.astype(BF).astype(FL)

    moves[0].wait()
    moves[1].wait()

    def da_step(idx, acc):
        for side_ref, half in ((own_side_ref, core), (other_side_ref, 1 - core)):
            for row in range(rows):
                j = (2 * idx + half) * rows + row
                b_j = side_ref[idx, row * cols : (row + 1) * cols, :].astype(FL)
                acc = tuple(
                    acc[at] + dx_ref[pl.ds(at * cols + j, 1), :] * b_j for at in range(rows)
                )
        return acc

    acc = lax.fori_loop(
        0, size // 2, da_step, tuple(jnp.zeros((cols, width), FL) for _ in range(rows))
    )
    da = jnp.concatenate(acc, axis=0).astype(BF).astype(FL)
    own = jnp.concatenate(
        [
            (da * fac).astype(BF),
            (da * a_val * (1.0 - fac)).astype(BF),
            dgate.astype(BF),
        ],
        axis=1,
    )
    for move in moves[2:]:
        move.wait()
    ones = jnp.ones((16, pairs), BF)

    def products(h0, grads):
        return dot(h0, grads, 0, 0), dot(ones, grads)

    dw_own, sum_own = products(own_ref[chip], own)

    a_rows = [a_val[idx * cols : (idx + 1) * cols] for idx in range(rows)]

    def db_step(idx, acc):
        for src, side_ref, fac_ref, half in (
            (own_ref, own_side_ref, own_fac_ref, core),
            (other_ref, other_side_ref, other_fac_ref, 1 - core),
        ):
            lines = []
            for row in range(rows):
                j = (2 * idx + half) * rows + row
                db = dx_ref[pl.ds(j, 1), :] * a_rows[0]
                for own_row in range(1, rows):
                    db = db + dx_ref[pl.ds(own_row * cols + j, 1), :] * a_rows[own_row]
                lines.append(db.astype(BF))
            db = jnp.concatenate(lines, axis=0)
            fac_b = fac_ref[idx]
            grads = jnp.concatenate([db * fac_b, db * (side_ref[idx] * (1.0 - fac_b))], axis=1)
            main, sums = products(src[idx], grads)
            acc = (acc[0] + main, acc[1] + sums)
        return acc

    dw_b = (jnp.zeros((width, 2 * width), FL), jnp.zeros((16, 2 * width), FL))
    for idx in range(size // 2):
        dw_b = db_step(idx, dw_b)
    dw_b, sum_b = dw_b

    parts = [
        (val[:, at * width : (at + 1) * width], sums[:1, at * width : (at + 1) * width])
        for val, sums, at in (
            (dw_own, sum_own, 0),
            (dw_own, sum_own, 1),
            (dw_b, sum_b, 0),
            (dw_b, sum_b, 1),
            (dw_own, sum_own, 2),
        )
    ]
    mixed = jnp.zeros((width, width), FL)
    summed = jnp.zeros((width, width), FL)
    for idx, (part, sums) in enumerate(parts):
        weight = wl_ref[idx].astype(FL)
        flat_ref[idx * width : (idx + 1) * width, :] = part
        mixed = mixed + weight * part
        summed = summed + weight * sums
    ds0 = lane_sums(summed)
    dg0 = (lane_sums(mixed) - norm_line(small_ref, 1) * ds0) / norm_line(small_ref, 0)
    flat_ref[5 * width : 6 * width, :] = dot(y_low, dout1, 0, 0)
    base = mats + dlog.shape[0]
    flat_ref[base : base + heads, :] = dpbt
    flat_ref[base + heads : base + 8, :] = jnp.zeros((8 - heads, width), FL)
    base += 8
    for idx, line in enumerate((dg0, ds0, dg2, ds2, dg4, ds4)):
        flat_ref[base + idx : base + idx + 1, :] = line
    flat_ref[base + 6 : base + 11, :] = stat_ref[0:5, :]
    total = flat_ref.shape[0]
    flat_ref[base + 11 :, :] = jnp.zeros((total - base - 11, width), FL)
    half = total // 2
    keep_ref[...] = flat_ref[pl.ds(pl.multiple_of(core * half, half), half), :]
    give_ref[...] = flat_ref[pl.ds(pl.multiple_of((1 - core) * half, half), half), :]


def update_kernel(
    dims,
    scal_ref,
    mine_ref,
    other_ref,
    mats_ref,
    mats_m_ref,
    mats_v_ref,
    pb_ref,
    small_ref,
    norm_out,
    loss_out,
    count_out,
    mats_m_out,
    mats_v_out,
    mats_out,
    mats_low_out,
    pb_m_out,
    pb_v_out,
    pb_out,
    head_m_out,
    head_v_out,
    head_out,
    norms_m_out,
    norms_v_out,
    norms_out,
    flat_ref,
    scalar_buf,
    small_buf,
    pb_buf,
    m_buf,
    v_buf,
    w_buf,
    low_buf,
    sems,
    small_sems,
):
    rows, cols, width, heads, size = dims
    bins_n = small_ref.shape[1] - 8
    core = scal_ref[3, 0]
    half = mine_ref.shape[0]
    flat_ref[pl.ds(pl.multiple_of(core * half, half), half), :] = mine_ref[...]
    flat_ref[pl.ds(pl.multiple_of((1 - core) * half, half), half), :] = other_ref[...]
    count = mats_ref.shape[0]
    mats = count * width
    base = mats + bins_n
    grads = flat_ref[: base + 16, :]
    square = jnp.sum(grads * grads, axis=0, keepdims=True)
    norm = jnp.sqrt(jnp.sum(square, axis=1, keepdims=True))
    factor = jnp.minimum(1.0, CLIP / norm)
    scalar_buf[0] = norm
    stats = jnp.mean(
        flat_ref[base + 16 : base + 24, :] / lane_ramp(width), axis=1, keepdims=True
    )
    scalar_buf[1] = stats[0:1]
    scalar_buf[2] = (DIGIT * jnp.round(stats[1:2]) + jnp.round(stats[2:3])) / size

    moves = []

    def send(at, idx, buf, out):
        move = pltpu.make_async_copy(buf.at[idx], out.at[idx], sems.at[at, idx])
        move.start()
        moves.append(move)

    def step(weight, grad, first, second):
        return adam(weight, grad * factor, first, second)

    def update_small():
        triples = []
        for at, tall, buf, ref, skip, outs in (
            (mats, bins_n, small_buf, small_ref, 0, (head_m_out, head_v_out, head_out)),
            (base + 8, 8, small_buf, small_ref, bins_n, (norms_m_out, norms_v_out, norms_out)),
            (base, heads, pb_buf, pb_ref, 0, (pb_m_out, pb_v_out, pb_out)),
        ):
            weight, first, second = (ref[idx, skip : skip + tall, :] for idx in range(3))
            now = step(weight, flat_ref[at : at + tall, :], first, second)
            for idx, (val, out) in enumerate(zip(now, outs)):
                buf[idx, skip : skip + tall, :] = val
                triples.append((buf.at[idx, pl.ds(skip, tall)], out))
        triples += [
            (scalar_buf.at[idx], out) for idx, out in enumerate((norm_out, loss_out, count_out))
        ]
        moves.extend(fetch(triples, small_sems))

    for idx in range(count):
        if idx == count // 2:
            update_small()
        m_buf[idx], v_buf[idx], weight = step(
            mats_ref[idx],
            flat_ref[idx * width : (idx + 1) * width, :],
            mats_m_ref[idx],
            mats_v_ref[idx],
        )
        w_buf[idx] = weight
        low_buf[idx] = weight.astype(BF)
        send(0, idx, m_buf, mats_m_out)
        send(1, idx, v_buf, mats_v_out)
        send(2, idx, w_buf, mats_out)
        send(3, idx, low_buf, mats_low_out)
    for move in moves:
        move.wait()


def call(kernel, args, outs, scratch=(), limit=VMEM_LIMIT, flops=10**7):
    spots = {"s": pltpu.SMEM, "v": pltpu.VMEM, "h": pltpu.HBM}
    return pl.pallas_call(
        kernel,
        out_shape=[
            pltpu.HBM(shape, kind) if spot == "h" else jax.ShapeDtypeStruct(shape, kind)
            for shape, kind, spot in outs
        ],
        in_specs=[pl.BlockSpec(memory_space=spots[spot]) for _, spot in args],
        out_specs=[pl.BlockSpec(memory_space=spots[spot]) for _, _, spot in outs],
        scratch_shapes=list(scratch),
        compiler_params=pltpu.CompilerParams(vmem_limit_bytes=limit),
        cost_estimate=pl.CostEstimate(flops=flops, bytes_accessed=10**6, transcendentals=0),
    )(
        *(
            pltpu.with_memory_space_constraint(value, pltpu.HBM) if spot == "h" else value
            for value, spot in args
        )
    )


def shrink(val):
    root = jnp.sqrt(jnp.abs(val) * SPAN)
    return jnp.where(val < 0.0, -root, root).astype(jnp.float16)


def grow(root):
    root = root.astype(FL)
    return root * jnp.abs(root) * (1.0 / SPAN)


def same_core_groups(crops, size):
    return [
        [crop * size + idx for crop in range(crops) for idx in range(core, size, 2)]
        for core in range(2)
    ]


def core_swap(value, size):
    return lax.ppermute(value, "row", [(idx, idx ^ 1) for idx in range(size)])


def fast_step(
    crops,
    size,
    pair,
    bins,
    lengths,
    mats,
    mats_m,
    mats_v,
    pbias,
    pbias_m,
    pbias_v,
    head,
    head_m,
    head_v,
    norms,
    norms_m,
    norms_v,
):
    rows, cols, width = pair.shape[1:]
    heads, bins_n = pbias.shape[1], head.shape[1]
    pairs, lines = rows * cols, heads * cols
    dims = (rows, cols, width, heads, size)
    chips = size // 2
    place = lax.axis_index("row")
    scal = jnp.stack([lengths[0], place * rows, place // 2, place % 2]).astype(jnp.int32)
    scal = jnp.broadcast_to(jnp.pad(scal, (0, 4))[:, None], (8, width))
    start = pair.reshape(pairs, width)
    pbt, headt = pbias.T, head.T

    copies, wl = call(
        functools.partial(start_kernel, chips),
        [(start, "h"), (norms, "h"), (mats, "h")],
        [((chips, pairs, width), BF, "v"), (mats.shape, BF, "v")],
        [
            pltpu.VMEM((pairs, width), FL),
            pltpu.VMEM(norms.shape, FL),
            pltpu.VMEM(mats.shape, FL),
            pltpu.SemaphoreType.DMA((3,)),
        ],
    )
    near = [list(range(core, size, 2)) for core in range(2)]
    own = lax.all_to_all(copies, "row", 0, 0, axis_index_groups=near, tiled=True)
    other = core_swap(own, size)
    a_val, gate, own_side, own_fac, part = call(
        functools.partial(own_kernel, dims),
        [(scal, "v"), (copies, "v"), (own, "v"), (wl, "v")],
        [
            ((pairs, width), FL, "v"),
            ((pairs, width), FL, "v"),
            (own.shape, BF, "v"),
            (own.shape, BF, "v"),
            ((rows, chips, rows * 8, width), FL, "v"),
        ],
    )
    tb, own_side, own_fac, other_side, other_fac, x_val, z1, h1 = call(
        functools.partial(triangle_kernel, dims),
        [
            (scal, "v"),
            (own, "v"),
            (other, "v"),
            (a_val, "v"),
            (gate, "v"),
            (own_side, "v"),
            (own_fac, "v"),
            (part, "v"),
            (start, "h"),
            (norms, "h"),
            (wl, "v"),
            (pbt, "h"),
        ],
        [((size, 2 * heads, 2 * cols), FL, "v")]
        + [(own.shape, BF, "h")] * 4
        + [
            ((pairs, width), FL, "v"),
            ((pairs, width), FL, "v"),
            ((pairs, width), BF, "v"),
        ],
        [
            pltpu.VMEM((pairs, width), FL),
            pltpu.VMEM(norms.shape, FL),
            pltpu.VMEM(pbt.shape, FL),
            pltpu.VMEM(own.shape, BF),
            pltpu.VMEM(own.shape, BF),
            pltpu.VMEM((pairs * 8, width), FL),
            pltpu.SemaphoreType.DMA((9,)),
        ],
    )

    tb_all = lax.all_to_all(tb, "row", 0, 0, tiled=True)
    bias_shape = (size * 2 * heads, 2 * cols)
    small_args = (
        pbt,
        pbias_m.T,
        pbias_v.T,
        headt,
        head_m.T,
        head_v.T,
        norms,
        norms_m,
        norms_v,
    )
    dtb, pack, dz2, stat, kcat, qblk, pb_all, small_all = call(
        functools.partial(attention_kernel, dims),
        [
            (scal, "v"),
            (tb_all.reshape(bias_shape), "v"),
            (h1, "v"),
            (z1, "v"),
            (wl, "v"),
            (bins[0], "h"),
        ]
        + [(value, "h") for value in small_args],
        [
            (bias_shape, FL, "v"),
            ((pack_places(dims)[1], width), BF, "v"),
            ((pairs, width), FL, "v"),
            ((8, width), FL, "v"),
            ((rows // 2, lines, 2 * width), BF, "v"),
            ((rows // 2, 2 * cols, 2 * width), BF, "v"),
            ((3, heads, width), FL, "v"),
            ((3, bins_n + norms.shape[0], width), FL, "v"),
        ],
        [
            pltpu.VMEM((rows // 2, lines, 2 * width), BF),
            pltpu.VMEM((heads // 2, 2 * cols, 2 * cols), FL),
            pltpu.VMEM((rows // 2, lines, 2 * cols), FL),
            pltpu.VMEM((heads // 2, cols, 2 * cols), FL),
            pltpu.VMEM((rows, cols), jnp.int32),
            pltpu.SemaphoreType.DMA((10,)),
        ],
    )

    dtb_all = lax.all_to_all(dtb.reshape(size, 2 * heads, 2 * cols), "row", 0, 0, tiled=True)
    used = mats.shape[0] * width + bins_n + 24
    unit = 8 * crops * size
    total = -(-used // unit) * unit
    keep, give = call(
        functools.partial(gradient_kernel, dims),
        [(scal, "v")]
        + [
            (value, "v")
            for value in (dtb_all, pack, kcat, qblk, dz2, stat, h1, x_val, z1, own, other)
        ]
        + [(value, "h") for value in (own_side, own_fac, other_side, other_fac)]
        + [(value, "v") for value in (small_all, wl, pb_all)],
        [((total // 2, width), FL, "v"), ((total // 2, width), FL, "v")],
        [
            pltpu.VMEM((total, width), FL),
            pltpu.VMEM((pairs, width), FL),
            pltpu.VMEM((pairs, 4 * width), BF),
        ]
        + [pltpu.VMEM(own.shape, BF)] * 4
        + [
            pltpu.SemaphoreType.DMA((4,)),
        ],
    )

    half = keep + core_swap(give, size)
    count = crops * chips
    groups = same_core_groups(crops, size)
    axes = ("crop", "row")
    parts = lax.all_to_all(
        shrink(half).reshape(count, -1, width), axes, 0, 0, axis_index_groups=groups, tiled=True
    )
    share = shrink(jnp.sum(grow(parts), axis=0))
    spread = jnp.broadcast_to(share[None], (count,) + share.shape)
    mine = lax.all_to_all(spread, axes, 0, 0, axis_index_groups=groups, tiled=True)
    mine = mine.reshape(total // 2, width)
    other_half = grow(core_swap(mine, size))
    mine = grow(mine)

    number = mats.shape[0]
    big, low = ((number, width, width), FL, "h"), ((number, width, width), BF, "h")
    pb_out, head_out = ((heads, width), FL, "h"), ((bins_n, width), FL, "h")
    norm_out = ((norms.shape[0], width), FL, "h")
    res = call(
        functools.partial(update_kernel, dims),
        [(scal, "v")]
        + [
            (value, "v")
            for value in (mine, other_half, mats, mats_m, mats_v, pb_all, small_all)
        ],
        [((1, 1), FL, "h")] * 3
        + [big, big, big, low]
        + [pb_out] * 3
        + [head_out] * 3
        + [norm_out] * 3,
        [
            pltpu.VMEM((total, width), FL),
            pltpu.VMEM((3, 1, 1), FL),
            pltpu.VMEM((3, bins_n + norms.shape[0], width), FL),
            pltpu.VMEM((3, heads, width), FL),
        ]
        + [pltpu.VMEM((number, width, width), FL)] * 3
        + [
            pltpu.VMEM((number, width, width), BF),
            pltpu.SemaphoreType.DMA((4, number)),
            pltpu.SemaphoreType.DMA((12,)),
        ],
    )
    return (
        *(value.reshape(()) for value in res[:3]),
        *res[3:7],
        *(value.T for value in res[7:13]),
        *res[13:16],
    )


def small_enough(pair, heads, size):
    _, rows, cols, width = pair.shape
    held = 4 * size * rows * cols * width * 4 + 4 * rows * heads * cols * cols * 4
    return (
        held <= 2**24
        and width == 2 * cols
        and rows == 4
        and heads == 4
        and size % 2 == 0
        and rows * size == cols
    )


def solution(mesh):
    crops, size = mesh.shape["crop"], mesh.shape["row"]

    def on_device(*args):
        if small_enough(args[0], args[6].shape[1], size):
            return fast_step(crops, size, *args)
        return general_step(*args)

    in_specs = (
        P("crop", "row", None, None),
        P("crop", "row", None),
        P("crop"),
        P(),
        P(),
        P(),
        P(),
        P(),
        P(),
        P(),
        P(),
        P(),
        P(),
        P(),
        P(),
    )
    out_specs = (P(), P(), P(), P(), P(), P(), P(), P(), P(), P(), P(), P(), P(), P(), P(), P())
    return jax.shard_map(
        on_device, mesh=mesh, in_specs=in_specs, out_specs=out_specs, check_vma=False
    )
```

```python
import functools

import jax
import jax.numpy as jnp
from jax import lax
from jax.experimental import pallas as pl
from jax.experimental.pallas import tpu as pltpu
from jax.sharding import PartitionSpec as P

STEP = 5


EPS_NORM = 1e-05
CLIP = 1.0
RATE = 0.05
BETA1 = 0.9
BETA2 = 0.95
ADAM_EPS = 1e-08
WDECAY = 0.01


def norm_fwd(v, gain, shift):
    mean = jnp.mean(v, axis=-1, keepdims=True)
    cent = v - mean
    rstd = lax.rsqrt(jnp.mean(cent * cent, axis=-1, keepdims=True) + EPS_NORM)
    unit = cent * rstd
    return (unit * gain + shift, unit, rstd)


def norm_back(grad, unit, rstd, gain):
    dgain = jnp.sum(grad * unit, axis=(0, 1))
    dshift = jnp.sum(grad, axis=(0, 1))
    dunit = grad * gain
    dval = rstd * (
        dunit
        - jnp.mean(dunit, axis=-1, keepdims=True)
        - unit * jnp.mean(dunit * unit, axis=-1, keepdims=True)
    )
    return (dval, dgain, dshift)


def matmul(value, weight):
    flat = value.reshape(-1, value.shape[-1])
    out = jnp.dot(flat, weight, preferred_element_type=jnp.float32)
    return out.reshape(value.shape[:-1] + (weight.shape[1],))


def wgrad(value, grad):
    return jnp.einsum("ijc,ijd->cd", value, grad, preferred_element_type=jnp.float32)


def adam(weight, grad, first, second):
    first_new = BETA1 * first + (1.0 - BETA1) * grad
    second_new = BETA2 * second + (1.0 - BETA2) * grad * grad
    m_hat = first_new / (1.0 - BETA1**STEP)
    v_hat = second_new / (1.0 - BETA2**STEP)
    weight_new = weight - RATE * (m_hat / (jnp.sqrt(v_hat) + ADAM_EPS) + WDECAY * weight)
    return (first_new, second_new, weight_new)


def general_step(
    pair,
    bins,
    lengths,
    mats,
    mats_m,
    mats_v,
    pbias,
    pbias_m,
    pbias_v,
    head,
    head_m,
    head_v,
    norms,
    norms_m,
    norms_v,
):
    bf = jnp.bfloat16
    fl = jnp.float32
    width = mats.shape[1]
    rows = pair.shape[1]
    cols = pair.shape[2]
    heads = pbias.shape[1]
    size_head = width // heads
    scale = size_head ** (-0.5)
    start_pair = pair[0]
    first_row = lax.axis_index("row") * rows
    limit = lengths[0]
    row_ok = first_row + jnp.arange(rows) < limit
    col_ok = jnp.arange(cols) < limit
    pmask = (row_ok[:, None] & col_ok[None, :]).astype(fl)
    m3 = pmask[..., None]
    wl = mats.astype(bf)
    pl = pbias.astype(bf)
    hl = head.astype(bf)
    w_tri = jnp.concatenate([wl[0], wl[1], wl[2], wl[3], wl[4]], axis=1)
    w_att = jnp.concatenate([wl[6], wl[7], wl[8], wl[9]], axis=1)
    h0, unit0, rstd0 = norm_fwd(start_pair, norms[0], norms[1])
    h0b = h0.astype(bf)
    proj = matmul(h0b, w_tri)
    sig_a = jax.nn.sigmoid(proj[..., width : 2 * width])
    sig_b = jax.nn.sigmoid(proj[..., 3 * width : 4 * width])
    gate = jax.nn.sigmoid(proj[..., 4 * width :])
    a_low = (sig_a * proj[..., :width] * m3).astype(bf)
    b_low = (sig_b * proj[..., 2 * width : 3 * width] * m3).astype(bf)
    b_all = lax.all_gather(b_low, "row", axis=0, tiled=True)
    prod = jnp.einsum("ikc,jkc->ijc", a_low, b_all, preferred_element_type=fl)
    y_val, unit2, rstd2 = norm_fwd(prod, norms[2], norms[3])
    y_low = y_val.astype(bf)
    out1 = matmul(y_low, wl[5])
    z1 = start_pair + gate * out1
    h1, unit4, rstd4 = norm_fwd(z1, norms[4], norms[5])
    h1b = h1.astype(bf)
    qkvg = matmul(h1b, w_att)
    query = qkvg[..., :width].astype(bf).reshape(rows, cols, heads, size_head)
    keys = qkvg[..., width : 2 * width].astype(bf).reshape(rows, cols, heads, size_head)
    values = qkvg[..., 2 * width : 3 * width].astype(bf).reshape(rows, cols, heads, size_head)
    gate2 = jax.nn.sigmoid(qkvg[..., 3 * width :])
    tb_low = matmul(h1b, pl).astype(bf)
    tb_all = lax.all_gather(tb_low, "row", axis=0, tiled=True)
    tb_heads = jnp.transpose(tb_all, (2, 0, 1)).astype(fl)
    scores = (
        jnp.einsum("ijhd,ikhd->ihjk", query, keys, preferred_element_type=fl) * scale
        + tb_heads[None]
    )
    scores = jnp.where(col_ok[None, None, None, :], scores, -1000000000.0)
    probs = jax.nn.softmax(scores, axis=-1)
    p_low = probs.astype(bf)
    att = jnp.einsum("ihjk,ikhd->ijhd", p_low, values, preferred_element_type=fl).reshape(
        rows, cols, width
    )
    u_low = (gate2 * att).astype(bf)
    z2 = z1 + matmul(u_low, wl[10])
    h2, unit6, rstd6 = norm_fwd(z2, norms[6], norms[7])
    h2b = h2.astype(bf)
    logits = matmul(h2b, hl)
    lse = jax.nn.logsumexp(logits, axis=-1)
    onehot = (bins[0][..., None] == jnp.arange(logits.shape[-1])).astype(fl)
    pick = jnp.sum(logits * onehot, axis=-1)
    loss = jnp.sum(pmask * (lse - pick))
    count = jnp.sum(pmask)
    dlog = (m3 * (jnp.exp(logits - lse[..., None]) - onehot)).astype(bf)
    dhead = wgrad(h2b, dlog)
    dz2, dg6, ds6 = norm_back(matmul(dlog, hl.T), unit6, rstd6, norms[6])
    dout2 = dz2.astype(bf)
    dw10 = wgrad(u_low, dout2)
    du = matmul(dout2, wl[10].T)
    dgate2 = du * att
    datt = (du * gate2).astype(bf).reshape(rows, cols, heads, size_head)
    dprob = jnp.einsum("ijhd,ikhd->ihjk", datt, values, preferred_element_type=fl)
    dvals = jnp.einsum("ihjk,ijhd->ikhd", p_low, datt, preferred_element_type=fl)
    dscore = (probs * (dprob - jnp.sum(dprob * probs, axis=-1, keepdims=True))).astype(bf)
    dquery = jnp.einsum("ihjk,ikhd->ijhd", dscore, keys, preferred_element_type=fl) * scale
    dkeys = jnp.einsum("ihjk,ijhd->ikhd", dscore, query, preferred_element_type=fl) * scale
    dtb = jnp.sum(dscore.astype(fl), axis=0)
    dtb_own = lax.psum_scatter(dtb, "row", scatter_dimension=1, tiled=True)
    dtb_low = jnp.transpose(dtb_own, (1, 2, 0)).astype(bf)
    dpbias = wgrad(h1b, dtb_low)
    dqkvg = jnp.concatenate(
        [
            dquery.reshape(rows, cols, width),
            dkeys.reshape(rows, cols, width),
            dvals.reshape(rows, cols, width),
            dgate2 * gate2 * (1.0 - gate2),
        ],
        axis=-1,
    ).astype(bf)
    dw_att = wgrad(h1b, dqkvg)
    dh1 = matmul(dqkvg, w_att.T) + matmul(dtb_low, pl.T)
    dn4, dg4, ds4 = norm_back(dh1, unit4, rstd4, norms[4])
    dz1 = dz2 + dn4
    dout1 = (dz1 * gate).astype(bf)
    dw5 = wgrad(y_low, dout1)
    dgate = dz1 * out1
    dxn, dg2, ds2 = norm_back(matmul(dout1, wl[5].T), unit2, rstd2, norms[2])
    dx_low = dxn.astype(bf)
    dside_a = jnp.einsum("ijc,jkc->ikc", dx_low, b_all, preferred_element_type=fl)
    dside_b = lax.psum_scatter(
        jnp.einsum("ijc,ikc->jkc", dx_low, a_low, preferred_element_type=fl),
        "row",
        scatter_dimension=0,
        tiled=True,
    )
    da_r = dside_a.astype(bf).astype(fl)
    db_r = dside_b.astype(bf).astype(fl)
    dproj = jnp.concatenate(
        [
            da_r * sig_a * m3,
            da_r * proj[..., :width] * m3 * sig_a * (1.0 - sig_a),
            db_r * sig_b * m3,
            db_r * proj[..., 2 * width : 3 * width] * m3 * sig_b * (1.0 - sig_b),
            dgate * gate * (1.0 - gate),
        ],
        axis=-1,
    ).astype(bf)
    dw_tri = wgrad(h0b, dproj)
    dh0 = matmul(dproj, w_tri.T)
    unused, dg0, ds0 = norm_back(dh0, unit0, rstd0, norms[0])
    pieces = [dw_tri[:, idx * width : (idx + 1) * width] for idx in range(5)]
    pieces = (
        pieces + [dw5] + [dw_att[:, idx * width : (idx + 1) * width] for idx in range(4)] + [dw10]
    )
    dmats = jnp.stack(pieces)
    dnorms = jnp.stack([dg0, ds0, dg2, ds2, dg4, ds4, dg6, ds6])
    dmats, dpbias, dhead, dnorms, loss, count = lax.psum(
        (dmats, dpbias, dhead, dnorms, loss, count), ("crop", "row")
    )
    grad_norm = jnp.sqrt(
        jnp.sum(dmats * dmats)
        + jnp.sum(dpbias * dpbias)
        + jnp.sum(dhead * dhead)
        + jnp.sum(dnorms * dnorms)
    )
    factor = jnp.minimum(1.0, CLIP / grad_norm)
    new_mats = adam(mats, dmats * factor, mats_m, mats_v)
    new_pbias = adam(pbias, dpbias * factor, pbias_m, pbias_v)
    new_head = adam(head, dhead * factor, head_m, head_v)
    new_norms = adam(norms, dnorms * factor, norms_m, norms_v)
    return (
        grad_norm,
        loss,
        count,
        new_mats[0],
        new_mats[1],
        new_mats[2],
        new_mats[2].astype(bf),
        new_pbias[0],
        new_pbias[1],
        new_pbias[2],
        new_head[0],
        new_head[1],
        new_head[2],
        new_norms[0],
        new_norms[1],
        new_norms[2],
    )


BF = jnp.bfloat16
FL = jnp.float32
VMEM_LIMIT = 24 * 2**20
SPAN = 2.0**-12
DIGIT = 64


def dot(lhs, rhs, left=1, right=0):
    return lax.dot_general(
        lhs, rhs, (((left,), (right,)), ((), ())), preferred_element_type=FL
    )


def lane_sums(val):
    return jnp.sum(val.T, axis=0, keepdims=True)


def row_norm(val, gain, shift):
    mean = jnp.mean(val, axis=-1, keepdims=True)
    cent = val - mean
    rstd = lax.rsqrt(jnp.mean(cent * cent, axis=-1, keepdims=True) + EPS_NORM)
    unit = cent * rstd
    return (unit * gain + shift).astype(BF), unit, rstd


def row_norm_back(grad, unit, rstd, gain):
    dgain = jnp.sum(grad * unit, axis=0, keepdims=True)
    dshift = jnp.sum(grad, axis=0, keepdims=True)
    dunit = grad * gain
    dval = rstd * (
        dunit
        - jnp.mean(dunit, axis=-1, keepdims=True)
        - unit * jnp.mean(dunit * unit, axis=-1, keepdims=True)
    )
    return dval, dgain, dshift


def iota(shape, dim):
    return lax.broadcasted_iota(jnp.int32, shape, dim)


def fetch(pairs, sems):
    moves = [
        pltpu.make_async_copy(src, dst, sems.at[idx]) for idx, (src, dst) in enumerate(pairs)
    ]
    for move in moves:
        move.start()
    return moves


def start_kernel(
    pair_hbm, norms_hbm, mats_hbm, h0_ref, wl_ref, pair_ref, norms_ref, mats_ref, sems
):
    moves = fetch(
        [(pair_hbm, pair_ref), (norms_hbm, norms_ref), (mats_hbm, mats_ref)], sems
    )
    moves[0].wait()
    moves[1].wait()
    h0_ref[...], _, _ = row_norm(pair_ref[...], norms_ref[0:1], norms_ref[1:2])
    moves[2].wait()
    wl_ref[...] = mats_ref[...].astype(BF)


def block_groups(chips):
    half = chips // 2
    first, late = range(half + 1), range(half + 1, chips)
    return (
        [(flip, other) for other in range(2) for flip in first],
        [(flip, 0) for flip in late],
        [(flip, 1) for flip in late],
    )


def block_at(scal_ref, tag):
    core = scal_ref[3, 0]
    return 2 * (scal_ref[2, 0] ^ tag[0]) + (1 - core if tag[1] else core)


def pair_mask(dims, limit):
    rows, cols, width, _, _ = dims
    spot = iota((rows * cols, width), 0)
    col_ok = spot % cols < limit
    row_in = spot // cols

    def mask_of(block_row):
        return jnp.where(jnp.logical_and(col_ok, row_in + block_row < limit), 1.0, 0.0).astype(FL)

    return mask_of


def own_sides(h0, wl_ref, mask):
    width = h0.shape[1]
    w_own = jnp.concatenate([wl_ref[0], wl_ref[1], wl_ref[4]], axis=1)
    proj = dot(h0, w_own)
    fac = jax.nn.sigmoid(proj[:, width : 2 * width]) * mask
    return fac * proj[:, :width], fac, jax.nn.sigmoid(proj[:, 2 * width :])


def b_block(dims, h0, w_b, col_mask, start, limit):
    rows, cols, width, _, _ = dims
    proj = dot(h0, w_b)
    sig = jax.nn.sigmoid(proj[:, width:])
    lines = []
    for row in range(rows):
        row_ok = jnp.where(start + row < limit, 1.0, 0.0).astype(FL)
        lines.append(sig[row * cols : (row + 1) * cols] * (col_mask * row_ok))
    fac = jnp.concatenate(lines, axis=0)
    return (fac * proj[:, :width]).astype(BF), fac.astype(BF)


def col_mask_of(dims, limit):
    _, cols, width, _, _ = dims
    return jnp.where(iota((cols, width), 0) < limit, 1.0, 0.0).astype(FL)


def x_products(dims, a_rows, side, put):
    rows, cols, width, _, _ = dims
    for row in range(rows):
        b_j = side[row * cols : (row + 1) * cols].astype(FL)
        for idx in range(rows):
            put(idx, row, jnp.sum((a_rows[idx] * b_j).reshape(cols // 8, 8, width), axis=0))


def blocks_kernel(dims, tags, scal_ref, wl_ref, *refs):
    first = tags[0] == (0, 0)
    if not first:
        a_ref, *refs = refs
    h0_refs, refs = refs[: len(tags)], refs[len(tags) :]
    part_ref, side_hbm, fac_hbm, *refs = refs
    if first:
        a_ref, gate_ref, *refs = refs
    side_ref, fac_ref, sems = refs
    rows, cols, width, heads, size = dims
    limit = scal_ref[0, 0]
    if first:
        mask = pair_mask(dims, limit)(scal_ref[1, 0])
        side, _, gate_ref[...] = own_sides(h0_refs[0][...], wl_ref, mask)
        a_ref[...] = side.astype(BF).astype(FL)
    a_rows = [a_ref[idx * cols : (idx + 1) * cols, :] for idx in range(rows)]
    col_mask = col_mask_of(dims, limit)
    w_b = jnp.concatenate([wl_ref[2], wl_ref[3]], axis=1)
    for idx, tag in enumerate(tags):
        start = block_at(scal_ref, tag) * rows
        side, fac = b_block(dims, h0_refs[idx][...], w_b, col_mask, start, limit)
        side_ref[idx] = side
        fac_ref[idx] = fac

        def put(at, row, fold, idx=idx):
            part_ref[at, idx, row * 8 : (row + 1) * 8, :] = fold

        x_products(dims, a_rows, side, put)
        if idx == len(tags) // 2:
            span = pl.ds(0, idx + 1)
            moves = fetch(
                [(side_ref.at[span], side_hbm.at[span]), (fac_ref.at[span], fac_hbm.at[span])],
                sems.at[pl.ds(0, 2)],
            )
    span = pl.ds(len(tags) // 2 + 1, len(tags) - len(tags) // 2 - 1)
    moves += fetch(
        [(side_ref.at[span], side_hbm.at[span]), (fac_ref.at[span], fac_hbm.at[span])],
        sems.at[pl.ds(2, 2)],
    )
    for move in moves:
        move.wait()


def triangle_kernel(
    dims, groups, scal_ref, a_ref, gate_ref, wl_ref, pair_hbm, norms_hbm, pbt_hbm, *refs
):
    tags, before = groups[-1], groups[:-1]
    part_refs, refs = refs[: len(before)], refs[len(before) :]
    h0_refs, refs = refs[: len(tags)], refs[len(tags) :]
    tb_ref, side_hbm, fac_hbm, x_ref, z1_ref, h1_ref, *refs = refs
    pair_ref, norms_ref, pbt_ref, side_ref, fac_ref, part_ref, sems = refs
    rows, cols, width, heads, size = dims
    pairs = rows * cols
    limit = scal_ref[0, 0]
    early_moves = fetch(
        [(norms_hbm, norms_ref), (pair_hbm, pair_ref), (pbt_hbm, pbt_ref)],
        sems.at[pl.ds(0, 3)],
    )
    col_mask = col_mask_of(dims, limit)
    w_b = jnp.concatenate([wl_ref[2], wl_ref[3]], axis=1)
    a_rows = [a_ref[idx * cols : (idx + 1) * cols, :] for idx in range(rows)]

    for idx, tag in enumerate(tags):
        block = block_at(scal_ref, tag)
        side, fac = b_block(dims, h0_refs[idx][...], w_b, col_mask, block * rows, limit)
        side_ref[idx] = side
        fac_ref[idx] = fac

        def put(at, row, fold, block=block):
            start = pl.multiple_of((at * cols + block * rows + row) * 8, 8)
            part_ref[pl.ds(start, 8), :] = fold

        x_products(dims, a_rows, side, put)
    moves = fetch([(side_ref, side_hbm), (fac_ref, fac_hbm)], sems.at[pl.ds(3, 2)])
    for group, ref in zip(before, part_refs):
        for idx, tag in enumerate(group):
            for at in range(rows):
                start = pl.multiple_of(
                    (at * cols + block_at(scal_ref, tag) * rows) * 8, 8 * rows
                )
                part_ref[pl.ds(start, 8 * rows), :] = ref[at, idx]
    x_val = part_ref[pl.ds(0, pairs, stride=8), :]
    for idx in range(1, 8):
        x_val = x_val + part_ref[pl.ds(idx, pairs, stride=8), :]

    x_ref[...] = x_val
    for move in early_moves:
        move.wait()
    y_low, _, _ = row_norm(x_val, norms_ref[2:3], norms_ref[3:4])
    z1 = pair_ref[...] + gate_ref[...] * dot(y_low, wl_ref[5])
    z1_ref[...] = z1
    h1, _, _ = row_norm(z1, norms_ref[4:5], norms_ref[5:6])
    h1_ref[...] = h1
    tbt = dot(pbt_ref[...].astype(BF), h1, 1, 1).astype(BF).astype(FL)
    half = pairs // 2
    block = jnp.concatenate([tbt[:, :half], tbt[:, half:]], axis=0)
    for idx in range(size):
        tb_ref[idx] = block
    for move in moves:
        move.wait()


def diagonal_block(first, second):
    zero = jnp.zeros(first.shape, first.dtype)
    return jnp.concatenate(
        [
            jnp.concatenate([first, zero], axis=1),
            jnp.concatenate([zero, second], axis=1),
        ],
        axis=0,
    )


def pack_places(dims):
    rows, cols, width, heads, _ = dims
    pairs, lines = rows * cols, heads * cols
    at, places = 0, {}
    for name, tall in (
        ("prob", rows // 2 * lines),
        ("dscore", rows // 2 * lines),
        ("datt", pairs),
        ("u", pairs),
        ("dout2", pairs),
        ("dgate2", pairs),
        ("h2", pairs),
        ("dlog", 2 * cols),
    ):
        places[name] = at
        at += tall
    return places, at


def lane_ramp(width):
    return 1.0 + iota((1, width), 1).astype(FL) / width


def norm_line(small_ref, idx):
    at = small_ref.shape[1] - 8 + idx
    return small_ref[0, at : at + 1, :]


def attention_kernel(
    dims,
    scal_ref,
    tb_ref,
    h1_ref,
    z1_ref,
    wl_ref,
    bins_hbm,
    pb_hbm,
    pb_m_hbm,
    pb_v_hbm,
    head_hbm,
    head_m_hbm,
    head_v_hbm,
    norms_hbm,
    norms_m_hbm,
    norms_v_hbm,
    dtb_ref,
    pack_ref,
    dz2_ref,
    stat_ref,
    kcat_ref,
    qblk_ref,
    pb_ref,
    small_ref,
    vcat_ref,
    bias_ref,
    prob_ref,
    swap_ref,
    bins_ref,
    sems,
):
    rows, cols, width, heads, size = dims
    pairs, lines = rows * cols, heads * cols
    places, _ = pack_places(dims)
    scale = (width // heads) ** (-0.5)
    limit, first_row = scal_ref[0, 0], scal_ref[1, 0]

    def put(name, val):
        pack_ref[places[name] : places[name] + val.shape[0], :] = val

    bins_n = head_hbm.shape[0]
    moves = [(bins_hbm, bins_ref)]
    for idx, (pb, head, norms) in enumerate(
        (
            (pb_hbm, head_hbm, norms_hbm),
            (pb_m_hbm, head_m_hbm, norms_m_hbm),
            (pb_v_hbm, head_v_hbm, norms_v_hbm),
        )
    ):
        moves += [
            (head, small_ref.at[idx, pl.ds(0, bins_n)]),
            (norms, small_ref.at[idx, pl.ds(bins_n, 8)]),
            (pb, pb_ref.at[idx]),
        ]
    moves = fetch(moves, sems)
    w_att = jnp.concatenate([wl_ref[6], wl_ref[7], wl_ref[8], wl_ref[9]], axis=1)
    proj = dot(h1_ref[...], w_att)
    gate2 = jax.nn.sigmoid(proj[:, 3 * width :])
    lane_head = iota((cols, width), 1) // (width // heads)
    zero = jnp.zeros((cols, width), BF)
    for idx in range(rows):
        at, side = idx // 2, idx % 2
        lanes = slice(side * width, (side + 1) * width)
        span = slice(idx * cols, (idx + 1) * cols)
        query = proj[span, :width].astype(BF)
        qblk_ref[at, side * cols : (side + 1) * cols, lanes] = query
        qblk_ref[at, (1 - side) * cols : (2 - side) * cols, lanes] = zero
        for head in range(heads):
            spot = slice(head * cols, (head + 1) * cols)
            keep = lane_head == head
            kcat_ref[at, spot, lanes] = jnp.where(
                keep, proj[span, width : 2 * width], 0.0
            ).astype(BF)
            vcat_ref[at, spot, lanes] = jnp.where(
                keep, proj[span, 2 * width : 3 * width], 0.0
            ).astype(BF)

    for half in range(2):
        for jl in range(2):
            lanes = slice(jl * cols, (jl + 1) * cols)
            got = [
                tb_ref[pl.ds(half * heads + head, size, stride=2 * heads), :][:, lanes]
                for head in range(heads)
            ]
            for duo in range(heads // 2):
                line = jnp.concatenate([got[2 * duo], got[2 * duo + 1]], axis=1)
                bias_ref[duo, pl.ds(2 * half + jl, size, stride=rows), :] = line
                bias_ref[duo, pl.ds(cols + 2 * half + jl, size, stride=rows), :] = line
    bias = jnp.concatenate([bias_ref[duo].T for duo in range(heads // 2)], axis=0)
    key_ok = iota((lines, 2 * cols), 0) % cols < limit
    att = []
    for at in range(rows // 2):
        score = dot(kcat_ref[at], qblk_ref[at], 1, 1) * scale + bias
        score = jnp.where(key_ok, score, -1000000000.0).reshape(heads, cols, 2 * cols)
        top = jnp.max(score, axis=1, keepdims=True)
        grown = jnp.exp(score - top)
        prob = (grown / jnp.sum(grown, axis=1, keepdims=True)).reshape(lines, 2 * cols)
        prob_ref[at] = prob
        low = prob.astype(BF)
        pack_ref[places["prob"] + at * lines : places["prob"] + (at + 1) * lines, :] = low
        both = dot(low, vcat_ref[at], 0, 0)
        att += [both[:cols, :width], both[cols:, width:]]
    att = jnp.concatenate(att, axis=0)
    u_low = (gate2 * att).astype(BF)
    put("u", u_low)
    z2 = z1_ref[...] + dot(u_low, wl_ref[10])
    for move in moves[:3]:
        move.wait()
    h2, unit6, rstd6 = row_norm(z2, norm_line(small_ref, 6), norm_line(small_ref, 7))
    put("h2", h2)
    headt = small_ref[0, :bins_n, :].astype(BF)
    logits = dot(headt, h2, 1, 1)
    spot = iota((1, pairs), 1)
    ok = jnp.logical_and(spot % cols < limit, spot // cols + first_row < limit)
    mask = jnp.where(ok, 1.0, 0.0).astype(FL)
    bins = jnp.concatenate([bins_ref[idx : idx + 1, :] for idx in range(rows)], axis=1)
    onehot = jnp.where(iota(logits.shape, 0) == bins, 1.0, 0.0).astype(FL)
    top = jnp.max(logits, axis=0, keepdims=True)
    lse = top + jnp.log(jnp.sum(jnp.exp(logits - top), axis=0, keepdims=True))
    pick = jnp.sum(logits * onehot, axis=0, keepdims=True)
    loss = jnp.sum(mask * (lse - pick), axis=1, keepdims=True)
    dlog = (mask * (jnp.exp(logits - lse) - onehot)).astype(BF)
    put("dlog", jnp.concatenate([dlog[:, :width], dlog[:, width:]], axis=0))
    dz2, dg6, ds6 = row_norm_back(dot(dlog, headt, 0, 0), unit6, rstd6, norm_line(small_ref, 6))
    dz2_ref[...] = dz2
    stat_ref[0:1, :] = dg6
    stat_ref[1:2, :] = ds6
    used = limit * limit
    ramp = lane_ramp(width)
    stat_ref[2:3, :] = loss * ramp
    stat_ref[3:4, :] = (used // DIGIT).astype(FL) * ramp
    stat_ref[4:5, :] = (used % DIGIT).astype(FL) * ramp
    stat_ref[5:8, :] = jnp.zeros((3, width), FL)
    dout2 = dz2.astype(BF)
    put("dout2", dout2)
    du = dot(dout2, wl_ref[10], 1, 1)
    put("dgate2", (du * att * gate2 * (1.0 - gate2)).astype(BF))
    datt = (du * gate2).astype(BF)
    put("datt", datt)
    total = None
    for at in range(rows // 2):
        first = datt[(2 * at) * cols : (2 * at + 1) * cols]
        second = datt[(2 * at + 1) * cols : (2 * at + 2) * cols]
        block = diagonal_block(first, second)
        dprob = dot(vcat_ref[at], block, 1, 1)
        prob = prob_ref[at]
        inner = jnp.sum((dprob * prob).reshape(heads, cols, 2 * cols), axis=1, keepdims=True)
        dscore = prob.reshape(heads, cols, 2 * cols) * (
            dprob.reshape(heads, cols, 2 * cols) - inner
        )
        low = dscore.reshape(lines, 2 * cols).astype(BF)
        pack_ref[places["dscore"] + at * lines : places["dscore"] + (at + 1) * lines, :] = low
        total = low.astype(FL) if total is None else total + low.astype(FL)
    for duo in range(heads // 2):
        turned = total[duo * 2 * cols : (duo + 1) * 2 * cols].T
        swap_ref[duo] = turned[:cols] + turned[cols:]
    for half in range(2):
        for head in range(heads):
            inside = slice((head % 2) * cols, (head % 2 + 1) * cols)
            line = jnp.concatenate(
                [
                    swap_ref[head // 2, pl.ds(2 * half + jl, size, stride=rows), :][:, inside]
                    for jl in range(2)
                ],
                axis=1,
            )
            dtb_ref[pl.ds(half * heads + head, size, stride=2 * heads), :] = line
    for move in moves[3:]:
        move.wait()


def gradient_kernel(
    dims,
    groups,
    scal_ref,
    dtb_ref,
    pack_ref,
    kcat_ref,
    qblk_ref,
    dz2_ref,
    stat_ref,
    h1_ref,
    x_ref,
    z1_ref,
    small_ref,
    wl_ref,
    pb_ref,
    *refs,
):
    tags = [tag for group in groups for tag in group]
    h0_refs, refs = refs[: len(tags)], refs[len(tags) :]
    count = len(groups)
    side_hbms, fac_hbms, refs = refs[:count], refs[count : 2 * count], refs[2 * count :]
    keep_ref, give_ref, flat_ref, dx_ref, dqkvg_ref, side_ref, fac_ref, sems = refs
    rows, cols, width, heads, size = dims
    pairs = rows * cols
    core = scal_ref[3, 0]
    moves, at = [], 0
    for group, side_hbm, fac_hbm in zip(groups, side_hbms, fac_hbms):
        span = pl.ds(at, len(group))
        moves += [(side_hbm, side_ref.at[span]), (fac_hbm, fac_ref.at[span])]
        at += len(group)
    moves = fetch(moves, sems)
    lines = heads * cols
    places, _ = pack_places(dims)

    def take(name, tall, skip=0):
        return pack_ref[places[name] + skip : places[name] + skip + tall, :]

    mask = pair_mask(dims, scal_ref[0, 0])(scal_ref[1, 0])
    side, fac, gate = own_sides(h0_refs[0][...], wl_ref, mask)
    a_val = side.astype(BF).astype(FL)
    y_low, unit2, rstd2 = row_norm(x_ref[...], norm_line(small_ref, 2), norm_line(small_ref, 3))
    _, unit4, rstd4 = row_norm(z1_ref[...], norm_line(small_ref, 4), norm_line(small_ref, 5))
    out1 = dot(y_low, wl_ref[5])
    scale = (width // heads) ** (-0.5)
    lane_head = iota((cols, width), 1) // (width // heads)

    def diagonal(val):
        out = jnp.zeros((cols, width), FL)
        for head in range(heads):
            out = jnp.where(lane_head == head, val[head * cols : (head + 1) * cols], out)
        return out

    for at in range(rows // 2):
        dscore = take("dscore", lines, at * lines)
        block = diagonal_block(
            take("datt", cols, 2 * at * cols), take("datt", cols, (2 * at + 1) * cols)
        )
        dquery = dot(dscore, kcat_ref[at], 0, 0)
        dkeys = dot(dscore, qblk_ref[at])
        dvals = dot(take("prob", lines, at * lines), block)
        for side in range(2):
            idx = 2 * at + side
            lanes = slice(side * width, (side + 1) * width)
            span = slice(idx * cols, (idx + 1) * cols)
            dqkvg_ref[span, :width] = (
                dquery[side * cols : (side + 1) * cols, lanes] * scale
            ).astype(BF)
            dqkvg_ref[span, width : 2 * width] = (diagonal(dkeys[:, lanes]) * scale).astype(BF)
            dqkvg_ref[span, 2 * width : 3 * width] = diagonal(dvals[:, lanes]).astype(BF)
    dqkvg_ref[:, 3 * width :] = take("dgate2", pairs)
    dqkvg = dqkvg_ref[...]
    w_att = jnp.concatenate([wl_ref[6], wl_ref[7], wl_ref[8], wl_ref[9]], axis=1)
    dh1 = dot(dqkvg, w_att, 1, 1)
    h1 = h1_ref[...]
    dw_att = dot(h1, dqkvg, 0, 0)
    for idx in range(4):
        flat_ref[(6 + idx) * width : (7 + idx) * width, :] = dw_att[
            :, idx * width : (idx + 1) * width
        ]
    flat_ref[10 * width : 11 * width, :] = dot(take("u", pairs), take("dout2", pairs), 0, 0)
    mats = 11 * width
    dlog = take("dlog", 2 * cols)
    dlog = jnp.concatenate([dlog[:cols], dlog[cols:]], axis=1)
    flat_ref[mats : mats + dlog.shape[0], :] = dot(dlog, take("h2", pairs))
    got = dtb_ref[0]
    for idx in range(1, size):
        got = got + dtb_ref[idx]
    dtbt = jnp.concatenate([got[:heads], got[heads:]], axis=1).astype(BF)
    dpbt = dot(dtbt, h1)
    dh1 = dh1 + dot(dtbt, pb_ref[0].astype(BF), 0, 0)
    dn4, dg4, ds4 = row_norm_back(dh1, unit4, rstd4, norm_line(small_ref, 4))
    dz1 = dz2_ref[...] + dn4
    dout1 = (dz1 * gate).astype(BF)
    dgate = dz1 * out1 * gate * (1.0 - gate)
    dx, dg2, ds2 = row_norm_back(dot(dout1, wl_ref[5], 1, 1), unit2, rstd2, norm_line(small_ref, 2))
    dx_ref[...] = dx.astype(BF).astype(FL)

    for move in moves:
        move.wait()
    acc = [jnp.zeros((cols, width), FL)] * rows
    for idx, tag in enumerate(tags):
        first = block_at(scal_ref, tag) * rows
        for row in range(rows):
            b_j = side_ref[idx, row * cols : (row + 1) * cols, :].astype(FL)
            acc = [
                acc[at] + dx_ref[pl.ds(at * cols + first + row, 1), :] * b_j
                for at in range(rows)
            ]
    da = jnp.concatenate(acc, axis=0).astype(BF).astype(FL)
    own = jnp.concatenate(
        [
            (da * fac).astype(BF),
            (da * a_val * (1.0 - fac)).astype(BF),
            dgate.astype(BF),
        ],
        axis=1,
    )
    ones = jnp.ones((16, pairs), BF)

    def products(h0, grads):
        return dot(h0, grads, 0, 0), dot(ones, grads)

    dw_own, sum_own = products(h0_refs[0][...], own)

    a_rows = [a_val[idx * cols : (idx + 1) * cols] for idx in range(rows)]

    dw_b, sum_b = jnp.zeros((width, 2 * width), FL), jnp.zeros((16, 2 * width), FL)
    for idx, tag in enumerate(tags):
        first = block_at(scal_ref, tag) * rows
        lines = []
        for row in range(rows):
            db = dx_ref[pl.ds(first + row, 1), :] * a_rows[0]
            for at in range(1, rows):
                db = db + dx_ref[pl.ds(at * cols + first + row, 1), :] * a_rows[at]
            lines.append(db.astype(BF))
        db = jnp.concatenate(lines, axis=0)
        fac_b = fac_ref[idx]
        grads = jnp.concatenate([db * fac_b, db * (side_ref[idx] * (1.0 - fac_b))], axis=1)
        main, sums = products(h0_refs[idx][...], grads)
        dw_b, sum_b = dw_b + main, sum_b + sums

    parts = [
        (val[:, at * width : (at + 1) * width], sums[:1, at * width : (at + 1) * width])
        for val, sums, at in (
            (dw_own, sum_own, 0),
            (dw_own, sum_own, 1),
            (dw_b, sum_b, 0),
            (dw_b, sum_b, 1),
            (dw_own, sum_own, 2),
        )
    ]
    mixed = jnp.zeros((width, width), FL)
    summed = jnp.zeros((width, width), FL)
    for idx, (part, sums) in enumerate(parts):
        weight = wl_ref[idx].astype(FL)
        flat_ref[idx * width : (idx + 1) * width, :] = part
        mixed = mixed + weight * part
        summed = summed + weight * sums
    ds0 = lane_sums(summed)
    dg0 = (lane_sums(mixed) - norm_line(small_ref, 1) * ds0) / norm_line(small_ref, 0)
    flat_ref[5 * width : 6 * width, :] = dot(y_low, dout1, 0, 0)
    base = mats + dlog.shape[0]
    flat_ref[base : base + heads, :] = dpbt
    flat_ref[base + heads : base + 8, :] = jnp.zeros((8 - heads, width), FL)
    base += 8
    for idx, line in enumerate((dg0, ds0, dg2, ds2, dg4, ds4)):
        flat_ref[base + idx : base + idx + 1, :] = line
    flat_ref[base + 6 : base + 11, :] = stat_ref[0:5, :]
    total = flat_ref.shape[0]
    flat_ref[base + 11 :, :] = jnp.zeros((total - base - 11, width), FL)
    half = total // 2
    keep_ref[...] = flat_ref[pl.ds(pl.multiple_of(core * half, half), half), :]
    give_ref[...] = flat_ref[pl.ds(pl.multiple_of((1 - core) * half, half), half), :]


def update_kernel(
    dims,
    scal_ref,
    mine_ref,
    other_ref,
    mats_ref,
    mats_m_ref,
    mats_v_ref,
    pb_ref,
    small_ref,
    norm_out,
    loss_out,
    count_out,
    mats_m_out,
    mats_v_out,
    mats_out,
    mats_low_out,
    pb_m_out,
    pb_v_out,
    pb_out,
    head_m_out,
    head_v_out,
    head_out,
    norms_m_out,
    norms_v_out,
    norms_out,
    flat_ref,
    scalar_buf,
    small_buf,
    pb_buf,
    m_buf,
    v_buf,
    w_buf,
    low_buf,
    sems,
    small_sems,
):
    rows, cols, width, heads, size = dims
    bins_n = small_ref.shape[1] - 8
    core = scal_ref[3, 0]
    half = mine_ref.shape[0]
    flat_ref[pl.ds(pl.multiple_of(core * half, half), half), :] = mine_ref[...]
    flat_ref[pl.ds(pl.multiple_of((1 - core) * half, half), half), :] = other_ref[...]
    count = mats_ref.shape[0]
    mats = count * width
    base = mats + bins_n
    grads = flat_ref[: base + 16, :]
    square = jnp.sum(grads * grads, axis=0, keepdims=True)
    norm = jnp.sqrt(jnp.sum(square, axis=1, keepdims=True))
    factor = jnp.minimum(1.0, CLIP / norm)
    scalar_buf[0] = norm
    stats = jnp.mean(
        flat_ref[base + 16 : base + 24, :] / lane_ramp(width), axis=1, keepdims=True
    )
    scalar_buf[1] = stats[0:1]
    scalar_buf[2] = (DIGIT * jnp.round(stats[1:2]) + jnp.round(stats[2:3])) / size

    moves = []

    def send(at, idx, buf, out):
        move = pltpu.make_async_copy(buf.at[idx], out.at[idx], sems.at[at, idx])
        move.start()
        moves.append(move)

    def step(weight, grad, first, second):
        return adam(weight, grad * factor, first, second)

    def update_small():
        triples = []
        for at, tall, buf, ref, skip, outs in (
            (mats, bins_n, small_buf, small_ref, 0, (head_m_out, head_v_out, head_out)),
            (base + 8, 8, small_buf, small_ref, bins_n, (norms_m_out, norms_v_out, norms_out)),
            (base, heads, pb_buf, pb_ref, 0, (pb_m_out, pb_v_out, pb_out)),
        ):
            weight, first, second = (ref[idx, skip : skip + tall, :] for idx in range(3))
            now = step(weight, flat_ref[at : at + tall, :], first, second)
            for idx, (val, out) in enumerate(zip(now, outs)):
                buf[idx, skip : skip + tall, :] = val
                triples.append((buf.at[idx, pl.ds(skip, tall)], out))
        triples += [
            (scalar_buf.at[idx], out) for idx, out in enumerate((norm_out, loss_out, count_out))
        ]
        moves.extend(fetch(triples, small_sems))

    for idx in range(count):
        if idx == count // 2:
            update_small()
        m_buf[idx], v_buf[idx], weight = step(
            mats_ref[idx],
            flat_ref[idx * width : (idx + 1) * width, :],
            mats_m_ref[idx],
            mats_v_ref[idx],
        )
        w_buf[idx] = weight
        low_buf[idx] = weight.astype(BF)
        send(0, idx, m_buf, mats_m_out)
        send(1, idx, v_buf, mats_v_out)
        send(2, idx, w_buf, mats_out)
        send(3, idx, low_buf, mats_low_out)
    for move in moves:
        move.wait()


def call(kernel, args, outs, scratch=(), limit=VMEM_LIMIT, flops=10**7):
    spots = {"v": pltpu.VMEM, "h": pltpu.HBM}
    return pl.pallas_call(
        kernel,
        out_shape=[
            pltpu.HBM(shape, kind) if spot == "h" else jax.ShapeDtypeStruct(shape, kind)
            for shape, kind, spot in outs
        ],
        in_specs=[pl.BlockSpec(memory_space=spots[spot]) for _, spot in args],
        out_specs=[pl.BlockSpec(memory_space=spots[spot]) for _, _, spot in outs],
        scratch_shapes=list(scratch),
        compiler_params=pltpu.CompilerParams(vmem_limit_bytes=limit),
        cost_estimate=pl.CostEstimate(flops=flops, bytes_accessed=10**6, transcendentals=0),
    )(
        *(
            pltpu.with_memory_space_constraint(value, pltpu.HBM) if spot == "h" else value
            for value, spot in args
        )
    )


def shrink(val):
    root = jnp.sqrt(jnp.abs(val) * SPAN)
    return jnp.where(val < 0.0, -root, root).astype(jnp.float16)


def grow(root):
    root = root.astype(FL)
    return root * jnp.abs(root) * (1.0 / SPAN)


def same_core_groups(crops, size):
    return [
        [crop * size + idx for crop in range(crops) for idx in range(core, size, 2)]
        for core in range(2)
    ]


def exchange(value, size, flip):
    return lax.ppermute(value, "row", [(idx, idx ^ flip) for idx in range(size)])


def core_swap(value, size):
    return exchange(value, size, 1)


def fast_step(
    crops,
    size,
    pair,
    bins,
    lengths,
    mats,
    mats_m,
    mats_v,
    pbias,
    pbias_m,
    pbias_v,
    head,
    head_m,
    head_v,
    norms,
    norms_m,
    norms_v,
):
    rows, cols, width = pair.shape[1:]
    heads, bins_n = pbias.shape[1], head.shape[1]
    pairs, lines = rows * cols, heads * cols
    dims = (rows, cols, width, heads, size)
    chips = size // 2
    place = lax.axis_index("row")
    scal = jnp.stack([lengths[0], place * rows, place >> 1, place & 1]).astype(jnp.int32)
    scal = jnp.broadcast_to(jnp.pad(scal, (0, 4))[:, None], (8, width))
    start = pair.reshape(pairs, width)
    pbt, headt = pbias.T, head.T

    h0, wl = call(
        start_kernel,
        [(start, "h"), (norms, "h"), (mats, "h")],
        [((pairs, width), BF, "v"), (mats.shape, BF, "v")],
        [
            pltpu.VMEM((pairs, width), FL),
            pltpu.VMEM(norms.shape, FL),
            pltpu.VMEM(mats.shape, FL),
            pltpu.SemaphoreType.DMA((3,)),
        ],
    )
    blocks = {(0, 0): h0}
    half = chips // 2
    blocks[half, 0] = exchange(h0, size, 2 * half)
    for flip in range(1, half):
        blocks[flip, 0] = exchange(h0, size, 2 * flip)
    for flip in range(1, half):
        blocks[half + flip, 0] = exchange(blocks[half, 0], size, 2 * flip)
    for flip in range(half + 1):
        blocks[flip, 1] = core_swap(blocks[flip, 0], size)
    groups = block_groups(chips)
    parts, sides, facs = [], [], []
    for at, tags in enumerate(groups[:-1]):
        shape = (len(tags), pairs, width)
        res = call(
            functools.partial(blocks_kernel, dims, tags),
            [(scal, "v"), (wl, "v")]
            + [(a_val, "v") for _ in range(at)]
            + [(blocks[tag], "v") for tag in tags],
            [((rows, len(tags), rows * 8, width), FL, "v"), (shape, BF, "h"), (shape, BF, "h")]
            + [((pairs, width), FL, "v")] * (2 - 2 * at),
            [pltpu.VMEM(shape, BF), pltpu.VMEM(shape, BF), pltpu.SemaphoreType.DMA((4,))],
            flops=2 * 10**8 * len(tags),
        )
        parts.append(res[0])
        sides.append(res[1])
        facs.append(res[2])
        if at == 0:
            a_val, gate = res[3:]
            late = [blocks[tag] for tag in groups[1]]
            parts[0], *late = lax.optimization_barrier((parts[0], *late))
            for tag, block in zip(groups[1], late):
                blocks[tag] = block
                blocks[tag[0], 1] = core_swap(block, size)
    shape = (len(groups[-1]), pairs, width)
    tb, side, fac, x_val, z1, h1 = call(
        functools.partial(triangle_kernel, dims, groups),
        [
            (scal, "v"),
            (a_val, "v"),
            (gate, "v"),
            (wl, "v"),
            (start, "h"),
            (norms, "h"),
            (pbt, "h"),
        ]
        + [(part, "v") for part in parts]
        + [(blocks[tag], "v") for tag in groups[-1]],
        [
            ((size, 2 * heads, 2 * cols), FL, "v"),
            (shape, BF, "h"),
            (shape, BF, "h"),
            ((pairs, width), FL, "v"),
            ((pairs, width), FL, "v"),
            ((pairs, width), BF, "v"),
        ],
        [
            pltpu.VMEM((pairs, width), FL),
            pltpu.VMEM(norms.shape, FL),
            pltpu.VMEM(pbt.shape, FL),
            pltpu.VMEM(shape, BF),
            pltpu.VMEM(shape, BF),
            pltpu.VMEM((pairs * 8, width), FL),
            pltpu.SemaphoreType.DMA((5,)),
        ],
    )
    sides.append(side)
    facs.append(fac)

    tb_all = lax.all_to_all(tb, "row", 0, 0, tiled=True)
    bias_shape = (size * 2 * heads, 2 * cols)
    small_args = (
        pbt,
        pbias_m.T,
        pbias_v.T,
        headt,
        head_m.T,
        head_v.T,
        norms,
        norms_m,
        norms_v,
    )
    dtb, pack, dz2, stat, kcat, qblk, pb_all, small_all = call(
        functools.partial(attention_kernel, dims),
        [
            (scal, "v"),
            (tb_all.reshape(bias_shape), "v"),
            (h1, "v"),
            (z1, "v"),
            (wl, "v"),
            (bins[0], "h"),
        ]
        + [(value, "h") for value in small_args],
        [
            (bias_shape, FL, "v"),
            ((pack_places(dims)[1], width), BF, "v"),
            ((pairs, width), FL, "v"),
            ((8, width), FL, "v"),
            ((rows // 2, lines, 2 * width), BF, "v"),
            ((rows // 2, 2 * cols, 2 * width), BF, "v"),
            ((3, heads, width), FL, "v"),
            ((3, bins_n + norms.shape[0], width), FL, "v"),
        ],
        [
            pltpu.VMEM((rows // 2, lines, 2 * width), BF),
            pltpu.VMEM((heads // 2, 2 * cols, 2 * cols), FL),
            pltpu.VMEM((rows // 2, lines, 2 * cols), FL),
            pltpu.VMEM((heads // 2, cols, 2 * cols), FL),
            pltpu.VMEM((rows, cols), jnp.int32),
            pltpu.SemaphoreType.DMA((10,)),
        ],
    )

    dtb_all = lax.all_to_all(dtb.reshape(size, 2 * heads, 2 * cols), "row", 0, 0, tiled=True)
    used = mats.shape[0] * width + bins_n + 24
    unit = 8 * crops * size
    total = -(-used // unit) * unit
    keep, give = call(
        functools.partial(gradient_kernel, dims, groups),
        [(scal, "v")]
        + [
            (value, "v")
            for value in (dtb_all, pack, kcat, qblk, dz2, stat, h1, x_val, z1, small_all, wl, pb_all)
        ]
        + [(blocks[tag], "v") for tags in groups for tag in tags]
        + [(value, "h") for value in sides + facs],
        [((total // 2, width), FL, "v"), ((total // 2, width), FL, "v")],
        [
            pltpu.VMEM((total, width), FL),
            pltpu.VMEM((pairs, width), FL),
            pltpu.VMEM((pairs, 4 * width), BF),
        ]
        + [pltpu.VMEM((size, pairs, width), BF)] * 2
        + [pltpu.SemaphoreType.DMA((2 * len(groups),))],
    )

    half = keep + core_swap(give, size)
    count = crops * chips
    cores = same_core_groups(crops, size)
    axes = ("crop", "row")
    parts = lax.all_to_all(
        shrink(half).reshape(count, -1, width), axes, 0, 0, axis_index_groups=cores, tiled=True
    )
    share = shrink(jnp.sum(grow(parts), axis=0))
    spread = jnp.broadcast_to(share[None], (count,) + share.shape)
    mine = lax.all_to_all(spread, axes, 0, 0, axis_index_groups=cores, tiled=True)
    mine = mine.reshape(total // 2, width)
    other_half = grow(core_swap(mine, size))
    mine = grow(mine)

    number = mats.shape[0]
    big, low = ((number, width, width), FL, "h"), ((number, width, width), BF, "h")
    pb_out, head_out = ((heads, width), FL, "h"), ((bins_n, width), FL, "h")
    norm_out = ((norms.shape[0], width), FL, "h")
    res = call(
        functools.partial(update_kernel, dims),
        [(scal, "v")]
        + [
            (value, "v")
            for value in (mine, other_half, mats, mats_m, mats_v, pb_all, small_all)
        ],
        [((1, 1), FL, "h")] * 3
        + [big, big, big, low]
        + [pb_out] * 3
        + [head_out] * 3
        + [norm_out] * 3,
        [
            pltpu.VMEM((total, width), FL),
            pltpu.VMEM((3, 1, 1), FL),
            pltpu.VMEM((3, bins_n + norms.shape[0], width), FL),
            pltpu.VMEM((3, heads, width), FL),
        ]
        + [pltpu.VMEM((number, width, width), FL)] * 3
        + [
            pltpu.VMEM((number, width, width), BF),
            pltpu.SemaphoreType.DMA((4, number)),
            pltpu.SemaphoreType.DMA((12,)),
        ],
    )
    return (
        *(value.reshape(()) for value in res[:3]),
        *res[3:7],
        *(value.T for value in res[7:13]),
        *res[13:16],
    )


def small_enough(pair, heads, size):
    _, rows, cols, width = pair.shape
    held = 4 * size * rows * cols * width * 4 + 4 * rows * heads * cols * cols * 4
    return (
        held <= 2**24
        and width == 2 * cols
        and rows == 4
        and heads == 4
        and size >= 4
        and size & (size - 1) == 0
        and rows * size == cols
    )


def solution(mesh):
    crops, size = mesh.shape["crop"], mesh.shape["row"]

    def on_device(*args):
        if small_enough(args[0], args[6].shape[1], size):
            return fast_step(crops, size, *args)
        return general_step(*args)

    in_specs = (
        P("crop", "row", None, None),
        P("crop", "row", None),
        P("crop"),
        P(),
        P(),
        P(),
        P(),
        P(),
        P(),
        P(),
        P(),
        P(),
        P(),
        P(),
        P(),
    )
    out_specs = (P(), P(), P(), P(), P(), P(), P(), P(), P(), P(), P(), P(), P(), P(), P(), P())
    return jax.shard_map(
        on_device, mesh=mesh, in_specs=in_specs, out_specs=out_specs, check_vma=False
    )
```

```python
import functools

import jax
import jax.numpy as jnp
from jax import lax
from jax.experimental import pallas as pl
from jax.experimental.pallas import tpu as pltpu
from jax.sharding import PartitionSpec as P

STEP = 5


EPS_NORM = 1e-05
CLIP = 1.0
RATE = 0.05
BETA1 = 0.9
BETA2 = 0.95
ADAM_EPS = 1e-08
WDECAY = 0.01


def norm_fwd(v, gain, shift):
    mean = jnp.mean(v, axis=-1, keepdims=True)
    cent = v - mean
    rstd = lax.rsqrt(jnp.mean(cent * cent, axis=-1, keepdims=True) + EPS_NORM)
    unit = cent * rstd
    return (unit * gain + shift, unit, rstd)


def norm_back(grad, unit, rstd, gain):
    dgain = jnp.sum(grad * unit, axis=(0, 1))
    dshift = jnp.sum(grad, axis=(0, 1))
    dunit = grad * gain
    dval = rstd * (
        dunit
        - jnp.mean(dunit, axis=-1, keepdims=True)
        - unit * jnp.mean(dunit * unit, axis=-1, keepdims=True)
    )
    return (dval, dgain, dshift)


def matmul(value, weight):
    flat = value.reshape(-1, value.shape[-1])
    out = jnp.dot(flat, weight, preferred_element_type=jnp.float32)
    return out.reshape(value.shape[:-1] + (weight.shape[1],))


def wgrad(value, grad):
    return jnp.einsum("ijc,ijd->cd", value, grad, preferred_element_type=jnp.float32)


def adam(weight, grad, first, second):
    first_new = BETA1 * first + (1.0 - BETA1) * grad
    second_new = BETA2 * second + (1.0 - BETA2) * grad * grad
    m_hat = first_new / (1.0 - BETA1**STEP)
    v_hat = second_new / (1.0 - BETA2**STEP)
    weight_new = weight - RATE * (m_hat / (jnp.sqrt(v_hat) + ADAM_EPS) + WDECAY * weight)
    return (first_new, second_new, weight_new)


def general_step(
    pair,
    bins,
    lengths,
    mats,
    mats_m,
    mats_v,
    pbias,
    pbias_m,
    pbias_v,
    head,
    head_m,
    head_v,
    norms,
    norms_m,
    norms_v,
):
    bf = jnp.bfloat16
    fl = jnp.float32
    width = mats.shape[1]
    rows = pair.shape[1]
    cols = pair.shape[2]
    heads = pbias.shape[1]
    size_head = width // heads
    scale = size_head ** (-0.5)
    start_pair = pair[0]
    first_row = lax.axis_index("row") * rows
    limit = lengths[0]
    row_ok = first_row + jnp.arange(rows) < limit
    col_ok = jnp.arange(cols) < limit
    pmask = (row_ok[:, None] & col_ok[None, :]).astype(fl)
    m3 = pmask[..., None]
    wl = mats.astype(bf)
    pl = pbias.astype(bf)
    hl = head.astype(bf)
    w_tri = jnp.concatenate([wl[0], wl[1], wl[2], wl[3], wl[4]], axis=1)
    w_att = jnp.concatenate([wl[6], wl[7], wl[8], wl[9]], axis=1)
    h0, unit0, rstd0 = norm_fwd(start_pair, norms[0], norms[1])
    h0b = h0.astype(bf)
    proj = matmul(h0b, w_tri)
    sig_a = jax.nn.sigmoid(proj[..., width : 2 * width])
    sig_b = jax.nn.sigmoid(proj[..., 3 * width : 4 * width])
    gate = jax.nn.sigmoid(proj[..., 4 * width :])
    a_low = (sig_a * proj[..., :width] * m3).astype(bf)
    b_low = (sig_b * proj[..., 2 * width : 3 * width] * m3).astype(bf)
    b_all = lax.all_gather(b_low, "row", axis=0, tiled=True)
    prod = jnp.einsum("ikc,jkc->ijc", a_low, b_all, preferred_element_type=fl)
    y_val, unit2, rstd2 = norm_fwd(prod, norms[2], norms[3])
    y_low = y_val.astype(bf)
    out1 = matmul(y_low, wl[5])
    z1 = start_pair + gate * out1
    h1, unit4, rstd4 = norm_fwd(z1, norms[4], norms[5])
    h1b = h1.astype(bf)
    qkvg = matmul(h1b, w_att)
    query = qkvg[..., :width].astype(bf).reshape(rows, cols, heads, size_head)
    keys = qkvg[..., width : 2 * width].astype(bf).reshape(rows, cols, heads, size_head)
    values = qkvg[..., 2 * width : 3 * width].astype(bf).reshape(rows, cols, heads, size_head)
    gate2 = jax.nn.sigmoid(qkvg[..., 3 * width :])
    tb_low = matmul(h1b, pl).astype(bf)
    tb_all = lax.all_gather(tb_low, "row", axis=0, tiled=True)
    tb_heads = jnp.transpose(tb_all, (2, 0, 1)).astype(fl)
    scores = (
        jnp.einsum("ijhd,ikhd->ihjk", query, keys, preferred_element_type=fl) * scale
        + tb_heads[None]
    )
    scores = jnp.where(col_ok[None, None, None, :], scores, -1000000000.0)
    probs = jax.nn.softmax(scores, axis=-1)
    p_low = probs.astype(bf)
    att = jnp.einsum("ihjk,ikhd->ijhd", p_low, values, preferred_element_type=fl).reshape(
        rows, cols, width
    )
    u_low = (gate2 * att).astype(bf)
    z2 = z1 + matmul(u_low, wl[10])
    h2, unit6, rstd6 = norm_fwd(z2, norms[6], norms[7])
    h2b = h2.astype(bf)
    logits = matmul(h2b, hl)
    lse = jax.nn.logsumexp(logits, axis=-1)
    onehot = (bins[0][..., None] == jnp.arange(logits.shape[-1])).astype(fl)
    pick = jnp.sum(logits * onehot, axis=-1)
    loss = jnp.sum(pmask * (lse - pick))
    count = jnp.sum(pmask)
    dlog = (m3 * (jnp.exp(logits - lse[..., None]) - onehot)).astype(bf)
    dhead = wgrad(h2b, dlog)
    dz2, dg6, ds6 = norm_back(matmul(dlog, hl.T), unit6, rstd6, norms[6])
    dout2 = dz2.astype(bf)
    dw10 = wgrad(u_low, dout2)
    du = matmul(dout2, wl[10].T)
    dgate2 = du * att
    datt = (du * gate2).astype(bf).reshape(rows, cols, heads, size_head)
    dprob = jnp.einsum("ijhd,ikhd->ihjk", datt, values, preferred_element_type=fl)
    dvals = jnp.einsum("ihjk,ijhd->ikhd", p_low, datt, preferred_element_type=fl)
    dscore = (probs * (dprob - jnp.sum(dprob * probs, axis=-1, keepdims=True))).astype(bf)
    dquery = jnp.einsum("ihjk,ikhd->ijhd", dscore, keys, preferred_element_type=fl) * scale
    dkeys = jnp.einsum("ihjk,ijhd->ikhd", dscore, query, preferred_element_type=fl) * scale
    dtb = jnp.sum(dscore.astype(fl), axis=0)
    dtb_own = lax.psum_scatter(dtb, "row", scatter_dimension=1, tiled=True)
    dtb_low = jnp.transpose(dtb_own, (1, 2, 0)).astype(bf)
    dpbias = wgrad(h1b, dtb_low)
    dqkvg = jnp.concatenate(
        [
            dquery.reshape(rows, cols, width),
            dkeys.reshape(rows, cols, width),
            dvals.reshape(rows, cols, width),
            dgate2 * gate2 * (1.0 - gate2),
        ],
        axis=-1,
    ).astype(bf)
    dw_att = wgrad(h1b, dqkvg)
    dh1 = matmul(dqkvg, w_att.T) + matmul(dtb_low, pl.T)
    dn4, dg4, ds4 = norm_back(dh1, unit4, rstd4, norms[4])
    dz1 = dz2 + dn4
    dout1 = (dz1 * gate).astype(bf)
    dw5 = wgrad(y_low, dout1)
    dgate = dz1 * out1
    dxn, dg2, ds2 = norm_back(matmul(dout1, wl[5].T), unit2, rstd2, norms[2])
    dx_low = dxn.astype(bf)
    dside_a = jnp.einsum("ijc,jkc->ikc", dx_low, b_all, preferred_element_type=fl)
    dside_b = lax.psum_scatter(
        jnp.einsum("ijc,ikc->jkc", dx_low, a_low, preferred_element_type=fl),
        "row",
        scatter_dimension=0,
        tiled=True,
    )
    da_r = dside_a.astype(bf).astype(fl)
    db_r = dside_b.astype(bf).astype(fl)
    dproj = jnp.concatenate(
        [
            da_r * sig_a * m3,
            da_r * proj[..., :width] * m3 * sig_a * (1.0 - sig_a),
            db_r * sig_b * m3,
            db_r * proj[..., 2 * width : 3 * width] * m3 * sig_b * (1.0 - sig_b),
            dgate * gate * (1.0 - gate),
        ],
        axis=-1,
    ).astype(bf)
    dw_tri = wgrad(h0b, dproj)
    dh0 = matmul(dproj, w_tri.T)
    unused, dg0, ds0 = norm_back(dh0, unit0, rstd0, norms[0])
    pieces = [dw_tri[:, idx * width : (idx + 1) * width] for idx in range(5)]
    pieces = (
        pieces + [dw5] + [dw_att[:, idx * width : (idx + 1) * width] for idx in range(4)] + [dw10]
    )
    dmats = jnp.stack(pieces)
    dnorms = jnp.stack([dg0, ds0, dg2, ds2, dg4, ds4, dg6, ds6])
    dmats, dpbias, dhead, dnorms, loss, count = lax.psum(
        (dmats, dpbias, dhead, dnorms, loss, count), ("crop", "row")
    )
    grad_norm = jnp.sqrt(
        jnp.sum(dmats * dmats)
        + jnp.sum(dpbias * dpbias)
        + jnp.sum(dhead * dhead)
        + jnp.sum(dnorms * dnorms)
    )
    factor = jnp.minimum(1.0, CLIP / grad_norm)
    new_mats = adam(mats, dmats * factor, mats_m, mats_v)
    new_pbias = adam(pbias, dpbias * factor, pbias_m, pbias_v)
    new_head = adam(head, dhead * factor, head_m, head_v)
    new_norms = adam(norms, dnorms * factor, norms_m, norms_v)
    return (
        grad_norm,
        loss,
        count,
        new_mats[0],
        new_mats[1],
        new_mats[2],
        new_mats[2].astype(bf),
        new_pbias[0],
        new_pbias[1],
        new_pbias[2],
        new_head[0],
        new_head[1],
        new_head[2],
        new_norms[0],
        new_norms[1],
        new_norms[2],
    )


BF = jnp.bfloat16
FL = jnp.float32
VMEM_LIMIT = 24 * 2**20
SPAN = 2.0**-12
DIGIT = 64


def dot(lhs, rhs, left=1, right=0):
    return lax.dot_general(
        lhs, rhs, (((left,), (right,)), ((), ())), preferred_element_type=FL
    )


def lane_sums(val):
    return jnp.sum(val.T, axis=0, keepdims=True)


def row_norm(val, gain, shift):
    mean = jnp.mean(val, axis=-1, keepdims=True)
    cent = val - mean
    rstd = lax.rsqrt(jnp.mean(cent * cent, axis=-1, keepdims=True) + EPS_NORM)
    unit = cent * rstd
    return (unit * gain + shift).astype(BF), unit, rstd


def row_norm_back(grad, unit, rstd, gain):
    dgain = jnp.sum(grad * unit, axis=0, keepdims=True)
    dshift = jnp.sum(grad, axis=0, keepdims=True)
    dunit = grad * gain
    dval = rstd * (
        dunit
        - jnp.mean(dunit, axis=-1, keepdims=True)
        - unit * jnp.mean(dunit * unit, axis=-1, keepdims=True)
    )
    return dval, dgain, dshift


def iota(shape, dim):
    return lax.broadcasted_iota(jnp.int32, shape, dim)


def fetch(pairs, sems):
    moves = [
        pltpu.make_async_copy(src, dst, sems.at[idx]) for idx, (src, dst) in enumerate(pairs)
    ]
    for move in moves:
        move.start()
    return moves


def start_kernel(
    pair_hbm, norms_hbm, mats_hbm, h0_ref, wl_ref, pair_ref, norms_ref, mats_ref, sems
):
    moves = fetch(
        [(pair_hbm, pair_ref), (norms_hbm, norms_ref), (mats_hbm, mats_ref)], sems
    )
    moves[0].wait()
    moves[1].wait()
    h0_ref[...], _, _ = row_norm(pair_ref[...], norms_ref[0:1], norms_ref[1:2])
    moves[2].wait()
    wl_ref[...] = mats_ref[...].astype(BF)


def block_groups(chips):
    half = chips // 2
    late = [flip for flip in range(chips) if flip % half]
    return (
        [(flip, other) for other in range(2) for flip in (0, half)],
        [(flip, 0) for flip in late],
        [(flip, 1) for flip in late],
    )


def block_at(scal_ref, tag):
    core = scal_ref[3, 0]
    return 2 * (scal_ref[2, 0] ^ tag[0]) + (1 - core if tag[1] else core)


def pair_mask(dims, limit):
    rows, cols, width, _, _ = dims
    spot = iota((rows * cols, width), 0)
    col_ok = spot % cols < limit
    row_in = spot // cols

    def mask_of(block_row):
        return jnp.where(jnp.logical_and(col_ok, row_in + block_row < limit), 1.0, 0.0).astype(FL)

    return mask_of


def own_sides(h0, wl_ref, mask):
    width = h0.shape[1]
    w_own = jnp.concatenate([wl_ref[0], wl_ref[1], wl_ref[4]], axis=1)
    proj = dot(h0, w_own)
    fac = jax.nn.sigmoid(proj[:, width : 2 * width]) * mask
    return fac * proj[:, :width], fac, jax.nn.sigmoid(proj[:, 2 * width :])


def b_block(dims, h0, w_b, col_mask, start, limit):
    rows, cols, width, _, _ = dims
    proj = dot(h0, w_b)
    sig = jax.nn.sigmoid(proj[:, width:])
    lines = []
    for row in range(rows):
        row_ok = jnp.where(start + row < limit, 1.0, 0.0).astype(FL)
        lines.append(sig[row * cols : (row + 1) * cols] * (col_mask * row_ok))
    fac = jnp.concatenate(lines, axis=0)
    return (fac * proj[:, :width]).astype(BF), fac.astype(BF)


def col_mask_of(dims, limit):
    _, cols, width, _, _ = dims
    return jnp.where(iota((cols, width), 0) < limit, 1.0, 0.0).astype(FL)


def x_products(dims, a_rows, side, put):
    rows, cols, width, _, _ = dims
    for row in range(rows):
        b_j = side[row * cols : (row + 1) * cols].astype(FL)
        for idx in range(rows):
            put(idx, row, jnp.sum((a_rows[idx] * b_j).reshape(cols // 8, 8, width), axis=0))


def blocks_kernel(dims, tags, scal_ref, wl_ref, *refs):
    first = tags[0] == (0, 0)
    if not first:
        a_ref, *refs = refs
    h0_refs, refs = refs[: len(tags)], refs[len(tags) :]
    part_ref, side_hbm, fac_hbm, *refs = refs
    if first:
        a_ref, gate_ref, *refs = refs
    side_ref, fac_ref, sems = refs
    rows, cols, width, heads, size = dims
    limit = scal_ref[0, 0]
    if first:
        mask = pair_mask(dims, limit)(scal_ref[1, 0])
        side, _, gate_ref[...] = own_sides(h0_refs[0][...], wl_ref, mask)
        a_ref[...] = side.astype(BF).astype(FL)
    a_rows = [a_ref[idx * cols : (idx + 1) * cols, :] for idx in range(rows)]
    col_mask = col_mask_of(dims, limit)
    w_b = jnp.concatenate([wl_ref[2], wl_ref[3]], axis=1)
    for idx, tag in enumerate(tags):
        start = block_at(scal_ref, tag) * rows
        side, fac = b_block(dims, h0_refs[idx][...], w_b, col_mask, start, limit)
        side_ref[idx] = side
        fac_ref[idx] = fac

        def put(at, row, fold, idx=idx):
            part_ref[at, idx, row * 8 : (row + 1) * 8, :] = fold

        x_products(dims, a_rows, side, put)
        if idx == len(tags) // 2:
            span = pl.ds(0, idx + 1)
            moves = fetch(
                [(side_ref.at[span], side_hbm.at[span]), (fac_ref.at[span], fac_hbm.at[span])],
                sems.at[pl.ds(0, 2)],
            )
    span = pl.ds(len(tags) // 2 + 1, len(tags) - len(tags) // 2 - 1)
    moves += fetch(
        [(side_ref.at[span], side_hbm.at[span]), (fac_ref.at[span], fac_hbm.at[span])],
        sems.at[pl.ds(2, 2)],
    )
    for move in moves:
        move.wait()


def triangle_kernel(
    dims, groups, scal_ref, a_ref, gate_ref, wl_ref, pair_hbm, norms_hbm, pbt_hbm, *refs
):
    tags, before = groups[-1], groups[:-1]
    part_refs, refs = refs[: len(before)], refs[len(before) :]
    h0_refs, refs = refs[: len(tags)], refs[len(tags) :]
    tb_ref, side_hbm, fac_hbm, x_ref, z1_ref, h1_ref, *refs = refs
    pair_ref, norms_ref, pbt_ref, side_ref, fac_ref, part_ref, sems = refs
    rows, cols, width, heads, size = dims
    pairs = rows * cols
    limit = scal_ref[0, 0]
    early_moves = fetch(
        [(norms_hbm, norms_ref), (pair_hbm, pair_ref), (pbt_hbm, pbt_ref)],
        sems.at[pl.ds(0, 3)],
    )
    col_mask = col_mask_of(dims, limit)
    w_b = jnp.concatenate([wl_ref[2], wl_ref[3]], axis=1)
    a_rows = [a_ref[idx * cols : (idx + 1) * cols, :] for idx in range(rows)]

    for idx, tag in enumerate(tags):
        block = block_at(scal_ref, tag)
        side, fac = b_block(dims, h0_refs[idx][...], w_b, col_mask, block * rows, limit)
        side_ref[idx] = side
        fac_ref[idx] = fac

        def put(at, row, fold, block=block):
            start = pl.multiple_of((at * cols + block * rows + row) * 8, 8)
            part_ref[pl.ds(start, 8), :] = fold

        x_products(dims, a_rows, side, put)
    moves = fetch([(side_ref, side_hbm), (fac_ref, fac_hbm)], sems.at[pl.ds(3, 2)])
    for group, ref in zip(before, part_refs):
        for idx, tag in enumerate(group):
            for at in range(rows):
                start = pl.multiple_of(
                    (at * cols + block_at(scal_ref, tag) * rows) * 8, 8 * rows
                )
                part_ref[pl.ds(start, 8 * rows), :] = ref[at, idx]
    x_val = part_ref[pl.ds(0, pairs, stride=8), :]
    for idx in range(1, 8):
        x_val = x_val + part_ref[pl.ds(idx, pairs, stride=8), :]

    x_ref[...] = x_val
    for move in early_moves:
        move.wait()
    y_low, _, _ = row_norm(x_val, norms_ref[2:3], norms_ref[3:4])
    z1 = pair_ref[...] + gate_ref[...] * dot(y_low, wl_ref[5])
    z1_ref[...] = z1
    h1, _, _ = row_norm(z1, norms_ref[4:5], norms_ref[5:6])
    h1_ref[...] = h1
    tbt = dot(pbt_ref[...].astype(BF), h1, 1, 1).astype(BF).astype(FL)
    half = pairs // 2
    block = jnp.concatenate([tbt[:, :half], tbt[:, half:]], axis=0)
    for idx in range(size):
        tb_ref[idx] = block
    for move in moves:
        move.wait()


def diagonal_block(first, second):
    zero = jnp.zeros(first.shape, first.dtype)
    return jnp.concatenate(
        [
            jnp.concatenate([first, zero], axis=1),
            jnp.concatenate([zero, second], axis=1),
        ],
        axis=0,
    )


def pack_places(dims):
    rows, cols, width, heads, _ = dims
    pairs, lines = rows * cols, heads * cols
    at, places = 0, {}
    for name, tall in (
        ("prob", rows // 2 * lines),
        ("dscore", rows // 2 * lines),
        ("datt", pairs),
        ("u", pairs),
        ("dout2", pairs),
        ("dgate2", pairs),
        ("h2", pairs),
        ("dlog", 2 * cols),
    ):
        places[name] = at
        at += tall
    return places, at


def lane_ramp(width):
    return 1.0 + iota((1, width), 1).astype(FL) / width


def norm_line(small_ref, idx):
    at = small_ref.shape[1] - 8 + idx
    return small_ref[0, at : at + 1, :]


def attention_kernel(
    dims,
    scal_ref,
    tb_ref,
    h1_ref,
    z1_ref,
    wl_ref,
    bins_hbm,
    pb_hbm,
    pb_m_hbm,
    pb_v_hbm,
    head_hbm,
    head_m_hbm,
    head_v_hbm,
    norms_hbm,
    norms_m_hbm,
    norms_v_hbm,
    dtb_ref,
    pack_ref,
    dz2_ref,
    stat_ref,
    kcat_ref,
    qblk_ref,
    pb_ref,
    small_ref,
    vcat_ref,
    bias_ref,
    prob_ref,
    swap_ref,
    bins_ref,
    sems,
):
    rows, cols, width, heads, size = dims
    pairs, lines = rows * cols, heads * cols
    places, _ = pack_places(dims)
    scale = (width // heads) ** (-0.5)
    limit, first_row = scal_ref[0, 0], scal_ref[1, 0]

    def put(name, val):
        pack_ref[places[name] : places[name] + val.shape[0], :] = val

    bins_n = head_hbm.shape[0]
    moves = [(bins_hbm, bins_ref)]
    for idx, (pb, head, norms) in enumerate(
        (
            (pb_hbm, head_hbm, norms_hbm),
            (pb_m_hbm, head_m_hbm, norms_m_hbm),
            (pb_v_hbm, head_v_hbm, norms_v_hbm),
        )
    ):
        moves += [
            (head, small_ref.at[idx, pl.ds(0, bins_n)]),
            (norms, small_ref.at[idx, pl.ds(bins_n, 8)]),
            (pb, pb_ref.at[idx]),
        ]
    moves = fetch(moves, sems)
    w_att = jnp.concatenate([wl_ref[6], wl_ref[7], wl_ref[8], wl_ref[9]], axis=1)
    proj = dot(h1_ref[...], w_att)
    gate2 = jax.nn.sigmoid(proj[:, 3 * width :])
    lane_head = iota((cols, width), 1) // (width // heads)
    zero = jnp.zeros((cols, width), BF)
    for idx in range(rows):
        at, side = idx // 2, idx % 2
        lanes = slice(side * width, (side + 1) * width)
        span = slice(idx * cols, (idx + 1) * cols)
        query = proj[span, :width].astype(BF)
        qblk_ref[at, side * cols : (side + 1) * cols, lanes] = query
        qblk_ref[at, (1 - side) * cols : (2 - side) * cols, lanes] = zero
        for head in range(heads):
            spot = slice(head * cols, (head + 1) * cols)
            keep = lane_head == head
            kcat_ref[at, spot, lanes] = jnp.where(
                keep, proj[span, width : 2 * width], 0.0
            ).astype(BF)
            vcat_ref[at, spot, lanes] = jnp.where(
                keep, proj[span, 2 * width : 3 * width], 0.0
            ).astype(BF)

    for half in range(2):
        for jl in range(2):
            lanes = slice(jl * cols, (jl + 1) * cols)
            got = [
                tb_ref[pl.ds(half * heads + head, size, stride=2 * heads), :][:, lanes]
                for head in range(heads)
            ]
            for duo in range(heads // 2):
                line = jnp.concatenate([got[2 * duo], got[2 * duo + 1]], axis=1)
                bias_ref[duo, pl.ds(2 * half + jl, size, stride=rows), :] = line
                bias_ref[duo, pl.ds(cols + 2 * half + jl, size, stride=rows), :] = line
    bias = jnp.concatenate([bias_ref[duo].T for duo in range(heads // 2)], axis=0)
    key_ok = iota((lines, 2 * cols), 0) % cols < limit
    att = []
    for at in range(rows // 2):
        score = dot(kcat_ref[at], qblk_ref[at], 1, 1) * scale + bias
        score = jnp.where(key_ok, score, -1000000000.0).reshape(heads, cols, 2 * cols)
        top = jnp.max(score, axis=1, keepdims=True)
        grown = jnp.exp(score - top)
        prob = (grown / jnp.sum(grown, axis=1, keepdims=True)).reshape(lines, 2 * cols)
        prob_ref[at] = prob
        low = prob.astype(BF)
        pack_ref[places["prob"] + at * lines : places["prob"] + (at + 1) * lines, :] = low
        both = dot(low, vcat_ref[at], 0, 0)
        att += [both[:cols, :width], both[cols:, width:]]
    att = jnp.concatenate(att, axis=0)
    u_low = (gate2 * att).astype(BF)
    put("u", u_low)
    z2 = z1_ref[...] + dot(u_low, wl_ref[10])
    for move in moves[:3]:
        move.wait()
    h2, unit6, rstd6 = row_norm(z2, norm_line(small_ref, 6), norm_line(small_ref, 7))
    put("h2", h2)
    headt = small_ref[0, :bins_n, :].astype(BF)
    logits = dot(headt, h2, 1, 1)
    spot = iota((1, pairs), 1)
    ok = jnp.logical_and(spot % cols < limit, spot // cols + first_row < limit)
    mask = jnp.where(ok, 1.0, 0.0).astype(FL)
    bins = jnp.concatenate([bins_ref[idx : idx + 1, :] for idx in range(rows)], axis=1)
    onehot = jnp.where(iota(logits.shape, 0) == bins, 1.0, 0.0).astype(FL)
    top = jnp.max(logits, axis=0, keepdims=True)
    lse = top + jnp.log(jnp.sum(jnp.exp(logits - top), axis=0, keepdims=True))
    pick = jnp.sum(logits * onehot, axis=0, keepdims=True)
    loss = jnp.sum(mask * (lse - pick), axis=1, keepdims=True)
    dlog = (mask * (jnp.exp(logits - lse) - onehot)).astype(BF)
    put("dlog", jnp.concatenate([dlog[:, :width], dlog[:, width:]], axis=0))
    dz2, dg6, ds6 = row_norm_back(dot(dlog, headt, 0, 0), unit6, rstd6, norm_line(small_ref, 6))
    dz2_ref[...] = dz2
    stat_ref[0:1, :] = dg6
    stat_ref[1:2, :] = ds6
    used = limit * limit
    ramp = lane_ramp(width)
    stat_ref[2:3, :] = loss * ramp
    stat_ref[3:4, :] = (used // DIGIT).astype(FL) * ramp
    stat_ref[4:5, :] = (used % DIGIT).astype(FL) * ramp
    stat_ref[5:8, :] = jnp.zeros((3, width), FL)
    dout2 = dz2.astype(BF)
    put("dout2", dout2)
    du = dot(dout2, wl_ref[10], 1, 1)
    put("dgate2", (du * att * gate2 * (1.0 - gate2)).astype(BF))
    datt = (du * gate2).astype(BF)
    put("datt", datt)
    total = None
    for at in range(rows // 2):
        first = datt[(2 * at) * cols : (2 * at + 1) * cols]
        second = datt[(2 * at + 1) * cols : (2 * at + 2) * cols]
        block = diagonal_block(first, second)
        dprob = dot(vcat_ref[at], block, 1, 1)
        prob = prob_ref[at]
        inner = jnp.sum((dprob * prob).reshape(heads, cols, 2 * cols), axis=1, keepdims=True)
        dscore = prob.reshape(heads, cols, 2 * cols) * (
            dprob.reshape(heads, cols, 2 * cols) - inner
        )
        low = dscore.reshape(lines, 2 * cols).astype(BF)
        pack_ref[places["dscore"] + at * lines : places["dscore"] + (at + 1) * lines, :] = low
        total = low.astype(FL) if total is None else total + low.astype(FL)
    for duo in range(heads // 2):
        turned = total[duo * 2 * cols : (duo + 1) * 2 * cols].T
        swap_ref[duo] = turned[:cols] + turned[cols:]
    for half in range(2):
        for head in range(heads):
            inside = slice((head % 2) * cols, (head % 2 + 1) * cols)
            line = jnp.concatenate(
                [
                    swap_ref[head // 2, pl.ds(2 * half + jl, size, stride=rows), :][:, inside]
                    for jl in range(2)
                ],
                axis=1,
            )
            dtb_ref[pl.ds(half * heads + head, size, stride=2 * heads), :] = line
    for move in moves[3:]:
        move.wait()


def gradient_kernel(
    dims,
    groups,
    scal_ref,
    dtb_ref,
    pack_ref,
    kcat_ref,
    qblk_ref,
    dz2_ref,
    stat_ref,
    h1_ref,
    x_ref,
    z1_ref,
    small_ref,
    wl_ref,
    pb_ref,
    *refs,
):
    tags = [tag for group in groups for tag in group]
    h0_refs, refs = refs[: len(tags)], refs[len(tags) :]
    count = len(groups)
    side_hbms, fac_hbms, refs = refs[:count], refs[count : 2 * count], refs[2 * count :]
    keep_ref, give_ref, flat_ref, dx_ref, dqkvg_ref, side_ref, fac_ref, sems = refs
    rows, cols, width, heads, size = dims
    pairs = rows * cols
    core = scal_ref[3, 0]
    moves = []
    for arrays, ref in ((side_hbms, side_ref), (fac_hbms, fac_ref)):
        at = 0
        for group, array in zip(groups, arrays):
            moves.append((array, ref.at[pl.ds(at, len(group))]))
            at += len(group)
    moves = fetch(moves, sems)
    lines = heads * cols
    places, _ = pack_places(dims)

    def take(name, tall, skip=0):
        return pack_ref[places[name] + skip : places[name] + skip + tall, :]

    mask = pair_mask(dims, scal_ref[0, 0])(scal_ref[1, 0])
    side, fac, gate = own_sides(h0_refs[0][...], wl_ref, mask)
    a_val = side.astype(BF).astype(FL)
    y_low, unit2, rstd2 = row_norm(x_ref[...], norm_line(small_ref, 2), norm_line(small_ref, 3))
    _, unit4, rstd4 = row_norm(z1_ref[...], norm_line(small_ref, 4), norm_line(small_ref, 5))
    out1 = dot(y_low, wl_ref[5])
    scale = (width // heads) ** (-0.5)
    lane_head = iota((cols, width), 1) // (width // heads)

    def diagonal(val):
        out = jnp.zeros((cols, width), FL)
        for head in range(heads):
            out = jnp.where(lane_head == head, val[head * cols : (head + 1) * cols], out)
        return out

    for at in range(rows // 2):
        dscore = take("dscore", lines, at * lines)
        block = diagonal_block(
            take("datt", cols, 2 * at * cols), take("datt", cols, (2 * at + 1) * cols)
        )
        dquery = dot(dscore, kcat_ref[at], 0, 0)
        dkeys = dot(dscore, qblk_ref[at])
        dvals = dot(take("prob", lines, at * lines), block)
        for side in range(2):
            idx = 2 * at + side
            lanes = slice(side * width, (side + 1) * width)
            span = slice(idx * cols, (idx + 1) * cols)
            dqkvg_ref[span, :width] = (
                dquery[side * cols : (side + 1) * cols, lanes] * scale
            ).astype(BF)
            dqkvg_ref[span, width : 2 * width] = (diagonal(dkeys[:, lanes]) * scale).astype(BF)
            dqkvg_ref[span, 2 * width : 3 * width] = diagonal(dvals[:, lanes]).astype(BF)
    dqkvg_ref[:, 3 * width :] = take("dgate2", pairs)
    dqkvg = dqkvg_ref[...]
    w_att = jnp.concatenate([wl_ref[6], wl_ref[7], wl_ref[8], wl_ref[9]], axis=1)
    dh1 = dot(dqkvg, w_att, 1, 1)
    h1 = h1_ref[...]
    dw_att = dot(h1, dqkvg, 0, 0)
    for idx in range(4):
        flat_ref[(6 + idx) * width : (7 + idx) * width, :] = dw_att[
            :, idx * width : (idx + 1) * width
        ]
    flat_ref[10 * width : 11 * width, :] = dot(take("u", pairs), take("dout2", pairs), 0, 0)
    mats = 11 * width
    dlog = take("dlog", 2 * cols)
    dlog = jnp.concatenate([dlog[:cols], dlog[cols:]], axis=1)
    flat_ref[mats : mats + dlog.shape[0], :] = dot(dlog, take("h2", pairs))
    got = dtb_ref[0]
    for idx in range(1, size):
        got = got + dtb_ref[idx]
    dtbt = jnp.concatenate([got[:heads], got[heads:]], axis=1).astype(BF)
    dpbt = dot(dtbt, h1)
    dh1 = dh1 + dot(dtbt, pb_ref[0].astype(BF), 0, 0)
    dn4, dg4, ds4 = row_norm_back(dh1, unit4, rstd4, norm_line(small_ref, 4))
    dz1 = dz2_ref[...] + dn4
    dout1 = (dz1 * gate).astype(BF)
    dgate = dz1 * out1 * gate * (1.0 - gate)
    dx, dg2, ds2 = row_norm_back(dot(dout1, wl_ref[5], 1, 1), unit2, rstd2, norm_line(small_ref, 2))
    dx_ref[...] = dx.astype(BF).astype(FL)

    for move in moves[:count]:
        move.wait()
    acc = [jnp.zeros((cols, width), FL)] * rows
    for idx, tag in enumerate(tags):
        first = block_at(scal_ref, tag) * rows
        for row in range(rows):
            b_j = side_ref[idx, row * cols : (row + 1) * cols, :].astype(FL)
            acc = [
                acc[at] + dx_ref[pl.ds(at * cols + first + row, 1), :] * b_j
                for at in range(rows)
            ]
    da = jnp.concatenate(acc, axis=0).astype(BF).astype(FL)
    own = jnp.concatenate(
        [
            (da * fac).astype(BF),
            (da * a_val * (1.0 - fac)).astype(BF),
            dgate.astype(BF),
        ],
        axis=1,
    )
    for move in moves[count:]:
        move.wait()
    ones = jnp.ones((16, pairs), BF)

    def products(h0, grads):
        return dot(h0, grads, 0, 0), dot(ones, grads)

    dw_own, sum_own = products(h0_refs[0][...], own)

    a_rows = [a_val[idx * cols : (idx + 1) * cols] for idx in range(rows)]

    dw_b, sum_b = jnp.zeros((width, 2 * width), FL), jnp.zeros((16, 2 * width), FL)
    for idx, tag in enumerate(tags):
        first = block_at(scal_ref, tag) * rows
        lines = []
        for row in range(rows):
            db = dx_ref[pl.ds(first + row, 1), :] * a_rows[0]
            for at in range(1, rows):
                db = db + dx_ref[pl.ds(at * cols + first + row, 1), :] * a_rows[at]
            lines.append(db.astype(BF))
        db = jnp.concatenate(lines, axis=0)
        fac_b = fac_ref[idx]
        grads = jnp.concatenate([db * fac_b, db * (side_ref[idx] * (1.0 - fac_b))], axis=1)
        main, sums = products(h0_refs[idx][...], grads)
        dw_b, sum_b = dw_b + main, sum_b + sums

    parts = [
        (val[:, at * width : (at + 1) * width], sums[:1, at * width : (at + 1) * width])
        for val, sums, at in (
            (dw_own, sum_own, 0),
            (dw_own, sum_own, 1),
            (dw_b, sum_b, 0),
            (dw_b, sum_b, 1),
            (dw_own, sum_own, 2),
        )
    ]
    mixed = jnp.zeros((width, width), FL)
    summed = jnp.zeros((width, width), FL)
    for idx, (part, sums) in enumerate(parts):
        weight = wl_ref[idx].astype(FL)
        flat_ref[idx * width : (idx + 1) * width, :] = part
        mixed = mixed + weight * part
        summed = summed + weight * sums
    ds0 = lane_sums(summed)
    dg0 = (lane_sums(mixed) - norm_line(small_ref, 1) * ds0) / norm_line(small_ref, 0)
    flat_ref[5 * width : 6 * width, :] = dot(y_low, dout1, 0, 0)
    base = mats + dlog.shape[0]
    flat_ref[base : base + heads, :] = dpbt
    flat_ref[base + heads : base + 8, :] = jnp.zeros((8 - heads, width), FL)
    base += 8
    for idx, line in enumerate((dg0, ds0, dg2, ds2, dg4, ds4)):
        flat_ref[base + idx : base + idx + 1, :] = line
    flat_ref[base + 6 : base + 11, :] = stat_ref[0:5, :]
    total = flat_ref.shape[0]
    flat_ref[base + 11 :, :] = jnp.zeros((total - base - 11, width), FL)
    half = total // 2
    keep_ref[...] = flat_ref[pl.ds(pl.multiple_of(core * half, half), half), :]
    give_ref[...] = flat_ref[pl.ds(pl.multiple_of((1 - core) * half, half), half), :]


def update_kernel(
    dims,
    scal_ref,
    mine_ref,
    other_ref,
    mats_ref,
    mats_m_ref,
    mats_v_ref,
    pb_ref,
    small_ref,
    norm_out,
    loss_out,
    count_out,
    mats_m_out,
    mats_v_out,
    mats_out,
    mats_low_out,
    pb_m_out,
    pb_v_out,
    pb_out,
    head_m_out,
    head_v_out,
    head_out,
    norms_m_out,
    norms_v_out,
    norms_out,
    flat_ref,
    scalar_buf,
    small_buf,
    pb_buf,
    m_buf,
    v_buf,
    w_buf,
    low_buf,
    sems,
    small_sems,
):
    rows, cols, width, heads, size = dims
    bins_n = small_ref.shape[1] - 8
    core = scal_ref[3, 0]
    half = mine_ref.shape[0]
    flat_ref[pl.ds(pl.multiple_of(core * half, half), half), :] = mine_ref[...]
    flat_ref[pl.ds(pl.multiple_of((1 - core) * half, half), half), :] = other_ref[...]
    count = mats_ref.shape[0]
    mats = count * width
    base = mats + bins_n
    grads = flat_ref[: base + 16, :]
    square = jnp.sum(grads * grads, axis=0, keepdims=True)
    norm = jnp.sqrt(jnp.sum(square, axis=1, keepdims=True))
    factor = jnp.minimum(1.0, CLIP / norm)
    scalar_buf[0] = norm
    stats = jnp.mean(
        flat_ref[base + 16 : base + 24, :] / lane_ramp(width), axis=1, keepdims=True
    )
    scalar_buf[1] = stats[0:1]
    scalar_buf[2] = (DIGIT * jnp.round(stats[1:2]) + jnp.round(stats[2:3])) / size

    moves = []

    def send(at, idx, buf, out):
        move = pltpu.make_async_copy(buf.at[idx], out.at[idx], sems.at[at, idx])
        move.start()
        moves.append(move)

    def step(weight, grad, first, second):
        return adam(weight, grad * factor, first, second)

    def update_small():
        triples = []
        for at, tall, buf, ref, skip, outs in (
            (mats, bins_n, small_buf, small_ref, 0, (head_m_out, head_v_out, head_out)),
            (base + 8, 8, small_buf, small_ref, bins_n, (norms_m_out, norms_v_out, norms_out)),
            (base, heads, pb_buf, pb_ref, 0, (pb_m_out, pb_v_out, pb_out)),
        ):
            weight, first, second = (ref[idx, skip : skip + tall, :] for idx in range(3))
            now = step(weight, flat_ref[at : at + tall, :], first, second)
            for idx, (val, out) in enumerate(zip(now, outs)):
                buf[idx, skip : skip + tall, :] = val
                triples.append((buf.at[idx, pl.ds(skip, tall)], out))
        triples += [
            (scalar_buf.at[idx], out) for idx, out in enumerate((norm_out, loss_out, count_out))
        ]
        moves.extend(fetch(triples, small_sems))

    for idx in range(count):
        if idx == count // 2:
            update_small()
        m_buf[idx], v_buf[idx], weight = step(
            mats_ref[idx],
            flat_ref[idx * width : (idx + 1) * width, :],
            mats_m_ref[idx],
            mats_v_ref[idx],
        )
        w_buf[idx] = weight
        low_buf[idx] = weight.astype(BF)
        send(0, idx, m_buf, mats_m_out)
        send(1, idx, v_buf, mats_v_out)
        send(2, idx, w_buf, mats_out)
        send(3, idx, low_buf, mats_low_out)
    for move in moves:
        move.wait()


def call(kernel, args, outs, scratch=(), limit=VMEM_LIMIT, flops=10**7):
    spots = {"v": pltpu.VMEM, "h": pltpu.HBM}
    return pl.pallas_call(
        kernel,
        out_shape=[
            pltpu.HBM(shape, kind) if spot == "h" else jax.ShapeDtypeStruct(shape, kind)
            for shape, kind, spot in outs
        ],
        in_specs=[pl.BlockSpec(memory_space=spots[spot]) for _, spot in args],
        out_specs=[pl.BlockSpec(memory_space=spots[spot]) for _, _, spot in outs],
        scratch_shapes=list(scratch),
        compiler_params=pltpu.CompilerParams(vmem_limit_bytes=limit),
        cost_estimate=pl.CostEstimate(flops=flops, bytes_accessed=10**6, transcendentals=0),
    )(
        *(
            pltpu.with_memory_space_constraint(value, pltpu.HBM) if spot == "h" else value
            for value, spot in args
        )
    )


def shrink(val):
    root = jnp.sqrt(jnp.abs(val) * SPAN)
    return jnp.where(val < 0.0, -root, root).astype(jnp.float16)


def grow(root):
    root = root.astype(FL)
    return root * jnp.abs(root) * (1.0 / SPAN)


def same_core_groups(crops, size):
    return [
        [crop * size + idx for crop in range(crops) for idx in range(core, size, 2)]
        for core in range(2)
    ]


def exchange(value, size, flip):
    return lax.ppermute(value, "row", [(idx, idx ^ flip) for idx in range(size)])


def core_swap(value, size):
    return exchange(value, size, 1)


def fast_step(
    crops,
    size,
    pair,
    bins,
    lengths,
    mats,
    mats_m,
    mats_v,
    pbias,
    pbias_m,
    pbias_v,
    head,
    head_m,
    head_v,
    norms,
    norms_m,
    norms_v,
):
    rows, cols, width = pair.shape[1:]
    heads, bins_n = pbias.shape[1], head.shape[1]
    pairs, lines = rows * cols, heads * cols
    dims = (rows, cols, width, heads, size)
    chips = size // 2
    place = lax.axis_index("row")
    scal = jnp.stack([lengths[0], place * rows, place >> 1, place & 1]).astype(jnp.int32)
    scal = jnp.broadcast_to(jnp.pad(scal, (0, 4))[:, None], (8, width))
    start = pair.reshape(pairs, width)
    pbt, headt = pbias.T, head.T

    h0, wl = call(
        start_kernel,
        [(start, "h"), (norms, "h"), (mats, "h")],
        [((pairs, width), BF, "v"), (mats.shape, BF, "v")],
        [
            pltpu.VMEM((pairs, width), FL),
            pltpu.VMEM(norms.shape, FL),
            pltpu.VMEM(mats.shape, FL),
            pltpu.SemaphoreType.DMA((3,)),
        ],
    )
    blocks = {(0, 0): h0}
    half = chips // 2
    blocks[half, 0] = exchange(h0, size, 2 * half)
    for flip in range(1, half):
        blocks[flip, 0] = exchange(h0, size, 2 * flip)
    for flip in range(1, half):
        blocks[half + flip, 0] = exchange(blocks[half, 0], size, 2 * flip)
    for flip in (0, half):
        blocks[flip, 1] = core_swap(blocks[flip, 0], size)
    groups = block_groups(chips)
    parts, sides, facs = [], [], []
    for at, tags in enumerate(groups[:-1]):
        shape = (len(tags), pairs, width)
        res = call(
            functools.partial(blocks_kernel, dims, tags),
            [(scal, "v"), (wl, "v")]
            + [(a_val, "v") for _ in range(at)]
            + [(blocks[tag], "v") for tag in tags],
            [((rows, len(tags), rows * 8, width), FL, "v"), (shape, BF, "h"), (shape, BF, "h")]
            + [((pairs, width), FL, "v")] * (2 - 2 * at),
            [pltpu.VMEM(shape, BF), pltpu.VMEM(shape, BF), pltpu.SemaphoreType.DMA((4,))],
            flops=2 * 10**8 * len(tags),
        )
        parts.append(res[0])
        sides.append(res[1])
        facs.append(res[2])
        if at == 0:
            a_val, gate = res[3:]
            for tag in groups[1]:
                blocks[tag[0], 1] = core_swap(blocks[tag], size)
    shape = (len(groups[-1]), pairs, width)
    tb, side, fac, x_val, z1, h1 = call(
        functools.partial(triangle_kernel, dims, groups),
        [
            (scal, "v"),
            (a_val, "v"),
            (gate, "v"),
            (wl, "v"),
            (start, "h"),
            (norms, "h"),
            (pbt, "h"),
        ]
        + [(part, "v") for part in parts]
        + [(blocks[tag], "v") for tag in groups[-1]],
        [
            ((size, 2 * heads, 2 * cols), FL, "v"),
            (shape, BF, "h"),
            (shape, BF, "h"),
            ((pairs, width), FL, "v"),
            ((pairs, width), FL, "v"),
            ((pairs, width), BF, "v"),
        ],
        [
            pltpu.VMEM((pairs, width), FL),
            pltpu.VMEM(norms.shape, FL),
            pltpu.VMEM(pbt.shape, FL),
            pltpu.VMEM(shape, BF),
            pltpu.VMEM(shape, BF),
            pltpu.VMEM((pairs * 8, width), FL),
            pltpu.SemaphoreType.DMA((5,)),
        ],
    )
    sides.append(side)
    facs.append(fac)

    tb_all = lax.all_to_all(tb, "row", 0, 0, tiled=True)
    bias_shape = (size * 2 * heads, 2 * cols)
    small_args = (
        pbt,
        pbias_m.T,
        pbias_v.T,
        headt,
        head_m.T,
        head_v.T,
        norms,
        norms_m,
        norms_v,
    )
    dtb, pack, dz2, stat, kcat, qblk, pb_all, small_all = call(
        functools.partial(attention_kernel, dims),
        [
            (scal, "v"),
            (tb_all.reshape(bias_shape), "v"),
            (h1, "v"),
            (z1, "v"),
            (wl, "v"),
            (bins[0], "h"),
        ]
        + [(value, "h") for value in small_args],
        [
            (bias_shape, FL, "v"),
            ((pack_places(dims)[1], width), BF, "v"),
            ((pairs, width), FL, "v"),
            ((8, width), FL, "v"),
            ((rows // 2, lines, 2 * width), BF, "v"),
            ((rows // 2, 2 * cols, 2 * width), BF, "v"),
            ((3, heads, width), FL, "v"),
            ((3, bins_n + norms.shape[0], width), FL, "v"),
        ],
        [
            pltpu.VMEM((rows // 2, lines, 2 * width), BF),
            pltpu.VMEM((heads // 2, 2 * cols, 2 * cols), FL),
            pltpu.VMEM((rows // 2, lines, 2 * cols), FL),
            pltpu.VMEM((heads // 2, cols, 2 * cols), FL),
            pltpu.VMEM((rows, cols), jnp.int32),
            pltpu.SemaphoreType.DMA((10,)),
        ],
    )

    dtb_all = lax.all_to_all(dtb.reshape(size, 2 * heads, 2 * cols), "row", 0, 0, tiled=True)
    used = mats.shape[0] * width + bins_n + 24
    unit = 8 * crops * size
    total = -(-used // unit) * unit
    keep, give = call(
        functools.partial(gradient_kernel, dims, groups),
        [(scal, "v")]
        + [
            (value, "v")
            for value in (dtb_all, pack, kcat, qblk, dz2, stat, h1, x_val, z1, small_all, wl, pb_all)
        ]
        + [(blocks[tag], "v") for tags in groups for tag in tags]
        + [(value, "h") for value in sides + facs],
        [((total // 2, width), FL, "v"), ((total // 2, width), FL, "v")],
        [
            pltpu.VMEM((total, width), FL),
            pltpu.VMEM((pairs, width), FL),
            pltpu.VMEM((pairs, 4 * width), BF),
        ]
        + [pltpu.VMEM((size, pairs, width), BF)] * 2
        + [pltpu.SemaphoreType.DMA((2 * len(groups),))],
    )

    half = keep + core_swap(give, size)
    count = crops * chips
    cores = same_core_groups(crops, size)
    axes = ("crop", "row")
    parts = lax.all_to_all(
        shrink(half).reshape(count, -1, width), axes, 0, 0, axis_index_groups=cores, tiled=True
    )
    share = shrink(jnp.sum(grow(parts), axis=0))
    spread = jnp.broadcast_to(share[None], (count,) + share.shape)
    mine = lax.all_to_all(spread, axes, 0, 0, axis_index_groups=cores, tiled=True)
    mine = mine.reshape(total // 2, width)
    other_half = grow(core_swap(mine, size))
    mine = grow(mine)

    number = mats.shape[0]
    big, low = ((number, width, width), FL, "h"), ((number, width, width), BF, "h")
    pb_out, head_out = ((heads, width), FL, "h"), ((bins_n, width), FL, "h")
    norm_out = ((norms.shape[0], width), FL, "h")
    res = call(
        functools.partial(update_kernel, dims),
        [(scal, "v")]
        + [
            (value, "v")
            for value in (mine, other_half, mats, mats_m, mats_v, pb_all, small_all)
        ],
        [((1, 1), FL, "h")] * 3
        + [big, big, big, low]
        + [pb_out] * 3
        + [head_out] * 3
        + [norm_out] * 3,
        [
            pltpu.VMEM((total, width), FL),
            pltpu.VMEM((3, 1, 1), FL),
            pltpu.VMEM((3, bins_n + norms.shape[0], width), FL),
            pltpu.VMEM((3, heads, width), FL),
        ]
        + [pltpu.VMEM((number, width, width), FL)] * 3
        + [
            pltpu.VMEM((number, width, width), BF),
            pltpu.SemaphoreType.DMA((4, number)),
            pltpu.SemaphoreType.DMA((12,)),
        ],
    )
    return (
        *(value.reshape(()) for value in res[:3]),
        *res[3:7],
        *(value.T for value in res[7:13]),
        *res[13:16],
    )


def small_enough(pair, heads, size):
    _, rows, cols, width = pair.shape
    held = 4 * size * rows * cols * width * 4 + 4 * rows * heads * cols * cols * 4
    return (
        held <= 2**24
        and width == 2 * cols
        and rows == 4
        and heads == 4
        and size >= 4
        and size & (size - 1) == 0
        and rows * size == cols
    )


def solution(mesh):
    crops, size = mesh.shape["crop"], mesh.shape["row"]

    def on_device(*args):
        if small_enough(args[0], args[6].shape[1], size):
            return fast_step(crops, size, *args)
        return general_step(*args)

    in_specs = (
        P("crop", "row", None, None),
        P("crop", "row", None),
        P("crop"),
        P(),
        P(),
        P(),
        P(),
        P(),
        P(),
        P(),
        P(),
        P(),
        P(),
        P(),
        P(),
    )
    out_specs = (P(), P(), P(), P(), P(), P(), P(), P(), P(), P(), P(), P(), P(), P(), P(), P())
    return jax.shard_map(
        on_device, mesh=mesh, in_specs=in_specs, out_specs=out_specs, check_vma=False
    )
```

```python
import functools

import jax
import jax.numpy as jnp
from jax import lax
from jax.experimental import pallas as pl
from jax.experimental.pallas import tpu as pltpu
from jax.sharding import PartitionSpec as P

STEP = 5


EPS_NORM = 1e-05
CLIP = 1.0
RATE = 0.05
BETA1 = 0.9
BETA2 = 0.95
ADAM_EPS = 1e-08
WDECAY = 0.01


def norm_fwd(v, gain, shift):
    mean = jnp.mean(v, axis=-1, keepdims=True)
    cent = v - mean
    rstd = lax.rsqrt(jnp.mean(cent * cent, axis=-1, keepdims=True) + EPS_NORM)
    unit = cent * rstd
    return (unit * gain + shift, unit, rstd)


def norm_back(grad, unit, rstd, gain):
    dgain = jnp.sum(grad * unit, axis=(0, 1))
    dshift = jnp.sum(grad, axis=(0, 1))
    dunit = grad * gain
    dval = rstd * (
        dunit
        - jnp.mean(dunit, axis=-1, keepdims=True)
        - unit * jnp.mean(dunit * unit, axis=-1, keepdims=True)
    )
    return (dval, dgain, dshift)


def matmul(value, weight):
    flat = value.reshape(-1, value.shape[-1])
    out = jnp.dot(flat, weight, preferred_element_type=jnp.float32)
    return out.reshape(value.shape[:-1] + (weight.shape[1],))


def wgrad(value, grad):
    return jnp.einsum("ijc,ijd->cd", value, grad, preferred_element_type=jnp.float32)


def adam(weight, grad, first, second):
    first_new = BETA1 * first + (1.0 - BETA1) * grad
    second_new = BETA2 * second + (1.0 - BETA2) * grad * grad
    m_hat = first_new / (1.0 - BETA1**STEP)
    v_hat = second_new / (1.0 - BETA2**STEP)
    weight_new = weight - RATE * (m_hat / (jnp.sqrt(v_hat) + ADAM_EPS) + WDECAY * weight)
    return (first_new, second_new, weight_new)


def general_step(
    pair,
    bins,
    lengths,
    mats,
    mats_m,
    mats_v,
    pbias,
    pbias_m,
    pbias_v,
    head,
    head_m,
    head_v,
    norms,
    norms_m,
    norms_v,
):
    bf = jnp.bfloat16
    fl = jnp.float32
    width = mats.shape[1]
    rows = pair.shape[1]
    cols = pair.shape[2]
    heads = pbias.shape[1]
    size_head = width // heads
    scale = size_head ** (-0.5)
    start_pair = pair[0]
    first_row = lax.axis_index("row") * rows
    limit = lengths[0]
    row_ok = first_row + jnp.arange(rows) < limit
    col_ok = jnp.arange(cols) < limit
    pmask = (row_ok[:, None] & col_ok[None, :]).astype(fl)
    m3 = pmask[..., None]
    wl = mats.astype(bf)
    pl = pbias.astype(bf)
    hl = head.astype(bf)
    w_tri = jnp.concatenate([wl[0], wl[1], wl[2], wl[3], wl[4]], axis=1)
    w_att = jnp.concatenate([wl[6], wl[7], wl[8], wl[9]], axis=1)
    h0, unit0, rstd0 = norm_fwd(start_pair, norms[0], norms[1])
    h0b = h0.astype(bf)
    proj = matmul(h0b, w_tri)
    sig_a = jax.nn.sigmoid(proj[..., width : 2 * width])
    sig_b = jax.nn.sigmoid(proj[..., 3 * width : 4 * width])
    gate = jax.nn.sigmoid(proj[..., 4 * width :])
    a_low = (sig_a * proj[..., :width] * m3).astype(bf)
    b_low = (sig_b * proj[..., 2 * width : 3 * width] * m3).astype(bf)
    b_all = lax.all_gather(b_low, "row", axis=0, tiled=True)
    prod = jnp.einsum("ikc,jkc->ijc", a_low, b_all, preferred_element_type=fl)
    y_val, unit2, rstd2 = norm_fwd(prod, norms[2], norms[3])
    y_low = y_val.astype(bf)
    out1 = matmul(y_low, wl[5])
    z1 = start_pair + gate * out1
    h1, unit4, rstd4 = norm_fwd(z1, norms[4], norms[5])
    h1b = h1.astype(bf)
    qkvg = matmul(h1b, w_att)
    query = qkvg[..., :width].astype(bf).reshape(rows, cols, heads, size_head)
    keys = qkvg[..., width : 2 * width].astype(bf).reshape(rows, cols, heads, size_head)
    values = qkvg[..., 2 * width : 3 * width].astype(bf).reshape(rows, cols, heads, size_head)
    gate2 = jax.nn.sigmoid(qkvg[..., 3 * width :])
    tb_low = matmul(h1b, pl).astype(bf)
    tb_all = lax.all_gather(tb_low, "row", axis=0, tiled=True)
    tb_heads = jnp.transpose(tb_all, (2, 0, 1)).astype(fl)
    scores = (
        jnp.einsum("ijhd,ikhd->ihjk", query, keys, preferred_element_type=fl) * scale
        + tb_heads[None]
    )
    scores = jnp.where(col_ok[None, None, None, :], scores, -1000000000.0)
    probs = jax.nn.softmax(scores, axis=-1)
    p_low = probs.astype(bf)
    att = jnp.einsum("ihjk,ikhd->ijhd", p_low, values, preferred_element_type=fl).reshape(
        rows, cols, width
    )
    u_low = (gate2 * att).astype(bf)
    z2 = z1 + matmul(u_low, wl[10])
    h2, unit6, rstd6 = norm_fwd(z2, norms[6], norms[7])
    h2b = h2.astype(bf)
    logits = matmul(h2b, hl)
    lse = jax.nn.logsumexp(logits, axis=-1)
    onehot = (bins[0][..., None] == jnp.arange(logits.shape[-1])).astype(fl)
    pick = jnp.sum(logits * onehot, axis=-1)
    loss = jnp.sum(pmask * (lse - pick))
    count = jnp.sum(pmask)
    dlog = (m3 * (jnp.exp(logits - lse[..., None]) - onehot)).astype(bf)
    dhead = wgrad(h2b, dlog)
    dz2, dg6, ds6 = norm_back(matmul(dlog, hl.T), unit6, rstd6, norms[6])
    dout2 = dz2.astype(bf)
    dw10 = wgrad(u_low, dout2)
    du = matmul(dout2, wl[10].T)
    dgate2 = du * att
    datt = (du * gate2).astype(bf).reshape(rows, cols, heads, size_head)
    dprob = jnp.einsum("ijhd,ikhd->ihjk", datt, values, preferred_element_type=fl)
    dvals = jnp.einsum("ihjk,ijhd->ikhd", p_low, datt, preferred_element_type=fl)
    dscore = (probs * (dprob - jnp.sum(dprob * probs, axis=-1, keepdims=True))).astype(bf)
    dquery = jnp.einsum("ihjk,ikhd->ijhd", dscore, keys, preferred_element_type=fl) * scale
    dkeys = jnp.einsum("ihjk,ijhd->ikhd", dscore, query, preferred_element_type=fl) * scale
    dtb = jnp.sum(dscore.astype(fl), axis=0)
    dtb_own = lax.psum_scatter(dtb, "row", scatter_dimension=1, tiled=True)
    dtb_low = jnp.transpose(dtb_own, (1, 2, 0)).astype(bf)
    dpbias = wgrad(h1b, dtb_low)
    dqkvg = jnp.concatenate(
        [
            dquery.reshape(rows, cols, width),
            dkeys.reshape(rows, cols, width),
            dvals.reshape(rows, cols, width),
            dgate2 * gate2 * (1.0 - gate2),
        ],
        axis=-1,
    ).astype(bf)
    dw_att = wgrad(h1b, dqkvg)
    dh1 = matmul(dqkvg, w_att.T) + matmul(dtb_low, pl.T)
    dn4, dg4, ds4 = norm_back(dh1, unit4, rstd4, norms[4])
    dz1 = dz2 + dn4
    dout1 = (dz1 * gate).astype(bf)
    dw5 = wgrad(y_low, dout1)
    dgate = dz1 * out1
    dxn, dg2, ds2 = norm_back(matmul(dout1, wl[5].T), unit2, rstd2, norms[2])
    dx_low = dxn.astype(bf)
    dside_a = jnp.einsum("ijc,jkc->ikc", dx_low, b_all, preferred_element_type=fl)
    dside_b = lax.psum_scatter(
        jnp.einsum("ijc,ikc->jkc", dx_low, a_low, preferred_element_type=fl),
        "row",
        scatter_dimension=0,
        tiled=True,
    )
    da_r = dside_a.astype(bf).astype(fl)
    db_r = dside_b.astype(bf).astype(fl)
    dproj = jnp.concatenate(
        [
            da_r * sig_a * m3,
            da_r * proj[..., :width] * m3 * sig_a * (1.0 - sig_a),
            db_r * sig_b * m3,
            db_r * proj[..., 2 * width : 3 * width] * m3 * sig_b * (1.0 - sig_b),
            dgate * gate * (1.0 - gate),
        ],
        axis=-1,
    ).astype(bf)
    dw_tri = wgrad(h0b, dproj)
    dh0 = matmul(dproj, w_tri.T)
    unused, dg0, ds0 = norm_back(dh0, unit0, rstd0, norms[0])
    pieces = [dw_tri[:, idx * width : (idx + 1) * width] for idx in range(5)]
    pieces = (
        pieces + [dw5] + [dw_att[:, idx * width : (idx + 1) * width] for idx in range(4)] + [dw10]
    )
    dmats = jnp.stack(pieces)
    dnorms = jnp.stack([dg0, ds0, dg2, ds2, dg4, ds4, dg6, ds6])
    dmats, dpbias, dhead, dnorms, loss, count = lax.psum(
        (dmats, dpbias, dhead, dnorms, loss, count), ("crop", "row")
    )
    grad_norm = jnp.sqrt(
        jnp.sum(dmats * dmats)
        + jnp.sum(dpbias * dpbias)
        + jnp.sum(dhead * dhead)
        + jnp.sum(dnorms * dnorms)
    )
    factor = jnp.minimum(1.0, CLIP / grad_norm)
    new_mats = adam(mats, dmats * factor, mats_m, mats_v)
    new_pbias = adam(pbias, dpbias * factor, pbias_m, pbias_v)
    new_head = adam(head, dhead * factor, head_m, head_v)
    new_norms = adam(norms, dnorms * factor, norms_m, norms_v)
    return (
        grad_norm,
        loss,
        count,
        new_mats[0],
        new_mats[1],
        new_mats[2],
        new_mats[2].astype(bf),
        new_pbias[0],
        new_pbias[1],
        new_pbias[2],
        new_head[0],
        new_head[1],
        new_head[2],
        new_norms[0],
        new_norms[1],
        new_norms[2],
    )


BF = jnp.bfloat16
FL = jnp.float32
VMEM_LIMIT = 24 * 2**20
SPAN = 2.0**-12
DIGIT = 64


def dot(lhs, rhs, left=1, right=0):
    return lax.dot_general(
        lhs, rhs, (((left,), (right,)), ((), ())), preferred_element_type=FL
    )


def lane_sums(val):
    return jnp.sum(val.T, axis=0, keepdims=True)


def row_norm(val, gain, shift):
    mean = jnp.mean(val, axis=-1, keepdims=True)
    cent = val - mean
    rstd = lax.rsqrt(jnp.mean(cent * cent, axis=-1, keepdims=True) + EPS_NORM)
    unit = cent * rstd
    return (unit * gain + shift).astype(BF), unit, rstd


def row_norm_back(grad, unit, rstd, gain):
    dgain = jnp.sum(grad * unit, axis=0, keepdims=True)
    dshift = jnp.sum(grad, axis=0, keepdims=True)
    dunit = grad * gain
    dval = rstd * (
        dunit
        - jnp.mean(dunit, axis=-1, keepdims=True)
        - unit * jnp.mean(dunit * unit, axis=-1, keepdims=True)
    )
    return dval, dgain, dshift


def iota(shape, dim):
    return lax.broadcasted_iota(jnp.int32, shape, dim)


def fetch(pairs, sems):
    moves = [
        pltpu.make_async_copy(src, dst, sems.at[idx]) for idx, (src, dst) in enumerate(pairs)
    ]
    for move in moves:
        move.start()
    return moves


def start_kernel(
    pair_hbm, norms_hbm, mats_hbm, h0_ref, wl_ref, pair_ref, norms_ref, mats_ref, sems
):
    moves = fetch(
        [(pair_hbm, pair_ref), (norms_hbm, norms_ref), (mats_hbm, mats_ref)], sems
    )
    moves[0].wait()
    moves[1].wait()
    h0_ref[...], _, _ = row_norm(pair_ref[...], norms_ref[0:1], norms_ref[1:2])
    moves[2].wait()
    wl_ref[...] = mats_ref[...].astype(BF)


def block_groups(chips):
    half = chips // 2
    late = [flip for flip in range(chips) if flip % half]
    return (
        [(flip, other) for other in range(2) for flip in (0, half)],
        [(flip, 0) for flip in late],
        [(flip, 1) for flip in late],
    )


def block_at(scal_ref, tag):
    core = scal_ref[3, 0]
    return 2 * (scal_ref[2, 0] ^ tag[0]) + (1 - core if tag[1] else core)


def pair_mask(dims, limit):
    rows, cols, width, _, _ = dims
    spot = iota((rows * cols, width), 0)
    col_ok = spot % cols < limit
    row_in = spot // cols

    def mask_of(block_row):
        return jnp.where(jnp.logical_and(col_ok, row_in + block_row < limit), 1.0, 0.0).astype(FL)

    return mask_of


def own_sides(h0, wl_ref, mask):
    width = h0.shape[1]
    w_own = jnp.concatenate([wl_ref[0], wl_ref[1], wl_ref[4]], axis=1)
    proj = dot(h0, w_own)
    fac = jax.nn.sigmoid(proj[:, width : 2 * width]) * mask
    return fac * proj[:, :width], fac, jax.nn.sigmoid(proj[:, 2 * width :])


def b_block(dims, h0, w_b, col_mask, start, limit):
    rows, cols, width, _, _ = dims
    proj = dot(h0, w_b)
    sig = jax.nn.sigmoid(proj[:, width:])
    lines = []
    for row in range(rows):
        row_ok = jnp.where(start + row < limit, 1.0, 0.0).astype(FL)
        lines.append(sig[row * cols : (row + 1) * cols] * (col_mask * row_ok))
    fac = jnp.concatenate(lines, axis=0)
    return (fac * proj[:, :width]).astype(BF), fac.astype(BF)


def col_mask_of(dims, limit):
    _, cols, width, _, _ = dims
    return jnp.where(iota((cols, width), 0) < limit, 1.0, 0.0).astype(FL)


def x_products(dims, a_rows, side, put):
    rows, cols, width, _, _ = dims
    for row in range(rows):
        b_j = side[row * cols : (row + 1) * cols].astype(FL)
        for idx in range(rows):
            put(idx, row, jnp.sum((a_rows[idx] * b_j).reshape(cols // 8, 8, width), axis=0))


def blocks_kernel(dims, tags, scal_ref, wl_ref, *refs):
    first = tags[0] == (0, 0)
    if not first:
        a_ref, *refs = refs
    h0_refs, refs = refs[: len(tags)], refs[len(tags) :]
    part_ref, side_ref, fac_ref, *refs = refs
    if first:
        a_ref, gate_ref = refs
    rows, cols, width, heads, size = dims
    limit = scal_ref[0, 0]
    if first:
        mask = pair_mask(dims, limit)(scal_ref[1, 0])
        side, _, gate_ref[...] = own_sides(h0_refs[0][...], wl_ref, mask)
        a_ref[...] = side.astype(BF).astype(FL)
    a_rows = [a_ref[idx * cols : (idx + 1) * cols, :] for idx in range(rows)]
    col_mask = col_mask_of(dims, limit)
    w_b = jnp.concatenate([wl_ref[2], wl_ref[3]], axis=1)
    for idx, tag in enumerate(tags):
        start = block_at(scal_ref, tag) * rows
        side, fac = b_block(dims, h0_refs[idx][...], w_b, col_mask, start, limit)
        side_ref[idx] = side
        fac_ref[idx] = fac

        def put(at, row, fold, idx=idx):
            part_ref[at, idx, row * 8 : (row + 1) * 8, :] = fold

        x_products(dims, a_rows, side, put)


def triangle_kernel(
    dims, groups, scal_ref, a_ref, gate_ref, wl_ref, pair_hbm, norms_hbm, pbt_hbm, *refs
):
    tags, before = groups[-1], groups[:-1]
    count = len(before)
    part_refs, side_refs, fac_refs = (refs[at * count : (at + 1) * count] for at in range(3))
    refs = refs[3 * count :]
    h0_refs, refs = refs[: len(tags)], refs[len(tags) :]
    side_hbms, fac_hbms, refs = refs[: count + 1], refs[count + 1 : 2 * count + 2], refs[2 * count + 2 :]
    tb_ref, x_ref, z1_ref, h1_ref, *refs = refs
    pair_ref, norms_ref, pbt_ref, side_ref, fac_ref, part_ref, sems = refs
    rows, cols, width, heads, size = dims
    pairs = rows * cols
    limit = scal_ref[0, 0]
    early_moves = fetch(
        [(norms_hbm, norms_ref), (pair_hbm, pair_ref), (pbt_hbm, pbt_ref)],
        sems.at[pl.ds(0, 3)],
    )
    moves = fetch(
        [*zip(side_refs, side_hbms), *zip(fac_refs, fac_hbms)], sems.at[pl.ds(3, 2 * count)]
    )
    col_mask = col_mask_of(dims, limit)
    w_b = jnp.concatenate([wl_ref[2], wl_ref[3]], axis=1)
    a_rows = [a_ref[idx * cols : (idx + 1) * cols, :] for idx in range(rows)]

    for idx, tag in enumerate(tags):
        block = block_at(scal_ref, tag)
        side, fac = b_block(dims, h0_refs[idx][...], w_b, col_mask, block * rows, limit)
        side_ref[idx] = side
        fac_ref[idx] = fac

        def put(at, row, fold, block=block):
            start = pl.multiple_of((at * cols + block * rows + row) * 8, 8)
            part_ref[pl.ds(start, 8), :] = fold

        x_products(dims, a_rows, side, put)
    moves += fetch(
        [(side_ref, side_hbms[-1]), (fac_ref, fac_hbms[-1])], sems.at[pl.ds(3 + 2 * count, 2)]
    )
    for group, ref in zip(before, part_refs):
        for idx, tag in enumerate(group):
            for at in range(rows):
                start = pl.multiple_of(
                    (at * cols + block_at(scal_ref, tag) * rows) * 8, 8 * rows
                )
                part_ref[pl.ds(start, 8 * rows), :] = ref[at, idx]
    x_val = part_ref[pl.ds(0, pairs, stride=8), :]
    for idx in range(1, 8):
        x_val = x_val + part_ref[pl.ds(idx, pairs, stride=8), :]

    x_ref[...] = x_val
    for move in early_moves:
        move.wait()
    y_low, _, _ = row_norm(x_val, norms_ref[2:3], norms_ref[3:4])
    z1 = pair_ref[...] + gate_ref[...] * dot(y_low, wl_ref[5])
    z1_ref[...] = z1
    h1, _, _ = row_norm(z1, norms_ref[4:5], norms_ref[5:6])
    h1_ref[...] = h1
    tbt = dot(pbt_ref[...].astype(BF), h1, 1, 1).astype(BF).astype(FL)
    half = pairs // 2
    block = jnp.concatenate([tbt[:, :half], tbt[:, half:]], axis=0)
    for idx in range(size):
        tb_ref[idx] = block
    for move in moves:
        move.wait()


def diagonal_block(first, second):
    zero = jnp.zeros(first.shape, first.dtype)
    return jnp.concatenate(
        [
            jnp.concatenate([first, zero], axis=1),
            jnp.concatenate([zero, second], axis=1),
        ],
        axis=0,
    )


def pack_places(dims):
    rows, cols, width, heads, _ = dims
    pairs, lines = rows * cols, heads * cols
    at, places = 0, {}
    for name, tall in (
        ("prob", rows // 2 * lines),
        ("dscore", rows // 2 * lines),
        ("datt", pairs),
        ("u", pairs),
        ("dout2", pairs),
        ("dgate2", pairs),
        ("h2", pairs),
        ("dlog", 2 * cols),
    ):
        places[name] = at
        at += tall
    return places, at


def lane_ramp(width):
    return 1.0 + iota((1, width), 1).astype(FL) / width


def norm_line(small_ref, idx):
    at = small_ref.shape[1] - 8 + idx
    return small_ref[0, at : at + 1, :]


def attention_kernel(
    dims,
    scal_ref,
    tb_ref,
    h1_ref,
    z1_ref,
    wl_ref,
    bins_hbm,
    pb_hbm,
    pb_m_hbm,
    pb_v_hbm,
    head_hbm,
    head_m_hbm,
    head_v_hbm,
    norms_hbm,
    norms_m_hbm,
    norms_v_hbm,
    dtb_ref,
    pack_ref,
    dz2_ref,
    stat_ref,
    kcat_ref,
    qblk_ref,
    pb_ref,
    small_ref,
    vcat_ref,
    bias_ref,
    prob_ref,
    swap_ref,
    bins_ref,
    sems,
):
    rows, cols, width, heads, size = dims
    pairs, lines = rows * cols, heads * cols
    places, _ = pack_places(dims)
    scale = (width // heads) ** (-0.5)
    limit, first_row = scal_ref[0, 0], scal_ref[1, 0]

    def put(name, val):
        pack_ref[places[name] : places[name] + val.shape[0], :] = val

    bins_n = head_hbm.shape[0]
    moves = [(bins_hbm, bins_ref)]
    for idx, (pb, head, norms) in enumerate(
        (
            (pb_hbm, head_hbm, norms_hbm),
            (pb_m_hbm, head_m_hbm, norms_m_hbm),
            (pb_v_hbm, head_v_hbm, norms_v_hbm),
        )
    ):
        moves += [
            (head, small_ref.at[idx, pl.ds(0, bins_n)]),
            (norms, small_ref.at[idx, pl.ds(bins_n, 8)]),
            (pb, pb_ref.at[idx]),
        ]
    moves = fetch(moves, sems)
    w_att = jnp.concatenate([wl_ref[6], wl_ref[7], wl_ref[8], wl_ref[9]], axis=1)
    proj = dot(h1_ref[...], w_att)
    gate2 = jax.nn.sigmoid(proj[:, 3 * width :])
    lane_head = iota((cols, width), 1) // (width // heads)
    zero = jnp.zeros((cols, width), BF)
    for idx in range(rows):
        at, side = idx // 2, idx % 2
        lanes = slice(side * width, (side + 1) * width)
        span = slice(idx * cols, (idx + 1) * cols)
        query = proj[span, :width].astype(BF)
        qblk_ref[at, side * cols : (side + 1) * cols, lanes] = query
        qblk_ref[at, (1 - side) * cols : (2 - side) * cols, lanes] = zero
        for head in range(heads):
            spot = slice(head * cols, (head + 1) * cols)
            keep = lane_head == head
            kcat_ref[at, spot, lanes] = jnp.where(
                keep, proj[span, width : 2 * width], 0.0
            ).astype(BF)
            vcat_ref[at, spot, lanes] = jnp.where(
                keep, proj[span, 2 * width : 3 * width], 0.0
            ).astype(BF)

    for half in range(2):
        for jl in range(2):
            lanes = slice(jl * cols, (jl + 1) * cols)
            got = [
                tb_ref[pl.ds(half * heads + head, size, stride=2 * heads), :][:, lanes]
                for head in range(heads)
            ]
            for duo in range(heads // 2):
                line = jnp.concatenate([got[2 * duo], got[2 * duo + 1]], axis=1)
                bias_ref[duo, pl.ds(2 * half + jl, size, stride=rows), :] = line
                bias_ref[duo, pl.ds(cols + 2 * half + jl, size, stride=rows), :] = line
    bias = jnp.concatenate([bias_ref[duo].T for duo in range(heads // 2)], axis=0)
    key_ok = iota((lines, 2 * cols), 0) % cols < limit
    att = []
    for at in range(rows // 2):
        score = dot(kcat_ref[at], qblk_ref[at], 1, 1) * scale + bias
        score = jnp.where(key_ok, score, -1000000000.0).reshape(heads, cols, 2 * cols)
        top = jnp.max(score, axis=1, keepdims=True)
        grown = jnp.exp(score - top)
        prob = (grown / jnp.sum(grown, axis=1, keepdims=True)).reshape(lines, 2 * cols)
        prob_ref[at] = prob
        low = prob.astype(BF)
        pack_ref[places["prob"] + at * lines : places["prob"] + (at + 1) * lines, :] = low
        both = dot(low, vcat_ref[at], 0, 0)
        att += [both[:cols, :width], both[cols:, width:]]
    att = jnp.concatenate(att, axis=0)
    u_low = (gate2 * att).astype(BF)
    put("u", u_low)
    z2 = z1_ref[...] + dot(u_low, wl_ref[10])
    for move in moves[:3]:
        move.wait()
    h2, unit6, rstd6 = row_norm(z2, norm_line(small_ref, 6), norm_line(small_ref, 7))
    put("h2", h2)
    headt = small_ref[0, :bins_n, :].astype(BF)
    logits = dot(headt, h2, 1, 1)
    spot = iota((1, pairs), 1)
    ok = jnp.logical_and(spot % cols < limit, spot // cols + first_row < limit)
    mask = jnp.where(ok, 1.0, 0.0).astype(FL)
    bins = jnp.concatenate([bins_ref[idx : idx + 1, :] for idx in range(rows)], axis=1)
    onehot = jnp.where(iota(logits.shape, 0) == bins, 1.0, 0.0).astype(FL)
    top = jnp.max(logits, axis=0, keepdims=True)
    lse = top + jnp.log(jnp.sum(jnp.exp(logits - top), axis=0, keepdims=True))
    pick = jnp.sum(logits * onehot, axis=0, keepdims=True)
    loss = jnp.sum(mask * (lse - pick), axis=1, keepdims=True)
    dlog = (mask * (jnp.exp(logits - lse) - onehot)).astype(BF)
    put("dlog", jnp.concatenate([dlog[:, :width], dlog[:, width:]], axis=0))
    dz2, dg6, ds6 = row_norm_back(dot(dlog, headt, 0, 0), unit6, rstd6, norm_line(small_ref, 6))
    dz2_ref[...] = dz2
    stat_ref[0:1, :] = dg6
    stat_ref[1:2, :] = ds6
    used = limit * limit
    ramp = lane_ramp(width)
    stat_ref[2:3, :] = loss * ramp
    stat_ref[3:4, :] = (used // DIGIT).astype(FL) * ramp
    stat_ref[4:5, :] = (used % DIGIT).astype(FL) * ramp
    stat_ref[5:8, :] = jnp.zeros((3, width), FL)
    dout2 = dz2.astype(BF)
    put("dout2", dout2)
    du = dot(dout2, wl_ref[10], 1, 1)
    put("dgate2", (du * att * gate2 * (1.0 - gate2)).astype(BF))
    datt = (du * gate2).astype(BF)
    put("datt", datt)
    total = None
    for at in range(rows // 2):
        first = datt[(2 * at) * cols : (2 * at + 1) * cols]
        second = datt[(2 * at + 1) * cols : (2 * at + 2) * cols]
        block = diagonal_block(first, second)
        dprob = dot(vcat_ref[at], block, 1, 1)
        prob = prob_ref[at]
        inner = jnp.sum((dprob * prob).reshape(heads, cols, 2 * cols), axis=1, keepdims=True)
        dscore = prob.reshape(heads, cols, 2 * cols) * (
            dprob.reshape(heads, cols, 2 * cols) - inner
        )
        low = dscore.reshape(lines, 2 * cols).astype(BF)
        pack_ref[places["dscore"] + at * lines : places["dscore"] + (at + 1) * lines, :] = low
        total = low.astype(FL) if total is None else total + low.astype(FL)
    for duo in range(heads // 2):
        turned = total[duo * 2 * cols : (duo + 1) * 2 * cols].T
        swap_ref[duo] = turned[:cols] + turned[cols:]
    for half in range(2):
        for head in range(heads):
            inside = slice((head % 2) * cols, (head % 2 + 1) * cols)
            line = jnp.concatenate(
                [
                    swap_ref[head // 2, pl.ds(2 * half + jl, size, stride=rows), :][:, inside]
                    for jl in range(2)
                ],
                axis=1,
            )
            dtb_ref[pl.ds(half * heads + head, size, stride=2 * heads), :] = line
    for move in moves[3:]:
        move.wait()


def gradient_kernel(
    dims,
    groups,
    scal_ref,
    dtb_ref,
    pack_ref,
    kcat_ref,
    qblk_ref,
    dz2_ref,
    stat_ref,
    h1_ref,
    x_ref,
    z1_ref,
    small_ref,
    wl_ref,
    pb_ref,
    *refs,
):
    tags = [tag for group in groups for tag in group]
    h0_refs, refs = refs[: len(tags)], refs[len(tags) :]
    count = len(groups)
    side_hbms, fac_hbms, refs = refs[:count], refs[count : 2 * count], refs[2 * count :]
    keep_ref, give_ref, flat_ref, dx_ref, dqkvg_ref, side_ref, fac_ref, sems = refs
    rows, cols, width, heads, size = dims
    pairs = rows * cols
    core = scal_ref[3, 0]
    moves = []
    for arrays, ref in ((side_hbms, side_ref), (fac_hbms, fac_ref)):
        at = 0
        for group, array in zip(groups, arrays):
            moves.append((array, ref.at[pl.ds(at, len(group))]))
            at += len(group)
    moves = fetch(moves, sems)
    lines = heads * cols
    places, _ = pack_places(dims)

    def take(name, tall, skip=0):
        return pack_ref[places[name] + skip : places[name] + skip + tall, :]

    mask = pair_mask(dims, scal_ref[0, 0])(scal_ref[1, 0])
    side, fac, gate = own_sides(h0_refs[0][...], wl_ref, mask)
    a_val = side.astype(BF).astype(FL)
    y_low, unit2, rstd2 = row_norm(x_ref[...], norm_line(small_ref, 2), norm_line(small_ref, 3))
    _, unit4, rstd4 = row_norm(z1_ref[...], norm_line(small_ref, 4), norm_line(small_ref, 5))
    out1 = dot(y_low, wl_ref[5])
    scale = (width // heads) ** (-0.5)
    lane_head = iota((cols, width), 1) // (width // heads)

    def diagonal(val):
        out = jnp.zeros((cols, width), FL)
        for head in range(heads):
            out = jnp.where(lane_head == head, val[head * cols : (head + 1) * cols], out)
        return out

    for at in range(rows // 2):
        dscore = take("dscore", lines, at * lines)
        block = diagonal_block(
            take("datt", cols, 2 * at * cols), take("datt", cols, (2 * at + 1) * cols)
        )
        dquery = dot(dscore, kcat_ref[at], 0, 0)
        dkeys = dot(dscore, qblk_ref[at])
        dvals = dot(take("prob", lines, at * lines), block)
        for side in range(2):
            idx = 2 * at + side
            lanes = slice(side * width, (side + 1) * width)
            span = slice(idx * cols, (idx + 1) * cols)
            dqkvg_ref[span, :width] = (
                dquery[side * cols : (side + 1) * cols, lanes] * scale
            ).astype(BF)
            dqkvg_ref[span, width : 2 * width] = (diagonal(dkeys[:, lanes]) * scale).astype(BF)
            dqkvg_ref[span, 2 * width : 3 * width] = diagonal(dvals[:, lanes]).astype(BF)
    dqkvg_ref[:, 3 * width :] = take("dgate2", pairs)
    dqkvg = dqkvg_ref[...]
    w_att = jnp.concatenate([wl_ref[6], wl_ref[7], wl_ref[8], wl_ref[9]], axis=1)
    dh1 = dot(dqkvg, w_att, 1, 1)
    h1 = h1_ref[...]
    dw_att = dot(h1, dqkvg, 0, 0)
    for idx in range(4):
        flat_ref[(6 + idx) * width : (7 + idx) * width, :] = dw_att[
            :, idx * width : (idx + 1) * width
        ]
    flat_ref[10 * width : 11 * width, :] = dot(take("u", pairs), take("dout2", pairs), 0, 0)
    mats = 11 * width
    dlog = take("dlog", 2 * cols)
    dlog = jnp.concatenate([dlog[:cols], dlog[cols:]], axis=1)
    flat_ref[mats : mats + dlog.shape[0], :] = dot(dlog, take("h2", pairs))
    got = dtb_ref[0]
    for idx in range(1, size):
        got = got + dtb_ref[idx]
    dtbt = jnp.concatenate([got[:heads], got[heads:]], axis=1).astype(BF)
    dpbt = dot(dtbt, h1)
    dh1 = dh1 + dot(dtbt, pb_ref[0].astype(BF), 0, 0)
    dn4, dg4, ds4 = row_norm_back(dh1, unit4, rstd4, norm_line(small_ref, 4))
    dz1 = dz2_ref[...] + dn4
    dout1 = (dz1 * gate).astype(BF)
    dgate = dz1 * out1 * gate * (1.0 - gate)
    dx, dg2, ds2 = row_norm_back(dot(dout1, wl_ref[5], 1, 1), unit2, rstd2, norm_line(small_ref, 2))
    dx_ref[...] = dx.astype(BF).astype(FL)

    for move in moves[:count]:
        move.wait()
    acc = [jnp.zeros((cols, width), FL)] * rows
    for idx, tag in enumerate(tags):
        first = block_at(scal_ref, tag) * rows
        for row in range(rows):
            b_j = side_ref[idx, row * cols : (row + 1) * cols, :].astype(FL)
            acc = [
                acc[at] + dx_ref[pl.ds(at * cols + first + row, 1), :] * b_j
                for at in range(rows)
            ]
    da = jnp.concatenate(acc, axis=0).astype(BF).astype(FL)
    own = jnp.concatenate(
        [
            (da * fac).astype(BF),
            (da * a_val * (1.0 - fac)).astype(BF),
            dgate.astype(BF),
        ],
        axis=1,
    )
    for move in moves[count:]:
        move.wait()
    ones = jnp.ones((16, pairs), BF)

    def products(h0, grads):
        return dot(h0, grads, 0, 0), dot(ones, grads)

    dw_own, sum_own = products(h0_refs[0][...], own)

    a_rows = [a_val[idx * cols : (idx + 1) * cols] for idx in range(rows)]

    dw_b, sum_b = jnp.zeros((width, 2 * width), FL), jnp.zeros((16, 2 * width), FL)
    for idx, tag in enumerate(tags):
        first = block_at(scal_ref, tag) * rows
        lines = []
        for row in range(rows):
            db = dx_ref[pl.ds(first + row, 1), :] * a_rows[0]
            for at in range(1, rows):
                db = db + dx_ref[pl.ds(at * cols + first + row, 1), :] * a_rows[at]
            lines.append(db.astype(BF))
        db = jnp.concatenate(lines, axis=0)
        fac_b = fac_ref[idx]
        grads = jnp.concatenate([db * fac_b, db * (side_ref[idx] * (1.0 - fac_b))], axis=1)
        main, sums = products(h0_refs[idx][...], grads)
        dw_b, sum_b = dw_b + main, sum_b + sums

    parts = [
        (val[:, at * width : (at + 1) * width], sums[:1, at * width : (at + 1) * width])
        for val, sums, at in (
            (dw_own, sum_own, 0),
            (dw_own, sum_own, 1),
            (dw_b, sum_b, 0),
            (dw_b, sum_b, 1),
            (dw_own, sum_own, 2),
        )
    ]
    mixed = jnp.zeros((width, width), FL)
    summed = jnp.zeros((width, width), FL)
    for idx, (part, sums) in enumerate(parts):
        weight = wl_ref[idx].astype(FL)
        flat_ref[idx * width : (idx + 1) * width, :] = part
        mixed = mixed + weight * part
        summed = summed + weight * sums
    ds0 = lane_sums(summed)
    dg0 = (lane_sums(mixed) - norm_line(small_ref, 1) * ds0) / norm_line(small_ref, 0)
    flat_ref[5 * width : 6 * width, :] = dot(y_low, dout1, 0, 0)
    base = mats + dlog.shape[0]
    flat_ref[base : base + heads, :] = dpbt
    flat_ref[base + heads : base + 8, :] = jnp.zeros((8 - heads, width), FL)
    base += 8
    for idx, line in enumerate((dg0, ds0, dg2, ds2, dg4, ds4)):
        flat_ref[base + idx : base + idx + 1, :] = line
    flat_ref[base + 6 : base + 11, :] = stat_ref[0:5, :]
    total = flat_ref.shape[0]
    flat_ref[base + 11 :, :] = jnp.zeros((total - base - 11, width), FL)
    half = total // 2
    keep_ref[...] = flat_ref[pl.ds(pl.multiple_of(core * half, half), half), :]
    give_ref[...] = flat_ref[pl.ds(pl.multiple_of((1 - core) * half, half), half), :]


def update_kernel(
    dims,
    scal_ref,
    mine_ref,
    other_ref,
    mats_ref,
    mats_m_ref,
    mats_v_ref,
    pb_ref,
    small_ref,
    norm_out,
    loss_out,
    count_out,
    mats_m_out,
    mats_v_out,
    mats_out,
    mats_low_out,
    pb_m_out,
    pb_v_out,
    pb_out,
    head_m_out,
    head_v_out,
    head_out,
    norms_m_out,
    norms_v_out,
    norms_out,
    flat_ref,
    scalar_buf,
    small_buf,
    pb_buf,
    m_buf,
    v_buf,
    w_buf,
    low_buf,
    sems,
    small_sems,
):
    rows, cols, width, heads, size = dims
    bins_n = small_ref.shape[1] - 8
    core = scal_ref[3, 0]
    half = mine_ref.shape[0]
    flat_ref[pl.ds(pl.multiple_of(core * half, half), half), :] = mine_ref[...]
    flat_ref[pl.ds(pl.multiple_of((1 - core) * half, half), half), :] = other_ref[...]
    count = mats_ref.shape[0]
    mats = count * width
    base = mats + bins_n
    grads = flat_ref[: base + 16, :]
    square = jnp.sum(grads * grads, axis=0, keepdims=True)
    norm = jnp.sqrt(jnp.sum(square, axis=1, keepdims=True))
    factor = jnp.minimum(1.0, CLIP / norm)
    scalar_buf[0] = norm
    stats = jnp.mean(
        flat_ref[base + 16 : base + 24, :] / lane_ramp(width), axis=1, keepdims=True
    )
    scalar_buf[1] = stats[0:1]
    scalar_buf[2] = (DIGIT * jnp.round(stats[1:2]) + jnp.round(stats[2:3])) / size

    moves = []

    def send(at, idx, buf, out):
        move = pltpu.make_async_copy(buf.at[idx], out.at[idx], sems.at[at, idx])
        move.start()
        moves.append(move)

    def step(weight, grad, first, second):
        return adam(weight, grad * factor, first, second)

    def update_small():
        triples = []
        for at, tall, buf, ref, skip, outs in (
            (mats, bins_n, small_buf, small_ref, 0, (head_m_out, head_v_out, head_out)),
            (base + 8, 8, small_buf, small_ref, bins_n, (norms_m_out, norms_v_out, norms_out)),
            (base, heads, pb_buf, pb_ref, 0, (pb_m_out, pb_v_out, pb_out)),
        ):
            weight, first, second = (ref[idx, skip : skip + tall, :] for idx in range(3))
            now = step(weight, flat_ref[at : at + tall, :], first, second)
            for idx, (val, out) in enumerate(zip(now, outs)):
                buf[idx, skip : skip + tall, :] = val
                triples.append((buf.at[idx, pl.ds(skip, tall)], out))
        triples += [
            (scalar_buf.at[idx], out) for idx, out in enumerate((norm_out, loss_out, count_out))
        ]
        moves.extend(fetch(triples, small_sems))

    for idx in range(count):
        if idx == count // 2:
            update_small()
        m_buf[idx], v_buf[idx], weight = step(
            mats_ref[idx],
            flat_ref[idx * width : (idx + 1) * width, :],
            mats_m_ref[idx],
            mats_v_ref[idx],
        )
        w_buf[idx] = weight
        low_buf[idx] = weight.astype(BF)
        send(0, idx, m_buf, mats_m_out)
        send(1, idx, v_buf, mats_v_out)
        send(2, idx, w_buf, mats_out)
        send(3, idx, low_buf, mats_low_out)
    for move in moves:
        move.wait()


def call(kernel, args, outs, scratch=(), limit=VMEM_LIMIT, flops=10**7):
    spots = {"v": pltpu.VMEM, "h": pltpu.HBM}
    return pl.pallas_call(
        kernel,
        out_shape=[
            pltpu.HBM(shape, kind) if spot == "h" else jax.ShapeDtypeStruct(shape, kind)
            for shape, kind, spot in outs
        ],
        in_specs=[pl.BlockSpec(memory_space=spots[spot]) for _, spot in args],
        out_specs=[pl.BlockSpec(memory_space=spots[spot]) for _, _, spot in outs],
        scratch_shapes=list(scratch),
        compiler_params=pltpu.CompilerParams(vmem_limit_bytes=limit),
        cost_estimate=pl.CostEstimate(flops=flops, bytes_accessed=10**6, transcendentals=0),
    )(
        *(
            pltpu.with_memory_space_constraint(value, pltpu.HBM) if spot == "h" else value
            for value, spot in args
        )
    )


def shrink(val):
    root = jnp.sqrt(jnp.abs(val) * SPAN)
    return jnp.where(val < 0.0, -root, root).astype(jnp.float16)


def grow(root):
    root = root.astype(FL)
    return root * jnp.abs(root) * (1.0 / SPAN)


def same_core_groups(crops, size):
    return [
        [crop * size + idx for crop in range(crops) for idx in range(core, size, 2)]
        for core in range(2)
    ]


def exchange(value, size, flip):
    return lax.ppermute(value, "row", [(idx, idx ^ flip) for idx in range(size)])


def core_swap(value, size):
    return exchange(value, size, 1)


def fast_step(
    crops,
    size,
    pair,
    bins,
    lengths,
    mats,
    mats_m,
    mats_v,
    pbias,
    pbias_m,
    pbias_v,
    head,
    head_m,
    head_v,
    norms,
    norms_m,
    norms_v,
):
    rows, cols, width = pair.shape[1:]
    heads, bins_n = pbias.shape[1], head.shape[1]
    pairs, lines = rows * cols, heads * cols
    dims = (rows, cols, width, heads, size)
    chips = size // 2
    place = lax.axis_index("row")
    scal = jnp.stack([lengths[0], place * rows, place >> 1, place & 1]).astype(jnp.int32)
    scal = jnp.broadcast_to(jnp.pad(scal, (0, 4))[:, None], (8, width))
    start = pair.reshape(pairs, width)
    pbt, headt = pbias.T, head.T

    h0, wl = call(
        start_kernel,
        [(start, "h"), (norms, "h"), (mats, "h")],
        [((pairs, width), BF, "v"), (mats.shape, BF, "v")],
        [
            pltpu.VMEM((pairs, width), FL),
            pltpu.VMEM(norms.shape, FL),
            pltpu.VMEM(mats.shape, FL),
            pltpu.SemaphoreType.DMA((3,)),
        ],
    )
    blocks = {(0, 0): h0}
    half = chips // 2
    blocks[half, 0] = exchange(h0, size, 2 * half)
    for flip in range(1, half):
        blocks[flip, 0] = exchange(h0, size, 2 * flip)
    for flip in range(1, half):
        blocks[half + flip, 0] = exchange(blocks[half, 0], size, 2 * flip)
    for flip in (0, half):
        blocks[flip, 1] = core_swap(blocks[flip, 0], size)
    groups = block_groups(chips)
    parts, sides, facs = [], [], []
    for at, tags in enumerate(groups[:-1]):
        shape = (len(tags), pairs, width)
        res = call(
            functools.partial(blocks_kernel, dims, tags),
            [(scal, "v"), (wl, "v")]
            + [(a_val, "v") for _ in range(at)]
            + [(blocks[tag], "v") for tag in tags],
            [((rows, len(tags), rows * 8, width), FL, "v"), (shape, BF, "v"), (shape, BF, "v")]
            + [((pairs, width), FL, "v")] * (2 - 2 * at),
            flops=10**8 * len(tags),
        )
        parts.append(res[0])
        sides.append(res[1])
        facs.append(res[2])
        if at == 0:
            a_val, gate = res[3:]
            for tag in groups[1]:
                blocks[tag[0], 1] = core_swap(blocks[tag], size)
    shape = (len(groups[-1]), pairs, width)
    count = len(groups)
    *far_sides, tb, x_val, z1, h1 = call(
        functools.partial(triangle_kernel, dims, groups),
        [
            (scal, "v"),
            (a_val, "v"),
            (gate, "v"),
            (wl, "v"),
            (start, "h"),
            (norms, "h"),
            (pbt, "h"),
        ]
        + [(value, "v") for value in parts + sides + facs]
        + [(blocks[tag], "v") for tag in groups[-1]],
        [((len(tags), pairs, width), BF, "h") for tags in groups] * 2
        + [
            ((size, 2 * heads, 2 * cols), FL, "v"),
            ((pairs, width), FL, "v"),
            ((pairs, width), FL, "v"),
            ((pairs, width), BF, "v"),
        ],
        [
            pltpu.VMEM((pairs, width), FL),
            pltpu.VMEM(norms.shape, FL),
            pltpu.VMEM(pbt.shape, FL),
            pltpu.VMEM(shape, BF),
            pltpu.VMEM(shape, BF),
            pltpu.VMEM((pairs * 8, width), FL),
            pltpu.SemaphoreType.DMA((3 + 2 * count,)),
        ],
    )

    tb_all = lax.all_to_all(tb, "row", 0, 0, tiled=True)
    bias_shape = (size * 2 * heads, 2 * cols)
    small_args = (
        pbt,
        pbias_m.T,
        pbias_v.T,
        headt,
        head_m.T,
        head_v.T,
        norms,
        norms_m,
        norms_v,
    )
    dtb, pack, dz2, stat, kcat, qblk, pb_all, small_all = call(
        functools.partial(attention_kernel, dims),
        [
            (scal, "v"),
            (tb_all.reshape(bias_shape), "v"),
            (h1, "v"),
            (z1, "v"),
            (wl, "v"),
            (bins[0], "h"),
        ]
        + [(value, "h") for value in small_args],
        [
            (bias_shape, FL, "v"),
            ((pack_places(dims)[1], width), BF, "v"),
            ((pairs, width), FL, "v"),
            ((8, width), FL, "v"),
            ((rows // 2, lines, 2 * width), BF, "v"),
            ((rows // 2, 2 * cols, 2 * width), BF, "v"),
            ((3, heads, width), FL, "v"),
            ((3, bins_n + norms.shape[0], width), FL, "v"),
        ],
        [
            pltpu.VMEM((rows // 2, lines, 2 * width), BF),
            pltpu.VMEM((heads // 2, 2 * cols, 2 * cols), FL),
            pltpu.VMEM((rows // 2, lines, 2 * cols), FL),
            pltpu.VMEM((heads // 2, cols, 2 * cols), FL),
            pltpu.VMEM((rows, cols), jnp.int32),
            pltpu.SemaphoreType.DMA((10,)),
        ],
    )

    dtb_all = lax.all_to_all(dtb.reshape(size, 2 * heads, 2 * cols), "row", 0, 0, tiled=True)
    used = mats.shape[0] * width + bins_n + 24
    unit = 8 * crops * size
    total = -(-used // unit) * unit
    keep, give = call(
        functools.partial(gradient_kernel, dims, groups),
        [(scal, "v")]
        + [
            (value, "v")
            for value in (dtb_all, pack, kcat, qblk, dz2, stat, h1, x_val, z1, small_all, wl, pb_all)
        ]
        + [(blocks[tag], "v") for tags in groups for tag in tags]
        + [(value, "h") for value in far_sides],
        [((total // 2, width), FL, "v"), ((total // 2, width), FL, "v")],
        [
            pltpu.VMEM((total, width), FL),
            pltpu.VMEM((pairs, width), FL),
            pltpu.VMEM((pairs, 4 * width), BF),
        ]
        + [pltpu.VMEM((size, pairs, width), BF)] * 2
        + [pltpu.SemaphoreType.DMA((2 * len(groups),))],
    )

    half = keep + core_swap(give, size)
    count = crops * chips
    cores = same_core_groups(crops, size)
    axes = ("crop", "row")
    parts = lax.all_to_all(
        shrink(half).reshape(count, -1, width), axes, 0, 0, axis_index_groups=cores, tiled=True
    )
    share = shrink(jnp.sum(grow(parts), axis=0))
    spread = jnp.broadcast_to(share[None], (count,) + share.shape)
    mine = lax.all_to_all(spread, axes, 0, 0, axis_index_groups=cores, tiled=True)
    mine = mine.reshape(total // 2, width)
    other_half = grow(core_swap(mine, size))
    mine = grow(mine)

    number = mats.shape[0]
    big, low = ((number, width, width), FL, "h"), ((number, width, width), BF, "h")
    pb_out, head_out = ((heads, width), FL, "h"), ((bins_n, width), FL, "h")
    norm_out = ((norms.shape[0], width), FL, "h")
    res = call(
        functools.partial(update_kernel, dims),
        [(scal, "v")]
        + [
            (value, "v")
            for value in (mine, other_half, mats, mats_m, mats_v, pb_all, small_all)
        ],
        [((1, 1), FL, "h")] * 3
        + [big, big, big, low]
        + [pb_out] * 3
        + [head_out] * 3
        + [norm_out] * 3,
        [
            pltpu.VMEM((total, width), FL),
            pltpu.VMEM((3, 1, 1), FL),
            pltpu.VMEM((3, bins_n + norms.shape[0], width), FL),
            pltpu.VMEM((3, heads, width), FL),
        ]
        + [pltpu.VMEM((number, width, width), FL)] * 3
        + [
            pltpu.VMEM((number, width, width), BF),
            pltpu.SemaphoreType.DMA((4, number)),
            pltpu.SemaphoreType.DMA((12,)),
        ],
    )
    return (
        *(value.reshape(()) for value in res[:3]),
        *res[3:7],
        *(value.T for value in res[7:13]),
        *res[13:16],
    )


def small_enough(pair, heads, size):
    _, rows, cols, width = pair.shape
    held = 4 * size * rows * cols * width * 4 + 4 * rows * heads * cols * cols * 4
    return (
        held <= 2**24
        and width == 2 * cols
        and rows == 4
        and heads == 4
        and size >= 4
        and size & (size - 1) == 0
        and rows * size == cols
    )


def solution(mesh):
    crops, size = mesh.shape["crop"], mesh.shape["row"]

    def on_device(*args):
        if small_enough(args[0], args[6].shape[1], size):
            return fast_step(crops, size, *args)
        return general_step(*args)

    in_specs = (
        P("crop", "row", None, None),
        P("crop", "row", None),
        P("crop"),
        P(),
        P(),
        P(),
        P(),
        P(),
        P(),
        P(),
        P(),
        P(),
        P(),
        P(),
        P(),
    )
    out_specs = (P(), P(), P(), P(), P(), P(), P(), P(), P(), P(), P(), P(), P(), P(), P(), P())
    return jax.shard_map(
        on_device, mesh=mesh, in_specs=in_specs, out_specs=out_specs, check_vma=False
    )
```

```python
import functools

import jax
import jax.numpy as jnp
from jax import lax
from jax.experimental import pallas as pl
from jax.experimental.pallas import tpu as pltpu
from jax.sharding import PartitionSpec as P

STEP = 5


EPS_NORM = 1e-05
CLIP = 1.0
RATE = 0.05
BETA1 = 0.9
BETA2 = 0.95
ADAM_EPS = 1e-08
WDECAY = 0.01


def norm_fwd(v, gain, shift):
    mean = jnp.mean(v, axis=-1, keepdims=True)
    cent = v - mean
    rstd = lax.rsqrt(jnp.mean(cent * cent, axis=-1, keepdims=True) + EPS_NORM)
    unit = cent * rstd
    return (unit * gain + shift, unit, rstd)


def norm_back(grad, unit, rstd, gain):
    dgain = jnp.sum(grad * unit, axis=(0, 1))
    dshift = jnp.sum(grad, axis=(0, 1))
    dunit = grad * gain
    dval = rstd * (
        dunit
        - jnp.mean(dunit, axis=-1, keepdims=True)
        - unit * jnp.mean(dunit * unit, axis=-1, keepdims=True)
    )
    return (dval, dgain, dshift)


def matmul(value, weight):
    flat = value.reshape(-1, value.shape[-1])
    out = jnp.dot(flat, weight, preferred_element_type=jnp.float32)
    return out.reshape(value.shape[:-1] + (weight.shape[1],))


def wgrad(value, grad):
    return jnp.einsum("ijc,ijd->cd", value, grad, preferred_element_type=jnp.float32)


def adam(weight, grad, first, second):
    first_new = BETA1 * first + (1.0 - BETA1) * grad
    second_new = BETA2 * second + (1.0 - BETA2) * grad * grad
    m_hat = first_new / (1.0 - BETA1**STEP)
    v_hat = second_new / (1.0 - BETA2**STEP)
    weight_new = weight - RATE * (m_hat / (jnp.sqrt(v_hat) + ADAM_EPS) + WDECAY * weight)
    return (first_new, second_new, weight_new)


def general_step(
    pair,
    bins,
    lengths,
    mats,
    mats_m,
    mats_v,
    pbias,
    pbias_m,
    pbias_v,
    head,
    head_m,
    head_v,
    norms,
    norms_m,
    norms_v,
):
    bf = jnp.bfloat16
    fl = jnp.float32
    width = mats.shape[1]
    rows = pair.shape[1]
    cols = pair.shape[2]
    heads = pbias.shape[1]
    size_head = width // heads
    scale = size_head ** (-0.5)
    start_pair = pair[0]
    first_row = lax.axis_index("row") * rows
    limit = lengths[0]
    row_ok = first_row + jnp.arange(rows) < limit
    col_ok = jnp.arange(cols) < limit
    pmask = (row_ok[:, None] & col_ok[None, :]).astype(fl)
    m3 = pmask[..., None]
    wl = mats.astype(bf)
    pl = pbias.astype(bf)
    hl = head.astype(bf)
    w_tri = jnp.concatenate([wl[0], wl[1], wl[2], wl[3], wl[4]], axis=1)
    w_att = jnp.concatenate([wl[6], wl[7], wl[8], wl[9]], axis=1)
    h0, unit0, rstd0 = norm_fwd(start_pair, norms[0], norms[1])
    h0b = h0.astype(bf)
    proj = matmul(h0b, w_tri)
    sig_a = jax.nn.sigmoid(proj[..., width : 2 * width])
    sig_b = jax.nn.sigmoid(proj[..., 3 * width : 4 * width])
    gate = jax.nn.sigmoid(proj[..., 4 * width :])
    a_low = (sig_a * proj[..., :width] * m3).astype(bf)
    b_low = (sig_b * proj[..., 2 * width : 3 * width] * m3).astype(bf)
    b_all = lax.all_gather(b_low, "row", axis=0, tiled=True)
    prod = jnp.einsum("ikc,jkc->ijc", a_low, b_all, preferred_element_type=fl)
    y_val, unit2, rstd2 = norm_fwd(prod, norms[2], norms[3])
    y_low = y_val.astype(bf)
    out1 = matmul(y_low, wl[5])
    z1 = start_pair + gate * out1
    h1, unit4, rstd4 = norm_fwd(z1, norms[4], norms[5])
    h1b = h1.astype(bf)
    qkvg = matmul(h1b, w_att)
    query = qkvg[..., :width].astype(bf).reshape(rows, cols, heads, size_head)
    keys = qkvg[..., width : 2 * width].astype(bf).reshape(rows, cols, heads, size_head)
    values = qkvg[..., 2 * width : 3 * width].astype(bf).reshape(rows, cols, heads, size_head)
    gate2 = jax.nn.sigmoid(qkvg[..., 3 * width :])
    tb_low = matmul(h1b, pl).astype(bf)
    tb_all = lax.all_gather(tb_low, "row", axis=0, tiled=True)
    tb_heads = jnp.transpose(tb_all, (2, 0, 1)).astype(fl)
    scores = (
        jnp.einsum("ijhd,ikhd->ihjk", query, keys, preferred_element_type=fl) * scale
        + tb_heads[None]
    )
    scores = jnp.where(col_ok[None, None, None, :], scores, -1000000000.0)
    probs = jax.nn.softmax(scores, axis=-1)
    p_low = probs.astype(bf)
    att = jnp.einsum("ihjk,ikhd->ijhd", p_low, values, preferred_element_type=fl).reshape(
        rows, cols, width
    )
    u_low = (gate2 * att).astype(bf)
    z2 = z1 + matmul(u_low, wl[10])
    h2, unit6, rstd6 = norm_fwd(z2, norms[6], norms[7])
    h2b = h2.astype(bf)
    logits = matmul(h2b, hl)
    lse = jax.nn.logsumexp(logits, axis=-1)
    onehot = (bins[0][..., None] == jnp.arange(logits.shape[-1])).astype(fl)
    pick = jnp.sum(logits * onehot, axis=-1)
    loss = jnp.sum(pmask * (lse - pick))
    count = jnp.sum(pmask)
    dlog = (m3 * (jnp.exp(logits - lse[..., None]) - onehot)).astype(bf)
    dhead = wgrad(h2b, dlog)
    dz2, dg6, ds6 = norm_back(matmul(dlog, hl.T), unit6, rstd6, norms[6])
    dout2 = dz2.astype(bf)
    dw10 = wgrad(u_low, dout2)
    du = matmul(dout2, wl[10].T)
    dgate2 = du * att
    datt = (du * gate2).astype(bf).reshape(rows, cols, heads, size_head)
    dprob = jnp.einsum("ijhd,ikhd->ihjk", datt, values, preferred_element_type=fl)
    dvals = jnp.einsum("ihjk,ijhd->ikhd", p_low, datt, preferred_element_type=fl)
    dscore = (probs * (dprob - jnp.sum(dprob * probs, axis=-1, keepdims=True))).astype(bf)
    dquery = jnp.einsum("ihjk,ikhd->ijhd", dscore, keys, preferred_element_type=fl) * scale
    dkeys = jnp.einsum("ihjk,ijhd->ikhd", dscore, query, preferred_element_type=fl) * scale
    dtb = jnp.sum(dscore.astype(fl), axis=0)
    dtb_own = lax.psum_scatter(dtb, "row", scatter_dimension=1, tiled=True)
    dtb_low = jnp.transpose(dtb_own, (1, 2, 0)).astype(bf)
    dpbias = wgrad(h1b, dtb_low)
    dqkvg = jnp.concatenate(
        [
            dquery.reshape(rows, cols, width),
            dkeys.reshape(rows, cols, width),
            dvals.reshape(rows, cols, width),
            dgate2 * gate2 * (1.0 - gate2),
        ],
        axis=-1,
    ).astype(bf)
    dw_att = wgrad(h1b, dqkvg)
    dh1 = matmul(dqkvg, w_att.T) + matmul(dtb_low, pl.T)
    dn4, dg4, ds4 = norm_back(dh1, unit4, rstd4, norms[4])
    dz1 = dz2 + dn4
    dout1 = (dz1 * gate).astype(bf)
    dw5 = wgrad(y_low, dout1)
    dgate = dz1 * out1
    dxn, dg2, ds2 = norm_back(matmul(dout1, wl[5].T), unit2, rstd2, norms[2])
    dx_low = dxn.astype(bf)
    dside_a = jnp.einsum("ijc,jkc->ikc", dx_low, b_all, preferred_element_type=fl)
    dside_b = lax.psum_scatter(
        jnp.einsum("ijc,ikc->jkc", dx_low, a_low, preferred_element_type=fl),
        "row",
        scatter_dimension=0,
        tiled=True,
    )
    da_r = dside_a.astype(bf).astype(fl)
    db_r = dside_b.astype(bf).astype(fl)
    dproj = jnp.concatenate(
        [
            da_r * sig_a * m3,
            da_r * proj[..., :width] * m3 * sig_a * (1.0 - sig_a),
            db_r * sig_b * m3,
            db_r * proj[..., 2 * width : 3 * width] * m3 * sig_b * (1.0 - sig_b),
            dgate * gate * (1.0 - gate),
        ],
        axis=-1,
    ).astype(bf)
    dw_tri = wgrad(h0b, dproj)
    dh0 = matmul(dproj, w_tri.T)
    unused, dg0, ds0 = norm_back(dh0, unit0, rstd0, norms[0])
    pieces = [dw_tri[:, idx * width : (idx + 1) * width] for idx in range(5)]
    pieces = (
        pieces + [dw5] + [dw_att[:, idx * width : (idx + 1) * width] for idx in range(4)] + [dw10]
    )
    dmats = jnp.stack(pieces)
    dnorms = jnp.stack([dg0, ds0, dg2, ds2, dg4, ds4, dg6, ds6])
    dmats, dpbias, dhead, dnorms, loss, count = lax.psum(
        (dmats, dpbias, dhead, dnorms, loss, count), ("crop", "row")
    )
    grad_norm = jnp.sqrt(
        jnp.sum(dmats * dmats)
        + jnp.sum(dpbias * dpbias)
        + jnp.sum(dhead * dhead)
        + jnp.sum(dnorms * dnorms)
    )
    factor = jnp.minimum(1.0, CLIP / grad_norm)
    new_mats = adam(mats, dmats * factor, mats_m, mats_v)
    new_pbias = adam(pbias, dpbias * factor, pbias_m, pbias_v)
    new_head = adam(head, dhead * factor, head_m, head_v)
    new_norms = adam(norms, dnorms * factor, norms_m, norms_v)
    return (
        grad_norm,
        loss,
        count,
        new_mats[0],
        new_mats[1],
        new_mats[2],
        new_mats[2].astype(bf),
        new_pbias[0],
        new_pbias[1],
        new_pbias[2],
        new_head[0],
        new_head[1],
        new_head[2],
        new_norms[0],
        new_norms[1],
        new_norms[2],
    )


BF = jnp.bfloat16
FL = jnp.float32
VMEM_LIMIT = 24 * 2**20
SPAN = 2.0**-12
DIGIT = 64


def dot(lhs, rhs, left=1, right=0):
    return lax.dot_general(
        lhs, rhs, (((left,), (right,)), ((), ())), preferred_element_type=FL
    )


def lane_sums(val):
    return jnp.sum(val.T, axis=0, keepdims=True)


def row_norm(val, gain, shift):
    mean = jnp.mean(val, axis=-1, keepdims=True)
    cent = val - mean
    rstd = lax.rsqrt(jnp.mean(cent * cent, axis=-1, keepdims=True) + EPS_NORM)
    unit = cent * rstd
    return (unit * gain + shift).astype(BF), unit, rstd


def row_norm_back(grad, unit, rstd, gain):
    dgain = jnp.sum(grad * unit, axis=0, keepdims=True)
    dshift = jnp.sum(grad, axis=0, keepdims=True)
    dunit = grad * gain
    dval = rstd * (
        dunit
        - jnp.mean(dunit, axis=-1, keepdims=True)
        - unit * jnp.mean(dunit * unit, axis=-1, keepdims=True)
    )
    return dval, dgain, dshift


def iota(shape, dim):
    return lax.broadcasted_iota(jnp.int32, shape, dim)


def fetch(pairs, sems):
    moves = [
        pltpu.make_async_copy(src, dst, sems.at[idx]) for idx, (src, dst) in enumerate(pairs)
    ]
    for move in moves:
        move.start()
    return moves


def start_kernel(
    pair_hbm, norms_hbm, mats_hbm, h0_ref, wl_ref, pair_ref, norms_ref, mats_ref, sems
):
    moves = fetch(
        [(pair_hbm, pair_ref), (norms_hbm, norms_ref), (mats_hbm, mats_ref)], sems
    )
    moves[0].wait()
    moves[1].wait()
    h0_ref[...], _, _ = row_norm(pair_ref[...], norms_ref[0:1], norms_ref[1:2])
    moves[2].wait()
    wl_ref[...] = mats_ref[...].astype(BF)


def block_groups(chips):
    half = chips // 2
    late = [flip for flip in range(chips) if flip % half]
    return (
        [(flip, other) for other in range(2) for flip in (0, half)] + [(flip, 0) for flip in late],
        [(flip, 1) for flip in late],
    )


def block_at(scal_ref, tag):
    core = scal_ref[3, 0]
    return 2 * (scal_ref[2, 0] ^ tag[0]) + (1 - core if tag[1] else core)


def pair_mask(dims, limit):
    rows, cols, width, _, _ = dims
    spot = iota((rows * cols, width), 0)
    col_ok = spot % cols < limit
    row_in = spot // cols

    def mask_of(block_row):
        return jnp.where(jnp.logical_and(col_ok, row_in + block_row < limit), 1.0, 0.0).astype(FL)

    return mask_of


def own_sides(h0, wl_ref, mask):
    width = h0.shape[1]
    w_own = jnp.concatenate([wl_ref[0], wl_ref[1], wl_ref[4]], axis=1)
    proj = dot(h0, w_own)
    fac = jax.nn.sigmoid(proj[:, width : 2 * width]) * mask
    return fac * proj[:, :width], fac, jax.nn.sigmoid(proj[:, 2 * width :])


def b_block(dims, h0, w_b, col_mask, start, limit):
    rows, cols, width, _, _ = dims
    proj = dot(h0, w_b)
    sig = jax.nn.sigmoid(proj[:, width:])
    lines = []
    for row in range(rows):
        row_ok = jnp.where(start + row < limit, 1.0, 0.0).astype(FL)
        lines.append(sig[row * cols : (row + 1) * cols] * (col_mask * row_ok))
    fac = jnp.concatenate(lines, axis=0)
    return (fac * proj[:, :width]).astype(BF), fac.astype(BF)


def col_mask_of(dims, limit):
    _, cols, width, _, _ = dims
    return jnp.where(iota((cols, width), 0) < limit, 1.0, 0.0).astype(FL)


def x_products(dims, a_rows, side, put):
    rows, cols, width, _, _ = dims
    for row in range(rows):
        b_j = side[row * cols : (row + 1) * cols].astype(FL)
        for idx in range(rows):
            put(idx, row, jnp.sum((a_rows[idx] * b_j).reshape(cols // 8, 8, width), axis=0))


def blocks_kernel(dims, tags, scal_ref, wl_ref, *refs):
    first = tags[0] == (0, 0)
    if not first:
        a_ref, *refs = refs
    h0_refs, refs = refs[: len(tags)], refs[len(tags) :]
    part_ref, side_ref, fac_ref, *refs = refs
    if first:
        a_ref, gate_ref = refs
    rows, cols, width, heads, size = dims
    limit = scal_ref[0, 0]
    if first:
        mask = pair_mask(dims, limit)(scal_ref[1, 0])
        side, _, gate_ref[...] = own_sides(h0_refs[0][...], wl_ref, mask)
        a_ref[...] = side.astype(BF).astype(FL)
    a_rows = [a_ref[idx * cols : (idx + 1) * cols, :] for idx in range(rows)]
    col_mask = col_mask_of(dims, limit)
    w_b = jnp.concatenate([wl_ref[2], wl_ref[3]], axis=1)
    for idx, tag in enumerate(tags):
        start = block_at(scal_ref, tag) * rows
        side, fac = b_block(dims, h0_refs[idx][...], w_b, col_mask, start, limit)
        side_ref[idx] = side
        fac_ref[idx] = fac

        def put(at, row, fold, idx=idx):
            part_ref[at, idx, row * 8 : (row + 1) * 8, :] = fold

        x_products(dims, a_rows, side, put)


def triangle_kernel(
    dims, groups, scal_ref, a_ref, gate_ref, wl_ref, pair_hbm, norms_hbm, pbt_hbm, *refs
):
    tags, before = groups[-1], groups[:-1]
    count = len(before)
    part_refs, side_refs, fac_refs = (refs[at * count : (at + 1) * count] for at in range(3))
    refs = refs[3 * count :]
    h0_refs, refs = refs[: len(tags)], refs[len(tags) :]
    side_hbms, fac_hbms, refs = refs[: count + 1], refs[count + 1 : 2 * count + 2], refs[2 * count + 2 :]
    tb_ref, x_ref, z1_ref, h1_ref, *refs = refs
    pair_ref, norms_ref, pbt_ref, side_ref, fac_ref, part_ref, sems = refs
    rows, cols, width, heads, size = dims
    pairs = rows * cols
    limit = scal_ref[0, 0]
    early_moves = fetch(
        [(norms_hbm, norms_ref), (pair_hbm, pair_ref), (pbt_hbm, pbt_ref)],
        sems.at[pl.ds(0, 3)],
    )
    moves = fetch(
        [*zip(side_refs, side_hbms), *zip(fac_refs, fac_hbms)], sems.at[pl.ds(3, 2 * count)]
    )
    col_mask = col_mask_of(dims, limit)
    w_b = jnp.concatenate([wl_ref[2], wl_ref[3]], axis=1)
    a_rows = [a_ref[idx * cols : (idx + 1) * cols, :] for idx in range(rows)]

    for idx, tag in enumerate(tags):
        block = block_at(scal_ref, tag)
        side, fac = b_block(dims, h0_refs[idx][...], w_b, col_mask, block * rows, limit)
        side_ref[idx] = side
        fac_ref[idx] = fac

        def put(at, row, fold, block=block):
            start = pl.multiple_of((at * cols + block * rows + row) * 8, 8)
            part_ref[pl.ds(start, 8), :] = fold

        x_products(dims, a_rows, side, put)
    moves += fetch(
        [(side_ref, side_hbms[-1]), (fac_ref, fac_hbms[-1])], sems.at[pl.ds(3 + 2 * count, 2)]
    )
    for group, ref in zip(before, part_refs):
        for idx, tag in enumerate(group):
            for at in range(rows):
                start = pl.multiple_of(
                    (at * cols + block_at(scal_ref, tag) * rows) * 8, 8 * rows
                )
                part_ref[pl.ds(start, 8 * rows), :] = ref[at, idx]
    x_val = part_ref[pl.ds(0, pairs, stride=8), :]
    for idx in range(1, 8):
        x_val = x_val + part_ref[pl.ds(idx, pairs, stride=8), :]

    x_ref[...] = x_val
    for move in early_moves:
        move.wait()
    y_low, _, _ = row_norm(x_val, norms_ref[2:3], norms_ref[3:4])
    z1 = pair_ref[...] + gate_ref[...] * dot(y_low, wl_ref[5])
    z1_ref[...] = z1
    h1, _, _ = row_norm(z1, norms_ref[4:5], norms_ref[5:6])
    h1_ref[...] = h1
    tbt = dot(pbt_ref[...].astype(BF), h1, 1, 1).astype(BF).astype(FL)
    half = pairs // 2
    block = jnp.concatenate([tbt[:, :half], tbt[:, half:]], axis=0)
    for idx in range(size):
        tb_ref[idx] = block
    for move in moves:
        move.wait()


def diagonal_block(first, second):
    zero = jnp.zeros(first.shape, first.dtype)
    return jnp.concatenate(
        [
            jnp.concatenate([first, zero], axis=1),
            jnp.concatenate([zero, second], axis=1),
        ],
        axis=0,
    )


def pack_places(dims):
    rows, cols, width, heads, _ = dims
    pairs, lines = rows * cols, heads * cols
    at, places = 0, {}
    for name, tall in (
        ("prob", rows // 2 * lines),
        ("dscore", rows // 2 * lines),
        ("datt", pairs),
        ("u", pairs),
        ("dout2", pairs),
        ("dgate2", pairs),
        ("h2", pairs),
        ("dlog", 2 * cols),
    ):
        places[name] = at
        at += tall
    return places, at


def lane_ramp(width):
    return 1.0 + iota((1, width), 1).astype(FL) / width


def norm_line(small_ref, idx):
    at = small_ref.shape[1] - 8 + idx
    return small_ref[0, at : at + 1, :]


def attention_kernel(
    dims,
    scal_ref,
    tb_ref,
    h1_ref,
    z1_ref,
    wl_ref,
    bins_hbm,
    pb_hbm,
    pb_m_hbm,
    pb_v_hbm,
    head_hbm,
    head_m_hbm,
    head_v_hbm,
    norms_hbm,
    norms_m_hbm,
    norms_v_hbm,
    dtb_ref,
    pack_ref,
    dz2_ref,
    stat_ref,
    kcat_ref,
    qblk_ref,
    pb_ref,
    small_ref,
    vcat_ref,
    bias_ref,
    prob_ref,
    swap_ref,
    bins_ref,
    sems,
):
    rows, cols, width, heads, size = dims
    pairs, lines = rows * cols, heads * cols
    places, _ = pack_places(dims)
    scale = (width // heads) ** (-0.5)
    limit, first_row = scal_ref[0, 0], scal_ref[1, 0]

    def put(name, val):
        pack_ref[places[name] : places[name] + val.shape[0], :] = val

    bins_n = head_hbm.shape[0]
    moves = [(bins_hbm, bins_ref)]
    for idx, (pb, head, norms) in enumerate(
        (
            (pb_hbm, head_hbm, norms_hbm),
            (pb_m_hbm, head_m_hbm, norms_m_hbm),
            (pb_v_hbm, head_v_hbm, norms_v_hbm),
        )
    ):
        moves += [
            (head, small_ref.at[idx, pl.ds(0, bins_n)]),
            (norms, small_ref.at[idx, pl.ds(bins_n, 8)]),
            (pb, pb_ref.at[idx]),
        ]
    moves = fetch(moves, sems)
    w_att = jnp.concatenate([wl_ref[6], wl_ref[7], wl_ref[8], wl_ref[9]], axis=1)
    proj = dot(h1_ref[...], w_att)
    gate2 = jax.nn.sigmoid(proj[:, 3 * width :])
    lane_head = iota((cols, width), 1) // (width // heads)
    zero = jnp.zeros((cols, width), BF)
    for idx in range(rows):
        at, side = idx // 2, idx % 2
        lanes = slice(side * width, (side + 1) * width)
        span = slice(idx * cols, (idx + 1) * cols)
        query = proj[span, :width].astype(BF)
        qblk_ref[at, side * cols : (side + 1) * cols, lanes] = query
        qblk_ref[at, (1 - side) * cols : (2 - side) * cols, lanes] = zero
        for head in range(heads):
            spot = slice(head * cols, (head + 1) * cols)
            keep = lane_head == head
            kcat_ref[at, spot, lanes] = jnp.where(
                keep, proj[span, width : 2 * width], 0.0
            ).astype(BF)
            vcat_ref[at, spot, lanes] = jnp.where(
                keep, proj[span, 2 * width : 3 * width], 0.0
            ).astype(BF)

    for half in range(2):
        for jl in range(2):
            lanes = slice(jl * cols, (jl + 1) * cols)
            got = [
                tb_ref[pl.ds(half * heads + head, size, stride=2 * heads), :][:, lanes]
                for head in range(heads)
            ]
            for duo in range(heads // 2):
                line = jnp.concatenate([got[2 * duo], got[2 * duo + 1]], axis=1)
                bias_ref[duo, pl.ds(2 * half + jl, size, stride=rows), :] = line
                bias_ref[duo, pl.ds(cols + 2 * half + jl, size, stride=rows), :] = line
    bias = jnp.concatenate([bias_ref[duo].T for duo in range(heads // 2)], axis=0)
    key_ok = iota((lines, 2 * cols), 0) % cols < limit
    att = []
    for at in range(rows // 2):
        score = dot(kcat_ref[at], qblk_ref[at], 1, 1) * scale + bias
        score = jnp.where(key_ok, score, -1000000000.0).reshape(heads, cols, 2 * cols)
        top = jnp.max(score, axis=1, keepdims=True)
        grown = jnp.exp(score - top)
        prob = (grown / jnp.sum(grown, axis=1, keepdims=True)).reshape(lines, 2 * cols)
        prob_ref[at] = prob
        low = prob.astype(BF)
        pack_ref[places["prob"] + at * lines : places["prob"] + (at + 1) * lines, :] = low
        both = dot(low, vcat_ref[at], 0, 0)
        att += [both[:cols, :width], both[cols:, width:]]
    att = jnp.concatenate(att, axis=0)
    u_low = (gate2 * att).astype(BF)
    put("u", u_low)
    z2 = z1_ref[...] + dot(u_low, wl_ref[10])
    for move in moves[:3]:
        move.wait()
    h2, unit6, rstd6 = row_norm(z2, norm_line(small_ref, 6), norm_line(small_ref, 7))
    put("h2", h2)
    headt = small_ref[0, :bins_n, :].astype(BF)
    logits = dot(headt, h2, 1, 1)
    spot = iota((1, pairs), 1)
    ok = jnp.logical_and(spot % cols < limit, spot // cols + first_row < limit)
    mask = jnp.where(ok, 1.0, 0.0).astype(FL)
    bins = jnp.concatenate([bins_ref[idx : idx + 1, :] for idx in range(rows)], axis=1)
    onehot = jnp.where(iota(logits.shape, 0) == bins, 1.0, 0.0).astype(FL)
    top = jnp.max(logits, axis=0, keepdims=True)
    lse = top + jnp.log(jnp.sum(jnp.exp(logits - top), axis=0, keepdims=True))
    pick = jnp.sum(logits * onehot, axis=0, keepdims=True)
    loss = jnp.sum(mask * (lse - pick), axis=1, keepdims=True)
    dlog = (mask * (jnp.exp(logits - lse) - onehot)).astype(BF)
    put("dlog", jnp.concatenate([dlog[:, :width], dlog[:, width:]], axis=0))
    dz2, dg6, ds6 = row_norm_back(dot(dlog, headt, 0, 0), unit6, rstd6, norm_line(small_ref, 6))
    dz2_ref[...] = dz2
    stat_ref[0:1, :] = dg6
    stat_ref[1:2, :] = ds6
    used = limit * limit
    ramp = lane_ramp(width)
    stat_ref[2:3, :] = loss * ramp
    stat_ref[3:4, :] = (used // DIGIT).astype(FL) * ramp
    stat_ref[4:5, :] = (used % DIGIT).astype(FL) * ramp
    stat_ref[5:8, :] = jnp.zeros((3, width), FL)
    dout2 = dz2.astype(BF)
    put("dout2", dout2)
    du = dot(dout2, wl_ref[10], 1, 1)
    put("dgate2", (du * att * gate2 * (1.0 - gate2)).astype(BF))
    datt = (du * gate2).astype(BF)
    put("datt", datt)
    total = None
    for at in range(rows // 2):
        first = datt[(2 * at) * cols : (2 * at + 1) * cols]
        second = datt[(2 * at + 1) * cols : (2 * at + 2) * cols]
        block = diagonal_block(first, second)
        dprob = dot(vcat_ref[at], block, 1, 1)
        prob = prob_ref[at]
        inner = jnp.sum((dprob * prob).reshape(heads, cols, 2 * cols), axis=1, keepdims=True)
        dscore = prob.reshape(heads, cols, 2 * cols) * (
            dprob.reshape(heads, cols, 2 * cols) - inner
        )
        low = dscore.reshape(lines, 2 * cols).astype(BF)
        pack_ref[places["dscore"] + at * lines : places["dscore"] + (at + 1) * lines, :] = low
        total = low.astype(FL) if total is None else total + low.astype(FL)
    for duo in range(heads // 2):
        turned = total[duo * 2 * cols : (duo + 1) * 2 * cols].T
        swap_ref[duo] = turned[:cols] + turned[cols:]
    for half in range(2):
        for head in range(heads):
            inside = slice((head % 2) * cols, (head % 2 + 1) * cols)
            line = jnp.concatenate(
                [
                    swap_ref[head // 2, pl.ds(2 * half + jl, size, stride=rows), :][:, inside]
                    for jl in range(2)
                ],
                axis=1,
            )
            dtb_ref[pl.ds(half * heads + head, size, stride=2 * heads), :] = line
    for move in moves[3:]:
        move.wait()


def gradient_kernel(
    dims,
    groups,
    scal_ref,
    dtb_ref,
    pack_ref,
    kcat_ref,
    qblk_ref,
    dz2_ref,
    stat_ref,
    h1_ref,
    x_ref,
    z1_ref,
    small_ref,
    wl_ref,
    pb_ref,
    *refs,
):
    tags = [tag for group in groups for tag in group]
    h0_refs, refs = refs[: len(tags)], refs[len(tags) :]
    count = len(groups)
    side_hbms, fac_hbms, refs = refs[:count], refs[count : 2 * count], refs[2 * count :]
    keep_ref, give_ref, flat_ref, dx_ref, dqkvg_ref, side_ref, fac_ref, sems = refs
    rows, cols, width, heads, size = dims
    pairs = rows * cols
    core = scal_ref[3, 0]
    moves = []
    for arrays, ref in ((side_hbms, side_ref), (fac_hbms, fac_ref)):
        at = 0
        for group, array in zip(groups, arrays):
            moves.append((array, ref.at[pl.ds(at, len(group))]))
            at += len(group)
    moves = fetch(moves, sems)
    lines = heads * cols
    places, _ = pack_places(dims)

    def take(name, tall, skip=0):
        return pack_ref[places[name] + skip : places[name] + skip + tall, :]

    mask = pair_mask(dims, scal_ref[0, 0])(scal_ref[1, 0])
    side, fac, gate = own_sides(h0_refs[0][...], wl_ref, mask)
    a_val = side.astype(BF).astype(FL)
    y_low, unit2, rstd2 = row_norm(x_ref[...], norm_line(small_ref, 2), norm_line(small_ref, 3))
    _, unit4, rstd4 = row_norm(z1_ref[...], norm_line(small_ref, 4), norm_line(small_ref, 5))
    out1 = dot(y_low, wl_ref[5])
    scale = (width // heads) ** (-0.5)
    lane_head = iota((cols, width), 1) // (width // heads)

    def diagonal(val):
        out = jnp.zeros((cols, width), FL)
        for head in range(heads):
            out = jnp.where(lane_head == head, val[head * cols : (head + 1) * cols], out)
        return out

    for at in range(rows // 2):
        dscore = take("dscore", lines, at * lines)
        block = diagonal_block(
            take("datt", cols, 2 * at * cols), take("datt", cols, (2 * at + 1) * cols)
        )
        dquery = dot(dscore, kcat_ref[at], 0, 0)
        dkeys = dot(dscore, qblk_ref[at])
        dvals = dot(take("prob", lines, at * lines), block)
        for side in range(2):
            idx = 2 * at + side
            lanes = slice(side * width, (side + 1) * width)
            span = slice(idx * cols, (idx + 1) * cols)
            dqkvg_ref[span, :width] = (
                dquery[side * cols : (side + 1) * cols, lanes] * scale
            ).astype(BF)
            dqkvg_ref[span, width : 2 * width] = (diagonal(dkeys[:, lanes]) * scale).astype(BF)
            dqkvg_ref[span, 2 * width : 3 * width] = diagonal(dvals[:, lanes]).astype(BF)
    dqkvg_ref[:, 3 * width :] = take("dgate2", pairs)
    dqkvg = dqkvg_ref[...]
    w_att = jnp.concatenate([wl_ref[6], wl_ref[7], wl_ref[8], wl_ref[9]], axis=1)
    dh1 = dot(dqkvg, w_att, 1, 1)
    h1 = h1_ref[...]
    dw_att = dot(h1, dqkvg, 0, 0)
    for idx in range(4):
        flat_ref[(6 + idx) * width : (7 + idx) * width, :] = dw_att[
            :, idx * width : (idx + 1) * width
        ]
    flat_ref[10 * width : 11 * width, :] = dot(take("u", pairs), take("dout2", pairs), 0, 0)
    mats = 11 * width
    dlog = take("dlog", 2 * cols)
    dlog = jnp.concatenate([dlog[:cols], dlog[cols:]], axis=1)
    flat_ref[mats : mats + dlog.shape[0], :] = dot(dlog, take("h2", pairs))
    got = dtb_ref[0]
    for idx in range(1, size):
        got = got + dtb_ref[idx]
    dtbt = jnp.concatenate([got[:heads], got[heads:]], axis=1).astype(BF)
    dpbt = dot(dtbt, h1)
    dh1 = dh1 + dot(dtbt, pb_ref[0].astype(BF), 0, 0)
    dn4, dg4, ds4 = row_norm_back(dh1, unit4, rstd4, norm_line(small_ref, 4))
    dz1 = dz2_ref[...] + dn4
    dout1 = (dz1 * gate).astype(BF)
    dgate = dz1 * out1 * gate * (1.0 - gate)
    dx, dg2, ds2 = row_norm_back(dot(dout1, wl_ref[5], 1, 1), unit2, rstd2, norm_line(small_ref, 2))
    dx_ref[...] = dx.astype(BF).astype(FL)

    for move in moves[:count]:
        move.wait()
    acc = [jnp.zeros((cols, width), FL)] * rows
    for idx, tag in enumerate(tags):
        first = block_at(scal_ref, tag) * rows
        for row in range(rows):
            b_j = side_ref[idx, row * cols : (row + 1) * cols, :].astype(FL)
            acc = [
                acc[at] + dx_ref[pl.ds(at * cols + first + row, 1), :] * b_j
                for at in range(rows)
            ]
    da = jnp.concatenate(acc, axis=0).astype(BF).astype(FL)
    own = jnp.concatenate(
        [
            (da * fac).astype(BF),
            (da * a_val * (1.0 - fac)).astype(BF),
            dgate.astype(BF),
        ],
        axis=1,
    )
    for move in moves[count:]:
        move.wait()
    ones = jnp.ones((16, pairs), BF)

    def products(h0, grads):
        return dot(h0, grads, 0, 0), dot(ones, grads)

    dw_own, sum_own = products(h0_refs[0][...], own)

    a_rows = [a_val[idx * cols : (idx + 1) * cols] for idx in range(rows)]

    dw_b, sum_b = jnp.zeros((width, 2 * width), FL), jnp.zeros((16, 2 * width), FL)
    for idx, tag in enumerate(tags):
        first = block_at(scal_ref, tag) * rows
        lines = []
        for row in range(rows):
            db = dx_ref[pl.ds(first + row, 1), :] * a_rows[0]
            for at in range(1, rows):
                db = db + dx_ref[pl.ds(at * cols + first + row, 1), :] * a_rows[at]
            lines.append(db.astype(BF))
        db = jnp.concatenate(lines, axis=0)
        fac_b = fac_ref[idx]
        grads = jnp.concatenate([db * fac_b, db * (side_ref[idx] * (1.0 - fac_b))], axis=1)
        main, sums = products(h0_refs[idx][...], grads)
        dw_b, sum_b = dw_b + main, sum_b + sums

    parts = [
        (val[:, at * width : (at + 1) * width], sums[:1, at * width : (at + 1) * width])
        for val, sums, at in (
            (dw_own, sum_own, 0),
            (dw_own, sum_own, 1),
            (dw_b, sum_b, 0),
            (dw_b, sum_b, 1),
            (dw_own, sum_own, 2),
        )
    ]
    mixed = jnp.zeros((width, width), FL)
    summed = jnp.zeros((width, width), FL)
    for idx, (part, sums) in enumerate(parts):
        weight = wl_ref[idx].astype(FL)
        flat_ref[idx * width : (idx + 1) * width, :] = part
        mixed = mixed + weight * part
        summed = summed + weight * sums
    ds0 = lane_sums(summed)
    dg0 = (lane_sums(mixed) - norm_line(small_ref, 1) * ds0) / norm_line(small_ref, 0)
    flat_ref[5 * width : 6 * width, :] = dot(y_low, dout1, 0, 0)
    base = mats + dlog.shape[0]
    flat_ref[base : base + heads, :] = dpbt
    flat_ref[base + heads : base + 8, :] = jnp.zeros((8 - heads, width), FL)
    base += 8
    for idx, line in enumerate((dg0, ds0, dg2, ds2, dg4, ds4)):
        flat_ref[base + idx : base + idx + 1, :] = line
    flat_ref[base + 6 : base + 11, :] = stat_ref[0:5, :]
    total = flat_ref.shape[0]
    flat_ref[base + 11 :, :] = jnp.zeros((total - base - 11, width), FL)
    half = total // 2
    keep_ref[...] = flat_ref[pl.ds(pl.multiple_of(core * half, half), half), :]
    give_ref[...] = flat_ref[pl.ds(pl.multiple_of((1 - core) * half, half), half), :]


def update_kernel(
    dims,
    scal_ref,
    mine_ref,
    other_ref,
    mats_ref,
    mats_m_ref,
    mats_v_ref,
    pb_ref,
    small_ref,
    norm_out,
    loss_out,
    count_out,
    mats_m_out,
    mats_v_out,
    mats_out,
    mats_low_out,
    pb_m_out,
    pb_v_out,
    pb_out,
    head_m_out,
    head_v_out,
    head_out,
    norms_m_out,
    norms_v_out,
    norms_out,
    flat_ref,
    scalar_buf,
    small_buf,
    pb_buf,
    m_buf,
    v_buf,
    w_buf,
    low_buf,
    sems,
    small_sems,
):
    rows, cols, width, heads, size = dims
    bins_n = small_ref.shape[1] - 8
    core = scal_ref[3, 0]
    half = mine_ref.shape[0]
    flat_ref[pl.ds(pl.multiple_of(core * half, half), half), :] = mine_ref[...]
    flat_ref[pl.ds(pl.multiple_of((1 - core) * half, half), half), :] = other_ref[...]
    count = mats_ref.shape[0]
    mats = count * width
    base = mats + bins_n
    grads = flat_ref[: base + 16, :]
    square = jnp.sum(grads * grads, axis=0, keepdims=True)
    norm = jnp.sqrt(jnp.sum(square, axis=1, keepdims=True))
    factor = jnp.minimum(1.0, CLIP / norm)
    scalar_buf[0] = norm
    stats = jnp.mean(
        flat_ref[base + 16 : base + 24, :] / lane_ramp(width), axis=1, keepdims=True
    )
    scalar_buf[1] = stats[0:1]
    scalar_buf[2] = (DIGIT * jnp.round(stats[1:2]) + jnp.round(stats[2:3])) / size

    moves = []

    def send(at, idx, buf, out):
        move = pltpu.make_async_copy(buf.at[idx], out.at[idx], sems.at[at, idx])
        move.start()
        moves.append(move)

    def step(weight, grad, first, second):
        return adam(weight, grad * factor, first, second)

    def update_small():
        triples = []
        for at, tall, buf, ref, skip, outs in (
            (mats, bins_n, small_buf, small_ref, 0, (head_m_out, head_v_out, head_out)),
            (base + 8, 8, small_buf, small_ref, bins_n, (norms_m_out, norms_v_out, norms_out)),
            (base, heads, pb_buf, pb_ref, 0, (pb_m_out, pb_v_out, pb_out)),
        ):
            weight, first, second = (ref[idx, skip : skip + tall, :] for idx in range(3))
            now = step(weight, flat_ref[at : at + tall, :], first, second)
            for idx, (val, out) in enumerate(zip(now, outs)):
                buf[idx, skip : skip + tall, :] = val
                triples.append((buf.at[idx, pl.ds(skip, tall)], out))
        triples += [
            (scalar_buf.at[idx], out) for idx, out in enumerate((norm_out, loss_out, count_out))
        ]
        moves.extend(fetch(triples, small_sems))

    for idx in range(count):
        if idx == count // 2:
            update_small()
        m_buf[idx], v_buf[idx], weight = step(
            mats_ref[idx],
            flat_ref[idx * width : (idx + 1) * width, :],
            mats_m_ref[idx],
            mats_v_ref[idx],
        )
        w_buf[idx] = weight
        low_buf[idx] = weight.astype(BF)
        send(0, idx, m_buf, mats_m_out)
        send(1, idx, v_buf, mats_v_out)
        send(2, idx, w_buf, mats_out)
        send(3, idx, low_buf, mats_low_out)
    for move in moves:
        move.wait()


def call(kernel, args, outs, scratch=(), limit=VMEM_LIMIT, flops=10**7):
    spots = {"v": pltpu.VMEM, "h": pltpu.HBM}
    return pl.pallas_call(
        kernel,
        out_shape=[
            pltpu.HBM(shape, kind) if spot == "h" else jax.ShapeDtypeStruct(shape, kind)
            for shape, kind, spot in outs
        ],
        in_specs=[pl.BlockSpec(memory_space=spots[spot]) for _, spot in args],
        out_specs=[pl.BlockSpec(memory_space=spots[spot]) for _, _, spot in outs],
        scratch_shapes=list(scratch),
        compiler_params=pltpu.CompilerParams(vmem_limit_bytes=limit),
        cost_estimate=pl.CostEstimate(flops=flops, bytes_accessed=10**6, transcendentals=0),
    )(
        *(
            pltpu.with_memory_space_constraint(value, pltpu.HBM) if spot == "h" else value
            for value, spot in args
        )
    )


def shrink(val):
    root = jnp.sqrt(jnp.abs(val) * SPAN)
    return jnp.where(val < 0.0, -root, root).astype(jnp.float16)


def grow(root):
    root = root.astype(FL)
    return root * jnp.abs(root) * (1.0 / SPAN)


def same_core_groups(crops, size):
    return [
        [crop * size + idx for crop in range(crops) for idx in range(core, size, 2)]
        for core in range(2)
    ]


def exchange(value, size, flip):
    return lax.ppermute(value, "row", [(idx, idx ^ flip) for idx in range(size)])


def core_swap(value, size):
    return exchange(value, size, 1)


def fast_step(
    crops,
    size,
    pair,
    bins,
    lengths,
    mats,
    mats_m,
    mats_v,
    pbias,
    pbias_m,
    pbias_v,
    head,
    head_m,
    head_v,
    norms,
    norms_m,
    norms_v,
):
    rows, cols, width = pair.shape[1:]
    heads, bins_n = pbias.shape[1], head.shape[1]
    pairs, lines = rows * cols, heads * cols
    dims = (rows, cols, width, heads, size)
    chips = size // 2
    place = lax.axis_index("row")
    scal = jnp.stack([lengths[0], place * rows, place >> 1, place & 1]).astype(jnp.int32)
    scal = jnp.broadcast_to(jnp.pad(scal, (0, 4))[:, None], (8, width))
    start = pair.reshape(pairs, width)
    pbt, headt = pbias.T, head.T

    h0, wl = call(
        start_kernel,
        [(start, "h"), (norms, "h"), (mats, "h")],
        [((pairs, width), BF, "v"), (mats.shape, BF, "v")],
        [
            pltpu.VMEM((pairs, width), FL),
            pltpu.VMEM(norms.shape, FL),
            pltpu.VMEM(mats.shape, FL),
            pltpu.SemaphoreType.DMA((3,)),
        ],
    )
    blocks = {(0, 0): h0}
    half = chips // 2
    blocks[half, 0] = exchange(h0, size, 2 * half)
    for flip in range(1, half):
        blocks[flip, 0] = exchange(h0, size, 2 * flip)
    for flip in range(1, half):
        blocks[half + flip, 0] = exchange(blocks[half, 0], size, 2 * flip)
    for flip in range(chips):
        blocks[flip, 1] = core_swap(blocks[flip, 0], size)
    groups = block_groups(chips)
    parts, sides, facs = [], [], []
    for at, tags in enumerate(groups[:-1]):
        shape = (len(tags), pairs, width)
        res = call(
            functools.partial(blocks_kernel, dims, tags),
            [(scal, "v"), (wl, "v")]
            + [(a_val, "v") for _ in range(at)]
            + [(blocks[tag], "v") for tag in tags],
            [((rows, len(tags), rows * 8, width), FL, "v"), (shape, BF, "v"), (shape, BF, "v")]
            + [((pairs, width), FL, "v")] * (2 - 2 * at),
            flops=10**8 * len(tags),
        )
        parts.append(res[0])
        sides.append(res[1])
        facs.append(res[2])
        if at == 0:
            a_val, gate = res[3:]
    shape = (len(groups[-1]), pairs, width)
    count = len(groups)
    *far_sides, tb, x_val, z1, h1 = call(
        functools.partial(triangle_kernel, dims, groups),
        [
            (scal, "v"),
            (a_val, "v"),
            (gate, "v"),
            (wl, "v"),
            (start, "h"),
            (norms, "h"),
            (pbt, "h"),
        ]
        + [(value, "v") for value in parts + sides + facs]
        + [(blocks[tag], "v") for tag in groups[-1]],
        [((len(tags), pairs, width), BF, "h") for tags in groups] * 2
        + [
            ((size, 2 * heads, 2 * cols), FL, "v"),
            ((pairs, width), FL, "v"),
            ((pairs, width), FL, "v"),
            ((pairs, width), BF, "v"),
        ],
        [
            pltpu.VMEM((pairs, width), FL),
            pltpu.VMEM(norms.shape, FL),
            pltpu.VMEM(pbt.shape, FL),
            pltpu.VMEM(shape, BF),
            pltpu.VMEM(shape, BF),
            pltpu.VMEM((pairs * 8, width), FL),
            pltpu.SemaphoreType.DMA((3 + 2 * count,)),
        ],
    )

    tb_all = lax.all_to_all(tb, "row", 0, 0, tiled=True)
    bias_shape = (size * 2 * heads, 2 * cols)
    small_args = (
        pbt,
        pbias_m.T,
        pbias_v.T,
        headt,
        head_m.T,
        head_v.T,
        norms,
        norms_m,
        norms_v,
    )
    dtb, pack, dz2, stat, kcat, qblk, pb_all, small_all = call(
        functools.partial(attention_kernel, dims),
        [
            (scal, "v"),
            (tb_all.reshape(bias_shape), "v"),
            (h1, "v"),
            (z1, "v"),
            (wl, "v"),
            (bins[0], "h"),
        ]
        + [(value, "h") for value in small_args],
        [
            (bias_shape, FL, "v"),
            ((pack_places(dims)[1], width), BF, "v"),
            ((pairs, width), FL, "v"),
            ((8, width), FL, "v"),
            ((rows // 2, lines, 2 * width), BF, "v"),
            ((rows // 2, 2 * cols, 2 * width), BF, "v"),
            ((3, heads, width), FL, "v"),
            ((3, bins_n + norms.shape[0], width), FL, "v"),
        ],
        [
            pltpu.VMEM((rows // 2, lines, 2 * width), BF),
            pltpu.VMEM((heads // 2, 2 * cols, 2 * cols), FL),
            pltpu.VMEM((rows // 2, lines, 2 * cols), FL),
            pltpu.VMEM((heads // 2, cols, 2 * cols), FL),
            pltpu.VMEM((rows, cols), jnp.int32),
            pltpu.SemaphoreType.DMA((10,)),
        ],
    )

    dtb_all = lax.all_to_all(dtb.reshape(size, 2 * heads, 2 * cols), "row", 0, 0, tiled=True)
    used = mats.shape[0] * width + bins_n + 24
    unit = 8 * crops * size
    total = -(-used // unit) * unit
    keep, give = call(
        functools.partial(gradient_kernel, dims, groups),
        [(scal, "v")]
        + [
            (value, "v")
            for value in (dtb_all, pack, kcat, qblk, dz2, stat, h1, x_val, z1, small_all, wl, pb_all)
        ]
        + [(blocks[tag], "v") for tags in groups for tag in tags]
        + [(value, "h") for value in far_sides],
        [((total // 2, width), FL, "v"), ((total // 2, width), FL, "v")],
        [
            pltpu.VMEM((total, width), FL),
            pltpu.VMEM((pairs, width), FL),
            pltpu.VMEM((pairs, 4 * width), BF),
        ]
        + [pltpu.VMEM((size, pairs, width), BF)] * 2
        + [pltpu.SemaphoreType.DMA((2 * len(groups),))],
    )

    half = keep + grow(core_swap(shrink(give), size))
    count = crops * chips
    cores = same_core_groups(crops, size)
    axes = ("crop", "row")
    parts = lax.all_to_all(
        shrink(half).reshape(count, -1, width), axes, 0, 0, axis_index_groups=cores, tiled=True
    )
    share = shrink(jnp.sum(grow(parts), axis=0))
    spread = jnp.broadcast_to(share[None], (count,) + share.shape)
    mine = lax.all_to_all(spread, axes, 0, 0, axis_index_groups=cores, tiled=True)
    mine = mine.reshape(total // 2, width)
    other_half = grow(core_swap(mine, size))
    mine = grow(mine)

    number = mats.shape[0]
    big, low = ((number, width, width), FL, "h"), ((number, width, width), BF, "h")
    pb_out, head_out = ((heads, width), FL, "h"), ((bins_n, width), FL, "h")
    norm_out = ((norms.shape[0], width), FL, "h")
    res = call(
        functools.partial(update_kernel, dims),
        [(scal, "v")]
        + [
            (value, "v")
            for value in (mine, other_half, mats, mats_m, mats_v, pb_all, small_all)
        ],
        [((1, 1), FL, "h")] * 3
        + [big, big, big, low]
        + [pb_out] * 3
        + [head_out] * 3
        + [norm_out] * 3,
        [
            pltpu.VMEM((total, width), FL),
            pltpu.VMEM((3, 1, 1), FL),
            pltpu.VMEM((3, bins_n + norms.shape[0], width), FL),
            pltpu.VMEM((3, heads, width), FL),
        ]
        + [pltpu.VMEM((number, width, width), FL)] * 3
        + [
            pltpu.VMEM((number, width, width), BF),
            pltpu.SemaphoreType.DMA((4, number)),
            pltpu.SemaphoreType.DMA((12,)),
        ],
    )
    return (
        *(value.reshape(()) for value in res[:3]),
        *res[3:7],
        *(value.T for value in res[7:13]),
        *res[13:16],
    )


def small_enough(pair, heads, size):
    _, rows, cols, width = pair.shape
    held = 4 * size * rows * cols * width * 4 + 4 * rows * heads * cols * cols * 4
    return (
        held <= 2**24
        and width == 2 * cols
        and rows == 4
        and heads == 4
        and size >= 4
        and size & (size - 1) == 0
        and rows * size == cols
    )


def solution(mesh):
    crops, size = mesh.shape["crop"], mesh.shape["row"]

    def on_device(*args):
        if small_enough(args[0], args[6].shape[1], size):
            return fast_step(crops, size, *args)
        return general_step(*args)

    in_specs = (
        P("crop", "row", None, None),
        P("crop", "row", None),
        P("crop"),
        P(),
        P(),
        P(),
        P(),
        P(),
        P(),
        P(),
        P(),
        P(),
        P(),
        P(),
        P(),
    )
    out_specs = (P(), P(), P(), P(), P(), P(), P(), P(), P(), P(), P(), P(), P(), P(), P(), P())
    return jax.shard_map(
        on_device, mesh=mesh, in_specs=in_specs, out_specs=out_specs, check_vma=False
    )
```
